32 devices in a mesh: parts: 2 (over x), owner: 8 (over z, y), split: 2 (over core).
Axes of the slice: x: 2, y: 2, z: 4, core: 2. Of those that a mesh axis runs over, the one named last changes fastest.
Arguments:
- states: bfloat16 [16384, 1024], P(('parts', 'owner', 'split')), parts along dimension 0, may hold values from -6 to 6
- proj_weight: bfloat16 [1024, 768], replicated, may hold values from -0.1875 to 0.1875
- cluster_of: int32 [16384], P(('parts', 'owner', 'split')), parts along dimension 0, may hold values from 0 to 15, as said below
Outputs:
- score: float32 [16384], P(('parts', 'owner', 'split')), parts along dimension 0
The draws below stay inside these ranges and needn't reach their ends.
There are 2 independent parts, one for each index of `parts`. The reference program is written for one: setup_inputs(seed, part) draws one part's arguments, and reference() takes and returns one part's arrays. A program takes and returns all parts, laid end to end along the dimension named above; an argument that names none is the same for every part. Nothing has to cross between parts.
Inputs may be any that keep to these rules, and one draw needn't show every extreme that they name: Call cluster_of // 2 a document's group. Among the 512 documents of one device (aligned blocks in order) at most 192 fall in any one group, and one group, the same for every device of a part, holds exactly 192 of them on every device.
All inputs are finite; a program needn't handle non-finite values. Where the reference program divides by a largest or mean magnitude, that divisor is 1e-20 or more.
Results may differ from the reference program's by a relative error of at most 0.0003.
Values may be sent and summed in bfloat16 or wider, within the bound.
No kernel may reach another device: no remote copies, remote signals or barrier semaphores. Data moves between devices by JAX's collectives and lax.ppermute only.
A program may use at most 64 MiB of HBM per device.

```python
import math
import jax
import jax.numpy as jnp
from jax import lax

D_IN = 1024
D_OUT = 768
DOC_DEV = 512
CLUS_OWN = 2
CAP = 192
DOCS = 8192
N_OWNER = 8
N_SPLIT = 2


def draw_cluster_of(key, part):
    key = jax.random.fold_in(key, 11)
    hot_key, block_key = jax.random.split(key)
    hot_group = jax.random.randint(hot_key, (), 0, N_OWNER)
    block_keys = jax.random.split(block_key, N_OWNER * N_SPLIT)

    def one_device(dev_key):
        pick_key, order_key, within_key = jax.random.split(dev_key, 3)
        pool = jnp.arange((N_OWNER - 1) * CAP, dtype=jnp.int32) // CAP
        picked = jax.random.permutation(pick_key, pool)[:DOC_DEV - CAP]
        others = picked + (picked >= hot_group).astype(jnp.int32)
        groups = jnp.concatenate([jnp.zeros((CAP,), jnp.int32) + hot_group, others.astype(jnp.int32)])
        groups = jax.random.permutation(order_key, groups)
        within = jax.random.randint(within_key, (DOC_DEV,), 0, CLUS_OWN)
        return (groups * CLUS_OWN + within).astype(jnp.int32)
    return jax.vmap(one_device)(block_keys).reshape(-1)


def levels(stream_key, dims, cuts, low, high):
    level = 1.0
    for dim, blocks in cuts:
        steps = jax.random.uniform(jax.random.fold_in(jax.random.fold_in(stream_key, 6), dim), (blocks,), jnp.float32, low / len(cuts), high / len(cuts))
        level = level * jnp.repeat(jnp.exp(steps), dims[dim] // blocks).reshape((-1,) + (1,) * (len(dims) - 1 - dim))
    return level


def scatter_about(own_key, shape, spread, bound, cuts=(), kind=jnp.bfloat16):
    level = levels(own_key, shape, cuts, -0.22, 0.18) if cuts else 1.0
    array = jax.random.normal(own_key, shape, jnp.float32) * spread * level
    return jnp.minimum(jnp.maximum(array, -bound), bound).astype(kind)


def setup_inputs(seed: int = 0, part: int = 0) -> dict:
    splits = jax.random.split(jax.random.key(seed), 4)
    own_keys = jax.random.split(jax.random.fold_in(splits[3], part), 4)
    states = scatter_about(own_keys[0], (DOCS, D_IN), 1.0, 6.0, ((0, 16),))
    proj_weight = scatter_about(splits[1], (D_IN, D_OUT), D_IN ** -0.5, 0.1875)
    cluster_of = draw_cluster_of(jax.random.fold_in(jax.random.fold_in(splits[3], part), 71), part)
    return dict(states=states, proj_weight=proj_weight, cluster_of=cluster_of)


TAU = 0.05
THRESH = 0.2
EPS = 1e-06

def prepare(states, proj_weight):
    projected = jnp.dot(states, proj_weight, preferred_element_type=jnp.float32)
    unit = projected * lax.rsqrt(lax.optimization_barrier(jnp.sum(projected * projected, axis=1, keepdims=True)) + EPS)
    peak = lax.optimization_barrier(jnp.max(jnp.abs(unit), axis=1)).astype(jnp.bfloat16)
    quant = (unit / peak.astype(jnp.float32)[:, None]).astype(jnp.bfloat16)
    return (quant, peak)

def reference(states, proj_weight, cluster_of):
    quant, peak = prepare(states, proj_weight)
    scale = peak.astype(jnp.float32)
    doc_total = quant.shape[0]
    block = math.gcd(doc_total, 512)
    doc_index = jnp.arange(doc_total, dtype=jnp.int32)

    def one_block(start):
        quant_rows = lax.dynamic_slice_in_dim(quant, start, block, 0)
        scale_rows = lax.dynamic_slice_in_dim(scale, start, block, 0)
        cluster_rows = lax.dynamic_slice_in_dim(cluster_of, start, block, 0)
        index_rows = lax.dynamic_slice_in_dim(doc_index, start, block, 0)
        inner = lax.dot_general(quant_rows, quant, (((1,), (1,)), ((), ())), preferred_element_type=jnp.float32)
        cosine = inner * scale_rows[:, None] * scale[None, :]
        same = (cluster_rows[:, None] == cluster_of[None, :]) & (index_rows[:, None] != doc_index[None, :])
        weights = jnp.where(same, jnp.exp((cosine - THRESH) / TAU), jnp.zeros_like(cosine))
        return jnp.log(1.0 + lax.optimization_barrier(jnp.sum(weights, axis=1)))
    starts = jnp.arange(doc_total // block, dtype=jnp.int32) * block
    return lax.map(one_block, starts).reshape(doc_total)
```

```python
import math

import jax
import jax.numpy as jnp
from jax import lax
from jax.experimental import pallas as pl
from jax.experimental.pallas import tpu as pltpu
from jax.sharding import PartitionSpec as P

CLUS_OWN = 2
TAU = 0.05
THRESH = 0.2
EPS = 1e-06
LOG2E = math.log2(math.e)
SCALE = LOG2E / TAU
SHIFT = THRESH * LOG2E / TAU

ROWS = 2
F32 = jnp.float32
BF16 = jnp.bfloat16


def prepare(states, proj_weight):
    projected = jnp.dot(states, proj_weight, preferred_element_type=jnp.float32)
    unit = projected * lax.rsqrt(jnp.sum(projected * projected, axis=1, keepdims=True) + EPS)
    peak = jnp.max(jnp.abs(unit), axis=1).astype(jnp.bfloat16)
    quant = (unit / peak.astype(jnp.float32)[:, None]).astype(jnp.bfloat16)
    return (quant, peak)


def similarity_scores(
    own_quant, own_peak, own_cluster, own_index, col_quant, col_peak, col_cluster, col_index
):
    row_count = own_quant.shape[0]
    block = math.gcd(row_count, 768)
    col_scale = col_peak.astype(jnp.float32)

    def one_block(start):
        quant_rows = lax.dynamic_slice_in_dim(own_quant, start, block, 0)
        scale_rows = lax.dynamic_slice_in_dim(own_peak, start, block, 0).astype(jnp.float32)
        cluster_rows = lax.dynamic_slice_in_dim(own_cluster, start, block, 0)
        index_rows = lax.dynamic_slice_in_dim(own_index, start, block, 0)
        inner = lax.dot_general(
            quant_rows, col_quant, (((1,), (1,)), ((), ())), preferred_element_type=jnp.float32
        )
        cosine = inner * scale_rows[:, None] * col_scale[None, :]
        same = (cluster_rows[:, None] == col_cluster[None, :]) & (
            index_rows[:, None] != col_index[None, :]
        )
        weights = jnp.where(same, jnp.exp((cosine - THRESH) / TAU), jnp.zeros_like(cosine))
        return jnp.log(1.0 + jnp.sum(weights, axis=1))

    starts = jnp.arange(row_count // block, dtype=jnp.int32) * block
    return lax.map(one_block, starts).reshape(row_count)


def owner_plan(states, proj_weight, cluster_of):
    owners = lax.axis_size("owner")
    splits = lax.axis_size("split")
    half_index = lax.axis_index("split")
    doc_count = states.shape[0]
    capacity = 3 * doc_count // owners
    width = proj_weight.shape[1]
    slot_total = owners * capacity
    quant, peak = prepare(states, proj_weight)
    group_of = cluster_of // CLUS_OWN
    onehot = (group_of[:, None] == jnp.arange(owners, dtype=jnp.int32)[None, :]).astype(jnp.int32)
    before = jnp.cumsum(onehot, axis=0) - onehot
    target = group_of * capacity + jnp.sum(before * onehot, axis=1)
    quant_slots = (
        jnp.zeros((slot_total, width), jnp.bfloat16)
        .at[target]
        .set(quant)
        .reshape(owners, capacity, width)
    )
    peak_slots = (
        jnp.zeros((slot_total,), jnp.bfloat16).at[target].set(peak).reshape(owners, capacity)
    )
    cluster_slots = (
        jnp.full((slot_total,), -1, jnp.int32).at[target].set(cluster_of).reshape(owners, capacity)
    )
    positions = (
        jnp.arange(owners, dtype=jnp.int32)[:, None] * (splits * capacity)
        + jnp.arange(capacity, dtype=jnp.int32)[None, :]
    )
    own_index = (positions + half_index * capacity).reshape(slot_total)
    col_index = jnp.arange(splits * slot_total, dtype=jnp.int32)
    own_quant, own_peak, own_cluster = (
        lax.all_to_all(a, "owner", split_axis=0, concat_axis=0, tiled=True)
        for a in (quant_slots, peak_slots, cluster_slots)
    )
    all_quant, all_peak, all_cluster = (
        lax.all_gather(a, "split", axis=1, tiled=True) for a in (own_quant, own_peak, own_cluster)
    )
    scores = similarity_scores(
        own_quant.reshape(slot_total, width),
        own_peak.reshape(slot_total),
        own_cluster.reshape(slot_total),
        own_index,
        all_quant.reshape(splits * slot_total, width),
        all_peak.reshape(splits * slot_total),
        all_cluster.reshape(splits * slot_total),
        col_index,
    )
    returned = lax.all_to_all(
        scores.reshape(owners, capacity), "owner", split_axis=0, concat_axis=0, tiled=True
    )
    return returned.reshape(slot_total)[target]


def up(n, m):
    return -(-n // m) * m


def prep_kernel(hot, cl_ref, st_ref, w_ref, h_ref, n_ref, na_ref, nb_ref, meta_ref, slot_ref, quant, peaks):
    docs = st_ref.shape[0]
    half = na_ref.shape[0]
    first = up(hot, 128)
    lanes = meta_ref.shape[1]
    tile = 128

    cluster = cl_ref[...]
    group = cluster // CLUS_OWN
    kinds = lax.broadcasted_iota(jnp.int32, (8, docs), 0)
    member = kinds == group
    count = jnp.sum(member.astype(F32), axis=1, keepdims=True)
    full = count == float(hot)
    kind_col = lax.broadcasted_iota(jnp.int32, (8, 1), 0)
    chosen = jnp.min(jnp.where(full, kind_col, 8), axis=0, keepdims=True)
    doubt = jnp.where(jnp.sum(full.astype(F32), axis=0, keepdims=True) == 1.0, 0.0, 1.0)
    in_hot = group == chosen

    for t in range(docs // tile):
        rows = slice(t * tile, (t + 1) * tile)
        projected = jnp.dot(st_ref[rows, :], w_ref[...], preferred_element_type=F32)
        unit = projected * lax.rsqrt(jnp.sum(projected * projected, axis=1, keepdims=True) + EPS)
        peak = jnp.max(jnp.abs(unit), axis=1, keepdims=True).astype(BF16)
        quant[rows, :] = (unit / peak.astype(F32)).astype(BF16)
        peaks[rows, :] = jnp.broadcast_to(peak, (tile, 128))

    ahead = (
        lax.broadcasted_iota(jnp.int32, (docs, docs), 0) < lax.broadcasted_iota(jnp.int32, (docs, docs), 1)
    ).astype(F32).astype(BF16)
    hot_rows = jnp.broadcast_to(in_hot.astype(F32), (8, docs)).astype(BF16)
    rank = jnp.dot(hot_rows, ahead, preferred_element_type=F32)[0:1, :].astype(jnp.int32)
    place = lax.broadcasted_iota(jnp.int32, (1, docs), 1)
    slot = jnp.where(in_hot, rank, first + place - rank)
    slot_ref[...] = slot

    sort = (lax.broadcasted_iota(jnp.int32, (lanes, docs), 0) == slot).astype(F32).astype(BF16)
    sorted_h = jnp.dot(sort[:hot, :], quant[...], preferred_element_type=F32).astype(BF16)
    sorted_n = jnp.dot(sort[first:first + docs - hot, :], quant[...], preferred_element_type=F32).astype(BF16)
    h_ref[...] = sorted_h
    n_ref[...] = sorted_n
    na_ref[...] = sorted_n[:half]
    nb_ref[...] = sorted_n[half:]

    sorted_peak = jnp.dot(sort, peaks[...], preferred_element_type=F32).T[0:8, :]
    sorted_cluster = lax.dot_general(
        jnp.broadcast_to(cluster.astype(F32), (8, docs)).astype(BF16), sort, (((1,), (1,)), ((), ())),
        preferred_element_type=F32,
    )
    field = lax.broadcasted_iota(jnp.int32, (8, lanes), 0)
    meta_ref[...] = jnp.where(field == 0, sorted_peak, jnp.where(field == 1, sorted_cluster, doubt))


def prep(hot, cluster_of, states, proj_weight):
    docs, width = states.shape[0], proj_weight.shape[1]
    rest = docs - hot
    lanes = up(hot, 128) + up(rest, 128)
    shape = jax.ShapeDtypeStruct
    return pl.pallas_call(
        lambda *refs: prep_kernel(hot, *refs),
        out_shape=(
            shape((hot, width), BF16),
            shape((rest, width), BF16),
            shape((rest // 2, width), BF16),
            shape((rest // 2, width), BF16),
            shape((8, lanes), F32),
            shape((1, docs), jnp.int32),
        ),
        scratch_shapes=[pltpu.VMEM((docs, width), BF16), pltpu.VMEM((docs, 128), BF16)],
        compiler_params=pltpu.CompilerParams(vmem_limit_bytes=48 * 2**20),
        name="prep",
    )(cluster_of.reshape(1, docs), states, proj_weight)


def weights_of(moving, still, row_meta, still_meta, diagonal):
    inner = lax.dot_general(moving, still, (((1,), (1,)), ((), ())), preferred_element_type=F32)
    exponent = inner * (row_meta[:, 0:1] * SCALE) * still_meta[0:1, :] - SHIFT
    same = row_meta[:, 1:2] == still_meta[1:2, :]
    if diagonal:
        same &= lax.broadcasted_iota(jnp.int32, inner.shape, 0) != lax.broadcasted_iota(jnp.int32, inner.shape, 1)
    return jnp.where(same, jnp.exp2(exponent), 0.0)


OWN = 3
SUMS = 7


def score_kernel(plan, geometry, *refs):
    hot, rest, first, lanes = geometry
    moving, stills = plan
    place_ref, meta_ref, before_ref = refs[0:3]
    at = 3
    move_refs = refs[at:at + len(moving)]
    at += len(moving)
    still_refs = refs[at:at + len(stills)]
    out_ref = refs[at + len(stills)]
    out_ref[...] = before_ref[...]
    z, y, c = place_ref[0], place_ref[1], place_ref[2]
    columns = lax.axis_size("owner") // ROWS
    start = {"h": 0, "n": first}
    size = {"h": hot, "n": rest}

    def device(target):
        if target < OWN:
            return ((lax.rem(z + target + 1, columns)) * ROWS + y) * 2 + c
        other = target - OWN
        return (z * ROWS + (1 - y if other // 2 else y)) * 2 + (1 - c if other % 2 else c)

    for (kind, row, target, holders, meets), move_ref in zip(moving, move_refs):

        def work(kind=kind, row=row, target=target, meets=meets, move_ref=move_ref):
            count = move_ref.shape[0]
            row_meta = meta_ref[device(target)].T[start[kind] + row:start[kind] + row + count, :]
            total = jnp.zeros((count, 1), F32)
            for index in meets:
                still_kind, still_target = stills[index]
                assert still_kind == kind
                lane = slice(start[kind], start[kind] + size[kind])
                weights = weights_of(
                    move_ref[...], still_refs[index][...], row_meta, meta_ref[device(still_target)][:, lane],
                    target == OWN and still_target == OWN,
                )
                total += jnp.sum(weights, axis=1, keepdims=True)
                if target != OWN:
                    out_ref[still_target, :, lane] += jnp.sum(weights, axis=0, keepdims=True)
            spot = slice(start[kind] + row, start[kind] + row + count)
            out_ref[target, :, spot] += jnp.broadcast_to(total, (count, 128)).T[0:1, :]

        if holders is None:
            work()
        else:
            held = z == holders[0]
            for holder in holders[1:]:
                held |= z == holder
            pl.when(held)(work)


def score(name, geometry, place, meta, before, moving, stills):
    lanes = geometry[3]
    plan = ([m[1:] for m in moving], [s[1:] for s in stills])
    vmem = pl.BlockSpec(memory_space=pltpu.VMEM)
    pairs = sum(m[0].shape[0] * sum(stills[i][0].shape[0] for i in m[5]) for m in moving)
    width = moving[0][0].shape[1]
    return pl.pallas_call(
        lambda *refs: score_kernel(plan, geometry, *refs),
        out_shape=jax.ShapeDtypeStruct((SUMS, 1, lanes), F32),
        in_specs=[pl.BlockSpec(memory_space=pltpu.SMEM)] + [vmem] * (2 + len(moving) + len(stills)),
        out_specs=vmem,
        compiler_params=pltpu.CompilerParams(vmem_limit_bytes=48 * 2**20),
        cost_estimate=pl.CostEstimate(
            flops=2 * pairs * width, bytes_accessed=4 * 2**20, transcendentals=pairs
        ),
        name=name,
    )(place, meta, before, *[m[0] for m in moving], *[s[0] for s in stills])


def finish_kernel(slot_ref, *refs):
    sums, out_ref = refs[:-1], refs[-1]
    total = sums[0][...]
    for ref in sums[1:]:
        total += ref[...]
    lanes, docs = total.shape[1], slot_ref.shape[1]
    values = jnp.broadcast_to(jnp.log(1.0 + total), (8, lanes)).T[:, 0:1]
    here = lax.broadcasted_iota(jnp.int32, (lanes, docs), 0) == slot_ref[...]
    out_ref[...] = jnp.sum(jnp.where(here, values, 0.0), axis=0, keepdims=True)


def finish(slot, sums):
    return pl.pallas_call(
        finish_kernel,
        out_shape=jax.ShapeDtypeStruct(slot.shape, F32),
        name="finish",
    )(slot, *sums)


def meeting_plan(states, proj_weight, cluster_of):
    owners = lax.axis_size("owner")
    columns = owners // ROWS
    docs = states.shape[0]
    hot = 3 * docs // owners
    rest = docs - hot
    first = up(hot, 128)
    geometry = (hot, rest, first, first + up(rest, 128))

    h, n, na, nb, meta, slot = prep(hot, cluster_of, states, proj_weight)
    metas = lax.all_gather(meta, ("parts", "owner", "split"))
    parts = lax.axis_size("parts")
    doubt = jnp.max(metas[:, 2, 0]) > 0.0
    meta = lax.dynamic_index_in_dim(
        metas.reshape((parts, metas.shape[0] // parts) + metas.shape[1:]), lax.axis_index("parts"), 0, keepdims=False
    )
    owner = lax.axis_index("owner")
    place = jnp.stack([owner // ROWS, owner % ROWS, lax.axis_index("split")]).astype(jnp.int32)

    def hop(a, sources, step):
        return lax.ppermute(
            a, "owner", [(z * ROWS + y, (z + step) * ROWS + y) for z in sources for y in range(ROWS)]
        )

    def other_row(a):
        return lax.ppermute(a, "owner", [(i, i ^ 1) for i in range(owners)])

    def other_core(a):
        return lax.ppermute(a, "split", [(0, 1), (1, 0)])

    left1 = [hop(a, (2, 3), -1) for a in (na, nb)]
    right1 = hop(h, (0, 1, 2), 1)
    nc, hc = other_core(n), other_core(h)
    ny, hy = other_row(n), other_row(h)
    left2 = [hop(a, (2, 1), -1) for a in left1]
    right2 = hop(right1, (1, 2), 1)
    rightn = hop(n, (0,), 1)
    left3 = [hop(a, (1,), -1) for a in left2]
    right3 = hop(right2, (2,), 1)
    nyc, hyc = other_core(ny), other_core(hy)

    near = [(n, "n", 3), (nc, "n", 4), (h, "h", 3), (hc, "h", 4)]
    far = [(ny, "n", 5), (nyc, "n", 6), (hy, "h", 5), (hyc, "h", 6)]
    everything = near + far

    sums = jnp.zeros((SUMS, 1, geometry[3]), F32)
    sums = score(
        "near", geometry, place, meta, sums,
        [(n, "n", 0, OWN, None, (0, 1)), (h, "h", 0, OWN, None, (2, 3))],
        near,
    )
    half = rest // 2
    hop1 = [
        (left1[0], "n", 0, 0, (1, 2)),
        (left1[1], "n", half, 0, (1, 2)),
        (right1, "h", 0, 2, (1, 2, 3)),
    ]
    sums = score(
        "hop1_near", geometry, place, meta, sums, [m + ((0, 1) if m[1] == "n" else (2, 3),) for m in hop1], near
    )
    own = [(n, "n", 0, OWN, None), (h, "h", 0, OWN, None)]
    sums = score(
        "far", geometry, place, meta, sums, [m + ((0, 1) if m[1] == "n" else (2, 3),) for m in own + hop1], far
    )
    hop2 = [
        (left2[0], "n", 0, 1, (0, 1)),
        (left2[1], "n", half, 1, (0, 1)),
        (right2, "h", 0, 1, (2, 3)),
        (rightn, "n", 0, 2, (1,)),
    ]
    every = {"n": (0, 1, 4, 5), "h": (2, 3, 6, 7)}
    sums = score("hop2", geometry, place, meta, sums, [m + (every[m[1]],) for m in hop2], everything)
    hop3 = [
        (left3[0], "n", 0, 2, (0,)),
        (left3[1], "n", half, 2, (0,)),
        (right3, "h", 0, 0, (3,)),
    ]
    sums = score("hop3", geometry, place, meta, sums, [m + (every[m[1]],) for m in hop3], everything)

    def ahead(a, step):
        return lax.ppermute(
            a, "owner",
            [(z * ROWS + y, (z + step) % columns * ROWS + y) for z in range(columns) for y in range(ROWS)],
        )

    across = lax.ppermute(sums[6], ("owner", "split"), [(i, i ^ 3) for i in range(2 * owners)])
    back = [sums[OWN], other_core(sums[4]), other_row(sums[5]), across]
    back += [ahead(sums[i], i + 1) for i in range(3)]
    fast = finish(slot, back).reshape(docs)
    return lax.cond(doubt, owner_plan, lambda *_: fast, states, proj_weight, cluster_of)


def on_device(states, proj_weight, cluster_of):
    if (lax.axis_size("owner"), lax.axis_size("split")) == (8, 2) and states.shape[0] == 512:
        return meeting_plan(states, proj_weight, cluster_of)
    return owner_plan(states, proj_weight, cluster_of)


def solution(mesh):
    placed = (P(("parts", "owner", "split"), None), P(), P(("parts", "owner", "split")))
    return jax.shard_map(
        on_device,
        mesh=mesh,
        in_specs=placed,
        out_specs=P(("parts", "owner", "split")),
        check_vma=False,
    )
```

```python
import math

import jax
import jax.numpy as jnp
from jax import lax
from jax.experimental import pallas as pl
from jax.experimental.pallas import tpu as pltpu
from jax.sharding import PartitionSpec as P

CLUS_OWN = 2
TAU = 0.05
THRESH = 0.2
EPS = 1e-06
LOG2E = math.log2(math.e)
SCALE = LOG2E / TAU
SHIFT = THRESH * LOG2E / TAU

ROWS = 2
F32 = jnp.float32
BF16 = jnp.bfloat16


def prepare(states, proj_weight):
    projected = jnp.dot(states, proj_weight, preferred_element_type=jnp.float32)
    unit = projected * lax.rsqrt(jnp.sum(projected * projected, axis=1, keepdims=True) + EPS)
    peak = jnp.max(jnp.abs(unit), axis=1).astype(jnp.bfloat16)
    quant = (unit / peak.astype(jnp.float32)[:, None]).astype(jnp.bfloat16)
    return (quant, peak)


def similarity_scores(
    own_quant, own_peak, own_cluster, own_index, col_quant, col_peak, col_cluster, col_index
):
    row_count = own_quant.shape[0]
    block = math.gcd(row_count, 768)
    col_scale = col_peak.astype(jnp.float32)

    def one_block(start):
        quant_rows = lax.dynamic_slice_in_dim(own_quant, start, block, 0)
        scale_rows = lax.dynamic_slice_in_dim(own_peak, start, block, 0).astype(jnp.float32)
        cluster_rows = lax.dynamic_slice_in_dim(own_cluster, start, block, 0)
        index_rows = lax.dynamic_slice_in_dim(own_index, start, block, 0)
        inner = lax.dot_general(
            quant_rows, col_quant, (((1,), (1,)), ((), ())), preferred_element_type=jnp.float32
        )
        cosine = inner * scale_rows[:, None] * col_scale[None, :]
        same = (cluster_rows[:, None] == col_cluster[None, :]) & (
            index_rows[:, None] != col_index[None, :]
        )
        weights = jnp.where(same, jnp.exp((cosine - THRESH) / TAU), jnp.zeros_like(cosine))
        return jnp.log(1.0 + jnp.sum(weights, axis=1))

    starts = jnp.arange(row_count // block, dtype=jnp.int32) * block
    return lax.map(one_block, starts).reshape(row_count)


def owner_plan(states, proj_weight, cluster_of):
    owners = lax.axis_size("owner")
    splits = lax.axis_size("split")
    half_index = lax.axis_index("split")
    doc_count = states.shape[0]
    capacity = 3 * doc_count // owners
    width = proj_weight.shape[1]
    slot_total = owners * capacity
    quant, peak = prepare(states, proj_weight)
    group_of = cluster_of // CLUS_OWN
    onehot = (group_of[:, None] == jnp.arange(owners, dtype=jnp.int32)[None, :]).astype(jnp.int32)
    before = jnp.cumsum(onehot, axis=0) - onehot
    target = group_of * capacity + jnp.sum(before * onehot, axis=1)
    quant_slots = (
        jnp.zeros((slot_total, width), jnp.bfloat16)
        .at[target]
        .set(quant)
        .reshape(owners, capacity, width)
    )
    peak_slots = (
        jnp.zeros((slot_total,), jnp.bfloat16).at[target].set(peak).reshape(owners, capacity)
    )
    cluster_slots = (
        jnp.full((slot_total,), -1, jnp.int32).at[target].set(cluster_of).reshape(owners, capacity)
    )
    positions = (
        jnp.arange(owners, dtype=jnp.int32)[:, None] * (splits * capacity)
        + jnp.arange(capacity, dtype=jnp.int32)[None, :]
    )
    own_index = (positions + half_index * capacity).reshape(slot_total)
    col_index = jnp.arange(splits * slot_total, dtype=jnp.int32)
    own_quant, own_peak, own_cluster = (
        lax.all_to_all(a, "owner", split_axis=0, concat_axis=0, tiled=True)
        for a in (quant_slots, peak_slots, cluster_slots)
    )
    all_quant, all_peak, all_cluster = (
        lax.all_gather(a, "split", axis=1, tiled=True) for a in (own_quant, own_peak, own_cluster)
    )
    scores = similarity_scores(
        own_quant.reshape(slot_total, width),
        own_peak.reshape(slot_total),
        own_cluster.reshape(slot_total),
        own_index,
        all_quant.reshape(splits * slot_total, width),
        all_peak.reshape(splits * slot_total),
        all_cluster.reshape(splits * slot_total),
        col_index,
    )
    returned = lax.all_to_all(
        scores.reshape(owners, capacity), "owner", split_axis=0, concat_axis=0, tiled=True
    )
    return returned.reshape(slot_total)[target]


def up(n, m):
    return -(-n // m) * m


META = 16


def layout(docs, hot):
    rest = docs - hot
    first = up(rest, 128)
    flag = first + hot
    return rest, first, flag, up(flag + 1, 128)


def prep_kernel(hot, cl_ref, st_ref, w_ref, q_ref, n_ref, na_ref, nb_ref, h_ref, slot_ref, vectors):
    docs = st_ref.shape[0]
    rest, first, flag, lanes = layout(docs, hot)
    half = rest // 2
    tile = 128

    cluster = cl_ref[...]
    group = cluster // CLUS_OWN
    member = lax.broadcasted_iota(jnp.int32, (8, docs), 0) == group
    full = jnp.sum(member.astype(F32), axis=1, keepdims=True) == float(hot)
    chosen = jnp.min(
        jnp.where(full, lax.broadcasted_iota(jnp.int32, (8, 1), 0), 8), axis=0, keepdims=True
    )
    doubt = jnp.where(jnp.sum(full.astype(F32), axis=0, keepdims=True) == 1.0, 0.0, 1.0)
    in_hot = group == chosen

    for t in range(docs // tile):
        rows = slice(t * tile, (t + 1) * tile)
        projected = jnp.dot(st_ref[rows, :], w_ref[...], preferred_element_type=F32)
        norm = lax.rsqrt(jnp.sum(projected * projected, axis=1, keepdims=True) + EPS)
        vectors[rows, :] = (projected * (norm * math.sqrt(SCALE))).astype(BF16)

    ahead = (
        lax.broadcasted_iota(jnp.int32, (docs, docs), 0) < lax.broadcasted_iota(jnp.int32, (docs, docs), 1)
    ).astype(F32).astype(BF16)
    hot_rows = jnp.broadcast_to(in_hot.astype(F32), (8, docs)).astype(BF16)
    rank = jnp.dot(hot_rows, ahead, preferred_element_type=F32)[0:1, :].astype(jnp.int32)
    place = lax.broadcasted_iota(jnp.int32, (1, docs), 1)
    slot = jnp.where(in_hot, first + rank, place - rank)
    slot_ref[...] = slot

    sort = (lax.broadcasted_iota(jnp.int32, (lanes, docs), 0) == slot).astype(F32).astype(BF16)
    cluster_rows = jnp.broadcast_to(cluster.astype(F32), (META, docs)).astype(BF16)
    sorted_n = jnp.dot(sort[:rest, :], vectors[...], preferred_element_type=F32).astype(BF16)
    sorted_h = jnp.dot(sort[first:flag, :], vectors[...], preferred_element_type=F32).astype(BF16)

    def meta(ref, row, start, stop):
        ids = lax.dot_general(
            cluster_rows, sort[start:stop, :], (((1,), (1,)), ((), ())), preferred_element_type=F32
        )
        spot = lax.broadcasted_iota(jnp.int32, ids.shape, 1) + start
        ids = jnp.where(spot == flag, doubt, ids)
        ref[row:row + META, :] = jnp.zeros((META, ref.shape[1]), BF16)
        ref[row:row + META, 0:stop - start] = ids.astype(BF16)

    q_ref[:rest, :] = sorted_n
    q_ref[rest:docs, :] = sorted_h
    meta(q_ref, docs, 0, lanes)
    n_ref[:rest, :] = sorted_n
    meta(n_ref, rest, 0, rest)
    na_ref[:half, :] = sorted_n[:half]
    meta(na_ref, half, 0, half)
    nb_ref[:half, :] = sorted_n[half:]
    meta(nb_ref, half, half, rest)
    h_ref[:hot, :] = sorted_h
    meta(h_ref, hot, first, flag)


def prep(hot, cluster_of, states, proj_weight):
    docs, width = states.shape[0], proj_weight.shape[1]
    rest = docs - hot
    shape = jax.ShapeDtypeStruct
    blocks = (docs, rest, rest // 2, rest // 2, hot)
    return pl.pallas_call(
        lambda *refs: prep_kernel(hot, *refs),
        out_shape=tuple(shape((b + META, width), BF16) for b in blocks) + (shape((1, docs), jnp.int32),),
        scratch_shapes=[pltpu.VMEM((docs, width), BF16)],
        compiler_params=pltpu.CompilerParams(vmem_limit_bytes=48 * 2**20),
        name="prep",
    )(cluster_of.reshape(1, docs), states, proj_weight)


OWN = 3
SUMS = 7


def score_kernel(plan, docs, hot, carries, flags, outs, *refs):
    moving, stills = plan
    rest, first, flag, lanes = layout(docs, hot)
    place_ref, refs = refs[0], refs[1:]
    before, refs = refs[:carries], refs[carries:]
    move_refs, refs = refs[:len(moving)], refs[len(moving):]
    still_refs, out_refs = refs[:len(stills)], dict(zip(outs, refs[len(stills):]))
    z = place_ref[0]
    for k, target in enumerate(outs):
        out_refs[target][...] = before[k][...] if carries else jnp.zeros((1, lanes), F32)
    metas = [ref[docs:docs + META, :].astype(F32)[0:1, :] for ref in still_refs]
    span = {"n": (0, slice(0, rest), slice(0, rest)), "h": (first, slice(rest, docs), slice(first, flag))}

    for (kind, row, target, holders, meets), move_ref in zip(moving, move_refs):

        def work(kind=kind, row=row, target=target, meets=meets, move_ref=move_ref):
            start, rows, lane = span[kind]
            if target == OWN:
                count = rows.stop - rows.start
                block = move_ref[rows, :]
                ids = move_ref[docs:docs + META, :].astype(F32)[0:8, lane]
            else:
                count = move_ref.shape[0] - META
                block = move_ref[:count, :]
                ids = move_ref[count:count + META, :].astype(F32)[0:8, 0:count]
            ids = ids.T[:, 0:1]
            total = jnp.zeros((count, 1), F32)
            for index in meets:
                inner = lax.dot_general(
                    block, still_refs[index][rows, :], (((1,), (1,)), ((), ())), preferred_element_type=F32
                )
                same = ids == metas[index][:, lane]
                if target == OWN and stills[index] == OWN:
                    same &= lax.broadcasted_iota(jnp.int32, inner.shape, 0) != lax.broadcasted_iota(
                        jnp.int32, inner.shape, 1
                    )
                weights = jnp.where(same, jnp.exp2(inner), 0.0)
                total += jnp.sum(weights, axis=1, keepdims=True)
                if target != OWN:
                    out_refs[stills[index]][:, lane] += jnp.sum(weights, axis=0, keepdims=True)
            spot = slice(start + row, start + row + count)
            out_refs[target][:, spot] += jnp.broadcast_to(total, (count, 128)).T[0:1, :]

        if holders is None:
            work()
        else:
            held = z == holders[0]
            for holder in holders[1:]:
                held |= z == holder
            pl.when(held)(work)

    if flags:
        doubt = metas[0]
        for other in metas[1:]:
            doubt = doubt + other
        spot = lax.broadcasted_iota(jnp.int32, (1, lanes), 1)
        for target in range(OWN + 1):
            out_refs[target][...] += jnp.where(spot == flag, doubt[:, :lanes], 0.0)


def score(name, docs, hot, place, before, moving, stills, flags=False, outs=tuple(range(SUMS))):
    lanes = layout(docs, hot)[3]
    plan = ([m[1:] for m in moving], [s[1] for s in stills])
    vmem = pl.BlockSpec(memory_space=pltpu.VMEM)
    pairs = sum(m[0].shape[0] * len(m[5]) * (hot if m[1] == "h" else docs - hot) for m in moving)
    arrays = [*before, *(m[0] for m in moving), *(s[0] for s in stills)]
    return pl.pallas_call(
        lambda *refs: score_kernel(plan, docs, hot, len(before), flags, outs, *refs),
        out_shape=tuple(jax.ShapeDtypeStruct((1, lanes), F32) for _ in outs),
        in_specs=[pl.BlockSpec(memory_space=pltpu.SMEM)] + [vmem] * len(arrays),
        out_specs=tuple(vmem for _ in outs),
        compiler_params=pltpu.CompilerParams(vmem_limit_bytes=48 * 2**20),
        cost_estimate=pl.CostEstimate(
            flops=pairs, bytes_accessed=2**10, transcendentals=0
        ),
        name=name,
    )(place, *arrays)


def finish_kernel(flag, slot_ref, *refs):
    sums, out_ref, doubt_ref = refs[:-2], refs[-2], refs[-1]
    total = sums[0][...]
    for ref in sums[1:]:
        total += ref[...]
    lanes, docs = total.shape[1], slot_ref.shape[1]
    doubt_ref[...] = (total[:, flag:flag + 1] > 0.0).astype(jnp.int32)
    values = jnp.broadcast_to(jnp.log(1.0 + total * 2.0**-SHIFT), (8, lanes)).T[:, 0:1]
    here = lax.broadcasted_iota(jnp.int32, (lanes, docs), 0) == slot_ref[...]
    out_ref[...] = jnp.sum(jnp.where(here, values, 0.0), axis=0, keepdims=True)


def finish(flag, slot, sums):
    return pl.pallas_call(
        lambda *refs: finish_kernel(flag, *refs),
        out_shape=(jax.ShapeDtypeStruct(slot.shape, F32), jax.ShapeDtypeStruct((1, 1), jnp.int32)),
        name="finish",
    )(slot, *sums)


def meeting_plan(states, proj_weight, cluster_of):
    owners = lax.axis_size("owner")
    columns = owners // ROWS
    docs = states.shape[0]
    hot = 3 * docs // owners
    rest = docs - hot
    half = rest // 2
    flag = layout(docs, hot)[2]

    q, n, na, nb, h, slot = prep(hot, cluster_of, states, proj_weight)
    owner = lax.axis_index("owner")
    place = (owner // ROWS).astype(jnp.int32).reshape(1)

    def hop(a, sources, step):
        return lax.ppermute(
            a, "owner", [(z * ROWS + y, (z + step) * ROWS + y) for z in sources for y in range(ROWS)]
        )

    def other_row(a):
        return lax.ppermute(a, "owner", [(i, i ^ 1) for i in range(owners)])

    def other_core(a):
        return lax.ppermute(a, "split", [(0, 1), (1, 0)])

    def across(a):
        return lax.ppermute(a, ("owner", "split"), [(i, i ^ 3) for i in range(2 * owners)])

    def ahead(a, step):
        return lax.ppermute(
            a, "owner",
            [(z * ROWS + y, (z + step) % columns * ROWS + y) for z in range(columns) for y in range(ROWS)],
        )

    def after(a, *others):
        return lax.optimization_barrier((a, *others))[0]

    left1 = [hop(a, (2, 3), -1) for a in (na, nb)]
    right1 = hop(h, (0, 1, 2), 1)
    qy = other_row(q)
    qc = other_core(q)
    near = [(q, 3), (qc, 4)]
    own = [(q, "n", 0, OWN, None), (q, "h", 0, OWN, None)]
    def meet(name, before, moving, stills, **options):
        every = tuple(range(len(stills)))
        return score(name, docs, hot, place, before, [m + (every,) for m in moving], stills, **options)

    sums = meet("near", (), own, near)

    left2 = [hop(after(left1[0], sums[0]), (2, 1), -1)]
    left2 += [hop(after(left1[1], left1[0]), (2, 1), -1)]
    right2 = hop(after(right1, left1[1]), (1, 2), 1)
    rightn = hop(n, (0,), 1)
    hop1 = [
        (left1[0], "n", 0, 0, (1, 2)),
        (left1[1], "n", half, 0, (1, 2)),
        (right1, "h", 0, 2, (1, 2, 3)),
    ]
    sums = meet("hop1_near", sums, hop1, near)

    left3 = [hop(after(left2[0], sums[0]), (1,), -1)]
    qy = after(qy, left2[0])
    qyc = other_core(qy)
    left3 += [hop(after(left2[1], qy), (1,), -1)]
    right3 = hop(after(right2, left2[1]), (2,), 1)
    far = [(qy, 5), (qyc, 6)]
    sums = meet("far", sums, own + hop1, far)
    hop2 = [
        (left2[0], "n", 0, 1, (0, 1)),
        (left2[1], "n", half, 1, (0, 1)),
        (right2, "h", 0, 1, (2, 3)),
        (rightn, "n", 0, 2, (1,)),
    ]
    sums = meet("hop2", sums, hop2, near + far)
    hop3 = [(left3[0], "n", 0, 2, (0,)), (right3, "h", 0, 0, (3,))]
    early = meet("hop3", sums, hop3, near + far, flags=True)
    back = [early[OWN], other_core(early[4]), other_row(early[5]), across(early[6])]
    back += [ahead(early[i], i + 1) for i in range(3)]
    last = [(after(left3[1], *back), "n", half, 2, (0,))]
    late = meet("last", (), last, near + far, outs=(2, 3, 4, 5, 6))
    back += [hop(late[0], (0,), 3), late[1], other_core(late[2]), other_row(late[3]), across(late[4])]
    fast, doubt = finish(flag, slot, back)
    return lax.cond(
        doubt[0, 0] > 0, owner_plan, lambda *_: fast.reshape(docs), states, proj_weight, cluster_of
    )


def on_device(states, proj_weight, cluster_of):
    if (lax.axis_size("owner"), lax.axis_size("split")) == (8, 2) and states.shape[0] == 512:
        return meeting_plan(states, proj_weight, cluster_of)
    return owner_plan(states, proj_weight, cluster_of)


def solution(mesh):
    placed = (P(("parts", "owner", "split"), None), P(), P(("parts", "owner", "split")))
    return jax.shard_map(
        on_device,
        mesh=mesh,
        in_specs=placed,
        out_specs=P(("parts", "owner", "split")),
        check_vma=False,
    )
```

```python
import math

import jax
import jax.numpy as jnp
from jax import lax
from jax.experimental import pallas as pl
from jax.experimental.pallas import tpu as pltpu
from jax.sharding import PartitionSpec as P

CLUS_OWN = 2
TAU = 0.05
THRESH = 0.2
EPS = 1e-06
LOG2E = math.log2(math.e)
SCALE = LOG2E / TAU
SHIFT = THRESH * LOG2E / TAU

ROWS = 2
F32 = jnp.float32
BF16 = jnp.bfloat16


def prepare(states, proj_weight):
    projected = jnp.dot(states, proj_weight, preferred_element_type=jnp.float32)
    unit = projected * lax.rsqrt(jnp.sum(projected * projected, axis=1, keepdims=True) + EPS)
    peak = jnp.max(jnp.abs(unit), axis=1).astype(jnp.bfloat16)
    quant = (unit / peak.astype(jnp.float32)[:, None]).astype(jnp.bfloat16)
    return (quant, peak)


def similarity_scores(
    own_quant, own_peak, own_cluster, own_index, col_quant, col_peak, col_cluster, col_index
):
    row_count = own_quant.shape[0]
    block = math.gcd(row_count, 768)
    col_scale = col_peak.astype(jnp.float32)

    def one_block(start):
        quant_rows = lax.dynamic_slice_in_dim(own_quant, start, block, 0)
        scale_rows = lax.dynamic_slice_in_dim(own_peak, start, block, 0).astype(jnp.float32)
        cluster_rows = lax.dynamic_slice_in_dim(own_cluster, start, block, 0)
        index_rows = lax.dynamic_slice_in_dim(own_index, start, block, 0)
        inner = lax.dot_general(
            quant_rows, col_quant, (((1,), (1,)), ((), ())), preferred_element_type=jnp.float32
        )
        cosine = inner * scale_rows[:, None] * col_scale[None, :]
        same = (cluster_rows[:, None] == col_cluster[None, :]) & (
            index_rows[:, None] != col_index[None, :]
        )
        weights = jnp.where(same, jnp.exp((cosine - THRESH) / TAU), jnp.zeros_like(cosine))
        return jnp.log(1.0 + jnp.sum(weights, axis=1))

    starts = jnp.arange(row_count // block, dtype=jnp.int32) * block
    return lax.map(one_block, starts).reshape(row_count)


def owner_plan(states, proj_weight, cluster_of):
    owners = lax.axis_size("owner")
    splits = lax.axis_size("split")
    half_index = lax.axis_index("split")
    doc_count = states.shape[0]
    capacity = 3 * doc_count // owners
    width = proj_weight.shape[1]
    slot_total = owners * capacity
    quant, peak = prepare(states, proj_weight)
    group_of = cluster_of // CLUS_OWN
    onehot = (group_of[:, None] == jnp.arange(owners, dtype=jnp.int32)[None, :]).astype(jnp.int32)
    before = jnp.cumsum(onehot, axis=0) - onehot
    target = group_of * capacity + jnp.sum(before * onehot, axis=1)
    quant_slots = (
        jnp.zeros((slot_total, width), jnp.bfloat16)
        .at[target]
        .set(quant)
        .reshape(owners, capacity, width)
    )
    peak_slots = (
        jnp.zeros((slot_total,), jnp.bfloat16).at[target].set(peak).reshape(owners, capacity)
    )
    cluster_slots = (
        jnp.full((slot_total,), -1, jnp.int32).at[target].set(cluster_of).reshape(owners, capacity)
    )
    positions = (
        jnp.arange(owners, dtype=jnp.int32)[:, None] * (splits * capacity)
        + jnp.arange(capacity, dtype=jnp.int32)[None, :]
    )
    own_index = (positions + half_index * capacity).reshape(slot_total)
    col_index = jnp.arange(splits * slot_total, dtype=jnp.int32)
    own_quant, own_peak, own_cluster = (
        lax.all_to_all(a, "owner", split_axis=0, concat_axis=0, tiled=True)
        for a in (quant_slots, peak_slots, cluster_slots)
    )
    all_quant, all_peak, all_cluster = (
        lax.all_gather(a, "split", axis=1, tiled=True) for a in (own_quant, own_peak, own_cluster)
    )
    scores = similarity_scores(
        own_quant.reshape(slot_total, width),
        own_peak.reshape(slot_total),
        own_cluster.reshape(slot_total),
        own_index,
        all_quant.reshape(splits * slot_total, width),
        all_peak.reshape(splits * slot_total),
        all_cluster.reshape(splits * slot_total),
        col_index,
    )
    returned = lax.all_to_all(
        scores.reshape(owners, capacity), "owner", split_axis=0, concat_axis=0, tiled=True
    )
    return returned.reshape(slot_total)[target]


def up(n, m):
    return -(-n // m) * m


META = 16


def layout(docs, hot):
    rest = docs - hot
    first = up(rest, 128)
    flag = first + hot
    return rest, first, flag, up(flag + 1, 128)


def prep_kernel(hot, cl_ref, st_ref, w_ref, q_ref, n_ref, na_ref, nb_ref, h_ref, slot_ref, vectors):
    docs = st_ref.shape[0]
    rest, first, flag, lanes = layout(docs, hot)
    half = rest // 2
    tile = 128

    cluster = cl_ref[...]
    group = cluster // CLUS_OWN
    member = lax.broadcasted_iota(jnp.int32, (8, docs), 0) == group
    full = jnp.sum(member.astype(F32), axis=1, keepdims=True) == float(hot)
    chosen = jnp.min(
        jnp.where(full, lax.broadcasted_iota(jnp.int32, (8, 1), 0), 8), axis=0, keepdims=True
    )
    doubt = jnp.where(jnp.sum(full.astype(F32), axis=0, keepdims=True) == 1.0, 0.0, 1.0)
    in_hot = group == chosen

    for t in range(docs // tile):
        rows = slice(t * tile, (t + 1) * tile)
        projected = jnp.dot(st_ref[rows, :], w_ref[...], preferred_element_type=F32)
        norm = lax.rsqrt(jnp.sum(projected * projected, axis=1, keepdims=True) + EPS)
        vectors[rows, :] = (projected * (norm * math.sqrt(SCALE))).astype(BF16)

    ahead = (
        lax.broadcasted_iota(jnp.int32, (docs, docs), 0) < lax.broadcasted_iota(jnp.int32, (docs, docs), 1)
    ).astype(F32).astype(BF16)
    hot_rows = jnp.broadcast_to(in_hot.astype(F32), (8, docs)).astype(BF16)
    rank = jnp.dot(hot_rows, ahead, preferred_element_type=F32)[0:1, :].astype(jnp.int32)
    place = lax.broadcasted_iota(jnp.int32, (1, docs), 1)
    slot = jnp.where(in_hot, first + rank, place - rank)
    slot_ref[...] = slot

    sort = (lax.broadcasted_iota(jnp.int32, (lanes, docs), 0) == slot).astype(F32).astype(BF16)
    cluster_rows = jnp.broadcast_to(cluster.astype(F32), (META, docs)).astype(BF16)
    sorted_n = jnp.dot(sort[:rest, :], vectors[...], preferred_element_type=F32).astype(BF16)
    sorted_h = jnp.dot(sort[first:flag, :], vectors[...], preferred_element_type=F32).astype(BF16)

    def meta(ref, row, start, stop):
        ids = lax.dot_general(
            cluster_rows, sort[start:stop, :], (((1,), (1,)), ((), ())), preferred_element_type=F32
        )
        spot = lax.broadcasted_iota(jnp.int32, ids.shape, 1) + start
        ids = jnp.where(spot == flag, doubt, ids)
        ref[row:row + META, :] = jnp.zeros((META, ref.shape[1]), BF16)
        ref[row:row + META, 0:stop - start] = ids.astype(BF16)

    q_ref[:rest, :] = sorted_n
    q_ref[rest:docs, :] = sorted_h
    meta(q_ref, docs, 0, lanes)
    n_ref[:rest, :] = sorted_n
    meta(n_ref, rest, 0, rest)
    na_ref[:half, :] = sorted_n[:half]
    meta(na_ref, half, 0, half)
    nb_ref[:half, :] = sorted_n[half:]
    meta(nb_ref, half, half, rest)
    h_ref[:hot, :] = sorted_h
    meta(h_ref, hot, first, flag)


def prep(hot, cluster_of, states, proj_weight):
    docs, width = states.shape[0], proj_weight.shape[1]
    rest = docs - hot
    shape = jax.ShapeDtypeStruct
    blocks = (docs, rest, rest // 2, rest // 2, hot)
    return pl.pallas_call(
        lambda *refs: prep_kernel(hot, *refs),
        out_shape=tuple(shape((b + META, width), BF16) for b in blocks) + (shape((1, docs), jnp.int32),),
        scratch_shapes=[pltpu.VMEM((docs, width), BF16)],
        compiler_params=pltpu.CompilerParams(vmem_limit_bytes=24 * 2**20),
        name="prep",
    )(cluster_of.reshape(1, docs), states, proj_weight)


OWN = 3
SUMS = 7


def score_kernel(plan, docs, hot, carries, flags, outs, *refs):
    moving, stills = plan
    rest, first, flag, lanes = layout(docs, hot)
    place_ref, refs = refs[0], refs[1:]
    before, refs = refs[:carries], refs[carries:]
    move_refs, refs = refs[:len(moving)], refs[len(moving):]
    still_refs, out_refs = refs[:len(stills)], dict(zip(outs, refs[len(stills):]))
    z = place_ref[0]
    for k, target in enumerate(outs):
        out_refs[target][...] = before[k][...] if carries else jnp.zeros((1, lanes), F32)
    metas = [ref[docs:docs + META, :].astype(F32)[0:1, :] for ref in still_refs]
    span = {"n": (0, slice(0, rest), slice(0, rest)), "h": (first, slice(rest, docs), slice(first, flag))}

    for (kind, row, target, holders, meets), move_ref in zip(moving, move_refs):

        def work(kind=kind, row=row, target=target, meets=meets, move_ref=move_ref):
            start, rows, lane = span[kind]
            if target == OWN:
                count = rows.stop - rows.start
                block = move_ref[rows, :]
                ids = move_ref[docs:docs + META, :].astype(F32)[0:8, lane]
            else:
                count = move_ref.shape[0] - META
                block = move_ref[:count, :]
                ids = move_ref[count:count + META, :].astype(F32)[0:8, 0:count]
            ids = ids.T[:, 0:1]
            total = jnp.zeros((count, 1), F32)
            for index in meets:
                inner = lax.dot_general(
                    block, still_refs[index][rows, :], (((1,), (1,)), ((), ())), preferred_element_type=F32
                )
                same = ids == metas[index][:, lane]
                if target == OWN and stills[index] == OWN:
                    same &= lax.broadcasted_iota(jnp.int32, inner.shape, 0) != lax.broadcasted_iota(
                        jnp.int32, inner.shape, 1
                    )
                weights = jnp.where(same, jnp.exp2(inner), 0.0)
                total += jnp.sum(weights, axis=1, keepdims=True)
                if target != OWN:
                    out_refs[stills[index]][:, lane] += jnp.sum(weights, axis=0, keepdims=True)
            spot = slice(start + row, start + row + count)
            out_refs[target][:, spot] += jnp.broadcast_to(total, (count, 128)).T[0:1, :]

        if holders is None:
            work()
        else:
            held = z == holders[0]
            for holder in holders[1:]:
                held |= z == holder
            pl.when(held)(work)

    if flags:
        doubt = metas[0]
        for other in metas[1:]:
            doubt = doubt + other
        spot = lax.broadcasted_iota(jnp.int32, (1, lanes), 1)
        for target in range(OWN + 1):
            out_refs[target][...] += jnp.where(spot == flag, doubt[:, :lanes], 0.0)


def score(name, docs, hot, place, before, moving, stills, flags=False, outs=tuple(range(SUMS))):
    lanes = layout(docs, hot)[3]
    plan = ([m[1:] for m in moving], [s[1] for s in stills])
    vmem = pl.BlockSpec(memory_space=pltpu.VMEM)
    pairs = sum(m[0].shape[0] * len(m[5]) * (hot if m[1] == "h" else docs - hot) for m in moving)
    arrays = [*before, *(m[0] for m in moving), *(s[0] for s in stills)]
    return pl.pallas_call(
        lambda *refs: score_kernel(plan, docs, hot, len(before), flags, outs, *refs),
        out_shape=tuple(jax.ShapeDtypeStruct((1, lanes), F32) for _ in outs),
        in_specs=[pl.BlockSpec(memory_space=pltpu.SMEM)] + [vmem] * len(arrays),
        out_specs=tuple(vmem for _ in outs),
        compiler_params=pltpu.CompilerParams(vmem_limit_bytes=20 * 2**20),
        cost_estimate=pl.CostEstimate(
            flops=pairs, bytes_accessed=2**10, transcendentals=0
        ),
        name=name,
    )(place, *arrays)


def finish_kernel(flag, slot_ref, *refs):
    sums, out_ref, doubt_ref = refs[:-2], refs[-2], refs[-1]
    total = sums[0][...]
    for ref in sums[1:]:
        total += ref[...]
    lanes, docs = total.shape[1], slot_ref.shape[1]
    doubt_ref[...] = (total[:, flag:flag + 1] > 0.0).astype(jnp.int32)
    values = jnp.broadcast_to(jnp.log(1.0 + total * 2.0**-SHIFT), (8, lanes)).T[:, 0:1]
    here = lax.broadcasted_iota(jnp.int32, (lanes, docs), 0) == slot_ref[...]
    out_ref[...] = jnp.sum(jnp.where(here, values, 0.0), axis=0, keepdims=True)


def finish(flag, slot, sums):
    return pl.pallas_call(
        lambda *refs: finish_kernel(flag, *refs),
        out_shape=(jax.ShapeDtypeStruct(slot.shape, F32), jax.ShapeDtypeStruct((1, 1), jnp.int32)),
        name="finish",
    )(slot, *sums)


def meeting_plan(states, proj_weight, cluster_of):
    owners = lax.axis_size("owner")
    columns = owners // ROWS
    docs = states.shape[0]
    hot = 3 * docs // owners
    rest = docs - hot
    half = rest // 2
    flag = layout(docs, hot)[2]

    q, n, na, nb, h, slot = prep(hot, cluster_of, states, proj_weight)
    owner = lax.axis_index("owner")
    place = (owner // ROWS).astype(jnp.int32).reshape(1)

    def hop(a, sources, step):
        return lax.ppermute(
            a, "owner", [(z * ROWS + y, (z + step) * ROWS + y) for z in sources for y in range(ROWS)]
        )

    def other_row(a):
        return lax.ppermute(a, "owner", [(i, i ^ 1) for i in range(owners)])

    def other_core(a):
        return lax.ppermute(a, "split", [(0, 1), (1, 0)])

    def across(a):
        return lax.ppermute(a, ("owner", "split"), [(i, i ^ 3) for i in range(2 * owners)])

    def ahead(a, step):
        return lax.ppermute(
            a, "owner",
            [(z * ROWS + y, (z + step) % columns * ROWS + y) for z in range(columns) for y in range(ROWS)],
        )

    def after(a, *others):
        return lax.optimization_barrier((a, *others))[0]

    qy = other_row(q)
    left1 = [hop(a, (2, 3), -1) for a in (na, nb)]
    right1 = hop(h, (0, 1, 2), 1)
    qc = other_core(q)
    rightn = hop(n, (0,), 1)
    near = [(q, 3), (qc, 4)]
    own = [(q, "n", 0, OWN, None), (q, "h", 0, OWN, None)]
    def meet(name, before, moving, stills, **options):
        every = tuple(range(len(stills)))
        return score(name, docs, hot, place, before, [m + (every,) for m in moving], stills, **options)

    sums = meet("near", (), own, near)

    left1[0], left1[1], right1, _ = lax.optimization_barrier((*left1, right1, sums[0]))
    left2 = [hop(a, (2, 1), -1) for a in left1]
    right2 = hop(right1, (1, 2), 1)
    left3 = [hop(left2[0], (1,), -1)]
    rightn = after(rightn, left2[0])
    hop1 = [
        (left1[0], "n", 0, 0, (1, 2)),
        (left1[1], "n", half, 0, (1, 2)),
        (right1, "h", 0, 2, (1, 2, 3)),
        (rightn, "n", 0, 2, (1,)),
    ]
    sums = meet("hop1_near", sums, hop1, near)

    qy = after(qy, sums[0], left2[1], right2)
    qyc = other_core(qy)
    right3 = hop(right2, (2,), 1)
    left3 += [hop(left2[1], (1,), -1)]
    far = [(qy, 5), (after(qyc, left3[0]), 6)]
    sums = meet("far", sums, own + hop1, far)
    hop2 = [
        (left2[0], "n", 0, 1, (0, 1)),
        (left2[1], "n", half, 1, (0, 1)),
        (right2, "h", 0, 1, (2, 3)),
    ]
    sums = meet("hop2", sums, hop2, near + far)
    hop3 = [(left3[0], "n", 0, 2, (0,)), (right3, "h", 0, 0, (3,))]
    sums = meet("hop3", sums, hop3, near + far, flags=True)
    last = [(left3[1], "n", half, 2, (0,))]
    sums = meet("last", sums, last, near + far)
    back = [ahead(sums[i], i + 1) for i in (2, 1, 0)]
    back += [across(sums[6]), other_row(sums[5]), other_core(sums[4]), sums[OWN]]
    fast, doubt = finish(flag, slot, back)
    return lax.cond(
        doubt[0, 0] > 0, owner_plan, lambda *_: fast.reshape(docs), states, proj_weight, cluster_of
    )


def on_device(states, proj_weight, cluster_of):
    if (lax.axis_size("owner"), lax.axis_size("split")) == (8, 2) and states.shape[0] == 512:
        return meeting_plan(states, proj_weight, cluster_of)
    return owner_plan(states, proj_weight, cluster_of)


def solution(mesh):
    placed = (P(("parts", "owner", "split"), None), P(), P(("parts", "owner", "split")))
    return jax.shard_map(
        on_device,
        mesh=mesh,
        in_specs=placed,
        out_specs=P(("parts", "owner", "split")),
        check_vma=False,
    )
```

```python
import math

import jax
import jax.numpy as jnp
from jax import lax
from jax.experimental import pallas as pl
from jax.experimental.pallas import tpu as pltpu
from jax.sharding import PartitionSpec as P

CLUS_OWN = 2
TAU = 0.05
THRESH = 0.2
EPS = 1e-06
LOG2E = math.log2(math.e)
SCALE = LOG2E / TAU
SHIFT = THRESH * LOG2E / TAU

ROWS = 2
F32 = jnp.float32
BF16 = jnp.bfloat16


def prepare(states, proj_weight):
    projected = jnp.dot(states, proj_weight, preferred_element_type=jnp.float32)
    unit = projected * lax.rsqrt(jnp.sum(projected * projected, axis=1, keepdims=True) + EPS)
    peak = jnp.max(jnp.abs(unit), axis=1).astype(jnp.bfloat16)
    quant = (unit / peak.astype(jnp.float32)[:, None]).astype(jnp.bfloat16)
    return (quant, peak)


def similarity_scores(
    own_quant, own_peak, own_cluster, own_index, col_quant, col_peak, col_cluster, col_index
):
    row_count = own_quant.shape[0]
    block = math.gcd(row_count, 768)
    col_scale = col_peak.astype(jnp.float32)

    def one_block(start):
        quant_rows = lax.dynamic_slice_in_dim(own_quant, start, block, 0)
        scale_rows = lax.dynamic_slice_in_dim(own_peak, start, block, 0).astype(jnp.float32)
        cluster_rows = lax.dynamic_slice_in_dim(own_cluster, start, block, 0)
        index_rows = lax.dynamic_slice_in_dim(own_index, start, block, 0)
        inner = lax.dot_general(
            quant_rows, col_quant, (((1,), (1,)), ((), ())), preferred_element_type=jnp.float32
        )
        cosine = inner * scale_rows[:, None] * col_scale[None, :]
        same = (cluster_rows[:, None] == col_cluster[None, :]) & (
            index_rows[:, None] != col_index[None, :]
        )
        weights = jnp.where(same, jnp.exp((cosine - THRESH) / TAU), jnp.zeros_like(cosine))
        return jnp.log(1.0 + jnp.sum(weights, axis=1))

    starts = jnp.arange(row_count // block, dtype=jnp.int32) * block
    return lax.map(one_block, starts).reshape(row_count)


def owner_plan(states, proj_weight, cluster_of):
    owners = lax.axis_size("owner")
    splits = lax.axis_size("split")
    half_index = lax.axis_index("split")
    doc_count = states.shape[0]
    capacity = 3 * doc_count // owners
    width = proj_weight.shape[1]
    slot_total = owners * capacity
    quant, peak = prepare(states, proj_weight)
    group_of = cluster_of // CLUS_OWN
    onehot = (group_of[:, None] == jnp.arange(owners, dtype=jnp.int32)[None, :]).astype(jnp.int32)
    before = jnp.cumsum(onehot, axis=0) - onehot
    target = group_of * capacity + jnp.sum(before * onehot, axis=1)
    quant_slots = (
        jnp.zeros((slot_total, width), jnp.bfloat16)
        .at[target]
        .set(quant)
        .reshape(owners, capacity, width)
    )
    peak_slots = (
        jnp.zeros((slot_total,), jnp.bfloat16).at[target].set(peak).reshape(owners, capacity)
    )
    cluster_slots = (
        jnp.full((slot_total,), -1, jnp.int32).at[target].set(cluster_of).reshape(owners, capacity)
    )
    positions = (
        jnp.arange(owners, dtype=jnp.int32)[:, None] * (splits * capacity)
        + jnp.arange(capacity, dtype=jnp.int32)[None, :]
    )
    own_index = (positions + half_index * capacity).reshape(slot_total)
    col_index = jnp.arange(splits * slot_total, dtype=jnp.int32)
    own_quant, own_peak, own_cluster = (
        lax.all_to_all(a, "owner", split_axis=0, concat_axis=0, tiled=True)
        for a in (quant_slots, peak_slots, cluster_slots)
    )
    all_quant, all_peak, all_cluster = (
        lax.all_gather(a, "split", axis=1, tiled=True) for a in (own_quant, own_peak, own_cluster)
    )
    scores = similarity_scores(
        own_quant.reshape(slot_total, width),
        own_peak.reshape(slot_total),
        own_cluster.reshape(slot_total),
        own_index,
        all_quant.reshape(splits * slot_total, width),
        all_peak.reshape(splits * slot_total),
        all_cluster.reshape(splits * slot_total),
        col_index,
    )
    returned = lax.all_to_all(
        scores.reshape(owners, capacity), "owner", split_axis=0, concat_axis=0, tiled=True
    )
    return returned.reshape(slot_total)[target]


def up(n, m):
    return -(-n // m) * m


META = 16


def layout(docs, hot):
    rest = docs - hot
    first = up(rest, 128)
    flag = first + hot
    return rest, first, flag, up(flag + 1, 128)


def prep_kernel(hot, place_ref, cl_ref, st_ref, w_ref, q_ref, even_ref, odd_ref, slot_ref, vectors):
    docs = st_ref.shape[0]
    rest, first, flag, lanes = layout(docs, hot)
    tile = 128

    cluster = cl_ref[...]
    group = cluster // CLUS_OWN
    member = lax.broadcasted_iota(jnp.int32, (8, docs), 0) == group
    full = jnp.sum(member.astype(F32), axis=1, keepdims=True) == float(hot)
    chosen = jnp.min(
        jnp.where(full, lax.broadcasted_iota(jnp.int32, (8, 1), 0), 8), axis=0, keepdims=True
    )
    doubt = jnp.where(jnp.sum(full.astype(F32), axis=0, keepdims=True) == 1.0, 0.0, 1.0)
    in_hot = group == chosen

    for t in range(docs // tile):
        rows = slice(t * tile, (t + 1) * tile)
        projected = jnp.dot(st_ref[rows, :], w_ref[...], preferred_element_type=F32)
        norm = lax.rsqrt(jnp.sum(projected * projected, axis=1, keepdims=True) + EPS)
        vectors[rows, :] = (projected * (norm * math.sqrt(SCALE))).astype(BF16)

    ahead = (
        lax.broadcasted_iota(jnp.int32, (docs, docs), 0) < lax.broadcasted_iota(jnp.int32, (docs, docs), 1)
    ).astype(F32).astype(BF16)
    hot_rows = jnp.broadcast_to(in_hot.astype(F32), (8, docs)).astype(BF16)
    rank = jnp.dot(hot_rows, ahead, preferred_element_type=F32)[0:1, :].astype(jnp.int32)
    place = lax.broadcasted_iota(jnp.int32, (1, docs), 1)
    slot = jnp.where(in_hot, first + rank, place - rank)
    slot_ref[...] = slot

    sort = (lax.broadcasted_iota(jnp.int32, (lanes, docs), 0) == slot).astype(F32).astype(BF16)
    cluster_rows = jnp.broadcast_to(cluster.astype(F32), (META, docs)).astype(BF16)
    sorted_n = jnp.dot(sort[:rest, :], vectors[...], preferred_element_type=F32).astype(BF16)
    sorted_h = jnp.dot(sort[first:flag, :], vectors[...], preferred_element_type=F32).astype(BF16)
    ids = lax.dot_general(
        cluster_rows, sort, (((1,), (1,)), ((), ())), preferred_element_type=F32
    )
    ids = jnp.where(lax.broadcasted_iota(jnp.int32, ids.shape, 1) == flag, doubt, ids).astype(BF16)

    q_ref[:rest, :] = sorted_n
    q_ref[rest:docs, :] = sorted_h
    q_ref[docs:, :] = jnp.zeros((META, q_ref.shape[1]), BF16)
    q_ref[docs:, :lanes] = ids

    def fill_n(ref):
        ref[:rest, :] = sorted_n
        ref[rest:, :] = jnp.zeros((META, ref.shape[1]), BF16)
        ref[rest:, :first] = ids[:, :first]

    def fill_h(ref):
        ref[:hot, :] = sorted_h
        ref[hot:, :] = jnp.zeros((rest + META - hot, ref.shape[1]), BF16)
        ref[rest:, :lanes - first] = ids[:, first:]

    even = lax.rem(place_ref[0], 2) == 0

    @pl.when(even)
    def _():
        fill_h(even_ref)
        fill_n(odd_ref)

    @pl.when(jnp.logical_not(even))
    def _():
        fill_n(even_ref)
        fill_h(odd_ref)


def prep(hot, place, cluster_of, states, proj_weight):
    docs, width = states.shape[0], proj_weight.shape[1]
    rest = docs - hot
    shape = jax.ShapeDtypeStruct
    vmem = pl.BlockSpec(memory_space=pltpu.VMEM)
    return pl.pallas_call(
        lambda *refs: prep_kernel(hot, *refs),
        out_shape=(
            shape((docs + META, width), BF16),
            shape((rest + META, width), BF16),
            shape((rest + META, width), BF16),
            shape((1, docs), jnp.int32),
        ),
        in_specs=[pl.BlockSpec(memory_space=pltpu.SMEM), vmem, vmem, vmem],
        scratch_shapes=[pltpu.VMEM((docs, width), BF16)],
        compiler_params=pltpu.CompilerParams(vmem_limit_bytes=24 * 2**20),
        name="prep",
    )(place, cluster_of.reshape(1, docs), states, proj_weight)


OWN = 3
SUMS = 7


def score_kernel(plan, docs, hot, carries, flags, outs, *refs):
    moving, stills = plan
    rest, first, flag, lanes = layout(docs, hot)
    place_ref, refs = refs[0], refs[1:]
    before, refs = refs[:carries], refs[carries:]
    move_refs, refs = refs[:len(moving)], refs[len(moving):]
    still_refs, out_refs = refs[:len(stills)], dict(zip(outs, refs[len(stills):]))
    z = place_ref[0]
    for k, target in enumerate(outs):
        out_refs[target][...] = before[k][...] if carries else jnp.zeros((1, lanes), F32)
    metas = [ref[docs:docs + META, :].astype(F32)[0:1, :] for ref in still_refs]
    span = {"n": (0, slice(0, rest), slice(0, rest)), "h": (first, slice(rest, docs), slice(first, flag))}

    for (kind, target, holder), move_ref in zip(moving, move_refs):

        def work(kind=kind, target=target, move_ref=move_ref):
            start, rows, lane = span[kind]
            count = rows.stop - rows.start
            if target == OWN:
                block = move_ref[rows, :]
                ids = move_ref[docs:docs + META, :].astype(F32)[0:8, lane]
            else:
                block = move_ref[:count, :]
                ids = move_ref[rest:rest + META, :].astype(F32)[0:8, 0:count]
            ids = ids.T[:, 0:1]
            total = jnp.zeros((count, 1), F32)
            for still, still_ref, still_ids in zip(stills, still_refs, metas):
                inner = lax.dot_general(
                    block, still_ref[rows, :], (((1,), (1,)), ((), ())), preferred_element_type=F32
                )
                same = ids == still_ids[:, lane]
                if target == OWN and still == OWN:
                    same &= lax.broadcasted_iota(jnp.int32, inner.shape, 0) != lax.broadcasted_iota(
                        jnp.int32, inner.shape, 1
                    )
                weights = jnp.where(same, jnp.exp2(inner), 0.0)
                total += jnp.sum(weights, axis=1, keepdims=True)
                if target != OWN:
                    out_refs[still][:, lane] += jnp.sum(weights, axis=0, keepdims=True)
            out_refs[target][:, lane] += jnp.broadcast_to(total, (count, 128)).T[0:1, :]

        if holder is None:
            work()
        else:
            pl.when(z == holder)(work)

    if flags:
        doubt = metas[0]
        for other in metas[1:]:
            doubt = doubt + other
        spot = lax.broadcasted_iota(jnp.int32, (1, lanes), 1)
        for target in range(OWN + 1):
            out_refs[target][...] += jnp.where(spot == flag, doubt[:, :lanes], 0.0)


def score(name, docs, hot, place, before, moving, stills, flags=False, outs=tuple(range(SUMS)), weight=1):
    lanes = layout(docs, hot)[3]
    plan = ([m[1:] for m in moving], [s[1] for s in stills])
    vmem = pl.BlockSpec(memory_space=pltpu.VMEM)
    pairs = len(stills) * sum((hot if m[1] == "h" else docs - hot) ** 2 for m in moving)
    arrays = [*before, *(m[0] for m in moving), *(s[0] for s in stills)]
    return pl.pallas_call(
        lambda *refs: score_kernel(plan, docs, hot, len(before), flags, outs, *refs),
        out_shape=tuple(jax.ShapeDtypeStruct((1, lanes), F32) for _ in outs),
        in_specs=[pl.BlockSpec(memory_space=pltpu.SMEM)] + [vmem] * len(arrays),
        out_specs=tuple(vmem for _ in outs),
        compiler_params=pltpu.CompilerParams(vmem_limit_bytes=20 * 2**20),
        cost_estimate=pl.CostEstimate(
            flops=weight * pairs, bytes_accessed=2**10, transcendentals=0
        ),
        name=name,
    )(place, *arrays)


def finish_kernel(flag, slot_ref, *refs):
    sums, out_ref, doubt_ref = refs[:-2], refs[-2], refs[-1]
    total = sums[0][...]
    for ref in sums[1:]:
        total += ref[...]
    lanes, docs = total.shape[1], slot_ref.shape[1]
    doubt_ref[...] = (total[:, flag:flag + 1] > 0.0).astype(jnp.int32)
    values = jnp.broadcast_to(jnp.log(1.0 + total * 2.0**-SHIFT), (8, lanes)).T[:, 0:1]
    here = lax.broadcasted_iota(jnp.int32, (lanes, docs), 0) == slot_ref[...]
    out_ref[...] = jnp.sum(jnp.where(here, values, 0.0), axis=0, keepdims=True)


def finish(flag, slot, sums):
    return pl.pallas_call(
        lambda *refs: finish_kernel(flag, *refs),
        out_shape=(jax.ShapeDtypeStruct(slot.shape, F32), jax.ShapeDtypeStruct((1, 1), jnp.int32)),
        name="finish",
    )(slot, *sums)


def meeting_plan(states, proj_weight, cluster_of):
    owners = lax.axis_size("owner")
    columns = owners // ROWS
    docs = states.shape[0]
    hot = 3 * docs // owners
    flag = layout(docs, hot)[2]

    owner = lax.axis_index("owner")
    place = (owner // ROWS).astype(jnp.int32).reshape(1)
    q, even, odd, slot = prep(hot, place, cluster_of, states, proj_weight)

    def move(a, to):
        return lax.ppermute(
            a, "owner", [(z * ROWS + y, to[z] * ROWS + y) for z in range(columns) for y in range(ROWS)]
        )

    def outer(a):
        return move(a, (1, 0, 3, 2))

    def middle(a):
        return move(a, (0, 2, 1, 3))

    def ends(a):
        return move(a, (3, 1, 2, 0))

    def other_row(a):
        return lax.ppermute(a, "owner", [(i, i ^ 1) for i in range(owners)])

    def other_core(a):
        return lax.ppermute(a, "split", [(0, 1), (1, 0)])

    def across(a):
        return lax.ppermute(a, ("owner", "split"), [(i, i ^ 3) for i in range(2 * owners)])

    def ahead(a, step):
        return move(a, tuple((z + step) % columns for z in range(columns)))

    def after(a, *others):
        return lax.optimization_barrier((a, *others))[0]

    def meet(name, before, moving, stills, **options):
        return score(name, docs, hot, place, before, moving, stills, **options)

    first_outer = outer(even)
    first_middle = middle(odd)
    qy = other_row(q)
    qc = other_core(q)
    first_ends = ends(even)
    own = [(q, "n", OWN, None), (q, "h", OWN, None)]
    near = [(q, 3), (qc, 4)]
    sums = meet("near", (), own, near)

    first_outer, first_middle, _ = lax.optimization_barrier((first_outer, first_middle, sums[0]))
    then_outer = outer(first_middle)
    then_middle = middle(first_outer)
    hop1 = [
        (first_outer, "n", 0, 0), (first_outer, "h", 2, 1), (first_outer, "n", 0, 2), (first_outer, "h", 2, 3),
        (first_middle, "n", 0, 1), (first_middle, "h", 2, 2),
    ]
    qyc = other_core(qy)
    sums = meet("own_far", sums, own, [(qy, 5)])
    sums = meet("hop1", sums, hop1, near + [(qy, 5)], weight=2**16)
    sums = meet("far", sums, own + hop1, [(qyc, 6)])
    far = [(qy, 5), (qyc, 6)]
    hop3 = [(first_ends, "n", 2, 0), (first_ends, "h", 0, 3)]
    sums = meet("hop3", sums, hop3, near + far, flags=True)
    hop2 = [
        (then_outer, "n", 1, 0), (then_outer, "h", 1, 3), (then_middle, "n", 1, 1), (then_middle, "h", 1, 2),
    ]
    sums = meet("hop2", sums, hop2, near + far)
    back = [ahead(sums[i], i + 1) for i in (2, 1, 0)]
    back += [across(sums[6]), other_row(sums[5]), other_core(sums[4]), sums[OWN]]
    fast, doubt = finish(flag, slot, back)
    return lax.cond(
        doubt[0, 0] > 0, owner_plan, lambda *_: fast.reshape(docs), states, proj_weight, cluster_of
    )


def on_device(states, proj_weight, cluster_of):
    if (lax.axis_size("owner"), lax.axis_size("split")) == (8, 2) and states.shape[0] == 512:
        return meeting_plan(states, proj_weight, cluster_of)
    return owner_plan(states, proj_weight, cluster_of)


def solution(mesh):
    placed = (P(("parts", "owner", "split"), None), P(), P(("parts", "owner", "split")))
    return jax.shard_map(
        on_device,
        mesh=mesh,
        in_specs=placed,
        out_specs=P(("parts", "owner", "split")),
        check_vma=False,
    )
```

```python
import math

import jax
import jax.numpy as jnp
from jax import lax
from jax.experimental import pallas as pl
from jax.experimental.pallas import tpu as pltpu
from jax.sharding import PartitionSpec as P

CLUS_OWN = 2
TAU = 0.05
THRESH = 0.2
EPS = 1e-06
LOG2E = math.log2(math.e)
SCALE = LOG2E / TAU
SHIFT = THRESH * LOG2E / TAU

ROWS = 2
F32 = jnp.float32
BF16 = jnp.bfloat16


def prepare(states, proj_weight):
    projected = jnp.dot(states, proj_weight, preferred_element_type=jnp.float32)
    unit = projected * lax.rsqrt(jnp.sum(projected * projected, axis=1, keepdims=True) + EPS)
    peak = jnp.max(jnp.abs(unit), axis=1).astype(jnp.bfloat16)
    quant = (unit / peak.astype(jnp.float32)[:, None]).astype(jnp.bfloat16)
    return (quant, peak)


def similarity_scores(
    own_quant, own_peak, own_cluster, own_index, col_quant, col_peak, col_cluster, col_index
):
    row_count = own_quant.shape[0]
    block = math.gcd(row_count, 768)
    col_scale = col_peak.astype(jnp.float32)

    def one_block(start):
        quant_rows = lax.dynamic_slice_in_dim(own_quant, start, block, 0)
        scale_rows = lax.dynamic_slice_in_dim(own_peak, start, block, 0).astype(jnp.float32)
        cluster_rows = lax.dynamic_slice_in_dim(own_cluster, start, block, 0)
        index_rows = lax.dynamic_slice_in_dim(own_index, start, block, 0)
        inner = lax.dot_general(
            quant_rows, col_quant, (((1,), (1,)), ((), ())), preferred_element_type=jnp.float32
        )
        cosine = inner * scale_rows[:, None] * col_scale[None, :]
        same = (cluster_rows[:, None] == col_cluster[None, :]) & (
            index_rows[:, None] != col_index[None, :]
        )
        weights = jnp.where(same, jnp.exp((cosine - THRESH) / TAU), jnp.zeros_like(cosine))
        return jnp.log(1.0 + jnp.sum(weights, axis=1))

    starts = jnp.arange(row_count // block, dtype=jnp.int32) * block
    return lax.map(one_block, starts).reshape(row_count)


def owner_plan(states, proj_weight, cluster_of):
    owners = lax.axis_size("owner")
    splits = lax.axis_size("split")
    half_index = lax.axis_index("split")
    doc_count = states.shape[0]
    capacity = 3 * doc_count // owners
    width = proj_weight.shape[1]
    slot_total = owners * capacity
    quant, peak = prepare(states, proj_weight)
    group_of = cluster_of // CLUS_OWN
    onehot = (group_of[:, None] == jnp.arange(owners, dtype=jnp.int32)[None, :]).astype(jnp.int32)
    before = jnp.cumsum(onehot, axis=0) - onehot
    target = group_of * capacity + jnp.sum(before * onehot, axis=1)
    quant_slots = (
        jnp.zeros((slot_total, width), jnp.bfloat16)
        .at[target]
        .set(quant)
        .reshape(owners, capacity, width)
    )
    peak_slots = (
        jnp.zeros((slot_total,), jnp.bfloat16).at[target].set(peak).reshape(owners, capacity)
    )
    cluster_slots = (
        jnp.full((slot_total,), -1, jnp.int32).at[target].set(cluster_of).reshape(owners, capacity)
    )
    positions = (
        jnp.arange(owners, dtype=jnp.int32)[:, None] * (splits * capacity)
        + jnp.arange(capacity, dtype=jnp.int32)[None, :]
    )
    own_index = (positions + half_index * capacity).reshape(slot_total)
    col_index = jnp.arange(splits * slot_total, dtype=jnp.int32)
    own_quant, own_peak, own_cluster = (
        lax.all_to_all(a, "owner", split_axis=0, concat_axis=0, tiled=True)
        for a in (quant_slots, peak_slots, cluster_slots)
    )
    all_quant, all_peak, all_cluster = (
        lax.all_gather(a, "split", axis=1, tiled=True) for a in (own_quant, own_peak, own_cluster)
    )
    scores = similarity_scores(
        own_quant.reshape(slot_total, width),
        own_peak.reshape(slot_total),
        own_cluster.reshape(slot_total),
        own_index,
        all_quant.reshape(splits * slot_total, width),
        all_peak.reshape(splits * slot_total),
        all_cluster.reshape(splits * slot_total),
        col_index,
    )
    returned = lax.all_to_all(
        scores.reshape(owners, capacity), "owner", split_axis=0, concat_axis=0, tiled=True
    )
    return returned.reshape(slot_total)[target]


def up(n, m):
    return -(-n // m) * m


META = 16


def layout(docs, hot):
    rest = docs - hot
    first = up(rest, 128)
    flag = first + hot
    return rest, first, flag, up(flag + 1, 128)


def prep_kernel(hot, place_ref, cl_ref, st_ref, w_ref, same_ref, other_ref, slot_ref, vectors):
    docs = st_ref.shape[0]
    rest, first, flag, lanes = layout(docs, hot)
    tile = 128

    cluster = cl_ref[...]
    group = cluster // CLUS_OWN
    member = lax.broadcasted_iota(jnp.int32, (8, docs), 0) == group
    full = jnp.sum(member.astype(F32), axis=1, keepdims=True) == float(hot)
    chosen = jnp.min(
        jnp.where(full, lax.broadcasted_iota(jnp.int32, (8, 1), 0), 8), axis=0, keepdims=True
    )
    doubt = jnp.where(jnp.sum(full.astype(F32), axis=0, keepdims=True) == 1.0, 0.0, 1.0)
    in_hot = group == chosen

    for t in range(docs // tile):
        rows = slice(t * tile, (t + 1) * tile)
        projected = jnp.dot(st_ref[rows, :], w_ref[...], preferred_element_type=F32)
        norm = lax.rsqrt(jnp.sum(projected * projected, axis=1, keepdims=True) + EPS)
        vectors[rows, :] = (projected * (norm * math.sqrt(SCALE))).astype(BF16)

    ahead = (
        lax.broadcasted_iota(jnp.int32, (docs, docs), 0) < lax.broadcasted_iota(jnp.int32, (docs, docs), 1)
    ).astype(F32).astype(BF16)
    hot_rows = jnp.broadcast_to(in_hot.astype(F32), (8, docs)).astype(BF16)
    rank = jnp.dot(hot_rows, ahead, preferred_element_type=F32)[0:1, :].astype(jnp.int32)
    place = lax.broadcasted_iota(jnp.int32, (1, docs), 1)
    slot = jnp.where(in_hot, first + rank, place - rank)
    slot_ref[...] = slot

    sort = (lax.broadcasted_iota(jnp.int32, (lanes, docs), 0) == slot).astype(F32).astype(BF16)
    cluster_rows = jnp.broadcast_to(cluster.astype(F32), (META, docs)).astype(BF16)
    sorted_n = jnp.dot(sort[:rest, :], vectors[...], preferred_element_type=F32).astype(BF16)
    sorted_h = jnp.dot(sort[first:flag, :], vectors[...], preferred_element_type=F32).astype(BF16)
    ids = lax.dot_general(
        cluster_rows, sort, (((1,), (1,)), ((), ())), preferred_element_type=F32
    )
    ids = ids.astype(BF16)


    def fill_n(ref):
        ref[:rest, :] = sorted_n
        ref[rest:, :] = jnp.zeros((META, ref.shape[1]), BF16)
        ref[rest:, :first] = ids[:, :first]
        ref[rest:, first:first + 128] = jnp.broadcast_to(doubt.astype(BF16), (META, 128))

    def fill_h(ref):
        ref[:hot, :] = sorted_h
        ref[hot:, :] = jnp.zeros((rest + META - hot, ref.shape[1]), BF16)
        ref[rest:, :lanes - first] = ids[:, first:]
        ref[rest:, first:first + 128] = jnp.broadcast_to(doubt.astype(BF16), (META, 128))

    even = lax.rem(place_ref[0], 2) == 0

    @pl.when(even)
    def _():
        fill_h(same_ref)
        fill_n(other_ref)

    @pl.when(jnp.logical_not(even))
    def _():
        fill_n(same_ref)
        fill_h(other_ref)


def prep(hot, place, cluster_of, states, proj_weight):
    docs, width = states.shape[0], proj_weight.shape[1]
    rest = docs - hot
    shape = jax.ShapeDtypeStruct
    vmem = pl.BlockSpec(memory_space=pltpu.VMEM)
    return pl.pallas_call(
        lambda *refs: prep_kernel(hot, *refs),
        out_shape=(
            shape((rest + META, width), BF16),
            shape((rest + META, width), BF16),
            shape((1, docs), jnp.int32),
        ),
        in_specs=[pl.BlockSpec(memory_space=pltpu.SMEM), vmem, vmem, vmem],
        scratch_shapes=[pltpu.VMEM((docs, width), BF16)],
        compiler_params=pltpu.CompilerParams(vmem_limit_bytes=24 * 2**20),
        name="prep",
    )(place, cluster_of.reshape(1, docs), states, proj_weight)


OWN, PAIR = "own", "pair"
CORE, PAIR_CORE = "core", "pair_core"
ROW, PAIR_ROW = "row", "pair_row"
DIAG, PAIR_DIAG = "diag", "pair_diag"
NEXT, FAR = "next", "far"


def score_kernel(docs, hot, names, tasks, carried, made, flagged, *refs):
    rest, first, flag, lanes = layout(docs, hot)
    place_ref, refs = refs[0], refs[1:]
    blocks, refs = dict(zip(names, refs[:len(names)])), refs[len(names):]
    before, sums = dict(zip(carried, refs[:len(carried)])), dict(zip(made, refs[len(carried):]))
    z, y, c = place_ref[0], place_ref[1], place_ref[2]
    for name in made:
        sums[name][...] = before[name][...] if name in before else jnp.zeros((1, lanes), F32)
    when = {"core0": c == 0, "core1": c == 1, "row0": y == 0, "row1": y == 1}
    middle = (z == 1) | (z == 2)

    def meet(count, start):
        lane = slice(start, start + count)
        ids = {name: ref[rest:, :].astype(F32)[0:8, 0:count] for name, ref in blocks.items()}
        for row in dict.fromkeys(task[0] for task in tasks):

            def work(row=row):
                row_ids = ids[row].T[:, 0:1]
                for _, col, condition in [task for task in tasks if task[0] == row]:

                    def one(col=col):
                        inner = lax.dot_general(
                            blocks[row][:count, :], blocks[col][:count, :], (((1,), (1,)), ((), ())),
                            preferred_element_type=F32,
                        )
                        same = row_ids == ids[col][0:1, :]
                        if row == col:
                            same &= lax.broadcasted_iota(jnp.int32, inner.shape, 0) != lax.broadcasted_iota(
                                jnp.int32, inner.shape, 1
                            )
                        weights = jnp.where(same, jnp.exp2(inner), 0.0)
                        if row != col:
                            total = jnp.sum(weights, axis=1, keepdims=True)
                            sums[row][:, lane] += jnp.broadcast_to(total, (count, 128)).T[0:1, :]
                        sums[col][:, lane] += jnp.sum(weights, axis=0, keepdims=True)

                    if condition is None:
                        one()
                    else:
                        pl.when(when[condition])(one)

            if row in (NEXT, FAR):
                pl.when(middle)(work)
            else:
                work()

    pl.when(lax.rem(z, 2) == 0)(lambda: meet(hot, first))
    pl.when(lax.rem(z, 2) == 1)(lambda: meet(rest, 0))

    if flagged:
        doubt = sum(ref[rest:, first:first + 128].astype(F32)[0:1, 0:1] for ref in blocks.values())
        spot = lax.broadcasted_iota(jnp.int32, (1, lanes), 1)
        for name in flagged:
            sums[name][...] += jnp.where(spot == flag, doubt, 0.0)


def score(name, docs, hot, place, blocks, tasks, sums, flagged=(), weight=1):
    lanes = layout(docs, hot)[3]
    names = [b for b in blocks if flagged or any(b in task[:2] for task in tasks)]
    made = [b for b in blocks if any(b in task[:2] for task in tasks)]
    made += [b for b in flagged if b not in made]
    carried = [b for b in made if b in sums]
    vmem = pl.BlockSpec(memory_space=pltpu.VMEM)
    arrays = [blocks[b] for b in names] + [sums[b] for b in carried]
    out = pl.pallas_call(
        lambda *refs: score_kernel(docs, hot, names, tasks, carried, made, flagged, *refs),
        out_shape=tuple(jax.ShapeDtypeStruct((1, lanes), F32) for _ in made),
        in_specs=[pl.BlockSpec(memory_space=pltpu.SMEM)] + [vmem] * len(arrays),
        out_specs=tuple(vmem for _ in made),
        compiler_params=pltpu.CompilerParams(vmem_limit_bytes=20 * 2**20),
        cost_estimate=pl.CostEstimate(flops=weight, bytes_accessed=2**10, transcendentals=0),
        name=name,
    )(place, *arrays)
    return {**sums, **dict(zip(made, out))}


def finish_kernel(flag, slot_ref, *refs):
    sums, out_ref, doubt_ref = refs[:-2], refs[-2], refs[-1]
    total = sums[0][...]
    for ref in sums[1:]:
        total += ref[...]
    lanes, docs = total.shape[1], slot_ref.shape[1]
    doubt_ref[...] = (total[:, flag:flag + 1] > 0.0).astype(jnp.int32)
    values = jnp.broadcast_to(jnp.log(1.0 + total * 2.0**-SHIFT), (8, lanes)).T[:, 0:1]
    here = lax.broadcasted_iota(jnp.int32, (lanes, docs), 0) == slot_ref[...]
    out_ref[...] = jnp.sum(jnp.where(here, values, 0.0), axis=0, keepdims=True)


def finish(flag, slot, sums):
    return pl.pallas_call(
        lambda *refs: finish_kernel(flag, *refs),
        out_shape=(jax.ShapeDtypeStruct(slot.shape, F32), jax.ShapeDtypeStruct((1, 1), jnp.int32)),
        name="finish",
    )(slot, *sums)


def meeting_plan(states, proj_weight, cluster_of):
    owners = lax.axis_size("owner")
    columns = owners // ROWS
    docs = states.shape[0]
    hot = 3 * docs // owners
    flag = layout(docs, hot)[2]

    owner, core = lax.axis_index("owner"), lax.axis_index("split")
    place = jnp.stack([owner // ROWS, owner % ROWS, core]).astype(jnp.int32)
    same, other, slot = prep(hot, place, cluster_of, states, proj_weight)

    def move(a, to, row=0, core=0):
        if not core:
            return lax.ppermute(
                a, "owner", [(z * ROWS + y, to[z] * ROWS + (y ^ row)) for z in range(columns) for y in range(ROWS)]
            )
        if not row and to == STAY:
            return lax.ppermute(a, "split", [(0, 1), (1, 0)])
        return lax.ppermute(
            a, ("owner", "split"),
            [
                ((z * ROWS + y) * 2 + c, (to[z] * ROWS + (y ^ row)) * 2 + (c ^ core))
                for z in range(columns) for y in range(ROWS) for c in range(2)
            ],
        )

    STAY, OUTER, MIDDLE, TWO = (0, 1, 2, 3), (1, 0, 3, 2), (0, 2, 1, 3), (2, 3, 0, 1)
    TO_MIDDLE = (2, 0, 3, 1)

    def meet(name, tasks, **options):
        return score(name, docs, hot, place, blocks, tasks, sums, **options)

    blocks, sums = {OWN: same}, {}
    blocks[PAIR] = move(other, OUTER)
    blocks[ROW] = move(same, STAY, row=1)
    blocks[NEXT] = move(other, MIDDLE)
    blocks[CORE] = move(same, STAY, core=1)
    blocks[FAR] = move(same, TO_MIDDLE)
    sums = meet("own", [(OWN, OWN, None), (OWN, CORE, "core0")], weight=2**33)

    pair, blocks[NEXT], _ = lax.optimization_barrier((blocks[PAIR], blocks[NEXT], sums[OWN]))
    blocks[PAIR] = pair
    blocks[PAIR_ROW] = move(pair, STAY, row=1)
    blocks[PAIR_CORE] = move(pair, STAY, core=1)
    blocks[DIAG] = move(blocks[ROW], STAY, core=1)
    sums = meet(
        "pair", [(PAIR, PAIR, None), (PAIR, OWN, None), (PAIR, CORE, None), (PAIR, PAIR_CORE, "core1")]
    )
    sums = meet("next", [(NEXT, b, None) for b in (OWN, CORE, PAIR, PAIR_CORE)], weight=2**33)
    sums = meet(
        "row",
        [(PAIR, ROW, None), (PAIR, DIAG, None), (OWN, ROW, "row0"), (OWN, DIAG, "row1"),
         (NEXT, ROW, None), (NEXT, DIAG, None)],
    )
    blocks[PAIR_ROW], _ = lax.optimization_barrier((blocks[PAIR_ROW], sums[ROW]))
    blocks[PAIR_DIAG] = move(blocks[PAIR_ROW], STAY, core=1)
    sums = meet("far", [(FAR, b, None) for b in (OWN, CORE, PAIR, PAIR_CORE, ROW, DIAG)])
    early = [
        move(sums[CORE], STAY, core=1),
        move(sums[PAIR_CORE], OUTER, core=1),
        move(sums[ROW], STAY, row=1),
        move(sums[DIAG], STAY, row=1, core=1),
    ]
    sums = meet("pair_row", [(PAIR, PAIR_ROW, "row1"), (NEXT, PAIR_ROW, None), (FAR, PAIR_ROW, None)])
    sums = meet(
        "pair_diag",
        [(PAIR, PAIR_DIAG, "row0"), (NEXT, PAIR_DIAG, None), (FAR, PAIR_DIAG, None)],
        flagged=(OWN, FAR),
    )
    back = early + [
        move(sums[FAR], TWO),
        move(sums[NEXT], MIDDLE),
        move(sums[PAIR_DIAG], OUTER, row=1, core=1),
        move(sums[PAIR_ROW], OUTER, row=1),
        move(sums[PAIR], OUTER),
        sums[OWN],
    ]
    fast, doubt = finish(flag, slot, back)
    return lax.cond(
        doubt[0, 0] > 0, owner_plan, lambda *_: fast.reshape(docs), states, proj_weight, cluster_of
    )


def on_device(states, proj_weight, cluster_of):
    if (lax.axis_size("owner"), lax.axis_size("split")) == (8, 2) and states.shape[0] == 512:
        return meeting_plan(states, proj_weight, cluster_of)
    return owner_plan(states, proj_weight, cluster_of)


def solution(mesh):
    placed = (P(("parts", "owner", "split"), None), P(), P(("parts", "owner", "split")))
    return jax.shard_map(
        on_device,
        mesh=mesh,
        in_specs=placed,
        out_specs=P(("parts", "owner", "split")),
        check_vma=False,
    )
```

```python
import math

import jax
import jax.numpy as jnp
from jax import lax
from jax.experimental import pallas as pl
from jax.experimental.pallas import tpu as pltpu
from jax.sharding import PartitionSpec as P

CLUS_OWN = 2
TAU = 0.05
THRESH = 0.2
EPS = 1e-06
LOG2E = math.log2(math.e)
SCALE = LOG2E / TAU
SHIFT = THRESH * LOG2E / TAU

ROWS = 2
F32 = jnp.float32
BF16 = jnp.bfloat16


def prepare(states, proj_weight):
    projected = jnp.dot(states, proj_weight, preferred_element_type=jnp.float32)
    unit = projected * lax.rsqrt(jnp.sum(projected * projected, axis=1, keepdims=True) + EPS)
    peak = jnp.max(jnp.abs(unit), axis=1).astype(jnp.bfloat16)
    quant = (unit / peak.astype(jnp.float32)[:, None]).astype(jnp.bfloat16)
    return (quant, peak)


def similarity_scores(
    own_quant, own_peak, own_cluster, own_index, col_quant, col_peak, col_cluster, col_index
):
    row_count = own_quant.shape[0]
    block = math.gcd(row_count, 768)
    col_scale = col_peak.astype(jnp.float32)

    def one_block(start):
        quant_rows = lax.dynamic_slice_in_dim(own_quant, start, block, 0)
        scale_rows = lax.dynamic_slice_in_dim(own_peak, start, block, 0).astype(jnp.float32)
        cluster_rows = lax.dynamic_slice_in_dim(own_cluster, start, block, 0)
        index_rows = lax.dynamic_slice_in_dim(own_index, start, block, 0)
        inner = lax.dot_general(
            quant_rows, col_quant, (((1,), (1,)), ((), ())), preferred_element_type=jnp.float32
        )
        cosine = inner * scale_rows[:, None] * col_scale[None, :]
        same = (cluster_rows[:, None] == col_cluster[None, :]) & (
            index_rows[:, None] != col_index[None, :]
        )
        weights = jnp.where(same, jnp.exp((cosine - THRESH) / TAU), jnp.zeros_like(cosine))
        return jnp.log(1.0 + jnp.sum(weights, axis=1))

    starts = jnp.arange(row_count // block, dtype=jnp.int32) * block
    return lax.map(one_block, starts).reshape(row_count)


def owner_plan(states, proj_weight, cluster_of):
    owners = lax.axis_size("owner")
    splits = lax.axis_size("split")
    half_index = lax.axis_index("split")
    doc_count = states.shape[0]
    capacity = 3 * doc_count // owners
    width = proj_weight.shape[1]
    slot_total = owners * capacity
    quant, peak = prepare(states, proj_weight)
    group_of = cluster_of // CLUS_OWN
    onehot = (group_of[:, None] == jnp.arange(owners, dtype=jnp.int32)[None, :]).astype(jnp.int32)
    before = jnp.cumsum(onehot, axis=0) - onehot
    target = group_of * capacity + jnp.sum(before * onehot, axis=1)
    quant_slots = (
        jnp.zeros((slot_total, width), jnp.bfloat16)
        .at[target]
        .set(quant)
        .reshape(owners, capacity, width)
    )
    peak_slots = (
        jnp.zeros((slot_total,), jnp.bfloat16).at[target].set(peak).reshape(owners, capacity)
    )
    cluster_slots = (
        jnp.full((slot_total,), -1, jnp.int32).at[target].set(cluster_of).reshape(owners, capacity)
    )
    positions = (
        jnp.arange(owners, dtype=jnp.int32)[:, None] * (splits * capacity)
        + jnp.arange(capacity, dtype=jnp.int32)[None, :]
    )
    own_index = (positions + half_index * capacity).reshape(slot_total)
    col_index = jnp.arange(splits * slot_total, dtype=jnp.int32)
    own_quant, own_peak, own_cluster = (
        lax.all_to_all(a, "owner", split_axis=0, concat_axis=0, tiled=True)
        for a in (quant_slots, peak_slots, cluster_slots)
    )
    all_quant, all_peak, all_cluster = (
        lax.all_gather(a, "split", axis=1, tiled=True) for a in (own_quant, own_peak, own_cluster)
    )
    scores = similarity_scores(
        own_quant.reshape(slot_total, width),
        own_peak.reshape(slot_total),
        own_cluster.reshape(slot_total),
        own_index,
        all_quant.reshape(splits * slot_total, width),
        all_peak.reshape(splits * slot_total),
        all_cluster.reshape(splits * slot_total),
        col_index,
    )
    returned = lax.all_to_all(
        scores.reshape(owners, capacity), "owner", split_axis=0, concat_axis=0, tiled=True
    )
    return returned.reshape(slot_total)[target]


def up(n, m):
    return -(-n // m) * m


META = 16


def layout(docs, hot):
    rest = docs - hot
    first = up(rest, 128)
    flag = first + hot
    return rest, first, flag, up(flag + 1, 128)


def prep_kernel(hot, place_ref, cl_ref, st_ref, w_ref, same_ref, other_ref, slot_ref, vectors):
    docs = st_ref.shape[0]
    rest, first, flag, lanes = layout(docs, hot)
    tile = 128

    cluster = cl_ref[...]
    group = cluster // CLUS_OWN
    member = lax.broadcasted_iota(jnp.int32, (8, docs), 0) == group
    full = jnp.sum(member.astype(F32), axis=1, keepdims=True) == float(hot)
    chosen = jnp.min(
        jnp.where(full, lax.broadcasted_iota(jnp.int32, (8, 1), 0), 8), axis=0, keepdims=True
    )
    doubt = jnp.where(jnp.sum(full.astype(F32), axis=0, keepdims=True) == 1.0, 0.0, 1.0)
    in_hot = group == chosen

    for t in range(docs // tile):
        rows = slice(t * tile, (t + 1) * tile)
        projected = jnp.dot(st_ref[rows, :], w_ref[...], preferred_element_type=F32)
        norm = lax.rsqrt(jnp.sum(projected * projected, axis=1, keepdims=True) + EPS)
        vectors[rows, :] = (projected * (norm * math.sqrt(SCALE))).astype(BF16)

    ahead = (
        lax.broadcasted_iota(jnp.int32, (docs, docs), 0) < lax.broadcasted_iota(jnp.int32, (docs, docs), 1)
    ).astype(F32).astype(BF16)
    hot_rows = jnp.broadcast_to(in_hot.astype(F32), (8, docs)).astype(BF16)
    rank = jnp.dot(hot_rows, ahead, preferred_element_type=F32)[0:1, :].astype(jnp.int32)
    place = lax.broadcasted_iota(jnp.int32, (1, docs), 1)
    slot = jnp.where(in_hot, first + rank, place - rank)
    slot_ref[...] = slot

    sort = (lax.broadcasted_iota(jnp.int32, (lanes, docs), 0) == slot).astype(F32).astype(BF16)
    cluster_rows = jnp.broadcast_to(cluster.astype(F32), (META, docs)).astype(BF16)
    sorted_n = jnp.dot(sort[:rest, :], vectors[...], preferred_element_type=F32).astype(BF16)
    sorted_h = jnp.dot(sort[first:flag, :], vectors[...], preferred_element_type=F32).astype(BF16)
    ids = lax.dot_general(
        cluster_rows, sort, (((1,), (1,)), ((), ())), preferred_element_type=F32
    )
    ids = ids.astype(BF16)


    def fill_n(ref):
        ref[:rest, :] = sorted_n
        ref[rest:, :] = jnp.zeros((META, ref.shape[1]), BF16)
        ref[rest:, :first] = ids[:, :first]
        ref[rest:, first:first + 128] = jnp.broadcast_to(doubt.astype(BF16), (META, 128))

    def fill_h(ref):
        ref[:hot, :] = sorted_h
        ref[hot:, :] = jnp.zeros((rest + META - hot, ref.shape[1]), BF16)
        ref[rest:, :lanes - first] = ids[:, first:]
        ref[rest:, first:first + 128] = jnp.broadcast_to(doubt.astype(BF16), (META, 128))

    even = lax.rem(place_ref[0], 2) == 0

    @pl.when(even)
    def _():
        fill_h(same_ref)
        fill_n(other_ref)

    @pl.when(jnp.logical_not(even))
    def _():
        fill_n(same_ref)
        fill_h(other_ref)


def prep(hot, place, cluster_of, states, proj_weight):
    docs, width = states.shape[0], proj_weight.shape[1]
    rest = docs - hot
    shape = jax.ShapeDtypeStruct
    vmem = pl.BlockSpec(memory_space=pltpu.VMEM)
    return pl.pallas_call(
        lambda *refs: prep_kernel(hot, *refs),
        out_shape=(
            shape((rest + META, width), BF16),
            shape((rest + META, width), BF16),
            shape((1, docs), jnp.int32),
        ),
        in_specs=[pl.BlockSpec(memory_space=pltpu.SMEM), vmem, vmem, vmem],
        scratch_shapes=[pltpu.VMEM((docs, width), BF16)],
        compiler_params=pltpu.CompilerParams(vmem_limit_bytes=24 * 2**20),
        name="prep",
    )(place, cluster_of.reshape(1, docs), states, proj_weight)


OWN, PAIR = "own", "pair"
CORE, PAIR_CORE = "core", "pair_core"
ROW, PAIR_ROW = "row", "pair_row"
DIAG, PAIR_DIAG = "diag", "pair_diag"
NEXT, FAR = "next", "far"
GROUPS = ((OWN, PAIR), (CORE, PAIR_CORE, DIAG, PAIR_DIAG), (ROW, PAIR_ROW), (NEXT,), (FAR,))


def score_kernel(docs, hot, names, tasks, flagged, carries, *refs):
    rest, first, flag, lanes = layout(docs, hot)
    place_ref, refs = refs[0], refs[1:]
    blocks, refs = dict(zip(names, refs[:len(names)])), refs[len(names):]
    before, refs = refs[:len(GROUPS) * carries], refs[len(GROUPS) * carries:]
    outs, (turned, parts) = refs[:len(GROUPS)], refs[len(GROUPS):]
    for k, out in enumerate(outs):
        out[...] = before[k][...] if carries else jnp.zeros(out.shape, F32)
    spots = {name: (out, k) for out, group in zip(outs, GROUPS) for k, name in enumerate(group)}
    z, y, c = place_ref[0], place_ref[1], place_ref[2]
    when = {"core0": c == 0, "core1": c == 1, "row0": y == 0, "row1": y == 1}
    middle = (z == 1) | (z == 2)
    lefts = list(dict.fromkeys(task[1] for task in tasks if task[0] != task[1]))
    width = turned.shape[0]

    def meet(count, start):
        lane = slice(start, start + count)
        wide = up(count, 128)
        ids = {name: ref[rest:, :].astype(F32)[0:8, 0:wide] for name, ref in blocks.items()}
        columns = {name: ids[name].T[0:count, 0:1] for name in dict.fromkeys(task[1] for task in tasks)}
        for k in range(len(lefts)):
            parts[k, 0:count, :] = jnp.zeros((count, 128), F32)

        for right in dict.fromkeys(task[0] for task in tasks):

            def work(right=right):
                inside = lax.broadcasted_iota(jnp.int32, (1, wide), 1) < count
                right_ids = jnp.where(inside, ids[right][0:1, :], -1.0)
                turned[:, 0:wide] = jnp.zeros((width, wide), BF16)
                turned[:, 0:count] = blocks[right][:count, :].T
                for _, left, condition in [task for task in tasks if task[0] == right]:

                    def one(left=left):
                        inner = jnp.dot(
                            blocks[left][:count, :], turned[:, 0:wide], preferred_element_type=F32
                        )
                        same = columns[left] == right_ids
                        if left == right:
                            same &= lax.broadcasted_iota(jnp.int32, inner.shape, 0) != lax.broadcasted_iota(
                                jnp.int32, inner.shape, 1
                            )
                        weights = jnp.where(same, jnp.exp2(inner), 0.0)
                        out, k = spots[right]
                        out[k, :, lane] += jnp.sum(weights, axis=0, keepdims=True)[:, 0:count]
                        if left != right:
                            part = weights[:, 0:128]
                            for t in range(128, wide, 128):
                                part += weights[:, t:t + 128]
                            parts[lefts.index(left), 0:count, :] += part

                    if condition is None:
                        one()
                    else:
                        pl.when(when[condition])(one)

            if right in (NEXT, FAR):
                pl.when(middle)(work)
            else:
                work()

        ones = jnp.ones((16, 128), BF16)
        for k, left in enumerate(lefts):
            part = parts[k, 0:count, :]
            high = part.astype(BF16)
            low = (part - high.astype(F32)).astype(BF16)
            total = sum(
                lax.dot_general(ones, term, (((1,), (1,)), ((), ())), preferred_element_type=F32)
                for term in (high, low)
            )
            out, spot = spots[left]
            out[spot, :, lane] += total[0:1, :]

    pl.when(lax.rem(z, 2) == 0)(lambda: meet(hot, first))
    pl.when(lax.rem(z, 2) == 1)(lambda: meet(rest, 0))

    if flagged:
        doubt = sum(ref[rest:, first:first + 128].astype(F32)[0:1, 0:1] for ref in blocks.values())
        spot = lax.broadcasted_iota(jnp.int32, (1, lanes), 1)
        for name in flagged:
            out, k = spots[name]
            out[k] += jnp.where(spot == flag, doubt, 0.0)


def score(name, docs, hot, place, blocks, tasks, sums, flagged=(), weight=1):
    rest, _, _, lanes = layout(docs, hot)
    names = [b for b in blocks if flagged or any(b in task[:2] for task in tasks)]
    lefts = len({task[1] for task in tasks if task[0] != task[1]})
    width = blocks[OWN].shape[1]
    vmem = pl.BlockSpec(memory_space=pltpu.VMEM)
    arrays = [blocks[b] for b in names] + list(sums)
    return pl.pallas_call(
        lambda *refs: score_kernel(docs, hot, names, tasks, flagged, bool(sums), *refs),
        out_shape=tuple(jax.ShapeDtypeStruct((len(group), 1, lanes), F32) for group in GROUPS),
        in_specs=[pl.BlockSpec(memory_space=pltpu.SMEM)] + [vmem] * len(arrays),
        out_specs=tuple(vmem for _ in GROUPS),
        scratch_shapes=[pltpu.VMEM((width, up(rest, 128)), BF16), pltpu.VMEM((lefts, rest, 128), F32)],
        compiler_params=pltpu.CompilerParams(vmem_limit_bytes=20 * 2**20),
        cost_estimate=pl.CostEstimate(flops=weight, bytes_accessed=2**10, transcendentals=0),
        name=name,
    )(place, *arrays)


def finish_kernel(flag, slot_ref, *refs):
    sums, out_ref, doubt_ref = refs[:-2], refs[-2], refs[-1]
    total = sums[0][0]
    for ref in sums[1:]:
        total += ref[0]
    lanes, docs = total.shape[1], slot_ref.shape[1]
    doubt_ref[...] = (total[:, flag:flag + 1] > 0.0).astype(jnp.int32)
    values = jnp.broadcast_to(jnp.log(1.0 + total * 2.0**-SHIFT), (8, lanes)).T[:, 0:1]
    here = lax.broadcasted_iota(jnp.int32, (lanes, docs), 0) == slot_ref[...]
    out_ref[...] = jnp.sum(jnp.where(here, values, 0.0), axis=0, keepdims=True)


def finish(flag, slot, sums):
    return pl.pallas_call(
        lambda *refs: finish_kernel(flag, *refs),
        out_shape=(jax.ShapeDtypeStruct(slot.shape, F32), jax.ShapeDtypeStruct((1, 1), jnp.int32)),
        name="finish",
    )(slot, *sums)


def meeting_plan(states, proj_weight, cluster_of):
    owners = lax.axis_size("owner")
    columns = owners // ROWS
    docs = states.shape[0]
    hot = 3 * docs // owners
    flag = layout(docs, hot)[2]

    owner, core = lax.axis_index("owner"), lax.axis_index("split")
    place = jnp.stack([owner // ROWS, owner % ROWS, core]).astype(jnp.int32)
    same, other, slot = prep(hot, place, cluster_of, states, proj_weight)

    def move(a, to, row=0, core=0):
        if not core:
            return lax.ppermute(
                a, "owner", [(z * ROWS + y, to[z] * ROWS + (y ^ row)) for z in range(columns) for y in range(ROWS)]
            )
        if not row and to == STAY:
            return lax.ppermute(a, "split", [(0, 1), (1, 0)])
        return lax.ppermute(
            a, ("owner", "split"),
            [
                ((z * ROWS + y) * 2 + c, (to[z] * ROWS + (y ^ row)) * 2 + (c ^ core))
                for z in range(columns) for y in range(ROWS) for c in range(2)
            ],
        )

    STAY, OUTER, MIDDLE, TWO = (0, 1, 2, 3), (1, 0, 3, 2), (0, 2, 1, 3), (2, 3, 0, 1)
    TO_MIDDLE = (2, 0, 3, 1)

    def meet(name, tasks, **options):
        return score(name, docs, hot, place, blocks, tasks, sums, **options)

    blocks, sums = {OWN: same}, ()
    blocks[NEXT] = move(other, MIDDLE)
    blocks[PAIR] = move(other, OUTER)
    blocks[ROW] = move(same, STAY, row=1)
    blocks[CORE] = move(same, STAY, core=1)
    sums = meet("own", [(OWN, OWN, None), (OWN, CORE, "core0")], weight=2**33)

    blocks[PAIR], blocks[NEXT], _ = lax.optimization_barrier((blocks[PAIR], blocks[NEXT], sums[0]))
    blocks[FAR] = move(same, TO_MIDDLE)
    blocks[PAIR_ROW] = move(blocks[PAIR], STAY, row=1)
    blocks[PAIR_CORE] = move(blocks[PAIR], STAY, core=1)
    blocks[DIAG] = move(blocks[ROW], STAY, core=1)
    sums = meet(
        "pair",
        [(PAIR, PAIR, None), (PAIR, OWN, None), (PAIR, CORE, None), (PAIR, PAIR_CORE, "core1")]
        + [(NEXT, b, None) for b in (OWN, CORE, PAIR, PAIR_CORE)],
        weight=2**33,
    )
    sums = meet(
        "row",
        [(PAIR, ROW, None), (PAIR, DIAG, None), (OWN, ROW, "row0"), (OWN, DIAG, "row1"),
         (NEXT, ROW, None), (NEXT, DIAG, None)],
    )
    blocks[PAIR_ROW], _ = lax.optimization_barrier((blocks[PAIR_ROW], sums[0]))
    blocks[PAIR_DIAG] = move(blocks[PAIR_ROW], STAY, core=1)
    sums = meet("far", [(FAR, b, None) for b in (OWN, CORE, PAIR, PAIR_CORE, ROW, DIAG)])
    sums = meet(
        "last",
        [(PAIR, PAIR_ROW, "row1"), (PAIR, PAIR_DIAG, "row0")]
        + [(b, c, None) for b in (NEXT, FAR) for c in (PAIR_ROW, PAIR_DIAG)],
        flagged=(OWN, FAR),
    )
    home, by_core, by_row, to_next, to_far = sums
    from_far, from_next = move(to_far, TWO), move(to_next, MIDDLE)
    from_core = move(by_core, STAY, core=1)
    from_row = move(by_row + from_core[2:4], STAY, row=1)
    home = home + from_core[0:2] + from_row
    from_pair = move(home[1:2], OUTER)
    fast, doubt = finish(flag, slot, (home, from_pair, from_far, from_next))
    return lax.cond(
        doubt[0, 0] > 0, owner_plan, lambda *_: fast.reshape(docs), states, proj_weight, cluster_of
    )


def on_device(states, proj_weight, cluster_of):
    if (lax.axis_size("owner"), lax.axis_size("split")) == (8, 2) and states.shape[0] == 512:
        return meeting_plan(states, proj_weight, cluster_of)
    return owner_plan(states, proj_weight, cluster_of)


def solution(mesh):
    placed = (P(("parts", "owner", "split"), None), P(), P(("parts", "owner", "split")))
    return jax.shard_map(
        on_device,
        mesh=mesh,
        in_specs=placed,
        out_specs=P(("parts", "owner", "split")),
        check_vma=False,
    )
```

```python
import math

import jax
import jax.numpy as jnp
from jax import lax
from jax.experimental import pallas as pl
from jax.experimental.pallas import tpu as pltpu
from jax.sharding import PartitionSpec as P

CLUS_OWN = 2
TAU = 0.05
THRESH = 0.2
EPS = 1e-06
LOG2E = math.log2(math.e)
SCALE = LOG2E / TAU
SHIFT = THRESH * LOG2E / TAU

ROWS = 2
F32 = jnp.float32
BF16 = jnp.bfloat16


def prepare(states, proj_weight):
    projected = jnp.dot(states, proj_weight, preferred_element_type=jnp.float32)
    unit = projected * lax.rsqrt(jnp.sum(projected * projected, axis=1, keepdims=True) + EPS)
    peak = jnp.max(jnp.abs(unit), axis=1).astype(jnp.bfloat16)
    quant = (unit / peak.astype(jnp.float32)[:, None]).astype(jnp.bfloat16)
    return (quant, peak)


def similarity_scores(
    own_quant, own_peak, own_cluster, own_index, col_quant, col_peak, col_cluster, col_index
):
    row_count = own_quant.shape[0]
    block = math.gcd(row_count, 768)
    col_scale = col_peak.astype(jnp.float32)

    def one_block(start):
        quant_rows = lax.dynamic_slice_in_dim(own_quant, start, block, 0)
        scale_rows = lax.dynamic_slice_in_dim(own_peak, start, block, 0).astype(jnp.float32)
        cluster_rows = lax.dynamic_slice_in_dim(own_cluster, start, block, 0)
        index_rows = lax.dynamic_slice_in_dim(own_index, start, block, 0)
        inner = lax.dot_general(
            quant_rows, col_quant, (((1,), (1,)), ((), ())), preferred_element_type=jnp.float32
        )
        cosine = inner * scale_rows[:, None] * col_scale[None, :]
        same = (cluster_rows[:, None] == col_cluster[None, :]) & (
            index_rows[:, None] != col_index[None, :]
        )
        weights = jnp.where(same, jnp.exp((cosine - THRESH) / TAU), jnp.zeros_like(cosine))
        return jnp.log(1.0 + jnp.sum(weights, axis=1))

    starts = jnp.arange(row_count // block, dtype=jnp.int32) * block
    return lax.map(one_block, starts).reshape(row_count)


def owner_plan(states, proj_weight, cluster_of):
    owners = lax.axis_size("owner")
    splits = lax.axis_size("split")
    half_index = lax.axis_index("split")
    doc_count = states.shape[0]
    capacity = 3 * doc_count // owners
    width = proj_weight.shape[1]
    slot_total = owners * capacity
    quant, peak = prepare(states, proj_weight)
    group_of = cluster_of // CLUS_OWN
    onehot = (group_of[:, None] == jnp.arange(owners, dtype=jnp.int32)[None, :]).astype(jnp.int32)
    before = jnp.cumsum(onehot, axis=0) - onehot
    target = group_of * capacity + jnp.sum(before * onehot, axis=1)
    quant_slots = (
        jnp.zeros((slot_total, width), jnp.bfloat16)
        .at[target]
        .set(quant)
        .reshape(owners, capacity, width)
    )
    peak_slots = (
        jnp.zeros((slot_total,), jnp.bfloat16).at[target].set(peak).reshape(owners, capacity)
    )
    cluster_slots = (
        jnp.full((slot_total,), -1, jnp.int32).at[target].set(cluster_of).reshape(owners, capacity)
    )
    positions = (
        jnp.arange(owners, dtype=jnp.int32)[:, None] * (splits * capacity)
        + jnp.arange(capacity, dtype=jnp.int32)[None, :]
    )
    own_index = (positions + half_index * capacity).reshape(slot_total)
    col_index = jnp.arange(splits * slot_total, dtype=jnp.int32)
    own_quant, own_peak, own_cluster = (
        lax.all_to_all(a, "owner", split_axis=0, concat_axis=0, tiled=True)
        for a in (quant_slots, peak_slots, cluster_slots)
    )
    all_quant, all_peak, all_cluster = (
        lax.all_gather(a, "split", axis=1, tiled=True) for a in (own_quant, own_peak, own_cluster)
    )
    scores = similarity_scores(
        own_quant.reshape(slot_total, width),
        own_peak.reshape(slot_total),
        own_cluster.reshape(slot_total),
        own_index,
        all_quant.reshape(splits * slot_total, width),
        all_peak.reshape(splits * slot_total),
        all_cluster.reshape(splits * slot_total),
        col_index,
    )
    returned = lax.all_to_all(
        scores.reshape(owners, capacity), "owner", split_axis=0, concat_axis=0, tiled=True
    )
    return returned.reshape(slot_total)[target]


def up(n, m):
    return -(-n // m) * m


META = 16


def layout(docs, hot):
    rest = docs - hot
    first = up(rest, 128)
    flag = first + hot
    return rest, first, flag, up(flag + 1, 128)


def prep_kernel(hot, place_ref, cl_ref, st_ref, w_ref, same_ref, other_ref, slot_ref, vectors):
    docs = st_ref.shape[0]
    rest, first, flag, lanes = layout(docs, hot)
    tile = 128

    cluster = cl_ref[...]
    group = cluster // CLUS_OWN
    member = lax.broadcasted_iota(jnp.int32, (8, docs), 0) == group
    full = jnp.sum(member.astype(F32), axis=1, keepdims=True) == float(hot)
    chosen = jnp.min(
        jnp.where(full, lax.broadcasted_iota(jnp.int32, (8, 1), 0), 8), axis=0, keepdims=True
    )
    doubt = jnp.where(jnp.sum(full.astype(F32), axis=0, keepdims=True) == 1.0, 0.0, 1.0)
    in_hot = group == chosen

    for t in range(docs // tile):
        rows = slice(t * tile, (t + 1) * tile)
        projected = jnp.dot(st_ref[rows, :], w_ref[...], preferred_element_type=F32)
        norm = lax.rsqrt(jnp.sum(projected * projected, axis=1, keepdims=True) + EPS)
        vectors[rows, :] = (projected * (norm * math.sqrt(SCALE))).astype(BF16)

    ahead = (
        lax.broadcasted_iota(jnp.int32, (docs, docs), 0) < lax.broadcasted_iota(jnp.int32, (docs, docs), 1)
    ).astype(F32).astype(BF16)
    hot_rows = jnp.broadcast_to(in_hot.astype(F32), (8, docs)).astype(BF16)
    rank = jnp.dot(hot_rows, ahead, preferred_element_type=F32)[0:1, :].astype(jnp.int32)
    place = lax.broadcasted_iota(jnp.int32, (1, docs), 1)
    slot = jnp.where(in_hot, first + rank, place - rank)
    slot_ref[...] = slot

    sort = (lax.broadcasted_iota(jnp.int32, (lanes, docs), 0) == slot).astype(F32).astype(BF16)
    cluster_rows = jnp.broadcast_to(cluster.astype(F32), (META, docs)).astype(BF16)
    sorted_n = jnp.dot(sort[:rest, :], vectors[...], preferred_element_type=F32).astype(BF16)
    sorted_h = jnp.dot(sort[first:flag, :], vectors[...], preferred_element_type=F32).astype(BF16)
    ids = lax.dot_general(
        cluster_rows, sort, (((1,), (1,)), ((), ())), preferred_element_type=F32
    )
    ids = ids.astype(BF16)


    def fill_n(ref):
        ref[:rest, :] = sorted_n
        ref[rest:, :] = jnp.zeros((META, ref.shape[1]), BF16)
        ref[rest:, :first] = ids[:, :first]
        ref[rest:, first:first + 128] = jnp.broadcast_to(doubt.astype(BF16), (META, 128))

    def fill_h(ref):
        ref[:hot, :] = sorted_h
        ref[hot:, :] = jnp.zeros((rest + META - hot, ref.shape[1]), BF16)
        ref[rest:, :lanes - first] = ids[:, first:]
        ref[rest:, first:first + 128] = jnp.broadcast_to(doubt.astype(BF16), (META, 128))

    even = lax.rem(place_ref[0], 2) == 0

    @pl.when(even)
    def _():
        fill_h(same_ref)
        fill_n(other_ref)

    @pl.when(jnp.logical_not(even))
    def _():
        fill_n(same_ref)
        fill_h(other_ref)


def prep(hot, place, cluster_of, states, proj_weight):
    docs, width = states.shape[0], proj_weight.shape[1]
    rest = docs - hot
    shape = jax.ShapeDtypeStruct
    vmem = pl.BlockSpec(memory_space=pltpu.VMEM)
    return pl.pallas_call(
        lambda *refs: prep_kernel(hot, *refs),
        out_shape=(
            shape((rest + META, width), BF16),
            shape((rest + META, width), BF16),
            shape((1, docs), jnp.int32),
        ),
        in_specs=[pl.BlockSpec(memory_space=pltpu.SMEM), vmem, vmem, vmem],
        scratch_shapes=[pltpu.VMEM((docs, width), BF16)],
        compiler_params=pltpu.CompilerParams(vmem_limit_bytes=24 * 2**20),
        name="prep",
    )(place, cluster_of.reshape(1, docs), states, proj_weight)


OWN, PAIR = "own", "pair"
CORE, PAIR_CORE = "core", "pair_core"
ROW, PAIR_ROW = "row", "pair_row"
DIAG, PAIR_DIAG = "diag", "pair_diag"
NEXT, FAR = "next", "far"
GROUPS = ((OWN, PAIR), (CORE, PAIR_CORE, DIAG, PAIR_DIAG), (ROW, PAIR_ROW), (NEXT, FAR))
HERE, THERE, ACROSS, BEYOND = (OWN, CORE), (PAIR, PAIR_CORE), (ROW, DIAG), (PAIR_ROW, PAIR_DIAG)


def score_kernel(docs, hot, names, given, made, tasks, flagged, carries, *refs):
    rest, first, flag, lanes = layout(docs, hot)
    place_ref, refs = refs[0], refs[1:]
    blocks, refs = dict(zip(names, refs[:len(names)])), refs[len(names):]
    pairs, refs = {p: refs[2 * k:2 * k + 2] for k, p in enumerate(given)}, refs[2 * len(given):]
    before, refs = refs[:len(GROUPS) * carries], refs[len(GROUPS) * carries:]
    outs, refs = refs[:len(GROUPS)], refs[len(GROUPS):]
    if made:
        pairs[made], refs = refs[:2], refs[2:]
    parts = refs[0]
    for k, out in enumerate(outs):
        out[...] = before[k][...] if carries else jnp.zeros(out.shape, F32)
    spots = {name: (out, k) for out, group in zip(outs, GROUPS) for k, name in enumerate(group)}
    z, y, c = place_ref[0], place_ref[1], place_ref[2]
    when = {"core0": c == 0, "core1": c == 1, "row0": y == 0, "row1": y == 1}
    middle = (z == 1) | (z == 2)

    def meet(count, start):
        lane = slice(start, start + count)
        wide, two = up(count, 128), 2 * count
        columns = {name: ref[rest:, 0:wide].astype(F32)[0:8, :].T[0:count, :] for name, ref in blocks.items()}
        if made:
            turned, notes = pairs[made]
            turned[:, 0:two] = jnp.concatenate([blocks[name][:count, :] for name in made], axis=0).T
            doubt = sum(blocks[name][rest:, first:first + 128].astype(F32)[0:1, 0:1] for name in made)
            ids = jnp.concatenate([columns[name] for name in made], axis=0).T
            notes[:, 0:two] = jnp.where(lax.broadcasted_iota(jnp.int32, ids.shape, 0) == 0, ids, doubt)

        for left in dict.fromkeys(task[0] for task in tasks):

            def work(left=left):
                own_tasks = [task for task in tasks if task[0] == left]
                for number, (_, pair, both, _) in enumerate(own_tasks):
                    turned, notes = pairs[pair]
                    span = two if both else wide
                    ids = notes[0:1, 0:span]
                    if not both:
                        ids = jnp.where(lax.broadcasted_iota(jnp.int32, ids.shape, 1) < count, ids, -1.0)
                    inner = jnp.dot(blocks[left][:count, :], turned[:, 0:span], preferred_element_type=F32)
                    same = columns[left][:, 0:1] == ids
                    diagonal = left == pair[0]
                    if diagonal:
                        same &= lax.broadcasted_iota(jnp.int32, inner.shape, 0) != lax.broadcasted_iota(
                            jnp.int32, inner.shape, 1
                        )
                    weights = jnp.where(same, jnp.exp2(inner), 0.0)
                    total = jnp.sum(weights, axis=0, keepdims=True)
                    for k, name in enumerate(pair[:1 + both]):
                        out, spot = spots[name]
                        out[spot, :, lane] += total[:, k * count:(k + 1) * count]
                    if not diagonal:
                        part = weights[:, 0:128]
                        for t in range(128, span, 128):
                            part += weights[:, t:t + 128]
                        if number:
                            parts[0:count, :] += part
                        else:
                            parts[0:count, :] = part
                if not diagonal:
                    part = parts[0:count, :]
                    high = part.astype(BF16)
                    low = (part - high.astype(F32)).astype(BF16)
                    ones = jnp.ones((16, 128), BF16)
                    total = sum(
                        lax.dot_general(ones, term, (((1,), (1,)), ((), ())), preferred_element_type=F32)
                        for term in (high, low)
                    )
                    out, spot = spots[left]
                    out[spot, :, lane] += total[0:1, :]

            condition = [task[3] for task in tasks if task[0] == left][0]
            if left in (NEXT, FAR):
                pl.when(middle)(work)
            elif condition:
                pl.when(when[condition])(work)
            else:
                work()

    pl.when(lax.rem(z, 2) == 0)(lambda: meet(hot, first))
    pl.when(lax.rem(z, 2) == 1)(lambda: meet(rest, 0))

    if flagged:
        doubt = sum(notes[1:2, 0:1] for _, notes in pairs.values())
        spot = lax.broadcasted_iota(jnp.int32, (1, lanes), 1)
        for name in flagged:
            out, k = spots[name]
            out[k] += jnp.where(spot == flag, doubt, 0.0)


def score(name, docs, hot, place, blocks, pairs, made, tasks, sums, flagged=(), weight=1):
    rest, _, _, lanes = layout(docs, hot)
    names = list(dict.fromkeys([*made, *(task[0] for task in tasks)]))
    given = [p for p in pairs if flagged or any(p == task[1] for task in tasks)]
    width = blocks[OWN].shape[1]
    vmem = pl.BlockSpec(memory_space=pltpu.VMEM)
    arrays = [blocks[b] for b in names] + [a for p in given for a in pairs[p]] + list(sums)
    shapes = [jax.ShapeDtypeStruct((len(group), 1, lanes), F32) for group in GROUPS]
    if made:
        shapes += [jax.ShapeDtypeStruct((width, 2 * rest), BF16), jax.ShapeDtypeStruct((8, 2 * rest), F32)]
    out = pl.pallas_call(
        lambda *refs: score_kernel(docs, hot, names, given, made, tasks, flagged, bool(sums), *refs),
        out_shape=tuple(shapes),
        in_specs=[pl.BlockSpec(memory_space=pltpu.SMEM)] + [vmem] * len(arrays),
        out_specs=tuple(vmem for _ in shapes),
        scratch_shapes=[pltpu.VMEM((rest, 128), F32)],
        compiler_params=pltpu.CompilerParams(vmem_limit_bytes=20 * 2**20),
        cost_estimate=pl.CostEstimate(flops=weight, bytes_accessed=2**10, transcendentals=0),
        name=name,
    )(place, *arrays)
    return out[:len(GROUPS)], {**pairs, made: out[len(GROUPS):]} if made else pairs


def finish_kernel(flag, slot_ref, home_ref, more_ref, out_ref, doubt_ref):
    total = home_ref[0] + more_ref[0]
    lanes, docs = total.shape[1], slot_ref.shape[1]
    doubt_ref[...] = (total[:, flag:flag + 1] > 0.0).astype(jnp.int32)
    values = jnp.broadcast_to(jnp.log(1.0 + total * 2.0**-SHIFT), (8, lanes)).T[:, 0:1]
    here = lax.broadcasted_iota(jnp.int32, (lanes, docs), 0) == slot_ref[...]
    out_ref[...] = jnp.sum(jnp.where(here, values, 0.0), axis=0, keepdims=True)


def finish(flag, slot, home, more):
    return pl.pallas_call(
        lambda *refs: finish_kernel(flag, *refs),
        out_shape=(jax.ShapeDtypeStruct(slot.shape, F32), jax.ShapeDtypeStruct((1, 1), jnp.int32)),
        compiler_params=pltpu.CompilerParams(vmem_limit_bytes=6 * 2**20),
        name="finish",
    )(slot, home, more)


def meeting_plan(states, proj_weight, cluster_of):
    owners = lax.axis_size("owner")
    columns = owners // ROWS
    docs = states.shape[0]
    hot = 3 * docs // owners
    flag = layout(docs, hot)[2]

    owner, core = lax.axis_index("owner"), lax.axis_index("split")
    place = jnp.stack([owner // ROWS, owner % ROWS, core]).astype(jnp.int32)
    same, other, slot = prep(hot, place, cluster_of, states, proj_weight)

    def move(a, to, row=0, core=0):
        if not core:
            return lax.ppermute(
                a, "owner", [(z * ROWS + y, to[z] * ROWS + (y ^ row)) for z in range(columns) for y in range(ROWS)]
            )
        if not row and to == STAY:
            return lax.ppermute(a, "split", [(0, 1), (1, 0)])
        return lax.ppermute(
            a, ("owner", "split"),
            [
                ((z * ROWS + y) * 2 + c, (to[z] * ROWS + (y ^ row)) * 2 + (c ^ core))
                for z in range(columns) for y in range(ROWS) for c in range(2)
            ],
        )

    STAY, OUTER, MIDDLE = (0, 1, 2, 3), (1, 0, 3, 2), (0, 2, 1, 3)
    TO_MIDDLE = (2, 0, 3, 1)

    def meet(name, made, tasks, **options):
        return score(name, docs, hot, place, blocks, pairs, made, tasks, sums, **options)

    blocks, pairs, sums = {OWN: same}, {}, ()
    blocks[CORE] = move(same, STAY, core=1)
    blocks[PAIR] = move(other, OUTER)
    blocks[ROW] = move(same, STAY, row=1)
    blocks[CORE], other = lax.optimization_barrier((blocks[CORE], other))
    blocks[NEXT] = move(other, MIDDLE)
    sums, pairs = meet("own", HERE, [(OWN, HERE, False, None), (CORE, HERE, False, "core0")], weight=2**33)

    blocks[PAIR], blocks[NEXT], _ = lax.optimization_barrier((blocks[PAIR], blocks[NEXT], sums[0]))
    blocks[FAR] = move(same, TO_MIDDLE)
    blocks[PAIR_ROW] = move(blocks[PAIR], STAY, row=1)
    blocks[PAIR_CORE] = move(blocks[PAIR], STAY, core=1)
    blocks[DIAG] = move(blocks[ROW], STAY, core=1)
    sums, pairs = meet(
        "pair", THERE,
        [(PAIR, THERE, False, None), (PAIR_CORE, THERE, False, "core1"), (NEXT, HERE, True, None),
         (NEXT, THERE, True, None)],
        weight=2**33,
    )
    sums, pairs = meet(
        "row", ACROSS,
        [(PAIR, HERE, True, None), (PAIR, ACROSS, True, None), (NEXT, ACROSS, True, None),
         (ROW, HERE, False, "row0"), (DIAG, HERE, False, "row1")],
    )
    blocks[PAIR_ROW], _ = lax.optimization_barrier((blocks[PAIR_ROW], sums[0]))
    blocks[PAIR_DIAG] = move(blocks[PAIR_ROW], STAY, core=1)
    sums, pairs = meet("far", (), [(FAR, p, True, None) for p in (HERE, THERE, ACROSS)])
    sums, pairs = meet(
        "last", BEYOND,
        [(NEXT, BEYOND, True, None), (FAR, BEYOND, True, None), (PAIR_ROW, THERE, False, "row1"),
         (PAIR_DIAG, THERE, False, "row0")],
        flagged=(OWN, NEXT, FAR),
    )
    home, by_core, by_row, by_middle = sums
    from_middle = move(by_middle, MIDDLE)
    from_core = move(by_core, STAY, core=1)
    from_row = move(by_row + from_core[2:4], STAY, row=1)
    home = home + from_core[0:2] + from_middle + from_row
    from_pair = move(home[1:2], OUTER)
    fast, doubt = finish(flag, slot, home, from_pair)
    return lax.cond(
        doubt[0, 0] > 0, owner_plan, lambda *_: fast.reshape(docs), states, proj_weight, cluster_of
    )


def on_device(states, proj_weight, cluster_of):
    if (lax.axis_size("owner"), lax.axis_size("split")) == (8, 2) and states.shape[0] == 512:
        return meeting_plan(states, proj_weight, cluster_of)
    return owner_plan(states, proj_weight, cluster_of)


def solution(mesh):
    placed = (P(("parts", "owner", "split"), None), P(), P(("parts", "owner", "split")))
    return jax.shard_map(
        on_device,
        mesh=mesh,
        in_specs=placed,
        out_specs=P(("parts", "owner", "split")),
        check_vma=False,
    )
```

```python
import math

import jax
import jax.numpy as jnp
from jax import lax
from jax.experimental import pallas as pl
from jax.experimental.pallas import tpu as pltpu
from jax.sharding import PartitionSpec as P

CLUS_OWN = 2
TAU = 0.05
THRESH = 0.2
EPS = 1e-06
LOG2E = math.log2(math.e)
SCALE = LOG2E / TAU
SHIFT = THRESH * LOG2E / TAU

ROWS = 2
F32 = jnp.float32
BF16 = jnp.bfloat16


def prepare(states, proj_weight):
    projected = jnp.dot(states, proj_weight, preferred_element_type=jnp.float32)
    unit = projected * lax.rsqrt(jnp.sum(projected * projected, axis=1, keepdims=True) + EPS)
    peak = jnp.max(jnp.abs(unit), axis=1).astype(jnp.bfloat16)
    quant = (unit / peak.astype(jnp.float32)[:, None]).astype(jnp.bfloat16)
    return (quant, peak)


def similarity_scores(
    own_quant, own_peak, own_cluster, own_index, col_quant, col_peak, col_cluster, col_index
):
    row_count = own_quant.shape[0]
    block = math.gcd(row_count, 768)
    col_scale = col_peak.astype(jnp.float32)

    def one_block(start):
        quant_rows = lax.dynamic_slice_in_dim(own_quant, start, block, 0)
        scale_rows = lax.dynamic_slice_in_dim(own_peak, start, block, 0).astype(jnp.float32)
        cluster_rows = lax.dynamic_slice_in_dim(own_cluster, start, block, 0)
        index_rows = lax.dynamic_slice_in_dim(own_index, start, block, 0)
        inner = lax.dot_general(
            quant_rows, col_quant, (((1,), (1,)), ((), ())), preferred_element_type=jnp.float32
        )
        cosine = inner * scale_rows[:, None] * col_scale[None, :]
        same = (cluster_rows[:, None] == col_cluster[None, :]) & (
            index_rows[:, None] != col_index[None, :]
        )
        weights = jnp.where(same, jnp.exp((cosine - THRESH) / TAU), jnp.zeros_like(cosine))
        return jnp.log(1.0 + jnp.sum(weights, axis=1))

    starts = jnp.arange(row_count // block, dtype=jnp.int32) * block
    return lax.map(one_block, starts).reshape(row_count)


def owner_plan(states, proj_weight, cluster_of):
    owners = lax.axis_size("owner")
    splits = lax.axis_size("split")
    half_index = lax.axis_index("split")
    doc_count = states.shape[0]
    capacity = 3 * doc_count // owners
    width = proj_weight.shape[1]
    slot_total = owners * capacity
    quant, peak = prepare(states, proj_weight)
    group_of = cluster_of // CLUS_OWN
    onehot = (group_of[:, None] == jnp.arange(owners, dtype=jnp.int32)[None, :]).astype(jnp.int32)
    before = jnp.cumsum(onehot, axis=0) - onehot
    target = group_of * capacity + jnp.sum(before * onehot, axis=1)
    quant_slots = (
        jnp.zeros((slot_total, width), jnp.bfloat16)
        .at[target]
        .set(quant)
        .reshape(owners, capacity, width)
    )
    peak_slots = (
        jnp.zeros((slot_total,), jnp.bfloat16).at[target].set(peak).reshape(owners, capacity)
    )
    cluster_slots = (
        jnp.full((slot_total,), -1, jnp.int32).at[target].set(cluster_of).reshape(owners, capacity)
    )
    positions = (
        jnp.arange(owners, dtype=jnp.int32)[:, None] * (splits * capacity)
        + jnp.arange(capacity, dtype=jnp.int32)[None, :]
    )
    own_index = (positions + half_index * capacity).reshape(slot_total)
    col_index = jnp.arange(splits * slot_total, dtype=jnp.int32)
    own_quant, own_peak, own_cluster = (
        lax.all_to_all(a, "owner", split_axis=0, concat_axis=0, tiled=True)
        for a in (quant_slots, peak_slots, cluster_slots)
    )
    all_quant, all_peak, all_cluster = (
        lax.all_gather(a, "split", axis=1, tiled=True) for a in (own_quant, own_peak, own_cluster)
    )
    scores = similarity_scores(
        own_quant.reshape(slot_total, width),
        own_peak.reshape(slot_total),
        own_cluster.reshape(slot_total),
        own_index,
        all_quant.reshape(splits * slot_total, width),
        all_peak.reshape(splits * slot_total),
        all_cluster.reshape(splits * slot_total),
        col_index,
    )
    returned = lax.all_to_all(
        scores.reshape(owners, capacity), "owner", split_axis=0, concat_axis=0, tiled=True
    )
    return returned.reshape(slot_total)[target]


def up(n, m):
    return -(-n // m) * m


META = 16


def layout(docs, hot):
    rest = docs - hot
    first = up(rest, 128)
    flag = first + hot
    return rest, first, flag, up(flag + 1, 128)


def prep_kernel(hot, place_ref, cl_ref, st_ref, w_ref, same_ref, other_ref, slot_ref, vectors):
    docs = st_ref.shape[0]
    rest, first, flag, lanes = layout(docs, hot)
    tile = 128

    cluster = cl_ref[...]
    group = cluster // CLUS_OWN
    member = lax.broadcasted_iota(jnp.int32, (8, docs), 0) == group
    full = jnp.sum(member.astype(F32), axis=1, keepdims=True) == float(hot)
    chosen = jnp.min(
        jnp.where(full, lax.broadcasted_iota(jnp.int32, (8, 1), 0), 8), axis=0, keepdims=True
    )
    doubt = jnp.where(jnp.sum(full.astype(F32), axis=0, keepdims=True) == 1.0, 0.0, 1.0)
    in_hot = group == chosen

    for t in range(docs // tile):
        rows = slice(t * tile, (t + 1) * tile)
        projected = jnp.dot(st_ref[rows, :], w_ref[...], preferred_element_type=F32)
        norm = lax.rsqrt(jnp.sum(projected * projected, axis=1, keepdims=True) + EPS)
        vectors[rows, :] = (projected * (norm * math.sqrt(SCALE))).astype(BF16)

    ahead = (
        lax.broadcasted_iota(jnp.int32, (docs, docs), 0) < lax.broadcasted_iota(jnp.int32, (docs, docs), 1)
    ).astype(F32).astype(BF16)
    hot_rows = jnp.broadcast_to(in_hot.astype(F32), (8, docs)).astype(BF16)
    rank = jnp.dot(hot_rows, ahead, preferred_element_type=F32)[0:1, :].astype(jnp.int32)
    place = lax.broadcasted_iota(jnp.int32, (1, docs), 1)
    slot = jnp.where(in_hot, first + rank, place - rank)
    slot_ref[...] = slot

    sort = (lax.broadcasted_iota(jnp.int32, (lanes, docs), 0) == slot).astype(F32).astype(BF16)
    cluster_rows = jnp.broadcast_to(cluster.astype(F32), (META, docs)).astype(BF16)
    sorted_n = jnp.dot(sort[:rest, :], vectors[...], preferred_element_type=F32).astype(BF16)
    sorted_h = jnp.dot(sort[first:flag, :], vectors[...], preferred_element_type=F32).astype(BF16)
    ids = lax.dot_general(
        cluster_rows, sort, (((1,), (1,)), ((), ())), preferred_element_type=F32
    )
    ids = ids.astype(BF16)


    def fill_n(ref):
        ref[:rest, :] = sorted_n
        ref[rest:, :] = jnp.zeros((META, ref.shape[1]), BF16)
        ref[rest:, :first] = ids[:, :first]
        ref[rest:, first:first + 128] = jnp.broadcast_to(doubt.astype(BF16), (META, 128))

    def fill_h(ref):
        ref[:hot, :] = sorted_h
        ref[hot:, :] = jnp.zeros((rest + META - hot, ref.shape[1]), BF16)
        ref[rest:, :lanes - first] = ids[:, first:]
        ref[rest:, first:first + 128] = jnp.broadcast_to(doubt.astype(BF16), (META, 128))

    even = lax.rem(place_ref[0], 2) == 0

    @pl.when(even)
    def _():
        fill_h(same_ref)
        fill_n(other_ref)

    @pl.when(jnp.logical_not(even))
    def _():
        fill_n(same_ref)
        fill_h(other_ref)


def prep(hot, place, cluster_of, states, proj_weight):
    docs, width = states.shape[0], proj_weight.shape[1]
    rest = docs - hot
    shape = jax.ShapeDtypeStruct
    vmem = pl.BlockSpec(memory_space=pltpu.VMEM)
    return pl.pallas_call(
        lambda *refs: prep_kernel(hot, *refs),
        out_shape=(
            shape((rest + META, width), BF16),
            shape((rest + META, width), BF16),
            shape((1, docs), jnp.int32),
        ),
        in_specs=[pl.BlockSpec(memory_space=pltpu.SMEM), vmem, vmem, vmem],
        scratch_shapes=[pltpu.VMEM((docs, width), BF16)],
        compiler_params=pltpu.CompilerParams(vmem_limit_bytes=24 * 2**20),
        name="prep",
    )(place, cluster_of.reshape(1, docs), states, proj_weight)


OWN, PAIR = "own", "pair"
CORE, PAIR_CORE = "core", "pair_core"
ROW, PAIR_ROW = "row", "pair_row"
DIAG, PAIR_DIAG = "diag", "pair_diag"
NEXT, FAR = "next", "far"
GROUPS = ((OWN, PAIR), (CORE, PAIR_CORE, DIAG, PAIR_DIAG), (ROW, PAIR_ROW), (NEXT, FAR))
HERE, THERE, ACROSS = (OWN, CORE), (PAIR, PAIR_CORE), (ROW, DIAG)


def score_kernel(docs, hot, names, given, made, tasks, flagged, carries, *refs):
    rest, first, flag, lanes = layout(docs, hot)
    place_ref, refs = refs[0], refs[1:]
    blocks, refs = dict(zip(names, refs[:len(names)])), refs[len(names):]
    pairs, refs = {p: refs[2 * k:2 * k + 2] for k, p in enumerate(given)}, refs[2 * len(given):]
    before, refs = refs[:len(GROUPS) * carries], refs[len(GROUPS) * carries:]
    outs, refs = refs[:len(GROUPS)], refs[len(GROUPS):]
    if made:
        pairs[made], refs = refs[:2], refs[2:]
    parts = refs[0]
    for k, out in enumerate(outs):
        out[...] = before[k][...] if carries else jnp.zeros(out.shape, F32)
    spots = {name: (out, k) for out, group in zip(outs, GROUPS) for k, name in enumerate(group)}
    z, y, c = place_ref[0], place_ref[1], place_ref[2]
    when = {"core0": c == 0, "core1": c == 1, "row0": y == 0, "row1": y == 1}
    middle = (z == 1) | (z == 2)

    def meet(count, start):
        lane = slice(start, start + count)
        wide, two = up(count, 128), 2 * count
        columns = {name: ref[rest:, 0:wide].astype(F32)[0:8, :].T[0:count, :] for name, ref in blocks.items()}
        if made:
            turned, notes = pairs[made]
            turned[:, 0:two] = jnp.concatenate([blocks[name][:count, :] for name in made], axis=0).T
            doubt = sum(blocks[name][rest:, first:first + 128].astype(F32)[0:1, 0:1] for name in made)
            ids = jnp.concatenate([columns[name] for name in made], axis=0).T
            notes[:, 0:two] = jnp.where(lax.broadcasted_iota(jnp.int32, ids.shape, 0) == 0, ids, doubt)

        for left in dict.fromkeys(task[0] for task in tasks):

            def work(left=left):
                own_tasks = [task for task in tasks if task[0] == left]
                for number, (_, right, both, _) in enumerate(own_tasks):
                    if right in blocks:
                        span, rights, diagonal = count, (right,), False
                        ids = blocks[right][rest:, 0:wide].astype(F32)[0:1, 0:count]
                        inner = lax.dot_general(
                            blocks[left][:count, :], blocks[right][:count, :], (((1,), (1,)), ((), ())),
                            preferred_element_type=F32,
                        )
                    else:
                        turned, notes = pairs[right]
                        span, rights, diagonal = two if both else wide, right[:1 + both], left == right[0]
                        ids = notes[0:1, 0:span]
                        if not both:
                            ids = jnp.where(lax.broadcasted_iota(jnp.int32, ids.shape, 1) < count, ids, -1.0)
                        inner = jnp.dot(
                            blocks[left][:count, :], turned[:, 0:span], preferred_element_type=F32
                        )
                    same = columns[left][:, 0:1] == ids
                    if diagonal:
                        same &= lax.broadcasted_iota(jnp.int32, inner.shape, 0) != lax.broadcasted_iota(
                            jnp.int32, inner.shape, 1
                        )
                    weights = jnp.where(same, jnp.exp2(inner), 0.0)
                    total = jnp.sum(weights, axis=0, keepdims=True)
                    for k, name in enumerate(rights):
                        out, spot = spots[name]
                        out[spot, :, lane] += total[:, k * count:(k + 1) * count]
                    if not diagonal:
                        part = weights[:, 0:128]
                        for t in range(128, span - span % 128, 128):
                            part += weights[:, t:t + 128]
                        if span % 128:
                            rest_of = weights[:, span - span % 128:]
                            part += jnp.concatenate([rest_of, jnp.zeros((count, 128 - span % 128), F32)], axis=1)
                        if number:
                            parts[0:count, :] += part
                        else:
                            parts[0:count, :] = part
                if not diagonal:
                    part = parts[0:count, :]
                    high = part.astype(BF16)
                    low = (part - high.astype(F32)).astype(BF16)
                    ones = jnp.ones((16, 128), BF16)
                    total = sum(
                        lax.dot_general(ones, term, (((1,), (1,)), ((), ())), preferred_element_type=F32)
                        for term in (high, low)
                    )
                    out, spot = spots[left]
                    out[spot, :, lane] += total[0:1, :]

            condition = [task[3] for task in tasks if task[0] == left][0]
            if left in (NEXT, FAR):
                pl.when(middle)(work)
            elif condition:
                pl.when(when[condition])(work)
            else:
                work()

    pl.when(lax.rem(z, 2) == 0)(lambda: meet(hot, first))
    pl.when(lax.rem(z, 2) == 1)(lambda: meet(rest, 0))

    if flagged:
        doubt = sum(notes[1:2, 0:1] for _, notes in pairs.values())
        doubt += sum(blocks[b][rest:, first:first + 128].astype(F32)[0:1, 0:1] for b in (PAIR_ROW, PAIR_DIAG))
        spot = lax.broadcasted_iota(jnp.int32, (1, lanes), 1)
        for name in flagged:
            out, k = spots[name]
            out[k] += jnp.where(spot == flag, doubt, 0.0)


def score(name, docs, hot, place, blocks, pairs, made, tasks, sums, flagged=(), weight=1):
    rest, _, _, lanes = layout(docs, hot)
    names = list(dict.fromkeys([*made, *(task[0] for task in tasks)]))
    given = [p for p in pairs if flagged or any(p == task[1] for task in tasks)]
    width = blocks[OWN].shape[1]
    vmem = pl.BlockSpec(memory_space=pltpu.VMEM)
    arrays = [blocks[b] for b in names] + [a for p in given for a in pairs[p]] + list(sums)
    shapes = [jax.ShapeDtypeStruct((len(group), 1, lanes), F32) for group in GROUPS]
    if made:
        shapes += [jax.ShapeDtypeStruct((width, 2 * rest), BF16), jax.ShapeDtypeStruct((8, 2 * rest), F32)]
    out = pl.pallas_call(
        lambda *refs: score_kernel(docs, hot, names, given, made, tasks, flagged, bool(sums), *refs),
        out_shape=tuple(shapes),
        in_specs=[pl.BlockSpec(memory_space=pltpu.SMEM)] + [vmem] * len(arrays),
        out_specs=tuple(vmem for _ in shapes),
        scratch_shapes=[pltpu.VMEM((rest, 128), F32)],
        compiler_params=pltpu.CompilerParams(vmem_limit_bytes=20 * 2**20),
        cost_estimate=pl.CostEstimate(flops=weight, bytes_accessed=2**10, transcendentals=0),
        name=name,
    )(place, *arrays)
    return out[:len(GROUPS)], {**pairs, made: out[len(GROUPS):]} if made else pairs


def finish_kernel(slot_ref, home_ref, more_ref, out_ref):
    total = home_ref[0] + more_ref[0]
    lanes, docs = total.shape[1], slot_ref.shape[1]
    values = jnp.broadcast_to(jnp.log(1.0 + total * 2.0**-SHIFT), (8, lanes)).T[:, 0:1]
    here = lax.broadcasted_iota(jnp.int32, (lanes, docs), 0) == slot_ref[...]
    out_ref[...] = jnp.sum(jnp.where(here, values, 0.0), axis=0, keepdims=True)


def finish(slot, home, more):
    return pl.pallas_call(
        finish_kernel,
        out_shape=jax.ShapeDtypeStruct(slot.shape, F32),
        compiler_params=pltpu.CompilerParams(vmem_limit_bytes=6 * 2**20),
        name="finish",
    )(slot, home, more)


def meeting_plan(states, proj_weight, cluster_of):
    owners = lax.axis_size("owner")
    columns = owners // ROWS
    docs = states.shape[0]
    hot = 3 * docs // owners
    flag = layout(docs, hot)[2]

    owner, core = lax.axis_index("owner"), lax.axis_index("split")
    place = jnp.stack([owner // ROWS, owner % ROWS, core]).astype(jnp.int32)
    same, other, slot = prep(hot, place, cluster_of, states, proj_weight)

    def move(a, to, row=0, core=0):
        pairs = [
            (
                (z * ROWS + y) * 2 + c,
                (to[z] * ROWS + (y ^ row)) * 2 + (c ^ (core if row or to[z] != z else 1)),
            )
            for z in range(columns) for y in range(ROWS) for c in range(2)
        ]
        return lax.ppermute(a, ("owner", "split"), pairs)

    STAY, OUTER, MIDDLE = (0, 1, 2, 3), (1, 0, 3, 2), (0, 2, 1, 3)
    TO_MIDDLE = (2, 0, 3, 1)

    def meet(name, made, tasks, **options):
        return score(name, docs, hot, place, blocks, pairs, made, tasks, sums, **options)

    blocks, pairs, sums = {OWN: same}, {}, ()
    blocks[CORE] = move(same, STAY, core=1)
    blocks[PAIR] = move(other, OUTER)
    blocks[ROW] = move(same, STAY, row=1)
    blocks[CORE], other = lax.optimization_barrier((blocks[CORE], other))
    blocks[NEXT] = move(other, MIDDLE)
    sums, pairs = meet("own", HERE, [(OWN, HERE, False, None), (CORE, HERE, False, "core0")], weight=2**33)

    blocks[PAIR], _ = lax.optimization_barrier((blocks[PAIR], sums[0]))
    blocks[ROW], blocks[NEXT] = lax.optimization_barrier((blocks[ROW], blocks[NEXT]))
    blocks[FAR] = move(same, TO_MIDDLE)
    blocks[PAIR_ROW] = move(blocks[PAIR], STAY, row=1)
    blocks[PAIR_CORE] = move(blocks[PAIR], STAY, core=1)
    blocks[DIAG] = move(blocks[ROW], STAY, core=1)
    sums, pairs = meet(
        "pair", THERE,
        [(PAIR, THERE, False, None), (PAIR_CORE, THERE, False, "core1"), (NEXT, HERE, True, None),
         (NEXT, THERE, True, None)],
        weight=2**33,
    )
    sums, pairs = meet(
        "row", ACROSS,
        [(PAIR, HERE, True, None), (PAIR, ACROSS, True, None), (NEXT, ACROSS, True, None),
         (ROW, HERE, False, "row0"), (DIAG, HERE, False, "row1")],
    )
    blocks[PAIR_ROW], _ = lax.optimization_barrier((blocks[PAIR_ROW], sums[0]))
    blocks[PAIR_DIAG] = move(blocks[PAIR_ROW], STAY, core=1)
    sums, pairs = meet("far", (), [(FAR, p, True, None) for p in (HERE, THERE, ACROSS)])
    sums, pairs = meet(
        "last", (),
        [(left, right, False, None) for left in (NEXT, FAR) for right in (PAIR_ROW, PAIR_DIAG)]
        + [(PAIR_ROW, THERE, False, "row1"), (PAIR_DIAG, THERE, False, "row0")],
        flagged=(OWN, NEXT, FAR),
    )
    home, by_core, by_row, by_middle = sums
    from_middle = move(by_middle, MIDDLE)
    from_core = move(by_core, STAY, core=1)
    from_row = move(by_row + from_core[2:4], STAY, row=1)
    home = home + from_core[0:2] + from_middle + from_row
    from_pair = move(home[1:2], OUTER)
    fast = finish(slot, home, from_pair)
    doubt = home[0, 0, flag] + from_pair[0, 0, flag] > 0.0
    return lax.cond(doubt, owner_plan, lambda *_: fast.reshape(docs), states, proj_weight, cluster_of)


def on_device(states, proj_weight, cluster_of):
    if (lax.axis_size("owner"), lax.axis_size("split")) == (8, 2) and states.shape[0] == 512:
        return meeting_plan(states, proj_weight, cluster_of)
    return owner_plan(states, proj_weight, cluster_of)


def solution(mesh):
    placed = (P(("parts", "owner", "split"), None), P(), P(("parts", "owner", "split")))
    return jax.shard_map(
        on_device,
        mesh=mesh,
        in_specs=placed,
        out_specs=P(("parts", "owner", "split")),
        check_vma=False,
    )
```

```python
import math

import jax
import jax.numpy as jnp
from jax import lax
from jax.experimental import pallas as pl
from jax.experimental.pallas import tpu as pltpu
from jax.sharding import PartitionSpec as P

CLUS_OWN = 2
TAU = 0.05
THRESH = 0.2
EPS = 1e-06
LOG2E = math.log2(math.e)
SCALE = LOG2E / TAU
SHIFT = THRESH * LOG2E / TAU

ROWS = 2
F32 = jnp.float32
BF16 = jnp.bfloat16


def prepare(states, proj_weight):
    projected = jnp.dot(states, proj_weight, preferred_element_type=jnp.float32)
    unit = projected * lax.rsqrt(jnp.sum(projected * projected, axis=1, keepdims=True) + EPS)
    peak = jnp.max(jnp.abs(unit), axis=1).astype(jnp.bfloat16)
    quant = (unit / peak.astype(jnp.float32)[:, None]).astype(jnp.bfloat16)
    return (quant, peak)


def similarity_scores(
    own_quant, own_peak, own_cluster, own_index, col_quant, col_peak, col_cluster, col_index
):
    row_count = own_quant.shape[0]
    block = math.gcd(row_count, 768)
    col_scale = col_peak.astype(jnp.float32)

    def one_block(start):
        quant_rows = lax.dynamic_slice_in_dim(own_quant, start, block, 0)
        scale_rows = lax.dynamic_slice_in_dim(own_peak, start, block, 0).astype(jnp.float32)
        cluster_rows = lax.dynamic_slice_in_dim(own_cluster, start, block, 0)
        index_rows = lax.dynamic_slice_in_dim(own_index, start, block, 0)
        inner = lax.dot_general(
            quant_rows, col_quant, (((1,), (1,)), ((), ())), preferred_element_type=jnp.float32
        )
        cosine = inner * scale_rows[:, None] * col_scale[None, :]
        same = (cluster_rows[:, None] == col_cluster[None, :]) & (
            index_rows[:, None] != col_index[None, :]
        )
        weights = jnp.where(same, jnp.exp((cosine - THRESH) / TAU), jnp.zeros_like(cosine))
        return jnp.log(1.0 + jnp.sum(weights, axis=1))

    starts = jnp.arange(row_count // block, dtype=jnp.int32) * block
    return lax.map(one_block, starts).reshape(row_count)


def owner_plan(states, proj_weight, cluster_of):
    owners = lax.axis_size("owner")
    splits = lax.axis_size("split")
    half_index = lax.axis_index("split")
    doc_count = states.shape[0]
    capacity = 3 * doc_count // owners
    width = proj_weight.shape[1]
    slot_total = owners * capacity
    quant, peak = prepare(states, proj_weight)
    group_of = cluster_of // CLUS_OWN
    onehot = (group_of[:, None] == jnp.arange(owners, dtype=jnp.int32)[None, :]).astype(jnp.int32)
    before = jnp.cumsum(onehot, axis=0) - onehot
    target = group_of * capacity + jnp.sum(before * onehot, axis=1)
    quant_slots = (
        jnp.zeros((slot_total, width), jnp.bfloat16)
        .at[target]
        .set(quant)
        .reshape(owners, capacity, width)
    )
    peak_slots = (
        jnp.zeros((slot_total,), jnp.bfloat16).at[target].set(peak).reshape(owners, capacity)
    )
    cluster_slots = (
        jnp.full((slot_total,), -1, jnp.int32).at[target].set(cluster_of).reshape(owners, capacity)
    )
    positions = (
        jnp.arange(owners, dtype=jnp.int32)[:, None] * (splits * capacity)
        + jnp.arange(capacity, dtype=jnp.int32)[None, :]
    )
    own_index = (positions + half_index * capacity).reshape(slot_total)
    col_index = jnp.arange(splits * slot_total, dtype=jnp.int32)
    own_quant, own_peak, own_cluster = (
        lax.all_to_all(a, "owner", split_axis=0, concat_axis=0, tiled=True)
        for a in (quant_slots, peak_slots, cluster_slots)
    )
    all_quant, all_peak, all_cluster = (
        lax.all_gather(a, "split", axis=1, tiled=True) for a in (own_quant, own_peak, own_cluster)
    )
    scores = similarity_scores(
        own_quant.reshape(slot_total, width),
        own_peak.reshape(slot_total),
        own_cluster.reshape(slot_total),
        own_index,
        all_quant.reshape(splits * slot_total, width),
        all_peak.reshape(splits * slot_total),
        all_cluster.reshape(splits * slot_total),
        col_index,
    )
    returned = lax.all_to_all(
        scores.reshape(owners, capacity), "owner", split_axis=0, concat_axis=0, tiled=True
    )
    return returned.reshape(slot_total)[target]


def up(n, m):
    return -(-n // m) * m


META = 16


def layout(docs, hot):
    rest = docs - hot
    first = up(rest, 128)
    flag = first + hot
    return rest, first, flag, up(flag + 1, 128)


def prep_kernel(hot, place_ref, cl_ref, st_hbm, w_hbm, same_ref, other_ref, slot_ref, vectors, st_ref, w_ref, sems):
    docs = st_ref.shape[0]
    rest, first, flag, lanes = layout(docs, hot)
    tile = 128
    copies = [
        pltpu.make_async_copy(w_hbm, w_ref, sems.at[0]), pltpu.make_async_copy(st_hbm, st_ref, sems.at[1])
    ]
    for copy in copies:
        copy.start()

    cluster = cl_ref[...]
    group = cluster // CLUS_OWN
    member = lax.broadcasted_iota(jnp.int32, (8, docs), 0) == group
    full = jnp.sum(member.astype(F32), axis=1, keepdims=True) == float(hot)
    chosen = jnp.min(
        jnp.where(full, lax.broadcasted_iota(jnp.int32, (8, 1), 0), 8), axis=0, keepdims=True
    )
    doubt = jnp.where(jnp.sum(full.astype(F32), axis=0, keepdims=True) == 1.0, 0.0, 1.0)
    in_hot = group == chosen

    ahead = (
        lax.broadcasted_iota(jnp.int32, (docs, docs), 0) < lax.broadcasted_iota(jnp.int32, (docs, docs), 1)
    ).astype(F32).astype(BF16)
    hot_rows = jnp.broadcast_to(in_hot.astype(F32), (8, docs)).astype(BF16)
    rank = jnp.dot(hot_rows, ahead, preferred_element_type=F32)[0:1, :].astype(jnp.int32)
    place = lax.broadcasted_iota(jnp.int32, (1, docs), 1)
    slot = jnp.where(in_hot, first + rank, place - rank)
    slot_ref[...] = slot

    sort = (lax.broadcasted_iota(jnp.int32, (lanes, docs), 0) == slot).astype(F32).astype(BF16)
    cluster_rows = jnp.broadcast_to(cluster.astype(F32), (META, docs)).astype(BF16)
    ids = lax.dot_general(
        cluster_rows, sort, (((1,), (1,)), ((), ())), preferred_element_type=F32
    )
    ids = ids.astype(BF16)


    for copy in copies:
        copy.wait()
    for t in range(docs // tile):
        rows = slice(t * tile, (t + 1) * tile)
        projected = jnp.dot(st_ref[rows, :], w_ref[...], preferred_element_type=F32)
        norm = lax.rsqrt(jnp.sum(projected * projected, axis=1, keepdims=True) + EPS)
        vectors[rows, :] = (projected * (norm * math.sqrt(SCALE))).astype(BF16)

    sorted_n = jnp.dot(sort[:rest, :], vectors[...], preferred_element_type=F32).astype(BF16)
    sorted_h = jnp.dot(sort[first:flag, :], vectors[...], preferred_element_type=F32).astype(BF16)

    def fill_n(ref):
        ref[:rest, :] = sorted_n
        ref[rest:, :] = jnp.zeros((META, ref.shape[1]), BF16)
        ref[rest:, :first] = ids[:, :first]
        ref[rest:, first:first + 128] = jnp.broadcast_to(doubt.astype(BF16), (META, 128))

    def fill_h(ref):
        ref[:hot, :] = sorted_h
        ref[hot:, :] = jnp.zeros((rest + META - hot, ref.shape[1]), BF16)
        ref[rest:, :lanes - first] = ids[:, first:]
        ref[rest:, first:first + 128] = jnp.broadcast_to(doubt.astype(BF16), (META, 128))

    even = lax.rem(place_ref[0], 2) == 0

    @pl.when(even)
    def _():
        fill_h(same_ref)
        fill_n(other_ref)

    @pl.when(jnp.logical_not(even))
    def _():
        fill_n(same_ref)
        fill_h(other_ref)


def prep(hot, place, cluster_of, states, proj_weight):
    docs, width = states.shape[0], proj_weight.shape[1]
    rest = docs - hot
    shape = jax.ShapeDtypeStruct
    vmem = pl.BlockSpec(memory_space=pltpu.VMEM)
    return pl.pallas_call(
        lambda *refs: prep_kernel(hot, *refs),
        out_shape=(
            shape((rest + META, width), BF16),
            shape((rest + META, width), BF16),
            shape((1, docs), jnp.int32),
        ),
        in_specs=[pl.BlockSpec(memory_space=pltpu.SMEM), vmem] + [pl.BlockSpec(memory_space=pl.ANY)] * 2,
        scratch_shapes=[
            pltpu.VMEM((docs, width), BF16), pltpu.VMEM(states.shape, BF16), pltpu.VMEM(proj_weight.shape, BF16),
            pltpu.SemaphoreType.DMA((2,)),
        ],
        compiler_params=pltpu.CompilerParams(vmem_limit_bytes=24 * 2**20),
        name="prep",
    )(place, cluster_of.reshape(1, docs), states, proj_weight)


OWN, PAIR = "own", "pair"
CORE, PAIR_CORE = "core", "pair_core"
ROW, PAIR_ROW = "row", "pair_row"
DIAG, PAIR_DIAG = "diag", "pair_diag"
NEXT, FAR = "next", "far"
GROUPS = ((OWN, PAIR, ROW, PAIR_ROW), (CORE, PAIR_CORE, DIAG, PAIR_DIAG), (NEXT,), (FAR,))
TILE = 256
HERE, THERE, ACROSS = (OWN, CORE), (PAIR, PAIR_CORE), (ROW, DIAG)


def score_kernel(docs, hot, names, given, made, tasks, doubted, carries, *refs):
    rest, first, flag, lanes = layout(docs, hot)
    place_ref, refs = refs[0], refs[1:]
    blocks, refs = dict(zip(names, refs[:len(names)])), refs[len(names):]
    pairs, refs = {p: refs[2 * k:2 * k + 2] for k, p in enumerate(given)}, refs[2 * len(given):]
    before, refs = refs[:len(GROUPS) * carries], refs[len(GROUPS) * carries:]
    outs, refs = refs[:len(GROUPS)], refs[len(GROUPS):]
    if made:
        pairs[made], refs = refs[:2], refs[2:]
    parts = refs[-1]
    for k, out in enumerate(outs):
        out[...] = before[k][...] if carries else jnp.zeros(out.shape, F32)
    spots = {name: (out, k) for out, group in zip(outs, GROUPS) for k, name in enumerate(group)}
    z, y, c = place_ref[0], place_ref[1], place_ref[2]
    when = {"core0": c == 0, "core1": c == 1, "row0": y == 0, "row1": y == 1}
    middle = (z == 1) | (z == 2)

    def meet(count, start):
        lane = slice(start, start + count)
        wide, two = up(count, 128), 2 * count
        columns = {name: ref[rest:, 0:wide].astype(F32)[0:8, :].T[0:count, :] for name, ref in blocks.items()}
        if made:
            turned, notes = pairs[made]
            turned[:, 0:two] = jnp.concatenate([blocks[name][:count, :] for name in made], axis=0).T
            notes[:, 0:two] = jnp.concatenate([columns[name] for name in made], axis=0).T

        for left in dict.fromkeys(task[0] for task in tasks):

            def work(left=left):
                own_tasks = [task for task in tasks if task[0] == left]
                block = blocks[left][:count, :]
                fresh = True
                for _, right, both, _ in own_tasks:
                    if right in blocks:
                        span, rights, diagonal = count, (right,), False
                        ids = blocks[right][rest:, 0:wide].astype(F32)[0:1, 0:count]
                    else:
                        turned, notes = pairs[right]
                        span, rights, diagonal = two if both else wide, right[:1 + both], left == right[0]
                        ids = notes[0:1, 0:span]
                        if not both:
                            ids = jnp.where(lax.broadcasted_iota(jnp.int32, ids.shape, 1) < count, ids, -1.0)
                    totals = []
                    for low in range(0, span, TILE):
                        high = min(low + TILE, span)
                        if right in blocks:
                            inner = lax.dot_general(
                                block, blocks[right][low:high, :], (((1,), (1,)), ((), ())),
                                preferred_element_type=F32,
                            )
                        else:
                            inner = jnp.dot(block, turned[:, low:high], preferred_element_type=F32)
                        same = columns[left][:, 0:1] == ids[:, low:high]
                        if diagonal:
                            same &= lax.broadcasted_iota(jnp.int32, inner.shape, 0) != (
                                lax.broadcasted_iota(jnp.int32, inner.shape, 1) + low
                            )
                        weights = jnp.where(same, jnp.exp2(inner), 0.0)
                        totals.append(jnp.sum(weights, axis=0, keepdims=True))
                        if not diagonal:
                            part = None
                            for t in range(0, high - low, 128):
                                piece = weights[:, t:t + 128]
                                if piece.shape[1] < 128:
                                    blank = jnp.zeros((count, 128 - piece.shape[1]), F32)
                                    piece = jnp.concatenate([piece, blank], axis=1)
                                part = piece if part is None else part + piece
                            if fresh:
                                parts[0:count, :] = part
                            else:
                                parts[0:count, :] += part
                            fresh = False
                    total = jnp.concatenate(totals, axis=1) if len(totals) > 1 else totals[0]
                    for k, name in enumerate(rights):
                        out, spot = spots[name]
                        out[spot, :, lane] += total[:, k * count:(k + 1) * count]
                if not fresh:
                    part = parts[0:count, :]
                    high = part.astype(BF16)
                    low = (part - high.astype(F32)).astype(BF16)
                    total = lax.dot_general(
                        jnp.ones((16, 256), BF16), jnp.concatenate([high, low], axis=1),
                        (((1,), (1,)), ((), ())), preferred_element_type=F32,
                    )
                    out, spot = spots[left]
                    out[spot, :, lane] += total[0:1, :]

            condition = [task[3] for task in tasks if task[0] == left][0]
            if left in (NEXT, FAR):
                pl.when(middle)(work)
            elif condition:
                pl.when(when[condition])(work)
            else:
                work()

    pl.when(lax.rem(z, 2) == 0)(lambda: meet(hot, first))
    pl.when(lax.rem(z, 2) == 1)(lambda: meet(rest, 0))

    if doubted:
        doubt = sum(blocks[name][rest:, first:first + 128].astype(F32)[0:1, 0:1] for name in doubted)
        out, k = spots[FAR]
        out[k] += jnp.where(lax.broadcasted_iota(jnp.int32, (1, lanes), 1) == flag, doubt, 0.0)


def score(name, docs, hot, place, blocks, pairs, made, tasks, sums, doubted=(), weight=1):
    rest, _, _, lanes = layout(docs, hot)
    names = list(dict.fromkeys([*made, *(task[0] for task in tasks)]))
    given = [p for p in pairs if any(p == task[1] for task in tasks)]
    width = blocks[OWN].shape[1]
    vmem = pl.BlockSpec(memory_space=pltpu.VMEM)
    arrays = [blocks[b] for b in names] + [a for p in given for a in pairs[p]] + list(sums)
    shapes = [jax.ShapeDtypeStruct((len(group), 1, lanes), F32) for group in GROUPS]
    if made:
        shapes += [jax.ShapeDtypeStruct((width, 2 * rest), BF16), jax.ShapeDtypeStruct((8, 2 * rest), F32)]
    out = pl.pallas_call(
        lambda *refs: score_kernel(docs, hot, names, given, made, tasks, doubted or made, bool(sums), *refs),
        out_shape=tuple(shapes),
        in_specs=[pl.BlockSpec(memory_space=pltpu.SMEM)] + [vmem] * len(arrays),
        out_specs=tuple(vmem for _ in shapes),
        scratch_shapes=[pltpu.VMEM((rest, 128), F32)],
        compiler_params=pltpu.CompilerParams(vmem_limit_bytes=20 * 2**20),
        cost_estimate=pl.CostEstimate(flops=weight, bytes_accessed=2**10, transcendentals=0),
        name=name,
    )(place, *arrays)
    count = len(GROUPS)
    return out[:count], {**pairs, made: out[count:]} if made else pairs


def finish_kernel(slot_ref, *refs):
    sums, out_ref = refs[:-1], refs[-1]
    total = sums[0][0]
    for ref in sums[1:]:
        total += ref[0]
    lanes, docs = total.shape[1], slot_ref.shape[1]
    values = jnp.broadcast_to(jnp.log(1.0 + total * 2.0**-SHIFT), (8, lanes)).T[:, 0:1]
    here = lax.broadcasted_iota(jnp.int32, (lanes, docs), 0) == slot_ref[...]
    out_ref[...] = jnp.sum(jnp.where(here, values, 0.0), axis=0, keepdims=True)


def finish(slot, sums):
    return pl.pallas_call(
        finish_kernel,
        out_shape=jax.ShapeDtypeStruct(slot.shape, F32),
        compiler_params=pltpu.CompilerParams(vmem_limit_bytes=6 * 2**20),
        name="finish",
    )(slot, *sums)


def meeting_plan(states, proj_weight, cluster_of):
    owners = lax.axis_size("owner")
    columns = owners // ROWS
    docs = states.shape[0]
    hot = 3 * docs // owners
    flag = layout(docs, hot)[2]

    owner, core = lax.axis_index("owner"), lax.axis_index("split")
    place = jnp.stack([owner // ROWS, owner % ROWS, core]).astype(jnp.int32)
    same, other, slot = prep(hot, place, cluster_of, states, proj_weight)

    def move(a, to, row=0, core=0):
        pairs = [
            (
                (z * ROWS + y) * 2 + c,
                (to[z] * ROWS + (y ^ row)) * 2 + (c ^ (core if row or to[z] != z else 1)),
            )
            for z in range(columns) for y in range(ROWS) for c in range(2)
        ]
        return lax.ppermute(a, ("owner", "split"), pairs)

    STAY, OUTER, MIDDLE, TWO = (0, 1, 2, 3), (1, 0, 3, 2), (0, 2, 1, 3), (2, 3, 0, 1)
    TO_MIDDLE = (2, 0, 3, 1)

    def meet(name, made, tasks, **options):
        return score(name, docs, hot, place, blocks, pairs, made, tasks, sums, **options)

    blocks, pairs, sums = {OWN: same}, {}, ()
    blocks[CORE] = move(same, STAY, core=1)
    blocks[PAIR] = move(other, OUTER)
    blocks[ROW] = move(same, STAY, row=1)
    blocks[CORE], other = lax.optimization_barrier((blocks[CORE], other))
    blocks[NEXT] = move(other, MIDDLE)
    sums, pairs = meet("own", HERE, [(OWN, HERE, False, None), (CORE, HERE, False, "core0")], weight=2**33)

    blocks[PAIR], _ = lax.optimization_barrier((blocks[PAIR], sums[0]))
    blocks[ROW], blocks[NEXT] = lax.optimization_barrier((blocks[ROW], blocks[NEXT]))
    blocks[FAR] = move(same, TO_MIDDLE)
    blocks[PAIR_ROW] = move(blocks[PAIR], STAY, row=1)
    blocks[PAIR_CORE] = move(blocks[PAIR], STAY, core=1)
    blocks[DIAG] = move(blocks[ROW], STAY, core=1)
    sums, pairs = meet(
        "pair", THERE,
        [(PAIR, THERE, False, None), (PAIR_CORE, THERE, False, "core1"), (NEXT, HERE, True, None),
         (NEXT, THERE, True, None)],
        weight=2**33,
    )
    sums, pairs = meet(
        "row", ACROSS,
        [(PAIR, HERE, True, None), (PAIR, ACROSS, True, None), (NEXT, ACROSS, True, None),
         (ROW, HERE, False, "row0"), (DIAG, HERE, False, "row1")],
    )
    blocks[PAIR_ROW], _ = lax.optimization_barrier((blocks[PAIR_ROW], sums[0]))
    blocks[PAIR_DIAG] = move(blocks[PAIR_ROW], STAY, core=1)
    sums, pairs = meet("far", (), [(FAR, p, True, None) for p in (HERE, THERE, ACROSS)])
    sums, pairs = meet(
        "last", (),
        [(left, right, False, None) for left in (NEXT, FAR) for right in (PAIR_ROW, PAIR_DIAG)]
        + [(PAIR_ROW, THERE, False, "row1"), (PAIR_DIAG, THERE, False, "row0")],
        doubted=(PAIR_ROW, PAIR_DIAG),
    )
    kept, by_core, to_next, to_far = sums
    from_core = move(by_core, STAY, core=1)
    from_next, from_far = move(to_next, MIDDLE), move(to_far, TWO)
    own, pair, row, pair_row = (kept[k:k + 1] + from_core[k:k + 1] for k in (0, 1, 2, 3))
    home = [
        own, from_next, from_far,
        move(pair, OUTER), move(row, STAY, row=1), move(pair_row, OUTER, row=1),
    ]
    return lax.cond(
        (to_far + from_far)[0, 0, flag] > 0.0,
        lambda states, proj_weight, cluster_of, *_: owner_plan(states, proj_weight, cluster_of),
        lambda states, proj_weight, cluster_of, slot, *home: finish(slot, home).reshape(docs),
        states, proj_weight, cluster_of, slot, *home,
    )


def on_device(states, proj_weight, cluster_of):
    if (lax.axis_size("owner"), lax.axis_size("split")) == (8, 2) and states.shape[0] == 512:
        return meeting_plan(states, proj_weight, cluster_of)
    return owner_plan(states, proj_weight, cluster_of)


def solution(mesh):
    placed = (P(("parts", "owner", "split"), None), P(), P(("parts", "owner", "split")))
    return jax.shard_map(
        on_device,
        mesh=mesh,
        in_specs=placed,
        out_specs=P(("parts", "owner", "split")),
        check_vma=False,
    )
```

```python
import math

import jax
import jax.numpy as jnp
from jax import lax
from jax.experimental import pallas as pl
from jax.experimental.pallas import tpu as pltpu
from jax.sharding import PartitionSpec as P

CLUS_OWN = 2
TAU = 0.05
THRESH = 0.2
EPS = 1e-06
LOG2E = math.log2(math.e)
SCALE = LOG2E / TAU
SHIFT = THRESH * LOG2E / TAU

ROWS = 2
F32 = jnp.float32
BF16 = jnp.bfloat16


def prepare(states, proj_weight):
    projected = jnp.dot(states, proj_weight, preferred_element_type=jnp.float32)
    unit = projected * lax.rsqrt(jnp.sum(projected * projected, axis=1, keepdims=True) + EPS)
    peak = jnp.max(jnp.abs(unit), axis=1).astype(jnp.bfloat16)
    quant = (unit / peak.astype(jnp.float32)[:, None]).astype(jnp.bfloat16)
    return (quant, peak)


def similarity_scores(
    own_quant, own_peak, own_cluster, own_index, col_quant, col_peak, col_cluster, col_index
):
    row_count = own_quant.shape[0]
    block = math.gcd(row_count, 768)
    col_scale = col_peak.astype(jnp.float32)

    def one_block(start):
        quant_rows = lax.dynamic_slice_in_dim(own_quant, start, block, 0)
        scale_rows = lax.dynamic_slice_in_dim(own_peak, start, block, 0).astype(jnp.float32)
        cluster_rows = lax.dynamic_slice_in_dim(own_cluster, start, block, 0)
        index_rows = lax.dynamic_slice_in_dim(own_index, start, block, 0)
        inner = lax.dot_general(
            quant_rows, col_quant, (((1,), (1,)), ((), ())), preferred_element_type=jnp.float32
        )
        cosine = inner * scale_rows[:, None] * col_scale[None, :]
        same = (cluster_rows[:, None] == col_cluster[None, :]) & (
            index_rows[:, None] != col_index[None, :]
        )
        weights = jnp.where(same, jnp.exp((cosine - THRESH) / TAU), jnp.zeros_like(cosine))
        return jnp.log(1.0 + jnp.sum(weights, axis=1))

    starts = jnp.arange(row_count // block, dtype=jnp.int32) * block
    return lax.map(one_block, starts).reshape(row_count)


def owner_plan(states, proj_weight, cluster_of):
    owners = lax.axis_size("owner")
    splits = lax.axis_size("split")
    half_index = lax.axis_index("split")
    doc_count = states.shape[0]
    capacity = 3 * doc_count // owners
    width = proj_weight.shape[1]
    slot_total = owners * capacity
    quant, peak = prepare(states, proj_weight)
    group_of = cluster_of // CLUS_OWN
    onehot = (group_of[:, None] == jnp.arange(owners, dtype=jnp.int32)[None, :]).astype(jnp.int32)
    before = jnp.cumsum(onehot, axis=0) - onehot
    target = group_of * capacity + jnp.sum(before * onehot, axis=1)
    quant_slots = (
        jnp.zeros((slot_total, width), jnp.bfloat16)
        .at[target]
        .set(quant)
        .reshape(owners, capacity, width)
    )
    peak_slots = (
        jnp.zeros((slot_total,), jnp.bfloat16).at[target].set(peak).reshape(owners, capacity)
    )
    cluster_slots = (
        jnp.full((slot_total,), -1, jnp.int32).at[target].set(cluster_of).reshape(owners, capacity)
    )
    positions = (
        jnp.arange(owners, dtype=jnp.int32)[:, None] * (splits * capacity)
        + jnp.arange(capacity, dtype=jnp.int32)[None, :]
    )
    own_index = (positions + half_index * capacity).reshape(slot_total)
    col_index = jnp.arange(splits * slot_total, dtype=jnp.int32)
    own_quant, own_peak, own_cluster = (
        lax.all_to_all(a, "owner", split_axis=0, concat_axis=0, tiled=True)
        for a in (quant_slots, peak_slots, cluster_slots)
    )
    all_quant, all_peak, all_cluster = (
        lax.all_gather(a, "split", axis=1, tiled=True) for a in (own_quant, own_peak, own_cluster)
    )
    scores = similarity_scores(
        own_quant.reshape(slot_total, width),
        own_peak.reshape(slot_total),
        own_cluster.reshape(slot_total),
        own_index,
        all_quant.reshape(splits * slot_total, width),
        all_peak.reshape(splits * slot_total),
        all_cluster.reshape(splits * slot_total),
        col_index,
    )
    returned = lax.all_to_all(
        scores.reshape(owners, capacity), "owner", split_axis=0, concat_axis=0, tiled=True
    )
    return returned.reshape(slot_total)[target]


def up(n, m):
    return -(-n // m) * m


META = 16


def layout(docs, hot):
    rest = docs - hot
    first = up(rest, 128)
    flag = first + hot
    return rest, first, flag, up(flag + 1, 128)


def prep_kernel(hot, place_ref, cl_ref, st_ref, w_ref, same_ref, other_ref, sa_ref, sb_ref, oa_ref, ob_ref, slot_ref, vectors):
    docs = st_ref.shape[0]
    rest, first, flag, lanes = layout(docs, hot)
    tile = 128

    cluster = cl_ref[...]
    group = cluster // CLUS_OWN
    member = lax.broadcasted_iota(jnp.int32, (8, docs), 0) == group
    full = jnp.sum(member.astype(F32), axis=1, keepdims=True) == float(hot)
    chosen = jnp.min(
        jnp.where(full, lax.broadcasted_iota(jnp.int32, (8, 1), 0), 8), axis=0, keepdims=True
    )
    doubt = jnp.where(jnp.sum(full.astype(F32), axis=0, keepdims=True) == 1.0, 0.0, 1.0)
    in_hot = group == chosen

    for t in range(docs // tile):
        rows = slice(t * tile, (t + 1) * tile)
        projected = jnp.dot(st_ref[rows, :], w_ref[...], preferred_element_type=F32)
        norm = lax.rsqrt(jnp.sum(projected * projected, axis=1, keepdims=True) + EPS)
        vectors[rows, :] = (projected * (norm * math.sqrt(SCALE))).astype(BF16)

    ahead = (
        lax.broadcasted_iota(jnp.int32, (docs, docs), 0) < lax.broadcasted_iota(jnp.int32, (docs, docs), 1)
    ).astype(F32).astype(BF16)
    hot_rows = jnp.broadcast_to(in_hot.astype(F32), (8, docs)).astype(BF16)
    rank = jnp.dot(hot_rows, ahead, preferred_element_type=F32)[0:1, :].astype(jnp.int32)
    place = lax.broadcasted_iota(jnp.int32, (1, docs), 1)
    slot = jnp.where(in_hot, first + rank, place - rank)
    slot_ref[...] = slot

    sort = (lax.broadcasted_iota(jnp.int32, (lanes, docs), 0) == slot).astype(F32).astype(BF16)
    cluster_rows = jnp.broadcast_to(cluster.astype(F32), (META, docs)).astype(BF16)
    ids = lax.dot_general(
        cluster_rows, sort, (((1,), (1,)), ((), ())), preferred_element_type=F32
    )
    ids = ids.astype(BF16)


    sorted_n = jnp.dot(sort[:rest, :], vectors[...], preferred_element_type=F32).astype(BF16)
    sorted_h = jnp.dot(sort[first:flag, :], vectors[...], preferred_element_type=F32).astype(BF16)

    def fill(ref, vectors, room, start, first_doc):
        count = vectors.shape[0]
        ref[:count, :] = vectors
        ref[count:, :] = jnp.zeros((ref.shape[0] - count, ref.shape[1]), BF16)
        wide = up(count, 128)
        if first_doc:
            spots = lax.broadcasted_iota(jnp.int32, (wide, lanes), 0) + (start + first_doc)
            pick = (lax.broadcasted_iota(jnp.int32, (wide, lanes), 1) == spots).astype(F32).astype(BF16)
            row = lax.dot_general(ids, pick, (((1,), (1,)), ((), ())), preferred_element_type=F32).astype(BF16)
        else:
            row = ids[:, start:start + wide]
        ref[room:, :wide] = row
        ref[room:, first:first + 128] = jnp.broadcast_to(doubt.astype(BF16), (META, 128))

    def fill_all(whole, half_a, half_b, vectors, start):
        half = vectors.shape[0] // 2
        fill(whole, vectors, rest, start, 0)
        fill(half_a, vectors[:half], rest // 2, start, 0)
        fill(half_b, vectors[half:], rest // 2, start, half)

    even = lax.rem(place_ref[0], 2) == 0
    sames, others = (same_ref, sa_ref, sb_ref), (other_ref, oa_ref, ob_ref)

    @pl.when(even)
    def _():
        fill_all(*sames, sorted_h, first)
        fill_all(*others, sorted_n, 0)

    @pl.when(jnp.logical_not(even))
    def _():
        fill_all(*sames, sorted_n, 0)
        fill_all(*others, sorted_h, first)


def prep(hot, place, cluster_of, states, proj_weight):
    docs, width = states.shape[0], proj_weight.shape[1]
    rest = docs - hot
    shape = jax.ShapeDtypeStruct
    vmem = pl.BlockSpec(memory_space=pltpu.VMEM)
    return pl.pallas_call(
        lambda *refs: prep_kernel(hot, *refs),
        out_shape=(
            *(shape((rest + META, width), BF16) for _ in range(2)),
            *(shape((rest // 2 + META, width), BF16) for _ in range(4)),
            shape((1, docs), jnp.int32),
        ),
        in_specs=[pl.BlockSpec(memory_space=pltpu.SMEM), vmem, vmem, vmem],
        scratch_shapes=[pltpu.VMEM((docs, width), BF16)],
        compiler_params=pltpu.CompilerParams(vmem_limit_bytes=24 * 2**20),
        name="prep",
    )(place, cluster_of.reshape(1, docs), states, proj_weight)


OWN, PAIR = "own", "pair"
CORE, PAIR_CORE = "core", "pair_core"
ROW, PAIR_ROW = "row", "pair_row"
DIAG, PAIR_DIAG = "diag", "pair_diag"
NEXT, FAR = "next", "far"
GROUPS = ((OWN, PAIR, ROW, PAIR_ROW), (CORE, PAIR_CORE, DIAG, PAIR_DIAG), (NEXT,), (FAR,))
TILE = 256


def halves(name):
    return (name + ".a", name + ".b")


def whole(name):
    return (name[:-2], "ab".index(name[-1])) if name[-2] == "." else (name, None)


HERE, THERE, ACROSS = (OWN, CORE), halves(PAIR) + halves(PAIR_CORE), (ROW, DIAG)


def score_kernel(docs, hot, names, given, made, tasks, doubted, carries, *refs):
    rest, first, flag, lanes = layout(docs, hot)
    place_ref, refs = refs[0], refs[1:]
    blocks, refs = dict(zip(names, refs[:len(names)])), refs[len(names):]
    pairs, refs = {p: refs[2 * k:2 * k + 2] for k, p in enumerate(given)}, refs[2 * len(given):]
    before, refs = refs[:len(GROUPS) * carries], refs[len(GROUPS) * carries:]
    outs, refs = refs[:len(GROUPS)], refs[len(GROUPS):]
    if made:
        pairs[made], refs = refs[:2], refs[2:]
    parts = refs[-1]
    for k, out in enumerate(outs):
        out[...] = before[k][...] if carries else jnp.zeros(out.shape, F32)
    spots = {name: (out, k) for out, group in zip(outs, GROUPS) for k, name in enumerate(group)}
    z, y, c = place_ref[0], place_ref[1], place_ref[2]
    when = {"core0": c == 0, "core1": c == 1, "row0": y == 0, "row1": y == 1}
    middle = (z == 1) | (z == 2)

    def meet(full, start):
        two = 2 * full
        count, base, room = {}, {}, {}
        for name in blocks:
            half = whole(name)[1]
            count[name] = full if half is None else full // 2
            base[name] = 0 if half is None else half * full // 2
            room[name] = rest if half is None else rest // 2

        def ids_of(name):
            return blocks[name][room[name]:, 0:up(count[name], 128)].astype(F32)[0:8, :]

        def lanes_of(name):
            return slice(start + base[name], start + base[name] + count[name])

        columns = {name: ids_of(name).T[0:count[name], :] for name in blocks}
        if made:
            turned, notes = pairs[made]
            turned[:, 0:two] = jnp.concatenate([blocks[name][:count[name], :] for name in made], axis=0).T
            notes[:, 0:two] = jnp.concatenate([columns[name] for name in made], axis=0).T

        for left in dict.fromkeys(task[0] for task in tasks):

            def work(left=left):
                rows = count[left]
                block = blocks[left][:rows, :]
                fresh = True
                for _, right, both, _ in [task for task in tasks if task[0] == left]:
                    if right in blocks:
                        span, diagonal = count[right], False
                        ids = ids_of(right)[0:1, 0:span]
                        rights = [(whole(right)[0], lanes_of(right))]
                    else:
                        turned, notes = pairs[right]
                        span, diagonal = two if both else up(full, 128), left in right[:len(right) // 2]
                        ids = notes[0:1, 0:span]
                        rights = [
                            (whole(right[k * len(right) // 2])[0], slice(start, start + full)) for k in range(1 + both)
                        ]
                        if not both:
                            ids = jnp.where(lax.broadcasted_iota(jnp.int32, ids.shape, 1) < full, ids, -1.0)
                    totals = []
                    for low in range(0, span, TILE):
                        high = min(low + TILE, span)
                        if right in blocks:
                            inner = lax.dot_general(
                                block, blocks[right][low:high, :], (((1,), (1,)), ((), ())),
                                preferred_element_type=F32,
                            )
                        else:
                            inner = jnp.dot(block, turned[:, low:high], preferred_element_type=F32)
                        same = columns[left][:, 0:1] == ids[:, low:high]
                        if diagonal:
                            same &= lax.broadcasted_iota(jnp.int32, inner.shape, 0) + base[left] != (
                                lax.broadcasted_iota(jnp.int32, inner.shape, 1) + low
                            )
                        weights = jnp.where(same, jnp.exp2(inner), 0.0)
                        totals.append(jnp.sum(weights, axis=0, keepdims=True))
                        if not diagonal:
                            part = None
                            for t in range(0, high - low, 128):
                                piece = weights[:, t:t + 128]
                                if piece.shape[1] < 128:
                                    blank = jnp.zeros((rows, 128 - piece.shape[1]), F32)
                                    piece = jnp.concatenate([piece, blank], axis=1)
                                part = piece if part is None else part + piece
                            if fresh:
                                parts[0:rows, :] = part
                            else:
                                parts[0:rows, :] += part
                            fresh = False
                    total = jnp.concatenate(totals, axis=1) if len(totals) > 1 else totals[0]
                    for k, (name, lane) in enumerate(rights):
                        out, spot = spots[name]
                        width = lane.stop - lane.start
                        out[spot, :, lane] += total[:, k * width:(k + 1) * width]
                if not fresh:
                    part = parts[0:rows, :]
                    high = part.astype(BF16)
                    low = (part - high.astype(F32)).astype(BF16)
                    total = lax.dot_general(
                        jnp.ones((16, 256), BF16), jnp.concatenate([high, low], axis=1),
                        (((1,), (1,)), ((), ())), preferred_element_type=F32,
                    )
                    out, spot = spots[whole(left)[0]]
                    out[spot, :, lanes_of(left)] += total[0:1, :]

            condition = [task[3] for task in tasks if task[0] == left][0]
            if whole(left)[0] in (NEXT, FAR):
                pl.when(middle)(work)
            elif condition:
                pl.when(when[condition])(work)
            else:
                work()

    pl.when(lax.rem(z, 2) == 0)(lambda: meet(hot, first))
    pl.when(lax.rem(z, 2) == 1)(lambda: meet(rest, 0))

    if doubted:
        doubt = sum(
            blocks[name][blocks[name].shape[0] - META:, first:first + 128].astype(F32)[0:1, 0:1] for name in doubted if whole(name)[1] != 1
        )
        out, k = spots[FAR]
        out[k] += jnp.where(lax.broadcasted_iota(jnp.int32, (1, lanes), 1) == flag, doubt, 0.0)


def score(name, docs, hot, place, blocks, pairs, made, tasks, sums, doubted=(), weight=1):
    rest, _, _, lanes = layout(docs, hot)
    names = list(dict.fromkeys([*made, *(task[0] for task in tasks), *(task[1] for task in tasks if task[1] in blocks)]))
    given = [p for p in pairs if any(p == task[1] for task in tasks)]
    width = blocks[OWN].shape[1]
    vmem = pl.BlockSpec(memory_space=pltpu.VMEM)
    arrays = [blocks[b] for b in names] + [a for p in given for a in pairs[p]] + list(sums)
    shapes = [jax.ShapeDtypeStruct((len(group), 1, lanes), F32) for group in GROUPS]
    if made:
        shapes += [jax.ShapeDtypeStruct((width, 2 * rest), BF16), jax.ShapeDtypeStruct((8, 2 * rest), F32)]
    out = pl.pallas_call(
        lambda *refs: score_kernel(docs, hot, names, given, made, tasks, doubted + made, bool(sums), *refs),
        out_shape=tuple(shapes),
        in_specs=[pl.BlockSpec(memory_space=pltpu.SMEM)] + [vmem] * len(arrays),
        out_specs=tuple(vmem for _ in shapes),
        scratch_shapes=[pltpu.VMEM((rest, 128), F32)],
        compiler_params=pltpu.CompilerParams(vmem_limit_bytes=20 * 2**20),
        cost_estimate=pl.CostEstimate(flops=weight, bytes_accessed=2**10, transcendentals=0),
        name=name,
    )(place, *arrays)
    count = len(GROUPS)
    return out[:count], {**pairs, made: out[count:]} if made else pairs


def finish_kernel(slot_ref, *refs):
    sums, out_ref = refs[:-1], refs[-1]
    total = sums[0][0]
    for ref in sums[1:]:
        total += ref[0]
    lanes, docs = total.shape[1], slot_ref.shape[1]
    values = jnp.broadcast_to(jnp.log(1.0 + total * 2.0**-SHIFT), (8, lanes)).T[:, 0:1]
    here = lax.broadcasted_iota(jnp.int32, (lanes, docs), 0) == slot_ref[...]
    out_ref[...] = jnp.sum(jnp.where(here, values, 0.0), axis=0, keepdims=True)


def finish(slot, sums):
    return pl.pallas_call(
        finish_kernel,
        out_shape=jax.ShapeDtypeStruct(slot.shape, F32),
        compiler_params=pltpu.CompilerParams(vmem_limit_bytes=6 * 2**20),
        name="finish",
    )(slot, *sums)


def meeting_plan(states, proj_weight, cluster_of):
    owners = lax.axis_size("owner")
    columns = owners // ROWS
    docs = states.shape[0]
    hot = 3 * docs // owners
    flag = layout(docs, hot)[2]

    owner, core = lax.axis_index("owner"), lax.axis_index("split")
    place = jnp.stack([owner // ROWS, owner % ROWS, core]).astype(jnp.int32)
    same, other, *parts, slot = prep(hot, place, cluster_of, states, proj_weight)

    def move(a, to, row=0, core=0):
        pairs = [
            (
                (z * ROWS + y) * 2 + c,
                (to[z] * ROWS + (y ^ row)) * 2 + (c ^ (core if row or to[z] != z else 1)),
            )
            for z in range(columns) for y in range(ROWS) for c in range(2)
        ]
        return lax.ppermute(a, ("owner", "split"), pairs)

    STAY, OUTER, MIDDLE, TWO = (0, 1, 2, 3), (1, 0, 3, 2), (0, 2, 1, 3), (2, 3, 0, 1)
    TO_MIDDLE = (2, 0, 3, 1)

    def meet(name, made, tasks, **options):
        return score(name, docs, hot, place, blocks, pairs, made, tasks, sums, **options)

    blocks, pairs, sums = {OWN: same}, {}, ()
    blocks[CORE] = move(same, STAY, core=1)
    for name, part in zip(halves(PAIR), parts[2:]):
        blocks[name] = move(part, OUTER)
    blocks[ROW] = move(same, STAY, row=1)
    blocks[CORE], other = lax.optimization_barrier((blocks[CORE], other))
    blocks[NEXT] = move(other, MIDDLE)
    sums, pairs = meet("own", HERE, [(OWN, HERE, False, None), (CORE, HERE, False, "core0")], weight=2**33)

    far, pair, pair_core, row, diag = (halves(b) for b in (FAR, PAIR, PAIR_CORE, PAIR_ROW, PAIR_DIAG))
    blocks[pair[0]], blocks[pair[1]], _ = lax.optimization_barrier((blocks[pair[0]], blocks[pair[1]], sums[0]))
    for k in (0, 1):
        blocks[row[k]] = move(blocks[pair[k]], STAY, row=1)
        blocks[far[k]] = move(parts[k], TO_MIDDLE)
        blocks[pair_core[k]] = move(blocks[pair[k]], STAY, core=1)
    blocks[ROW], blocks[NEXT] = lax.optimization_barrier((blocks[ROW], blocks[NEXT]))
    blocks[DIAG] = move(blocks[ROW], STAY, core=1)
    sums, pairs = meet(
        "pair", THERE,
        [(b, THERE, False, None) for b in pair] + [(b, THERE, False, "core1") for b in pair_core]
        + [(NEXT, HERE, True, None), (NEXT, THERE, True, None)],
        weight=2**33,
    )
    sums, pairs = meet(
        "row", ACROSS,
        [(b, p, True, None) for b in pair for p in (HERE, ACROSS)]
        + [(NEXT, ACROSS, True, None), (ROW, HERE, False, "row0"), (DIAG, HERE, False, "row1")],
    )
    sums, pairs = meet(
        "far_a", (),
        [(far[0], p, True, None) for p in (HERE, THERE, ACROSS)]
        + [(left, row[0], False, None) for left in (NEXT, far[0])] + [(row[0], THERE, False, "row1")],
        doubted=(row[0],), weight=1,
    )
    blocks[row[0]], blocks[row[1]], _ = lax.optimization_barrier((blocks[row[0]], blocks[row[1]], sums[0]))
    for k in (0, 1):
        blocks[diag[k]] = move(blocks[row[k]], STAY, core=1)
    sums, pairs = meet(
        "far_b", (),
        [(far[1], p, True, None) for p in (HERE, THERE, ACROSS)]
        + [(left, right, False, None) for left, right in ((far[1], row[0]), (NEXT, row[1]), (far[0], row[1]))]
        + [(far[1], row[1], False, None), (row[1], THERE, False, "row1")],
    )
    sums, pairs = meet(
        "last", (),
        [(left, right, False, None) for left in (NEXT, *far) for right in diag]
        + [(b, THERE, False, "row0") for b in diag],
        doubted=(diag[0],),
    )
    kept, by_core, to_next, to_far = sums
    from_core = move(by_core, STAY, core=1)
    from_next, from_far = move(to_next, MIDDLE), move(to_far, TWO)
    own, pair, row, pair_row = (kept[k:k + 1] + from_core[k:k + 1] for k in (0, 1, 2, 3))
    home = [
        own, from_next, from_far,
        move(pair, OUTER), move(row, STAY, row=1), move(pair_row, OUTER, row=1),
    ]
    return lax.cond(
        (to_far + from_far)[0, 0, flag] > 0.0,
        lambda states, proj_weight, cluster_of, *_: owner_plan(states, proj_weight, cluster_of),
        lambda states, proj_weight, cluster_of, slot, *home: finish(slot, home).reshape(docs),
        states, proj_weight, cluster_of, slot, *home,
    )


def on_device(states, proj_weight, cluster_of):
    if (lax.axis_size("owner"), lax.axis_size("split")) == (8, 2) and states.shape[0] == 512:
        return meeting_plan(states, proj_weight, cluster_of)
    return owner_plan(states, proj_weight, cluster_of)


def solution(mesh):
    placed = (P(("parts", "owner", "split"), None), P(), P(("parts", "owner", "split")))
    return jax.shard_map(
        on_device,
        mesh=mesh,
        in_specs=placed,
        out_specs=P(("parts", "owner", "split")),
        check_vma=False,
    )
```

```python
import math

import jax
import jax.numpy as jnp
from jax import lax
from jax.experimental import pallas as pl
from jax.experimental.pallas import tpu as pltpu
from jax.sharding import PartitionSpec as P

CLUS_OWN = 2
TAU = 0.05
THRESH = 0.2
EPS = 1e-06
LOG2E = math.log2(math.e)
SCALE = LOG2E / TAU
SHIFT = THRESH * LOG2E / TAU

ROWS = 2
F32 = jnp.float32
BF16 = jnp.bfloat16


def prepare(states, proj_weight):
    projected = jnp.dot(states, proj_weight, preferred_element_type=jnp.float32)
    unit = projected * lax.rsqrt(jnp.sum(projected * projected, axis=1, keepdims=True) + EPS)
    peak = jnp.max(jnp.abs(unit), axis=1).astype(jnp.bfloat16)
    quant = (unit / peak.astype(jnp.float32)[:, None]).astype(jnp.bfloat16)
    return (quant, peak)


def similarity_scores(
    own_quant, own_peak, own_cluster, own_index, col_quant, col_peak, col_cluster, col_index
):
    row_count = own_quant.shape[0]
    block = math.gcd(row_count, 768)
    col_scale = col_peak.astype(jnp.float32)

    def one_block(start):
        quant_rows = lax.dynamic_slice_in_dim(own_quant, start, block, 0)
        scale_rows = lax.dynamic_slice_in_dim(own_peak, start, block, 0).astype(jnp.float32)
        cluster_rows = lax.dynamic_slice_in_dim(own_cluster, start, block, 0)
        index_rows = lax.dynamic_slice_in_dim(own_index, start, block, 0)
        inner = lax.dot_general(
            quant_rows, col_quant, (((1,), (1,)), ((), ())), preferred_element_type=jnp.float32
        )
        cosine = inner * scale_rows[:, None] * col_scale[None, :]
        same = (cluster_rows[:, None] == col_cluster[None, :]) & (
            index_rows[:, None] != col_index[None, :]
        )
        weights = jnp.where(same, jnp.exp((cosine - THRESH) / TAU), jnp.zeros_like(cosine))
        return jnp.log(1.0 + jnp.sum(weights, axis=1))

    starts = jnp.arange(row_count // block, dtype=jnp.int32) * block
    return lax.map(one_block, starts).reshape(row_count)


def owner_plan(states, proj_weight, cluster_of):
    owners = lax.axis_size("owner")
    splits = lax.axis_size("split")
    half_index = lax.axis_index("split")
    doc_count = states.shape[0]
    capacity = 3 * doc_count // owners
    width = proj_weight.shape[1]
    slot_total = owners * capacity
    quant, peak = prepare(states, proj_weight)
    group_of = cluster_of // CLUS_OWN
    onehot = (group_of[:, None] == jnp.arange(owners, dtype=jnp.int32)[None, :]).astype(jnp.int32)
    before = jnp.cumsum(onehot, axis=0) - onehot
    target = group_of * capacity + jnp.sum(before * onehot, axis=1)
    quant_slots = (
        jnp.zeros((slot_total, width), jnp.bfloat16)
        .at[target]
        .set(quant)
        .reshape(owners, capacity, width)
    )
    peak_slots = (
        jnp.zeros((slot_total,), jnp.bfloat16).at[target].set(peak).reshape(owners, capacity)
    )
    cluster_slots = (
        jnp.full((slot_total,), -1, jnp.int32).at[target].set(cluster_of).reshape(owners, capacity)
    )
    positions = (
        jnp.arange(owners, dtype=jnp.int32)[:, None] * (splits * capacity)
        + jnp.arange(capacity, dtype=jnp.int32)[None, :]
    )
    own_index = (positions + half_index * capacity).reshape(slot_total)
    col_index = jnp.arange(splits * slot_total, dtype=jnp.int32)
    own_quant, own_peak, own_cluster = (
        lax.all_to_all(a, "owner", split_axis=0, concat_axis=0, tiled=True)
        for a in (quant_slots, peak_slots, cluster_slots)
    )
    all_quant, all_peak, all_cluster = (
        lax.all_gather(a, "split", axis=1, tiled=True) for a in (own_quant, own_peak, own_cluster)
    )
    scores = similarity_scores(
        own_quant.reshape(slot_total, width),
        own_peak.reshape(slot_total),
        own_cluster.reshape(slot_total),
        own_index,
        all_quant.reshape(splits * slot_total, width),
        all_peak.reshape(splits * slot_total),
        all_cluster.reshape(splits * slot_total),
        col_index,
    )
    returned = lax.all_to_all(
        scores.reshape(owners, capacity), "owner", split_axis=0, concat_axis=0, tiled=True
    )
    return returned.reshape(slot_total)[target]


def up(n, m):
    return -(-n // m) * m


META = 16


def layout(docs, hot):
    rest = docs - hot
    first = up(rest, 128)
    flag = first + hot
    return rest, first, flag, up(flag + 1, 128)


def prep_kernel(hot, place_ref, cl_ref, st_ref, w_ref, same_ref, other_ref, slot_ref, vectors):
    docs = st_ref.shape[0]
    rest, first, flag, lanes = layout(docs, hot)
    tile = 128

    cluster = cl_ref[...]
    group = cluster // CLUS_OWN
    member = lax.broadcasted_iota(jnp.int32, (8, docs), 0) == group
    full = jnp.sum(member.astype(F32), axis=1, keepdims=True) == float(hot)
    chosen = jnp.min(
        jnp.where(full, lax.broadcasted_iota(jnp.int32, (8, 1), 0), 8), axis=0, keepdims=True
    )
    doubt = jnp.where(jnp.sum(full.astype(F32), axis=0, keepdims=True) == 1.0, 0.0, 1.0)
    in_hot = group == chosen

    for t in range(docs // tile):
        rows = slice(t * tile, (t + 1) * tile)
        projected = jnp.dot(st_ref[rows, :], w_ref[...], preferred_element_type=F32)
        norm = lax.rsqrt(jnp.sum(projected * projected, axis=1, keepdims=True) + EPS)
        vectors[rows, :] = (projected * (norm * math.sqrt(SCALE))).astype(BF16)

    ahead = (
        lax.broadcasted_iota(jnp.int32, (docs, docs), 0) < lax.broadcasted_iota(jnp.int32, (docs, docs), 1)
    ).astype(F32).astype(BF16)
    hot_rows = jnp.broadcast_to(in_hot.astype(F32), (8, docs)).astype(BF16)
    rank = jnp.dot(hot_rows, ahead, preferred_element_type=F32)[0:1, :].astype(jnp.int32)
    place = lax.broadcasted_iota(jnp.int32, (1, docs), 1)
    slot = jnp.where(in_hot, first + rank, place - rank)
    slot_ref[...] = slot

    sort = (lax.broadcasted_iota(jnp.int32, (lanes, docs), 0) == slot).astype(F32).astype(BF16)
    cluster_rows = jnp.broadcast_to(cluster.astype(F32), (META, docs)).astype(BF16)
    sorted_n = jnp.dot(sort[:rest, :], vectors[...], preferred_element_type=F32).astype(BF16)
    sorted_h = jnp.dot(sort[first:flag, :], vectors[...], preferred_element_type=F32).astype(BF16)
    ids = lax.dot_general(
        cluster_rows, sort, (((1,), (1,)), ((), ())), preferred_element_type=F32
    )
    ids = ids.astype(BF16)


    def fill_n(ref):
        ref[:rest, :] = sorted_n
        ref[rest:, :] = jnp.zeros((META, ref.shape[1]), BF16)
        ref[rest:, :first] = ids[:, :first]
        ref[rest:, first:first + 128] = jnp.broadcast_to(doubt.astype(BF16), (META, 128))

    def fill_h(ref):
        ref[:hot, :] = sorted_h
        ref[hot:, :] = jnp.zeros((rest + META - hot, ref.shape[1]), BF16)
        ref[rest:, :lanes - first] = ids[:, first:]
        ref[rest:, first:first + 128] = jnp.broadcast_to(doubt.astype(BF16), (META, 128))

    even = lax.rem(place_ref[0], 2) == 0

    @pl.when(even)
    def _():
        fill_h(same_ref)
        fill_n(other_ref)

    @pl.when(jnp.logical_not(even))
    def _():
        fill_n(same_ref)
        fill_h(other_ref)


def prep(hot, place, cluster_of, states, proj_weight):
    docs, width = states.shape[0], proj_weight.shape[1]
    rest = docs - hot
    shape = jax.ShapeDtypeStruct
    vmem = pl.BlockSpec(memory_space=pltpu.VMEM)
    return pl.pallas_call(
        lambda *refs: prep_kernel(hot, *refs),
        out_shape=(
            shape((rest + META, width), BF16),
            shape((rest + META, width), BF16),
            shape((1, docs), jnp.int32),
        ),
        in_specs=[pl.BlockSpec(memory_space=pltpu.SMEM), vmem, vmem, vmem],
        scratch_shapes=[pltpu.VMEM((docs, width), BF16)],
        compiler_params=pltpu.CompilerParams(vmem_limit_bytes=24 * 2**20),
        name="prep",
    )(place, cluster_of.reshape(1, docs), states, proj_weight)


OWN, PAIR = "own", "pair"
CORE, PAIR_CORE = "core", "pair_core"
ROW, PAIR_ROW = "row", "pair_row"
DIAG, PAIR_DIAG = "diag", "pair_diag"
NEXT, FAR = "next", "far"
GROUPS = ((OWN, PAIR, ROW, PAIR_ROW), (CORE, PAIR_CORE, DIAG, PAIR_DIAG), (NEXT,), (FAR,))
TILE = 256
HERE, THERE, ACROSS = (OWN, CORE), (PAIR, PAIR_CORE), (ROW, DIAG)


def score_kernel(docs, hot, names, given, made, tasks, doubted, carries, *refs):
    rest, first, flag, lanes = layout(docs, hot)
    place_ref, refs = refs[0], refs[1:]
    blocks, refs = dict(zip(names, refs[:len(names)])), refs[len(names):]
    pairs, refs = {p: refs[2 * k:2 * k + 2] for k, p in enumerate(given)}, refs[2 * len(given):]
    before, refs = refs[:len(GROUPS) * carries], refs[len(GROUPS) * carries:]
    outs, refs = refs[:len(GROUPS)], refs[len(GROUPS):]
    if made:
        pairs[made], refs = refs[:2], refs[2:]
    parts = refs[-1]
    for k, out in enumerate(outs):
        out[...] = before[k][...] if carries else jnp.zeros(out.shape, F32)
    spots = {name: (out, k) for out, group in zip(outs, GROUPS) for k, name in enumerate(group)}
    z, y, c = place_ref[0], place_ref[1], place_ref[2]
    when = {"core0": c == 0, "core1": c == 1, "row0": y == 0, "row1": y == 1}
    middle = (z == 1) | (z == 2)

    def meet(count, start):
        lane = slice(start, start + count)
        wide, two = up(count, 128), 2 * count
        columns = {name: ref[rest:, 0:wide].astype(F32)[0:8, :].T[0:count, :] for name, ref in blocks.items()}
        if made:
            turned, notes = pairs[made]
            turned[:, 0:two] = jnp.concatenate([blocks[name][:count, :] for name in made], axis=0).T
            notes[:, 0:two] = jnp.concatenate([columns[name] for name in made], axis=0).T

        for left in dict.fromkeys(task[0] for task in tasks):

            def work(left=left):
                own_tasks = [task for task in tasks if task[0] == left]
                rows = count * len(left)
                block = blocks[left[0]][:count, :]
                column = columns[left[0]][:, 0:1]
                for name in left[1:]:
                    block = jnp.concatenate([block, blocks[name][:count, :]], axis=0)
                    column = jnp.concatenate([column, columns[name][:, 0:1]], axis=0)
                fresh = True
                for _, right, both, _ in own_tasks:
                    if right in blocks:
                        span, rights, diagonal = count, (right,), False
                        ids = blocks[right][rest:, 0:wide].astype(F32)[0:1, 0:count]
                    else:
                        turned, notes = pairs[right]
                        span, rights, diagonal = two if both else wide, right[:1 + both], left == right[:1]
                        ids = notes[0:1, 0:span]
                        if not both:
                            ids = jnp.where(lax.broadcasted_iota(jnp.int32, ids.shape, 1) < count, ids, -1.0)
                    totals = []
                    for low in range(0, span, TILE):
                        high = min(low + TILE, span)
                        if right in blocks:
                            inner = lax.dot_general(
                                block, blocks[right][low:high, :], (((1,), (1,)), ((), ())),
                                preferred_element_type=F32,
                            )
                        else:
                            inner = jnp.dot(block, turned[:, low:high], preferred_element_type=F32)
                        same = column == ids[:, low:high]
                        if diagonal:
                            same &= lax.broadcasted_iota(jnp.int32, inner.shape, 0) != (
                                lax.broadcasted_iota(jnp.int32, inner.shape, 1) + low
                            )
                        weights = jnp.where(same, jnp.exp2(inner), 0.0)
                        totals.append(jnp.sum(weights, axis=0, keepdims=True))
                        if not diagonal:
                            part = None
                            for t in range(0, high - low, 128):
                                piece = weights[:, t:t + 128]
                                if piece.shape[1] < 128:
                                    blank = jnp.zeros((rows, 128 - piece.shape[1]), F32)
                                    piece = jnp.concatenate([piece, blank], axis=1)
                                part = piece if part is None else part + piece
                            if fresh:
                                parts[0:rows, :] = part
                            else:
                                parts[0:rows, :] += part
                            fresh = False
                    total = jnp.concatenate(totals, axis=1) if len(totals) > 1 else totals[0]
                    for k, name in enumerate(rights):
                        out, spot = spots[name]
                        out[spot, :, lane] += total[:, k * count:(k + 1) * count]
                if not fresh:
                    part = parts[0:rows, :]
                    high = part.astype(BF16)
                    low = (part - high.astype(F32)).astype(BF16)
                    total = lax.dot_general(
                        jnp.ones((16, 256), BF16), jnp.concatenate([high, low], axis=1),
                        (((1,), (1,)), ((), ())), preferred_element_type=F32,
                    )
                    for k, name in enumerate(left):
                        out, spot = spots[name]
                        out[spot, :, lane] += total[0:1, k * count:(k + 1) * count]

            condition = [task[3] for task in tasks if task[0] == left][0]
            if left[0] in (NEXT, FAR):
                pl.when(middle)(work)
            elif condition:
                pl.when(when[condition])(work)
            else:
                work()

    pl.when(lax.rem(z, 2) == 0)(lambda: meet(hot, first))
    pl.when(lax.rem(z, 2) == 1)(lambda: meet(rest, 0))

    if doubted:
        doubt = sum(blocks[name][rest:, first:first + 128].astype(F32)[0:1, 0:1] for name in doubted)
        out, k = spots[FAR]
        out[k] += jnp.where(lax.broadcasted_iota(jnp.int32, (1, lanes), 1) == flag, doubt, 0.0)


def score(name, docs, hot, place, blocks, pairs, made, tasks, sums, doubted=(), weight=1):
    rest, _, _, lanes = layout(docs, hot)
    names = list(dict.fromkeys([*made, *(name for task in tasks for name in task[0])]))
    given = [p for p in pairs if any(p == task[1] for task in tasks)]
    width = blocks[OWN].shape[1]
    vmem = pl.BlockSpec(memory_space=pltpu.VMEM)
    arrays = [blocks[b] for b in names] + [a for p in given for a in pairs[p]] + list(sums)
    shapes = [jax.ShapeDtypeStruct((len(group), 1, lanes), F32) for group in GROUPS]
    if made:
        shapes += [jax.ShapeDtypeStruct((width, 2 * rest), BF16), jax.ShapeDtypeStruct((8, 2 * rest), F32)]
    out = pl.pallas_call(
        lambda *refs: score_kernel(docs, hot, names, given, made, tasks, doubted or made, bool(sums), *refs),
        out_shape=tuple(shapes),
        in_specs=[pl.BlockSpec(memory_space=pltpu.SMEM)] + [vmem] * len(arrays),
        out_specs=tuple(vmem for _ in shapes),
        scratch_shapes=[pltpu.VMEM((2 * rest, 128), F32)],
        compiler_params=pltpu.CompilerParams(vmem_limit_bytes=20 * 2**20),
        cost_estimate=pl.CostEstimate(flops=weight, bytes_accessed=2**10, transcendentals=0),
        name=name,
    )(place, *arrays)
    count = len(GROUPS)
    return out[:count], {**pairs, made: out[count:]} if made else pairs


def finish_kernel(slot_ref, *refs):
    sums, out_ref = refs[:-1], refs[-1]
    total = sums[0][0]
    for ref in sums[1:]:
        total += ref[0]
    lanes, docs = total.shape[1], slot_ref.shape[1]
    values = jnp.broadcast_to(jnp.log(1.0 + total * 2.0**-SHIFT), (8, lanes)).T[:, 0:1]
    here = lax.broadcasted_iota(jnp.int32, (lanes, docs), 0) == slot_ref[...]
    out_ref[...] = jnp.sum(jnp.where(here, values, 0.0), axis=0, keepdims=True)


def finish(slot, sums):
    return pl.pallas_call(
        finish_kernel,
        out_shape=jax.ShapeDtypeStruct(slot.shape, F32),
        compiler_params=pltpu.CompilerParams(vmem_limit_bytes=6 * 2**20),
        name="finish",
    )(slot, *sums)


def meeting_plan(states, proj_weight, cluster_of):
    owners = lax.axis_size("owner")
    columns = owners // ROWS
    docs = states.shape[0]
    hot = 3 * docs // owners
    flag = layout(docs, hot)[2]

    owner, core = lax.axis_index("owner"), lax.axis_index("split")
    place = jnp.stack([owner // ROWS, owner % ROWS, core]).astype(jnp.int32)
    same, other, slot = prep(hot, place, cluster_of, states, proj_weight)

    def move(a, to, row=0, core=0):
        pairs = [
            (
                (z * ROWS + y) * 2 + c,
                (to[z] * ROWS + (y ^ row)) * 2 + (c ^ (core if row or to[z] != z else 1)),
            )
            for z in range(columns) for y in range(ROWS) for c in range(2)
        ]
        return lax.ppermute(a, ("owner", "split"), pairs)

    STAY, OUTER, MIDDLE, TWO = (0, 1, 2, 3), (1, 0, 3, 2), (0, 2, 1, 3), (2, 3, 0, 1)
    TO_MIDDLE = (2, 0, 3, 1)

    def meet(name, made, tasks, **options):
        return score(name, docs, hot, place, blocks, pairs, made, tasks, sums, **options)

    blocks, pairs, sums = {OWN: same}, {}, ()
    blocks[CORE] = move(same, STAY, core=1)
    blocks[PAIR] = move(other, OUTER)
    blocks[ROW] = move(same, STAY, row=1)
    blocks[CORE], other = lax.optimization_barrier((blocks[CORE], other))
    blocks[NEXT] = move(other, MIDDLE)
    sums, pairs = meet("own", HERE, [((OWN,), HERE, False, None), ((CORE,), HERE, False, "core0")], weight=2**33)

    blocks[PAIR], _ = lax.optimization_barrier((blocks[PAIR], sums[0]))
    blocks[ROW], blocks[NEXT] = lax.optimization_barrier((blocks[ROW], blocks[NEXT]))
    blocks[FAR] = move(same, TO_MIDDLE)
    blocks[PAIR_ROW] = move(blocks[PAIR], STAY, row=1)
    blocks[PAIR_CORE] = move(blocks[PAIR], STAY, core=1)
    blocks[DIAG] = move(blocks[ROW], STAY, core=1)
    sums, pairs = meet(
        "pair", THERE,
        [((PAIR,), THERE, False, None), ((PAIR_CORE,), THERE, False, "core1"), ((NEXT,), HERE, True, None),
         ((NEXT,), THERE, True, None)],
        weight=2**33,
    )
    sums, pairs = meet(
        "row", ACROSS,
        [((PAIR,), HERE, True, None), ((PAIR,), ACROSS, True, None), ((NEXT,), ACROSS, True, None),
         ((ROW,), HERE, False, "row0"), ((DIAG,), HERE, False, "row1")],
    )
    blocks[PAIR_ROW], _ = lax.optimization_barrier((blocks[PAIR_ROW], sums[0]))
    blocks[PAIR_DIAG] = move(blocks[PAIR_ROW], STAY, core=1)
    sums, pairs = meet("far", (), [((FAR,), p, True, None) for p in (HERE, THERE, ACROSS)])
    sums, pairs = meet(
        "last", (),
        [((NEXT, FAR), right, False, None) for right in (PAIR_ROW, PAIR_DIAG)]
        + [((PAIR_ROW,), THERE, False, "row1"), ((PAIR_DIAG,), THERE, False, "row0")],
        doubted=(PAIR_ROW, PAIR_DIAG),
    )
    kept, by_core, to_next, to_far = sums
    from_core, from_far = move(by_core, STAY, core=1), move(to_far, TWO)
    from_core, to_next = lax.optimization_barrier((from_core, to_next))
    from_next = move(to_next, MIDDLE)
    own, pair, row, pair_row = (kept[k:k + 1] + from_core[k:k + 1] for k in (0, 1, 2, 3))
    home = [
        own, from_next, from_far,
        move(pair, OUTER), move(row, STAY, row=1), move(pair_row, OUTER, row=1),
    ]
    return lax.cond(
        (to_far + from_far)[0, 0, flag] > 0.0,
        lambda states, proj_weight, cluster_of, *_: owner_plan(states, proj_weight, cluster_of),
        lambda states, proj_weight, cluster_of, slot, *home: finish(slot, home).reshape(docs),
        states, proj_weight, cluster_of, slot, *home,
    )


def on_device(states, proj_weight, cluster_of):
    if (lax.axis_size("owner"), lax.axis_size("split")) == (8, 2) and states.shape[0] == 512:
        return meeting_plan(states, proj_weight, cluster_of)
    return owner_plan(states, proj_weight, cluster_of)


def solution(mesh):
    placed = (P(("parts", "owner", "split"), None), P(), P(("parts", "owner", "split")))
    return jax.shard_map(
        on_device,
        mesh=mesh,
        in_specs=placed,
        out_specs=P(("parts", "owner", "split")),
        check_vma=False,
    )
```

```python
import math

import jax
import jax.numpy as jnp
from jax import lax
from jax.experimental import pallas as pl
from jax.experimental.pallas import tpu as pltpu
from jax.sharding import PartitionSpec as P

CLUS_OWN = 2
TAU = 0.05
THRESH = 0.2
EPS = 1e-06
LOG2E = math.log2(math.e)
SCALE = LOG2E / TAU
SHIFT = THRESH * LOG2E / TAU

ROWS = 2
F32 = jnp.float32
BF16 = jnp.bfloat16


def prepare(states, proj_weight):
    projected = jnp.dot(states, proj_weight, preferred_element_type=jnp.float32)
    unit = projected * lax.rsqrt(jnp.sum(projected * projected, axis=1, keepdims=True) + EPS)
    peak = jnp.max(jnp.abs(unit), axis=1).astype(jnp.bfloat16)
    quant = (unit / peak.astype(jnp.float32)[:, None]).astype(jnp.bfloat16)
    return (quant, peak)


def similarity_scores(
    own_quant, own_peak, own_cluster, own_index, col_quant, col_peak, col_cluster, col_index
):
    row_count = own_quant.shape[0]
    block = math.gcd(row_count, 768)
    col_scale = col_peak.astype(jnp.float32)

    def one_block(start):
        quant_rows = lax.dynamic_slice_in_dim(own_quant, start, block, 0)
        scale_rows = lax.dynamic_slice_in_dim(own_peak, start, block, 0).astype(jnp.float32)
        cluster_rows = lax.dynamic_slice_in_dim(own_cluster, start, block, 0)
        index_rows = lax.dynamic_slice_in_dim(own_index, start, block, 0)
        inner = lax.dot_general(
            quant_rows, col_quant, (((1,), (1,)), ((), ())), preferred_element_type=jnp.float32
        )
        cosine = inner * scale_rows[:, None] * col_scale[None, :]
        same = (cluster_rows[:, None] == col_cluster[None, :]) & (
            index_rows[:, None] != col_index[None, :]
        )
        weights = jnp.where(same, jnp.exp((cosine - THRESH) / TAU), jnp.zeros_like(cosine))
        return jnp.log(1.0 + jnp.sum(weights, axis=1))

    starts = jnp.arange(row_count // block, dtype=jnp.int32) * block
    return lax.map(one_block, starts).reshape(row_count)


def owner_plan(states, proj_weight, cluster_of):
    owners = lax.axis_size("owner")
    splits = lax.axis_size("split")
    half_index = lax.axis_index("split")
    doc_count = states.shape[0]
    capacity = 3 * doc_count // owners
    width = proj_weight.shape[1]
    slot_total = owners * capacity
    quant, peak = prepare(states, proj_weight)
    group_of = cluster_of // CLUS_OWN
    onehot = (group_of[:, None] == jnp.arange(owners, dtype=jnp.int32)[None, :]).astype(jnp.int32)
    before = jnp.cumsum(onehot, axis=0) - onehot
    target = group_of * capacity + jnp.sum(before * onehot, axis=1)
    quant_slots = (
        jnp.zeros((slot_total, width), jnp.bfloat16)
        .at[target]
        .set(quant)
        .reshape(owners, capacity, width)
    )
    peak_slots = (
        jnp.zeros((slot_total,), jnp.bfloat16).at[target].set(peak).reshape(owners, capacity)
    )
    cluster_slots = (
        jnp.full((slot_total,), -1, jnp.int32).at[target].set(cluster_of).reshape(owners, capacity)
    )
    positions = (
        jnp.arange(owners, dtype=jnp.int32)[:, None] * (splits * capacity)
        + jnp.arange(capacity, dtype=jnp.int32)[None, :]
    )
    own_index = (positions + half_index * capacity).reshape(slot_total)
    col_index = jnp.arange(splits * slot_total, dtype=jnp.int32)
    own_quant, own_peak, own_cluster = (
        lax.all_to_all(a, "owner", split_axis=0, concat_axis=0, tiled=True)
        for a in (quant_slots, peak_slots, cluster_slots)
    )
    all_quant, all_peak, all_cluster = (
        lax.all_gather(a, "split", axis=1, tiled=True) for a in (own_quant, own_peak, own_cluster)
    )
    scores = similarity_scores(
        own_quant.reshape(slot_total, width),
        own_peak.reshape(slot_total),
        own_cluster.reshape(slot_total),
        own_index,
        all_quant.reshape(splits * slot_total, width),
        all_peak.reshape(splits * slot_total),
        all_cluster.reshape(splits * slot_total),
        col_index,
    )
    returned = lax.all_to_all(
        scores.reshape(owners, capacity), "owner", split_axis=0, concat_axis=0, tiled=True
    )
    return returned.reshape(slot_total)[target]


def up(n, m):
    return -(-n // m) * m


META = 8


def layout(docs, hot):
    rest = docs - hot
    first = up(rest, 128)
    flag = first + hot
    return rest, first, flag, up(flag + 1, 128)


def prep_kernel(hot, place_ref, cl_ref, st_ref, w_ref, same_ref, other_ref, slot_ref, vectors):
    docs = st_ref.shape[0]
    rest, first, flag, lanes = layout(docs, hot)
    tile = 128

    cluster = cl_ref[...]
    group = cluster // CLUS_OWN
    member = lax.broadcasted_iota(jnp.int32, (8, docs), 0) == group
    full = jnp.sum(member.astype(F32), axis=1, keepdims=True) == float(hot)
    chosen = jnp.min(
        jnp.where(full, lax.broadcasted_iota(jnp.int32, (8, 1), 0), 8), axis=0, keepdims=True
    )
    doubt = jnp.where(jnp.sum(full.astype(F32), axis=0, keepdims=True) == 1.0, 0.0, 1.0)
    in_hot = group == chosen

    for t in range(docs // tile):
        rows = slice(t * tile, (t + 1) * tile)
        projected = jnp.dot(st_ref[rows, :], w_ref[...], preferred_element_type=F32)
        norm = lax.rsqrt(jnp.sum(projected * projected, axis=1, keepdims=True) + EPS)
        vectors[rows, :] = (projected * (norm * math.sqrt(SCALE))).astype(BF16)

    ahead = (
        lax.broadcasted_iota(jnp.int32, (docs, docs), 0) < lax.broadcasted_iota(jnp.int32, (docs, docs), 1)
    ).astype(F32).astype(BF16)
    hot_rows = jnp.broadcast_to(in_hot.astype(F32), (8, docs)).astype(BF16)
    rank = jnp.dot(hot_rows, ahead, preferred_element_type=F32)[0:1, :].astype(jnp.int32)
    place = lax.broadcasted_iota(jnp.int32, (1, docs), 1)
    slot = jnp.where(in_hot, first + rank, place - rank)
    slot_ref[...] = slot

    sort = (lax.broadcasted_iota(jnp.int32, (lanes, docs), 0) == slot).astype(F32).astype(BF16)
    cluster_rows = jnp.broadcast_to(cluster.astype(F32), (META, docs)).astype(BF16)
    sorted_n = jnp.dot(sort[:rest, :], vectors[...], preferred_element_type=F32).astype(BF16)
    sorted_h = jnp.dot(sort[first:flag, :], vectors[...], preferred_element_type=F32).astype(BF16)
    ids = lax.dot_general(
        cluster_rows, sort, (((1,), (1,)), ((), ())), preferred_element_type=F32
    )
    ids = ids.astype(BF16)


    def fill_n(ref):
        ref[:rest, :] = sorted_n
        ref[rest:, :] = jnp.zeros((META, ref.shape[1]), BF16)
        ref[rest:, :first] = ids[:, :first]
        ref[rest:, first:first + 128] = jnp.broadcast_to(doubt.astype(BF16), (META, 128))

    def fill_h(ref):
        ref[:hot, :] = sorted_h
        ref[hot:, :] = jnp.zeros((rest + META - hot, ref.shape[1]), BF16)
        ref[rest:, :lanes - first] = ids[:, first:]
        ref[rest:, first:first + 128] = jnp.broadcast_to(doubt.astype(BF16), (META, 128))

    even = lax.rem(place_ref[0], 2) == 0

    @pl.when(even)
    def _():
        fill_h(same_ref)
        fill_n(other_ref)

    @pl.when(jnp.logical_not(even))
    def _():
        fill_n(same_ref)
        fill_h(other_ref)


def prep(hot, place, cluster_of, states, proj_weight):
    docs, width = states.shape[0], proj_weight.shape[1]
    rest = docs - hot
    shape = jax.ShapeDtypeStruct
    vmem = pl.BlockSpec(memory_space=pltpu.VMEM)
    return pl.pallas_call(
        lambda *refs: prep_kernel(hot, *refs),
        out_shape=(
            shape((rest + META, width), BF16),
            shape((rest + META, width), BF16),
            shape((1, docs), jnp.int32),
        ),
        in_specs=[pl.BlockSpec(memory_space=pltpu.SMEM), vmem, vmem, vmem],
        scratch_shapes=[pltpu.VMEM((docs, width), BF16)],
        compiler_params=pltpu.CompilerParams(vmem_limit_bytes=24 * 2**20),
        name="prep",
    )(place, cluster_of.reshape(1, docs), states, proj_weight)


OWN, PAIR = "own", "pair"
CORE, PAIR_CORE = "core", "pair_core"
ROW, PAIR_ROW = "row", "pair_row"
DIAG, PAIR_DIAG = "diag", "pair_diag"
NEXT, FAR = "next", "far"
GROUPS = ((OWN, PAIR, ROW, PAIR_ROW), (CORE, PAIR_CORE, DIAG, PAIR_DIAG), (NEXT,), (FAR,))
TILE = 256
HERE, THERE, ACROSS = (OWN, CORE), (PAIR, PAIR_CORE), (ROW, DIAG)


def score_kernel(docs, hot, names, given, made, tasks, doubted, carries, *refs):
    rest, first, flag, lanes = layout(docs, hot)
    place_ref, refs = refs[0], refs[1:]
    blocks, refs = dict(zip(names, refs[:len(names)])), refs[len(names):]
    pairs, refs = {p: refs[2 * k:2 * k + 2] for k, p in enumerate(given)}, refs[2 * len(given):]
    before, refs = refs[:len(GROUPS) * carries], refs[len(GROUPS) * carries:]
    outs, refs = refs[:len(GROUPS)], refs[len(GROUPS):]
    if made:
        pairs[made], refs = refs[:2], refs[2:]
    parts = refs[-1]
    for k, out in enumerate(outs):
        out[...] = before[k][...] if carries else jnp.zeros(out.shape, F32)
    spots = {name: (out, k) for out, group in zip(outs, GROUPS) for k, name in enumerate(group)}
    z, y, c = place_ref[0], place_ref[1], place_ref[2]
    when = {"core0": c == 0, "core1": c == 1, "row0": y == 0, "row1": y == 1}
    middle = (z == 1) | (z == 2)

    def meet(count, start):
        lane = slice(start, start + count)
        wide, two = up(count, 128), 2 * count
        columns = {name: ref[rest:, 0:wide].astype(F32)[0:8, :].T[0:count, :] for name, ref in blocks.items()}
        if made:
            turned, notes = pairs[made]
            turned[:, 0:two] = jnp.concatenate([blocks[name][:count, :] for name in made], axis=0).T
            notes[:, 0:two] = jnp.concatenate([columns[name] for name in made], axis=0).T

        for left in dict.fromkeys(task[0] for task in tasks):

            def work(left=left):
                own_tasks = [task for task in tasks if task[0] == left]
                rows = count * len(left)
                block = blocks[left[0]][:count, :]
                column = columns[left[0]][:, 0:1]
                for name in left[1:]:
                    block = jnp.concatenate([block, blocks[name][:count, :]], axis=0)
                    column = jnp.concatenate([column, columns[name][:, 0:1]], axis=0)
                fresh = True
                for _, right, both, _ in own_tasks:
                    if right in blocks:
                        span, rights, diagonal = count, (right,), False
                        ids = blocks[right][rest:, 0:wide].astype(F32)[0:1, 0:count]
                    else:
                        turned, notes = pairs[right]
                        span, rights, diagonal = two if both else wide, right[:1 + both], left == right[:1]
                        ids = notes[0:1, 0:span]
                        if not both:
                            ids = jnp.where(lax.broadcasted_iota(jnp.int32, ids.shape, 1) < count, ids, -1.0)
                    totals = []
                    for low in range(0, span, TILE):
                        high = min(low + TILE, span)
                        if right in blocks:
                            inner = lax.dot_general(
                                block, blocks[right][low:high, :], (((1,), (1,)), ((), ())),
                                preferred_element_type=F32,
                            )
                        else:
                            inner = jnp.dot(block, turned[:, low:high], preferred_element_type=F32)
                        same = column == ids[:, low:high]
                        if diagonal:
                            same &= lax.broadcasted_iota(jnp.int32, inner.shape, 0) != (
                                lax.broadcasted_iota(jnp.int32, inner.shape, 1) + low
                            )
                        weights = jnp.where(same, jnp.exp2(inner), 0.0)
                        totals.append(jnp.sum(weights, axis=0, keepdims=True))
                        if not diagonal:
                            part = None
                            for t in range(0, high - low, 128):
                                piece = weights[:, t:t + 128]
                                if piece.shape[1] < 128:
                                    blank = jnp.zeros((rows, 128 - piece.shape[1]), F32)
                                    piece = jnp.concatenate([piece, blank], axis=1)
                                part = piece if part is None else part + piece
                            if fresh:
                                parts[0:rows, :] = part
                            else:
                                parts[0:rows, :] += part
                            fresh = False
                    total = jnp.concatenate(totals, axis=1) if len(totals) > 1 else totals[0]
                    for k, name in enumerate(rights):
                        out, spot = spots[name]
                        out[spot, :, lane] += total[:, k * count:(k + 1) * count]
                if not fresh:
                    part = parts[0:rows, :]
                    high = part.astype(BF16)
                    low = (part - high.astype(F32)).astype(BF16)
                    total = lax.dot_general(
                        jnp.ones((16, 256), BF16), jnp.concatenate([high, low], axis=1),
                        (((1,), (1,)), ((), ())), preferred_element_type=F32,
                    )
                    for k, name in enumerate(left):
                        out, spot = spots[name]
                        out[spot, :, lane] += total[0:1, k * count:(k + 1) * count]

            condition = [task[3] for task in tasks if task[0] == left][0]
            if left[0] in (NEXT, FAR):
                pl.when(middle)(work)
            elif condition:
                pl.when(when[condition])(work)
            else:
                work()

    pl.when(lax.rem(z, 2) == 0)(lambda: meet(hot, first))
    pl.when(lax.rem(z, 2) == 1)(lambda: meet(rest, 0))

    if doubted:
        doubt = sum(blocks[name][rest:, first:first + 128].astype(F32)[0:1, 0:1] for name in doubted)
        out, k = spots[FAR]
        out[k] += jnp.where(lax.broadcasted_iota(jnp.int32, (1, lanes), 1) == flag, doubt, 0.0)


def score(name, docs, hot, place, blocks, pairs, made, tasks, sums, doubted=(), weight=1):
    rest, _, _, lanes = layout(docs, hot)
    names = list(dict.fromkeys([*made, *(name for task in tasks for name in task[0])]))
    given = [p for p in pairs if any(p == task[1] for task in tasks)]
    width = blocks[OWN].shape[1]
    vmem = pl.BlockSpec(memory_space=pltpu.VMEM)
    arrays = [blocks[b] for b in names] + [a for p in given for a in pairs[p]] + list(sums)
    shapes = [jax.ShapeDtypeStruct((len(group), 1, lanes), F32) for group in GROUPS]
    if made:
        shapes += [jax.ShapeDtypeStruct((width, 2 * rest), BF16), jax.ShapeDtypeStruct((8, 2 * rest), F32)]
    out = pl.pallas_call(
        lambda *refs: score_kernel(docs, hot, names, given, made, tasks, doubted or made, bool(sums), *refs),
        out_shape=tuple(shapes),
        in_specs=[pl.BlockSpec(memory_space=pltpu.SMEM)] + [vmem] * len(arrays),
        out_specs=tuple(vmem for _ in shapes),
        scratch_shapes=[pltpu.VMEM((2 * rest, 128), F32)],
        compiler_params=pltpu.CompilerParams(vmem_limit_bytes=20 * 2**20),
        cost_estimate=pl.CostEstimate(flops=weight, bytes_accessed=2**10, transcendentals=0),
        name=name,
    )(place, *arrays)
    count = len(GROUPS)
    return out[:count], {**pairs, made: out[count:]} if made else pairs


def finish_kernel(slot_ref, *refs):
    sums, out_ref = refs[:-1], refs[-1]
    total = sums[0][0]
    for ref in sums[1:]:
        total += ref[0]
    lanes, docs = total.shape[1], slot_ref.shape[1]
    values = jnp.broadcast_to(jnp.log(1.0 + total * 2.0**-SHIFT), (8, lanes)).T[:, 0:1]
    here = lax.broadcasted_iota(jnp.int32, (lanes, docs), 0) == slot_ref[...]
    out_ref[...] = jnp.sum(jnp.where(here, values, 0.0), axis=0, keepdims=True)


def finish(slot, sums):
    return pl.pallas_call(
        finish_kernel,
        out_shape=jax.ShapeDtypeStruct(slot.shape, F32),
        compiler_params=pltpu.CompilerParams(vmem_limit_bytes=6 * 2**20),
        name="finish",
    )(slot, *sums)


def decide_kernel(flag, mine_ref, theirs_ref, out_ref):
    out_ref[0] = (jnp.sum(mine_ref[0][:, flag:flag + 1] + theirs_ref[0][:, flag:flag + 1]) > 0.0).astype(jnp.int32)


def decide(flag, mine, theirs):
    return pl.pallas_call(
        lambda *refs: decide_kernel(flag, *refs),
        out_shape=jax.ShapeDtypeStruct((1,), jnp.int32),
        out_specs=pl.BlockSpec(memory_space=pltpu.SMEM),
        compiler_params=pltpu.CompilerParams(vmem_limit_bytes=2 * 2**20),
        name="decide",
    )(mine, theirs)


def meeting_plan(states, proj_weight, cluster_of):
    owners = lax.axis_size("owner")
    columns = owners // ROWS
    docs = states.shape[0]
    hot = 3 * docs // owners
    flag = layout(docs, hot)[2]

    owner, core = lax.axis_index("owner"), lax.axis_index("split")
    place = jnp.stack([owner // ROWS, owner % ROWS, core]).astype(jnp.int32)
    same, other, slot = prep(hot, place, cluster_of, states, proj_weight)

    def move(a, to, row=0, core=0):
        pairs = [
            (
                (z * ROWS + y) * 2 + c,
                (to[z] * ROWS + (y ^ row)) * 2 + (c ^ (core if row or to[z] != z else 1)),
            )
            for z in range(columns) for y in range(ROWS) for c in range(2)
        ]
        return lax.ppermute(a, ("owner", "split"), pairs)

    STAY, OUTER, MIDDLE, TWO = (0, 1, 2, 3), (1, 0, 3, 2), (0, 2, 1, 3), (2, 3, 0, 1)
    TO_MIDDLE = (2, 0, 3, 1)

    def meet(name, made, tasks, **options):
        return score(name, docs, hot, place, blocks, pairs, made, tasks, sums, **options)

    blocks, pairs, sums = {OWN: same}, {}, ()
    blocks[CORE] = move(same, STAY, core=1)
    blocks[PAIR] = move(other, OUTER)
    blocks[CORE], still_same, other = lax.optimization_barrier((blocks[CORE], same, other))
    blocks[ROW] = move(still_same, STAY, row=1)
    blocks[NEXT] = move(other, MIDDLE)
    sums, pairs = meet("own", HERE, [((OWN,), HERE, False, None), ((CORE,), HERE, False, "core0")], weight=2**33)

    blocks[PAIR], _ = lax.optimization_barrier((blocks[PAIR], sums[0]))
    blocks[ROW], blocks[NEXT] = lax.optimization_barrier((blocks[ROW], blocks[NEXT]))
    blocks[FAR] = move(same, TO_MIDDLE)
    blocks[PAIR_ROW] = move(blocks[PAIR], STAY, row=1)
    blocks[PAIR_CORE] = move(blocks[PAIR], STAY, core=1)
    blocks[DIAG] = move(blocks[ROW], STAY, core=1)
    sums, pairs = meet(
        "pair", THERE,
        [((PAIR,), THERE, False, None), ((PAIR_CORE,), THERE, False, "core1"), ((NEXT,), HERE, True, None),
         ((NEXT,), THERE, True, None)],
        weight=2**33,
    )
    sums, pairs = meet(
        "row", ACROSS,
        [((PAIR,), HERE, True, None), ((PAIR,), ACROSS, True, None), ((NEXT,), ACROSS, True, None),
         ((ROW,), HERE, False, "row0"), ((DIAG,), HERE, False, "row1")],
    )
    blocks[PAIR_ROW], _ = lax.optimization_barrier((blocks[PAIR_ROW], sums[0]))
    blocks[PAIR_DIAG] = move(blocks[PAIR_ROW], STAY, core=1)
    sums, pairs = meet("far", (), [((FAR,), p, True, None) for p in (HERE, THERE, ACROSS)])
    sums, pairs = meet(
        "last", (),
        [((NEXT, FAR), right, False, None) for right in (PAIR_ROW, PAIR_DIAG)]
        + [((PAIR_ROW,), THERE, False, "row1"), ((PAIR_DIAG,), THERE, False, "row0")],
        doubted=(PAIR_ROW, PAIR_DIAG),
    )
    kept, by_core, to_next, to_far = sums
    from_core, from_far = move(by_core, STAY, core=1), move(to_far, TWO)
    from_core, to_next = lax.optimization_barrier((from_core, to_next))
    from_next = move(to_next, MIDDLE)
    own, pair, row, pair_row = (kept[k:k + 1] + from_core[k:k + 1] for k in (0, 1, 2, 3))
    home = [
        own, from_next, from_far,
        move(pair, OUTER), move(row, STAY, row=1), move(pair_row, OUTER, row=1),
    ]
    return lax.cond(
        decide(flag, to_far, from_far)[0] > 0,
        lambda states, proj_weight, cluster_of, *_: owner_plan(states, proj_weight, cluster_of),
        lambda states, proj_weight, cluster_of, slot, *home: finish(slot, home).reshape(docs),
        states, proj_weight, cluster_of, slot, *home,
    )


def on_device(states, proj_weight, cluster_of):
    if (lax.axis_size("owner"), lax.axis_size("split")) == (8, 2) and states.shape[0] == 512:
        return meeting_plan(states, proj_weight, cluster_of)
    return owner_plan(states, proj_weight, cluster_of)


def solution(mesh):
    placed = (P(("parts", "owner", "split"), None), P(), P(("parts", "owner", "split")))
    return jax.shard_map(
        on_device,
        mesh=mesh,
        in_specs=placed,
        out_specs=P(("parts", "owner", "split")),
        check_vma=False,
    )
```

```python
import math

import jax
import jax.numpy as jnp
from jax import lax
from jax.experimental import pallas as pl
from jax.experimental.pallas import tpu as pltpu
from jax.sharding import PartitionSpec as P

CLUS_OWN = 2
TAU = 0.05
THRESH = 0.2
EPS = 1e-06
LOG2E = math.log2(math.e)
SCALE = LOG2E / TAU
SHIFT = THRESH * LOG2E / TAU

ROWS = 2
F32 = jnp.float32
BF16 = jnp.bfloat16


def prepare(states, proj_weight):
    projected = jnp.dot(states, proj_weight, preferred_element_type=jnp.float32)
    unit = projected * lax.rsqrt(jnp.sum(projected * projected, axis=1, keepdims=True) + EPS)
    peak = jnp.max(jnp.abs(unit), axis=1).astype(jnp.bfloat16)
    quant = (unit / peak.astype(jnp.float32)[:, None]).astype(jnp.bfloat16)
    return (quant, peak)


def similarity_scores(
    own_quant, own_peak, own_cluster, own_index, col_quant, col_peak, col_cluster, col_index
):
    row_count = own_quant.shape[0]
    block = math.gcd(row_count, 768)
    col_scale = col_peak.astype(jnp.float32)

    def one_block(start):
        quant_rows = lax.dynamic_slice_in_dim(own_quant, start, block, 0)
        scale_rows = lax.dynamic_slice_in_dim(own_peak, start, block, 0).astype(jnp.float32)
        cluster_rows = lax.dynamic_slice_in_dim(own_cluster, start, block, 0)
        index_rows = lax.dynamic_slice_in_dim(own_index, start, block, 0)
        inner = lax.dot_general(
            quant_rows, col_quant, (((1,), (1,)), ((), ())), preferred_element_type=jnp.float32
        )
        cosine = inner * scale_rows[:, None] * col_scale[None, :]
        same = (cluster_rows[:, None] == col_cluster[None, :]) & (
            index_rows[:, None] != col_index[None, :]
        )
        weights = jnp.where(same, jnp.exp((cosine - THRESH) / TAU), jnp.zeros_like(cosine))
        return jnp.log(1.0 + jnp.sum(weights, axis=1))

    starts = jnp.arange(row_count // block, dtype=jnp.int32) * block
    return lax.map(one_block, starts).reshape(row_count)


def owner_plan(states, proj_weight, cluster_of):
    owners = lax.axis_size("owner")
    splits = lax.axis_size("split")
    half_index = lax.axis_index("split")
    doc_count = states.shape[0]
    capacity = 3 * doc_count // owners
    width = proj_weight.shape[1]
    slot_total = owners * capacity
    quant, peak = prepare(states, proj_weight)
    group_of = cluster_of // CLUS_OWN
    onehot = (group_of[:, None] == jnp.arange(owners, dtype=jnp.int32)[None, :]).astype(jnp.int32)
    before = jnp.cumsum(onehot, axis=0) - onehot
    target = group_of * capacity + jnp.sum(before * onehot, axis=1)
    quant_slots = (
        jnp.zeros((slot_total, width), jnp.bfloat16)
        .at[target]
        .set(quant)
        .reshape(owners, capacity, width)
    )
    peak_slots = (
        jnp.zeros((slot_total,), jnp.bfloat16).at[target].set(peak).reshape(owners, capacity)
    )
    cluster_slots = (
        jnp.full((slot_total,), -1, jnp.int32).at[target].set(cluster_of).reshape(owners, capacity)
    )
    positions = (
        jnp.arange(owners, dtype=jnp.int32)[:, None] * (splits * capacity)
        + jnp.arange(capacity, dtype=jnp.int32)[None, :]
    )
    own_index = (positions + half_index * capacity).reshape(slot_total)
    col_index = jnp.arange(splits * slot_total, dtype=jnp.int32)
    own_quant, own_peak, own_cluster = (
        lax.all_to_all(a, "owner", split_axis=0, concat_axis=0, tiled=True)
        for a in (quant_slots, peak_slots, cluster_slots)
    )
    all_quant, all_peak, all_cluster = (
        lax.all_gather(a, "split", axis=1, tiled=True) for a in (own_quant, own_peak, own_cluster)
    )
    scores = similarity_scores(
        own_quant.reshape(slot_total, width),
        own_peak.reshape(slot_total),
        own_cluster.reshape(slot_total),
        own_index,
        all_quant.reshape(splits * slot_total, width),
        all_peak.reshape(splits * slot_total),
        all_cluster.reshape(splits * slot_total),
        col_index,
    )
    returned = lax.all_to_all(
        scores.reshape(owners, capacity), "owner", split_axis=0, concat_axis=0, tiled=True
    )
    return returned.reshape(slot_total)[target]


def up(n, m):
    return -(-n // m) * m


META = 8


def layout(docs, hot):
    rest = docs - hot
    first = up(rest, 128)
    flag = first + hot
    return rest, first, flag, up(flag + 1, 128)


def prep_kernel(hot, place_ref, cl_ref, st_ref, w_ref, same_ref, other_ref, slot_ref, vectors):
    docs = st_ref.shape[0]
    rest, first, flag, lanes = layout(docs, hot)
    tile = 128

    cluster = cl_ref[...]
    group = cluster // CLUS_OWN
    member = lax.broadcasted_iota(jnp.int32, (8, docs), 0) == group
    full = jnp.sum(member.astype(F32), axis=1, keepdims=True) == float(hot)
    chosen = jnp.min(
        jnp.where(full, lax.broadcasted_iota(jnp.int32, (8, 1), 0), 8), axis=0, keepdims=True
    )
    doubt = jnp.where(jnp.sum(full.astype(F32), axis=0, keepdims=True) == 1.0, 0.0, 1.0)
    in_hot = group == chosen

    for t in range(docs // tile):
        rows = slice(t * tile, (t + 1) * tile)
        projected = jnp.dot(st_ref[rows, :], w_ref[...], preferred_element_type=F32)
        norm = lax.rsqrt(jnp.sum(projected * projected, axis=1, keepdims=True) + EPS)
        vectors[rows, :] = (projected * (norm * math.sqrt(SCALE))).astype(BF16)

    ahead = (
        lax.broadcasted_iota(jnp.int32, (docs, docs), 0) < lax.broadcasted_iota(jnp.int32, (docs, docs), 1)
    ).astype(F32).astype(BF16)
    hot_rows = jnp.broadcast_to(in_hot.astype(F32), (8, docs)).astype(BF16)
    rank = jnp.dot(hot_rows, ahead, preferred_element_type=F32)[0:1, :].astype(jnp.int32)
    place = lax.broadcasted_iota(jnp.int32, (1, docs), 1)
    slot = jnp.where(in_hot, first + rank, place - rank)
    slot_ref[...] = slot

    sort = (lax.broadcasted_iota(jnp.int32, (lanes, docs), 0) == slot).astype(F32).astype(BF16)
    cluster_rows = jnp.broadcast_to(cluster.astype(F32), (META, docs)).astype(BF16)
    sorted_n = jnp.dot(sort[:rest, :], vectors[...], preferred_element_type=F32).astype(BF16)
    sorted_h = jnp.dot(sort[first:flag, :], vectors[...], preferred_element_type=F32).astype(BF16)
    ids = lax.dot_general(
        cluster_rows, sort, (((1,), (1,)), ((), ())), preferred_element_type=F32
    )
    ids = ids.astype(BF16)


    def fill_n(ref):
        ref[:rest, :] = sorted_n
        ref[rest:, :] = jnp.zeros((META, ref.shape[1]), BF16)
        ref[rest:, :first] = ids[:, :first]
        ref[rest:, first:first + 128] = jnp.broadcast_to(doubt.astype(BF16), (META, 128))

    def fill_h(ref):
        ref[:hot, :] = sorted_h
        ref[hot:, :] = jnp.zeros((rest + META - hot, ref.shape[1]), BF16)
        ref[rest:, :lanes - first] = ids[:, first:]
        ref[rest:, first:first + 128] = jnp.broadcast_to(doubt.astype(BF16), (META, 128))

    even = lax.rem(place_ref[0], 2) == 0

    @pl.when(even)
    def _():
        fill_h(same_ref)
        fill_n(other_ref)

    @pl.when(jnp.logical_not(even))
    def _():
        fill_n(same_ref)
        fill_h(other_ref)


def prep(hot, place, cluster_of, states, proj_weight):
    docs, width = states.shape[0], proj_weight.shape[1]
    rest = docs - hot
    shape = jax.ShapeDtypeStruct
    vmem = pl.BlockSpec(memory_space=pltpu.VMEM)
    return pl.pallas_call(
        lambda *refs: prep_kernel(hot, *refs),
        out_shape=(
            shape((rest + META, width), BF16),
            shape((rest + META, width), BF16),
            shape((1, docs), jnp.int32),
        ),
        in_specs=[pl.BlockSpec(memory_space=pltpu.SMEM), vmem, vmem, vmem],
        scratch_shapes=[pltpu.VMEM((docs, width), BF16)],
        compiler_params=pltpu.CompilerParams(vmem_limit_bytes=24 * 2**20),
        name="prep",
    )(place, cluster_of.reshape(1, docs), states, proj_weight)


OWN, PAIR = "own", "pair"
CORE, PAIR_CORE = "core", "pair_core"
ROW, PAIR_ROW = "row", "pair_row"
DIAG, PAIR_DIAG = "diag", "pair_diag"
NEXT, FAR = "next", "far"
GROUPS = ((OWN, PAIR, ROW, PAIR_ROW), (CORE, PAIR_CORE, DIAG, PAIR_DIAG), (NEXT,), (FAR,))
TILE = 256
HERE, THERE, ACROSS = (OWN, CORE), (PAIR, PAIR_CORE), (ROW, DIAG)


def score_kernel(docs, hot, names, given, made, tasks, doubted, carries, *refs):
    rest, first, flag, lanes = layout(docs, hot)
    place_ref, refs = refs[0], refs[1:]
    blocks, refs = dict(zip(names, refs[:len(names)])), refs[len(names):]
    pairs, refs = {p: refs[2 * k:2 * k + 2] for k, p in enumerate(given)}, refs[2 * len(given):]
    before, refs = refs[:len(GROUPS) * carries], refs[len(GROUPS) * carries:]
    outs, refs = refs[:len(GROUPS)], refs[len(GROUPS):]
    if made:
        pairs[made], refs = refs[:2], refs[2:]
    parts = refs[-1]
    for k, out in enumerate(outs):
        out[...] = before[k][...] if carries else jnp.zeros(out.shape, F32)
    spots = {name: (out, k) for out, group in zip(outs, GROUPS) for k, name in enumerate(group)}
    z, y, c = place_ref[0], place_ref[1], place_ref[2]
    when = {"core0": c == 0, "core1": c == 1, "row0": y == 0, "row1": y == 1}
    middle = (z == 1) | (z == 2)

    def meet(count, start):
        lane = slice(start, start + count)
        wide, two = up(count, 128), 2 * count
        columns = {name: ref[rest:, 0:wide].astype(F32)[0:8, :].T[0:count, :] for name, ref in blocks.items()}
        if made:
            turned, notes = pairs[made]
            turned[:, 0:two] = jnp.concatenate([blocks[name][:count, :] for name in made], axis=0).T
            notes[:, 0:two] = jnp.concatenate([columns[name] for name in made], axis=0).T

        for left in dict.fromkeys(task[0] for task in tasks):

            def work(left=left):
                own_tasks = [task for task in tasks if task[0] == left]
                rows = count * len(left)
                block = blocks[left[0]][:count, :]
                column = columns[left[0]][:, 0:1]
                for name in left[1:]:
                    block = jnp.concatenate([block, blocks[name][:count, :]], axis=0)
                    column = jnp.concatenate([column, columns[name][:, 0:1]], axis=0)
                fresh = True
                for _, right, both, _ in own_tasks:
                    if right in blocks:
                        span, rights, diagonal = count, (right,), False
                        ids = blocks[right][rest:, 0:wide].astype(F32)[0:1, 0:count]
                    else:
                        turned, notes = pairs[right]
                        span, rights, diagonal = two if both else wide, right[:1 + both], left == right[:1]
                        ids = notes[0:1, 0:span]
                        if not both:
                            ids = jnp.where(lax.broadcasted_iota(jnp.int32, ids.shape, 1) < count, ids, -1.0)
                    totals = []
                    for low in range(0, span, TILE):
                        high = min(low + TILE, span)
                        if right in blocks:
                            inner = lax.dot_general(
                                block, blocks[right][low:high, :], (((1,), (1,)), ((), ())),
                                preferred_element_type=F32,
                            )
                        else:
                            inner = jnp.dot(block, turned[:, low:high], preferred_element_type=F32)
                        same = column == ids[:, low:high]
                        if diagonal:
                            same &= lax.broadcasted_iota(jnp.int32, inner.shape, 0) != (
                                lax.broadcasted_iota(jnp.int32, inner.shape, 1) + low
                            )
                        weights = jnp.where(same, jnp.exp2(inner), 0.0)
                        totals.append(jnp.sum(weights, axis=0, keepdims=True))
                        if not diagonal:
                            part = None
                            for t in range(0, high - low, 128):
                                piece = weights[:, t:t + 128]
                                if piece.shape[1] < 128:
                                    blank = jnp.zeros((rows, 128 - piece.shape[1]), F32)
                                    piece = jnp.concatenate([piece, blank], axis=1)
                                part = piece if part is None else part + piece
                            if fresh:
                                parts[0:rows, :] = part
                            else:
                                parts[0:rows, :] += part
                            fresh = False
                    total = jnp.concatenate(totals, axis=1) if len(totals) > 1 else totals[0]
                    for k, name in enumerate(rights):
                        out, spot = spots[name]
                        out[spot, :, lane] += total[:, k * count:(k + 1) * count]
                if not fresh:
                    part = parts[0:rows, :]
                    high = part.astype(BF16)
                    low = (part - high.astype(F32)).astype(BF16)
                    total = lax.dot_general(
                        jnp.ones((16, 256), BF16), jnp.concatenate([high, low], axis=1),
                        (((1,), (1,)), ((), ())), preferred_element_type=F32,
                    )
                    for k, name in enumerate(left):
                        out, spot = spots[name]
                        out[spot, :, lane] += total[0:1, k * count:(k + 1) * count]

            condition = [task[3] for task in tasks if task[0] == left][0]
            if left[0] in (NEXT, FAR):
                pl.when(middle)(work)
            elif condition:
                pl.when(when[condition])(work)
            else:
                work()

    pl.when(lax.rem(z, 2) == 0)(lambda: meet(hot, first))
    pl.when(lax.rem(z, 2) == 1)(lambda: meet(rest, 0))

    if doubted:
        doubt = sum(blocks[name][rest:, first:first + 128].astype(F32)[0:1, 0:1] for name in doubted)
        out, k = spots[FAR]
        out[k] += jnp.where(lax.broadcasted_iota(jnp.int32, (1, lanes), 1) == flag, doubt, 0.0)


def score(name, docs, hot, place, blocks, pairs, made, tasks, sums, doubted=(), weight=1):
    rest, _, _, lanes = layout(docs, hot)
    names = list(dict.fromkeys([*made, *(name for task in tasks for name in task[0])]))
    given = [p for p in pairs if any(p == task[1] for task in tasks)]
    width = blocks[OWN].shape[1]
    vmem = pl.BlockSpec(memory_space=pltpu.VMEM)
    arrays = [blocks[b] for b in names] + [a for p in given for a in pairs[p]] + list(sums)
    shapes = [jax.ShapeDtypeStruct((len(group), 1, lanes), F32) for group in GROUPS]
    if made:
        shapes += [jax.ShapeDtypeStruct((width, 2 * rest), BF16), jax.ShapeDtypeStruct((8, 2 * rest), F32)]
    out = pl.pallas_call(
        lambda *refs: score_kernel(docs, hot, names, given, made, tasks, doubted or made, bool(sums), *refs),
        out_shape=tuple(shapes),
        in_specs=[pl.BlockSpec(memory_space=pltpu.SMEM)] + [vmem] * len(arrays),
        out_specs=tuple(vmem for _ in shapes),
        scratch_shapes=[pltpu.VMEM((2 * rest, 128), F32)],
        compiler_params=pltpu.CompilerParams(vmem_limit_bytes=20 * 2**20),
        cost_estimate=pl.CostEstimate(flops=weight, bytes_accessed=2**10, transcendentals=0),
        name=name,
    )(place, *arrays)
    count = len(GROUPS)
    return out[:count], {**pairs, made: out[count:]} if made else pairs


def finish_kernel(slot_ref, *refs):
    sums, out_ref = refs[:-1], refs[-1]
    total = sums[0][0]
    for ref in sums[1:]:
        total += ref[0]
    lanes, docs = total.shape[1], slot_ref.shape[1]
    values = jnp.broadcast_to(jnp.log(1.0 + total * 2.0**-SHIFT), (8, lanes)).T[:, 0:1]
    here = lax.broadcasted_iota(jnp.int32, (lanes, docs), 0) == slot_ref[...]
    out_ref[...] = jnp.sum(jnp.where(here, values, 0.0), axis=0, keepdims=True)


def finish(slot, sums):
    return pl.pallas_call(
        finish_kernel,
        out_shape=jax.ShapeDtypeStruct(slot.shape, F32),
        compiler_params=pltpu.CompilerParams(vmem_limit_bytes=6 * 2**20),
        name="finish",
    )(slot, *sums)


def decide_kernel(flag, mine_ref, theirs_ref, out_ref):
    out_ref[0] = (jnp.sum(mine_ref[0][:, flag:flag + 1] + theirs_ref[0][:, flag:flag + 1]) > 0.0).astype(jnp.int32)


def decide(flag, mine, theirs):
    return pl.pallas_call(
        lambda *refs: decide_kernel(flag, *refs),
        out_shape=jax.ShapeDtypeStruct((1,), jnp.int32),
        out_specs=pl.BlockSpec(memory_space=pltpu.SMEM),
        compiler_params=pltpu.CompilerParams(vmem_limit_bytes=2 * 2**20),
        name="decide",
    )(mine, theirs)


def meeting_plan(states, proj_weight, cluster_of):
    owners = lax.axis_size("owner")
    columns = owners // ROWS
    docs = states.shape[0]
    hot = 3 * docs // owners
    flag = layout(docs, hot)[2]

    owner, core = lax.axis_index("owner"), lax.axis_index("split")
    place = jnp.stack([owner // ROWS, owner % ROWS, core]).astype(jnp.int32)
    same, other, slot = prep(hot, place, cluster_of, states, proj_weight)

    def move(a, to, row=0, core=0):
        pairs = [
            (
                (z * ROWS + y) * 2 + c,
                (to[z] * ROWS + (y ^ row)) * 2 + (c ^ (core if row or to[z] != z else 1)),
            )
            for z in range(columns) for y in range(ROWS) for c in range(2)
        ]
        return lax.ppermute(a, ("owner", "split"), pairs)

    STAY, OUTER, MIDDLE, TWO = (0, 1, 2, 3), (1, 0, 3, 2), (0, 2, 1, 3), (2, 3, 0, 1)
    TO_MIDDLE = (2, 0, 3, 1)

    def meet(name, made, tasks, **options):
        return score(name, docs, hot, place, blocks, pairs, made, tasks, sums, **options)

    blocks, pairs, sums = {OWN: same}, {}, ()
    blocks[CORE] = move(same, STAY, core=1)
    blocks[PAIR] = move(other, OUTER)
    blocks[CORE], still_same, other = lax.optimization_barrier((blocks[CORE], same, other))
    blocks[ROW] = move(still_same, STAY, row=1)
    blocks[NEXT] = move(other, MIDDLE)
    sums, pairs = meet("own", HERE, [((OWN,), HERE, False, None), ((CORE,), HERE, False, "core0")], weight=2**33)

    blocks[PAIR], _ = lax.optimization_barrier((blocks[PAIR], sums[0]))
    blocks[ROW], blocks[NEXT] = lax.optimization_barrier((blocks[ROW], blocks[NEXT]))
    blocks[FAR] = move(same, TO_MIDDLE)
    blocks[PAIR_ROW] = move(blocks[PAIR], STAY, row=1)
    blocks[PAIR_CORE] = move(blocks[PAIR], STAY, core=1)
    blocks[DIAG] = move(blocks[ROW], STAY, core=1)
    sums, pairs = meet(
        "pair", THERE,
        [((PAIR,), THERE, False, None), ((PAIR_CORE,), THERE, False, "core1"), ((NEXT,), HERE, True, None),
         ((NEXT,), THERE, True, None)],
        weight=2**33,
    )
    sums, pairs = meet(
        "row", ACROSS,
        [((PAIR,), HERE, True, None), ((PAIR,), ACROSS, True, None), ((NEXT,), ACROSS, True, None),
         ((ROW,), HERE, False, "row0"), ((DIAG,), HERE, False, "row1")],
    )
    blocks[PAIR_ROW], _ = lax.optimization_barrier((blocks[PAIR_ROW], sums[0]))
    blocks[PAIR_DIAG] = move(blocks[PAIR_ROW], STAY, core=1)
    sums, pairs = meet("far", (), [((FAR,), p, True, None) for p in (HERE, THERE, ACROSS)])
    sums, pairs = meet(
        "last", (),
        [((NEXT, FAR), right, False, None) for right in (PAIR_ROW, PAIR_DIAG)]
        + [((PAIR_ROW,), THERE, False, "row1"), ((PAIR_DIAG,), THERE, False, "row0")],
        doubted=(PAIR_ROW, PAIR_DIAG),
    )
    kept, by_core, to_next, to_far = sums
    from_core, from_far = move(by_core, STAY, core=1), move(to_far, TWO)
    from_core, to_next = lax.optimization_barrier((from_core, to_next))
    from_next = move(to_next, MIDDLE)
    own, pair, row, pair_row = (kept[k:k + 1] + from_core[k:k + 1] for k in (0, 1, 2, 3))
    home = [
        own, from_next, from_far,
        move(pair_row, OUTER, row=1), move(pair, OUTER), move(row, STAY, row=1),
    ]
    return lax.cond(
        decide(flag, to_far, from_far)[0] > 0,
        lambda states, proj_weight, cluster_of, *_: owner_plan(states, proj_weight, cluster_of),
        lambda states, proj_weight, cluster_of, slot, *home: finish(slot, home).reshape(docs),
        states, proj_weight, cluster_of, slot, *home,
    )


def on_device(states, proj_weight, cluster_of):
    if (lax.axis_size("owner"), lax.axis_size("split")) == (8, 2) and states.shape[0] == 512:
        return meeting_plan(states, proj_weight, cluster_of)
    return owner_plan(states, proj_weight, cluster_of)


def solution(mesh):
    placed = (P(("parts", "owner", "split"), None), P(), P(("parts", "owner", "split")))
    return jax.shard_map(
        on_device,
        mesh=mesh,
        in_specs=placed,
        out_specs=P(("parts", "owner", "split")),
        check_vma=False,
    )
```

```python
import math

import jax
import jax.numpy as jnp
from jax import lax
from jax.experimental import pallas as pl
from jax.experimental.pallas import tpu as pltpu
from jax.sharding import PartitionSpec as P

CLUS_OWN = 2
TAU = 0.05
THRESH = 0.2
EPS = 1e-06
LOG2E = math.log2(math.e)
SCALE = LOG2E / TAU
SHIFT = THRESH * LOG2E / TAU

ROWS = 2
F32 = jnp.float32
BF16 = jnp.bfloat16


def prepare(states, proj_weight):
    projected = jnp.dot(states, proj_weight, preferred_element_type=jnp.float32)
    unit = projected * lax.rsqrt(jnp.sum(projected * projected, axis=1, keepdims=True) + EPS)
    peak = jnp.max(jnp.abs(unit), axis=1).astype(jnp.bfloat16)
    quant = (unit / peak.astype(jnp.float32)[:, None]).astype(jnp.bfloat16)
    return (quant, peak)


def similarity_scores(
    own_quant, own_peak, own_cluster, own_index, col_quant, col_peak, col_cluster, col_index
):
    row_count = own_quant.shape[0]
    block = math.gcd(row_count, 768)
    col_scale = col_peak.astype(jnp.float32)

    def one_block(start):
        quant_rows = lax.dynamic_slice_in_dim(own_quant, start, block, 0)
        scale_rows = lax.dynamic_slice_in_dim(own_peak, start, block, 0).astype(jnp.float32)
        cluster_rows = lax.dynamic_slice_in_dim(own_cluster, start, block, 0)
        index_rows = lax.dynamic_slice_in_dim(own_index, start, block, 0)
        inner = lax.dot_general(
            quant_rows, col_quant, (((1,), (1,)), ((), ())), preferred_element_type=jnp.float32
        )
        cosine = inner * scale_rows[:, None] * col_scale[None, :]
        same = (cluster_rows[:, None] == col_cluster[None, :]) & (
            index_rows[:, None] != col_index[None, :]
        )
        weights = jnp.where(same, jnp.exp((cosine - THRESH) / TAU), jnp.zeros_like(cosine))
        return jnp.log(1.0 + jnp.sum(weights, axis=1))

    starts = jnp.arange(row_count // block, dtype=jnp.int32) * block
    return lax.map(one_block, starts).reshape(row_count)


def owner_plan(states, proj_weight, cluster_of):
    owners = lax.axis_size("owner")
    splits = lax.axis_size("split")
    half_index = lax.axis_index("split")
    doc_count = states.shape[0]
    capacity = 3 * doc_count // owners
    width = proj_weight.shape[1]
    slot_total = owners * capacity
    quant, peak = prepare(states, proj_weight)
    group_of = cluster_of // CLUS_OWN
    onehot = (group_of[:, None] == jnp.arange(owners, dtype=jnp.int32)[None, :]).astype(jnp.int32)
    before = jnp.cumsum(onehot, axis=0) - onehot
    target = group_of * capacity + jnp.sum(before * onehot, axis=1)
    quant_slots = (
        jnp.zeros((slot_total, width), jnp.bfloat16)
        .at[target]
        .set(quant)
        .reshape(owners, capacity, width)
    )
    peak_slots = (
        jnp.zeros((slot_total,), jnp.bfloat16).at[target].set(peak).reshape(owners, capacity)
    )
    cluster_slots = (
        jnp.full((slot_total,), -1, jnp.int32).at[target].set(cluster_of).reshape(owners, capacity)
    )
    positions = (
        jnp.arange(owners, dtype=jnp.int32)[:, None] * (splits * capacity)
        + jnp.arange(capacity, dtype=jnp.int32)[None, :]
    )
    own_index = (positions + half_index * capacity).reshape(slot_total)
    col_index = jnp.arange(splits * slot_total, dtype=jnp.int32)
    own_quant, own_peak, own_cluster = (
        lax.all_to_all(a, "owner", split_axis=0, concat_axis=0, tiled=True)
        for a in (quant_slots, peak_slots, cluster_slots)
    )
    all_quant, all_peak, all_cluster = (
        lax.all_gather(a, "split", axis=1, tiled=True) for a in (own_quant, own_peak, own_cluster)
    )
    scores = similarity_scores(
        own_quant.reshape(slot_total, width),
        own_peak.reshape(slot_total),
        own_cluster.reshape(slot_total),
        own_index,
        all_quant.reshape(splits * slot_total, width),
        all_peak.reshape(splits * slot_total),
        all_cluster.reshape(splits * slot_total),
        col_index,
    )
    returned = lax.all_to_all(
        scores.reshape(owners, capacity), "owner", split_axis=0, concat_axis=0, tiled=True
    )
    return returned.reshape(slot_total)[target]


def ring_plan(states, proj_weight, cluster_of):
    axes = ("owner", "split")
    devices = lax.axis_size("owner") * lax.axis_size("split")
    ring = [(i, (i + 1) % devices) for i in range(devices)]
    quant, peak = prepare(states, proj_weight)
    scale = peak.astype(F32)
    place = jnp.arange(states.shape[0], dtype=jnp.int32)

    def weights(block, block_peak, block_cluster):
        inner = lax.dot_general(quant, block, (((1,), (1,)), ((), ())), preferred_element_type=F32)
        cosine = inner * scale[:, None] * block_peak.astype(F32)[None, :]
        same = cluster_of[:, None] == block_cluster[None, :]
        return jnp.where(same, jnp.exp((cosine - THRESH) / TAU), jnp.zeros_like(cosine))

    def meet(_, carry):
        passed = [lax.ppermute(a, axes, ring) for a in carry[1:]]
        return (carry[0] + jnp.sum(weights(*passed), axis=1), *passed)

    own = (quant, peak, cluster_of)
    others = place[:, None] != place[None, :]
    total = jnp.sum(jnp.where(others, weights(*own), 0.0), axis=1)
    total = lax.fori_loop(1, devices, meet, (total, *own))[0]
    return jnp.log(1.0 + total)


def up(n, m):
    return -(-n // m) * m


META = 8


def layout(docs, hot):
    rest = docs - hot
    first = up(rest, 128)
    flag = first + hot
    return rest, first, flag, up(flag + 1, 128)


def prep_kernel(hot, place_ref, cl_ref, st_ref, w_ref, same_ref, other_ref, slot_ref, vectors):
    docs = st_ref.shape[0]
    rest, first, flag, lanes = layout(docs, hot)
    tile = 128

    cluster = cl_ref[...]
    group = cluster // CLUS_OWN
    member = lax.broadcasted_iota(jnp.int32, (8, docs), 0) == group
    full = jnp.sum(member.astype(F32), axis=1, keepdims=True) == float(hot)
    chosen = jnp.min(
        jnp.where(full, lax.broadcasted_iota(jnp.int32, (8, 1), 0), 8), axis=0, keepdims=True
    )
    doubt = jnp.where(jnp.sum(full.astype(F32), axis=0, keepdims=True) == 1.0, 0.0, 1.0)
    in_hot = group == chosen

    for t in range(docs // tile):
        rows = slice(t * tile, (t + 1) * tile)
        projected = jnp.dot(st_ref[rows, :], w_ref[...], preferred_element_type=F32)
        norm = lax.rsqrt(jnp.sum(projected * projected, axis=1, keepdims=True) + EPS)
        vectors[rows, :] = (projected * (norm * math.sqrt(SCALE))).astype(BF16)

    ahead = (
        lax.broadcasted_iota(jnp.int32, (docs, docs), 0) < lax.broadcasted_iota(jnp.int32, (docs, docs), 1)
    ).astype(F32).astype(BF16)
    hot_rows = jnp.broadcast_to(in_hot.astype(F32), (8, docs)).astype(BF16)
    rank = jnp.dot(hot_rows, ahead, preferred_element_type=F32)[0:1, :].astype(jnp.int32)
    place = lax.broadcasted_iota(jnp.int32, (1, docs), 1)
    slot = jnp.where(in_hot, first + rank, place - rank)
    slot_ref[...] = slot

    sort = (lax.broadcasted_iota(jnp.int32, (lanes, docs), 0) == slot).astype(F32).astype(BF16)
    cluster_rows = jnp.broadcast_to(cluster.astype(F32), (META, docs)).astype(BF16)
    sorted_n = jnp.dot(sort[:rest, :], vectors[...], preferred_element_type=F32).astype(BF16)
    sorted_h = jnp.dot(sort[first:flag, :], vectors[...], preferred_element_type=F32).astype(BF16)
    ids = lax.dot_general(
        cluster_rows, sort, (((1,), (1,)), ((), ())), preferred_element_type=F32
    )
    ids = ids.astype(BF16)


    def fill_n(ref):
        ref[:rest, :] = sorted_n
        ref[rest:, :] = jnp.zeros((META, ref.shape[1]), BF16)
        ref[rest:, :first] = ids[:, :first]
        ref[rest:, first:first + 128] = jnp.broadcast_to(doubt.astype(BF16), (META, 128))

    def fill_h(ref):
        ref[:hot, :] = sorted_h
        ref[hot:, :] = jnp.zeros((rest + META - hot, ref.shape[1]), BF16)
        ref[rest:, :lanes - first] = ids[:, first:]
        ref[rest:, first:first + 128] = jnp.broadcast_to(doubt.astype(BF16), (META, 128))

    even = lax.rem(place_ref[0], 2) == 0

    @pl.when(even)
    def _():
        fill_h(same_ref)
        fill_n(other_ref)

    @pl.when(jnp.logical_not(even))
    def _():
        fill_n(same_ref)
        fill_h(other_ref)


def prep(hot, place, cluster_of, states, proj_weight):
    docs, width = states.shape[0], proj_weight.shape[1]
    rest = docs - hot
    shape = jax.ShapeDtypeStruct
    vmem = pl.BlockSpec(memory_space=pltpu.VMEM)
    return pl.pallas_call(
        lambda *refs: prep_kernel(hot, *refs),
        out_shape=(
            shape((rest + META, width), BF16),
            shape((rest + META, width), BF16),
            shape((1, docs), jnp.int32),
        ),
        in_specs=[pl.BlockSpec(memory_space=pltpu.SMEM), vmem, vmem, vmem],
        scratch_shapes=[pltpu.VMEM((docs, width), BF16)],
        compiler_params=pltpu.CompilerParams(vmem_limit_bytes=24 * 2**20),
        name="prep",
    )(place, cluster_of.reshape(1, docs), states, proj_weight)


OWN, PAIR = "own", "pair"
CORE, PAIR_CORE = "core", "pair_core"
ROW, PAIR_ROW = "row", "pair_row"
DIAG, PAIR_DIAG = "diag", "pair_diag"
NEXT, FAR = "next", "far"
GROUPS = ((OWN, PAIR, ROW, PAIR_ROW), (CORE, PAIR_CORE, DIAG, PAIR_DIAG), (NEXT,), (FAR,))
TILE = 256
HERE, THERE, ACROSS = (OWN, CORE), (PAIR, PAIR_CORE), (ROW, DIAG)


def score_kernel(docs, hot, names, given, made, tasks, doubted, carries, *refs):
    rest, first, flag, lanes = layout(docs, hot)
    place_ref, refs = refs[0], refs[1:]
    blocks, refs = dict(zip(names, refs[:len(names)])), refs[len(names):]
    pairs, refs = {p: refs[2 * k:2 * k + 2] for k, p in enumerate(given)}, refs[2 * len(given):]
    before, refs = refs[:len(GROUPS) * carries], refs[len(GROUPS) * carries:]
    outs, refs = refs[:len(GROUPS)], refs[len(GROUPS):]
    if made:
        pairs[made], refs = refs[:2], refs[2:]
    parts = refs[-1]
    for k, out in enumerate(outs):
        out[...] = before[k][...] if carries else jnp.zeros(out.shape, F32)
    spots = {name: (out, k) for out, group in zip(outs, GROUPS) for k, name in enumerate(group)}
    z, y, c = place_ref[0], place_ref[1], place_ref[2]
    when = {"core0": c == 0, "core1": c == 1, "row0": y == 0, "row1": y == 1}
    middle = (z == 1) | (z == 2)

    def meet(count, start):
        lane = slice(start, start + count)
        wide, two = up(count, 128), 2 * count
        columns = {name: ref[rest:, 0:wide].astype(F32)[0:8, :].T[0:count, :] for name, ref in blocks.items()}
        if made:
            turned, notes = pairs[made]
            turned[:, 0:two] = jnp.concatenate([blocks[name][:count, :] for name in made], axis=0).T
            notes[:, 0:two] = jnp.concatenate([columns[name] for name in made], axis=0).T

        for left in dict.fromkeys(task[0] for task in tasks):

            def work(left=left):
                own_tasks = [task for task in tasks if task[0] == left]
                rows = count * len(left)
                block = blocks[left[0]][:count, :]
                column = columns[left[0]][:, 0:1]
                for name in left[1:]:
                    block = jnp.concatenate([block, blocks[name][:count, :]], axis=0)
                    column = jnp.concatenate([column, columns[name][:, 0:1]], axis=0)
                fresh = True
                for _, right, both, _ in own_tasks:
                    if right in blocks:
                        span, rights, diagonal = count, (right,), False
                        ids = blocks[right][rest:, 0:wide].astype(F32)[0:1, 0:count]
                    else:
                        turned, notes = pairs[right]
                        span, rights, diagonal = two if both else wide, right[:1 + both], left == right[:1]
                        ids = notes[0:1, 0:span]
                        if not both:
                            ids = jnp.where(lax.broadcasted_iota(jnp.int32, ids.shape, 1) < count, ids, -1.0)
                    totals = []
                    for low in range(0, span, TILE):
                        high = min(low + TILE, span)
                        if right in blocks:
                            inner = lax.dot_general(
                                block, blocks[right][low:high, :], (((1,), (1,)), ((), ())),
                                preferred_element_type=F32,
                            )
                        else:
                            inner = jnp.dot(block, turned[:, low:high], preferred_element_type=F32)
                        same = column == ids[:, low:high]
                        if diagonal:
                            same &= lax.broadcasted_iota(jnp.int32, inner.shape, 0) != (
                                lax.broadcasted_iota(jnp.int32, inner.shape, 1) + low
                            )
                        weights = jnp.where(same, jnp.exp2(inner), 0.0)
                        totals.append(jnp.sum(weights, axis=0, keepdims=True))
                        if not diagonal:
                            part = None
                            for t in range(0, high - low, 128):
                                piece = weights[:, t:t + 128]
                                if piece.shape[1] < 128:
                                    blank = jnp.zeros((rows, 128 - piece.shape[1]), F32)
                                    piece = jnp.concatenate([piece, blank], axis=1)
                                part = piece if part is None else part + piece
                            if fresh:
                                parts[0:rows, :] = part
                            else:
                                parts[0:rows, :] += part
                            fresh = False
                    total = jnp.concatenate(totals, axis=1) if len(totals) > 1 else totals[0]
                    for k, name in enumerate(rights):
                        out, spot = spots[name]
                        out[spot, :, lane] += total[:, k * count:(k + 1) * count]
                if not fresh:
                    part = parts[0:rows, :]
                    high = part.astype(BF16)
                    low = (part - high.astype(F32)).astype(BF16)
                    total = lax.dot_general(
                        jnp.ones((16, 256), BF16), jnp.concatenate([high, low], axis=1),
                        (((1,), (1,)), ((), ())), preferred_element_type=F32,
                    )
                    for k, name in enumerate(left):
                        out, spot = spots[name]
                        out[spot, :, lane] += total[0:1, k * count:(k + 1) * count]

            condition = [task[3] for task in tasks if task[0] == left][0]
            if left[0] in (NEXT, FAR):
                pl.when(middle)(work)
            elif condition:
                pl.when(when[condition])(work)
            else:
                work()

    pl.when(lax.rem(z, 2) == 0)(lambda: meet(hot, first))
    pl.when(lax.rem(z, 2) == 1)(lambda: meet(rest, 0))

    if doubted:
        doubt = sum(blocks[name][rest:, first:first + 128].astype(F32)[0:1, 0:1] for name in doubted)
        out, k = spots[FAR]
        out[k] += jnp.where(lax.broadcasted_iota(jnp.int32, (1, lanes), 1) == flag, doubt, 0.0)


def score(name, docs, hot, place, blocks, pairs, made, tasks, sums, doubted=(), weight=1):
    rest, _, _, lanes = layout(docs, hot)
    names = list(dict.fromkeys([*made, *(name for task in tasks for name in task[0])]))
    given = [p for p in pairs if any(p == task[1] for task in tasks)]
    width = blocks[OWN].shape[1]
    vmem = pl.BlockSpec(memory_space=pltpu.VMEM)
    arrays = [blocks[b] for b in names] + [a for p in given for a in pairs[p]] + list(sums)
    shapes = [jax.ShapeDtypeStruct((len(group), 1, lanes), F32) for group in GROUPS]
    if made:
        shapes += [jax.ShapeDtypeStruct((width, 2 * rest), BF16), jax.ShapeDtypeStruct((8, 2 * rest), F32)]
    out = pl.pallas_call(
        lambda *refs: score_kernel(docs, hot, names, given, made, tasks, doubted or made, bool(sums), *refs),
        out_shape=tuple(shapes),
        in_specs=[pl.BlockSpec(memory_space=pltpu.SMEM)] + [vmem] * len(arrays),
        out_specs=tuple(vmem for _ in shapes),
        scratch_shapes=[pltpu.VMEM((2 * rest, 128), F32)],
        compiler_params=pltpu.CompilerParams(vmem_limit_bytes=20 * 2**20),
        cost_estimate=pl.CostEstimate(flops=weight, bytes_accessed=2**10, transcendentals=0),
        name=name,
    )(place, *arrays)
    count = len(GROUPS)
    return out[:count], {**pairs, made: out[count:]} if made else pairs


def finish_kernel(slot_ref, *refs):
    sums, out_ref = refs[:-1], refs[-1]
    total = sums[0][0]
    for ref in sums[1:]:
        total += ref[0]
    lanes, docs = total.shape[1], slot_ref.shape[1]
    values = jnp.broadcast_to(jnp.log(1.0 + total * 2.0**-SHIFT), (8, lanes)).T[:, 0:1]
    here = lax.broadcasted_iota(jnp.int32, (lanes, docs), 0) == slot_ref[...]
    out_ref[...] = jnp.sum(jnp.where(here, values, 0.0), axis=0, keepdims=True)


def finish(slot, sums):
    return pl.pallas_call(
        finish_kernel,
        out_shape=jax.ShapeDtypeStruct(slot.shape, F32),
        compiler_params=pltpu.CompilerParams(vmem_limit_bytes=6 * 2**20),
        name="finish",
    )(slot, *sums)


def decide_kernel(flag, mine_ref, theirs_ref, out_ref):
    out_ref[0] = (jnp.sum(mine_ref[0][:, flag:flag + 1] + theirs_ref[0][:, flag:flag + 1]) > 0.0).astype(jnp.int32)


def decide(flag, mine, theirs):
    return pl.pallas_call(
        lambda *refs: decide_kernel(flag, *refs),
        out_shape=jax.ShapeDtypeStruct((1,), jnp.int32),
        out_specs=pl.BlockSpec(memory_space=pltpu.SMEM),
        compiler_params=pltpu.CompilerParams(vmem_limit_bytes=2 * 2**20),
        name="decide",
    )(mine, theirs)


def meeting_plan(states, proj_weight, cluster_of):
    owners = lax.axis_size("owner")
    columns = owners // ROWS
    docs = states.shape[0]
    hot = 3 * docs // owners
    flag = layout(docs, hot)[2]

    owner, core = lax.axis_index("owner"), lax.axis_index("split")
    place = jnp.stack([owner // ROWS, owner % ROWS, core]).astype(jnp.int32)
    same, other, slot = prep(hot, place, cluster_of, states, proj_weight)

    def move(a, to, row=0, core=0):
        pairs = [
            (
                (z * ROWS + y) * 2 + c,
                (to[z] * ROWS + (y ^ row)) * 2 + (c ^ (core if row or to[z] != z else 1)),
            )
            for z in range(columns) for y in range(ROWS) for c in range(2)
        ]
        return lax.ppermute(a, ("owner", "split"), pairs)

    STAY, OUTER, MIDDLE, TWO = (0, 1, 2, 3), (1, 0, 3, 2), (0, 2, 1, 3), (2, 3, 0, 1)
    TO_MIDDLE = (2, 0, 3, 1)

    def meet(name, made, tasks, **options):
        return score(name, docs, hot, place, blocks, pairs, made, tasks, sums, **options)

    blocks, pairs, sums = {OWN: same}, {}, ()
    blocks[CORE] = move(same, STAY, core=1)
    blocks[PAIR] = move(other, OUTER)
    blocks[CORE], still_same, other = lax.optimization_barrier((blocks[CORE], same, other))
    blocks[ROW] = move(still_same, STAY, row=1)
    blocks[NEXT] = move(other, MIDDLE)
    sums, pairs = meet("own", HERE, [((OWN,), HERE, False, None), ((CORE,), HERE, False, "core0")], weight=2**33)

    blocks[PAIR], _ = lax.optimization_barrier((blocks[PAIR], sums[0]))
    blocks[ROW], blocks[NEXT] = lax.optimization_barrier((blocks[ROW], blocks[NEXT]))
    blocks[FAR] = move(same, TO_MIDDLE)
    blocks[PAIR_ROW] = move(blocks[PAIR], STAY, row=1)
    blocks[PAIR_CORE] = move(blocks[PAIR], STAY, core=1)
    blocks[DIAG] = move(blocks[ROW], STAY, core=1)
    sums, pairs = meet(
        "pair", THERE,
        [((PAIR,), THERE, False, None), ((PAIR_CORE,), THERE, False, "core1"), ((NEXT,), HERE, True, None),
         ((NEXT,), THERE, True, None)],
        weight=2**33,
    )
    sums, pairs = meet(
        "row", ACROSS,
        [((PAIR,), HERE, True, None), ((PAIR,), ACROSS, True, None), ((NEXT,), ACROSS, True, None),
         ((ROW,), HERE, False, "row0"), ((DIAG,), HERE, False, "row1")],
    )
    blocks[PAIR_ROW], _ = lax.optimization_barrier((blocks[PAIR_ROW], sums[0]))
    blocks[PAIR_DIAG] = move(blocks[PAIR_ROW], STAY, core=1)
    sums, pairs = meet("far", (), [((FAR,), p, True, None) for p in (HERE, THERE, ACROSS)])
    sums, pairs = meet(
        "last", (),
        [((NEXT, FAR), right, False, None) for right in (PAIR_ROW, PAIR_DIAG)]
        + [((PAIR_ROW,), THERE, False, "row1"), ((PAIR_DIAG,), THERE, False, "row0")],
        doubted=(PAIR_ROW, PAIR_DIAG),
    )
    kept, by_core, to_next, to_far = sums
    from_core, from_far = move(by_core, STAY, core=1), move(to_far, TWO)
    from_core, to_next = lax.optimization_barrier((from_core, to_next))
    from_next = move(to_next, MIDDLE)
    own, pair, row, pair_row = (kept[k:k + 1] + from_core[k:k + 1] for k in (0, 1, 2, 3))
    home = [
        own, from_next, from_far,
        move(pair, OUTER), move(row, STAY, row=1), move(pair_row, OUTER, row=1),
    ]
    return lax.cond(
        decide(flag, to_far, from_far)[0] > 0,
        lambda states, proj_weight, cluster_of, *_: ring_plan(states, proj_weight, cluster_of),
        lambda states, proj_weight, cluster_of, slot, *home: finish(slot, home).reshape(docs),
        states, proj_weight, cluster_of, slot, *home,
    )


def on_device(states, proj_weight, cluster_of):
    if (lax.axis_size("owner"), lax.axis_size("split")) == (8, 2) and states.shape[0] == 512:
        return meeting_plan(states, proj_weight, cluster_of)
    return owner_plan(states, proj_weight, cluster_of)


def solution(mesh):
    placed = (P(("parts", "owner", "split"), None), P(), P(("parts", "owner", "split")))
    return jax.shard_map(
        on_device,
        mesh=mesh,
        in_specs=placed,
        out_specs=P(("parts", "owner", "split")),
        check_vma=False,
    )
```

```python
import math

import jax
import jax.numpy as jnp
from jax import lax
from jax.experimental import pallas as pl
from jax.experimental.pallas import tpu as pltpu
from jax.sharding import PartitionSpec as P

CLUS_OWN = 2
TAU = 0.05
THRESH = 0.2
EPS = 1e-06
LOG2E = math.log2(math.e)
SCALE = LOG2E / TAU
SHIFT = THRESH * LOG2E / TAU

ROWS = 2
F32 = jnp.float32
BF16 = jnp.bfloat16


def prepare(states, proj_weight):
    projected = jnp.dot(states, proj_weight, preferred_element_type=jnp.float32)
    unit = projected * lax.rsqrt(jnp.sum(projected * projected, axis=1, keepdims=True) + EPS)
    peak = jnp.max(jnp.abs(unit), axis=1).astype(jnp.bfloat16)
    quant = (unit / peak.astype(jnp.float32)[:, None]).astype(jnp.bfloat16)
    return (quant, peak)


def similarity_scores(
    own_quant, own_peak, own_cluster, own_index, col_quant, col_peak, col_cluster, col_index
):
    row_count = own_quant.shape[0]
    block = math.gcd(row_count, 768)
    col_scale = col_peak.astype(jnp.float32)

    def one_block(start):
        quant_rows = lax.dynamic_slice_in_dim(own_quant, start, block, 0)
        scale_rows = lax.dynamic_slice_in_dim(own_peak, start, block, 0).astype(jnp.float32)
        cluster_rows = lax.dynamic_slice_in_dim(own_cluster, start, block, 0)
        index_rows = lax.dynamic_slice_in_dim(own_index, start, block, 0)
        inner = lax.dot_general(
            quant_rows, col_quant, (((1,), (1,)), ((), ())), preferred_element_type=jnp.float32
        )
        cosine = inner * scale_rows[:, None] * col_scale[None, :]
        same = (cluster_rows[:, None] == col_cluster[None, :]) & (
            index_rows[:, None] != col_index[None, :]
        )
        weights = jnp.where(same, jnp.exp((cosine - THRESH) / TAU), jnp.zeros_like(cosine))
        return jnp.log(1.0 + jnp.sum(weights, axis=1))

    starts = jnp.arange(row_count // block, dtype=jnp.int32) * block
    return lax.map(one_block, starts).reshape(row_count)


def owner_plan(states, proj_weight, cluster_of):
    owners = lax.axis_size("owner")
    splits = lax.axis_size("split")
    half_index = lax.axis_index("split")
    doc_count = states.shape[0]
    capacity = 3 * doc_count // owners
    width = proj_weight.shape[1]
    slot_total = owners * capacity
    quant, peak = prepare(states, proj_weight)
    group_of = cluster_of // CLUS_OWN
    onehot = (group_of[:, None] == jnp.arange(owners, dtype=jnp.int32)[None, :]).astype(jnp.int32)
    before = jnp.cumsum(onehot, axis=0) - onehot
    target = group_of * capacity + jnp.sum(before * onehot, axis=1)
    quant_slots = (
        jnp.zeros((slot_total, width), jnp.bfloat16)
        .at[target]
        .set(quant)
        .reshape(owners, capacity, width)
    )
    peak_slots = (
        jnp.zeros((slot_total,), jnp.bfloat16).at[target].set(peak).reshape(owners, capacity)
    )
    cluster_slots = (
        jnp.full((slot_total,), -1, jnp.int32).at[target].set(cluster_of).reshape(owners, capacity)
    )
    positions = (
        jnp.arange(owners, dtype=jnp.int32)[:, None] * (splits * capacity)
        + jnp.arange(capacity, dtype=jnp.int32)[None, :]
    )
    own_index = (positions + half_index * capacity).reshape(slot_total)
    col_index = jnp.arange(splits * slot_total, dtype=jnp.int32)
    own_quant, own_peak, own_cluster = (
        lax.all_to_all(a, "owner", split_axis=0, concat_axis=0, tiled=True)
        for a in (quant_slots, peak_slots, cluster_slots)
    )
    all_quant, all_peak, all_cluster = (
        lax.all_gather(a, "split", axis=1, tiled=True) for a in (own_quant, own_peak, own_cluster)
    )
    scores = similarity_scores(
        own_quant.reshape(slot_total, width),
        own_peak.reshape(slot_total),
        own_cluster.reshape(slot_total),
        own_index,
        all_quant.reshape(splits * slot_total, width),
        all_peak.reshape(splits * slot_total),
        all_cluster.reshape(splits * slot_total),
        col_index,
    )
    returned = lax.all_to_all(
        scores.reshape(owners, capacity), "owner", split_axis=0, concat_axis=0, tiled=True
    )
    return returned.reshape(slot_total)[target]


def ring_plan(states, proj_weight, cluster_of):
    axes = ("owner", "split")
    devices = lax.axis_size("owner") * lax.axis_size("split")
    ring = [(i, (i + 1) % devices) for i in range(devices)]
    quant, peak = prepare(states, proj_weight)
    scale = peak.astype(F32)
    place = jnp.arange(states.shape[0], dtype=jnp.int32)

    def weights(block, block_peak, block_cluster):
        inner = lax.dot_general(quant, block, (((1,), (1,)), ((), ())), preferred_element_type=F32)
        cosine = inner * scale[:, None] * block_peak.astype(F32)[None, :]
        same = cluster_of[:, None] == block_cluster[None, :]
        return jnp.where(same, jnp.exp((cosine - THRESH) / TAU), jnp.zeros_like(cosine))

    def meet(_, carry):
        passed = [lax.ppermute(a, axes, ring) for a in carry[1:]]
        return (carry[0] + jnp.sum(weights(*passed), axis=1), *passed)

    own = (quant, peak, cluster_of)
    others = place[:, None] != place[None, :]
    total = jnp.sum(jnp.where(others, weights(*own), 0.0), axis=1)
    total = lax.fori_loop(1, devices, meet, (total, *own))[0]
    return jnp.log(1.0 + total)


def up(n, m):
    return -(-n // m) * m


META = 8


def layout(docs, hot):
    rest = docs - hot
    first = up(rest, 128)
    flag = first + hot
    return rest, first, flag, up(flag + 1, 128)


def prep_kernel(hot, place_ref, cl_ref, st_hbm, w_hbm, same_ref, other_ref, slot_ref, vectors, st_ref, w_ref, half, sems):
    docs = st_ref.shape[0]
    rest, first, flag, lanes = layout(docs, hot)
    tile = 128
    depth = st_ref.shape[1] // 2
    copies = []
    for k in (0, 1):
        span = pl.ds(k * depth, depth)
        copies.append((
            pltpu.make_async_copy(w_hbm.at[span, :], w_ref.at[span, :], sems.at[2 * k]),
            pltpu.make_async_copy(st_hbm.at[:, span], st_ref.at[:, span], sems.at[2 * k + 1]),
        ))
        for copy in copies[k]:
            copy.start()

    cluster = cl_ref[...]
    group = cluster // CLUS_OWN
    member = lax.broadcasted_iota(jnp.int32, (8, docs), 0) == group
    full = jnp.sum(member.astype(F32), axis=1, keepdims=True) == float(hot)
    chosen = jnp.min(
        jnp.where(full, lax.broadcasted_iota(jnp.int32, (8, 1), 0), 8), axis=0, keepdims=True
    )
    doubt = jnp.where(jnp.sum(full.astype(F32), axis=0, keepdims=True) == 1.0, 0.0, 1.0)
    in_hot = group == chosen

    for k in (0, 1):
        for copy in copies[k]:
            copy.wait()
        span = slice(k * depth, (k + 1) * depth)
        for t in range(docs // tile):
            rows = slice(t * tile, (t + 1) * tile)
            projected = jnp.dot(st_ref[rows, span], w_ref[span, :], preferred_element_type=F32)
            if k == 0:
                half[rows, :] = projected
            else:
                projected += half[rows, :]
                norm = lax.rsqrt(jnp.sum(projected * projected, axis=1, keepdims=True) + EPS)
                vectors[rows, :] = (projected * (norm * math.sqrt(SCALE))).astype(BF16)

    ahead = (
        lax.broadcasted_iota(jnp.int32, (docs, docs), 0) < lax.broadcasted_iota(jnp.int32, (docs, docs), 1)
    ).astype(F32).astype(BF16)
    hot_rows = jnp.broadcast_to(in_hot.astype(F32), (8, docs)).astype(BF16)
    rank = jnp.dot(hot_rows, ahead, preferred_element_type=F32)[0:1, :].astype(jnp.int32)
    place = lax.broadcasted_iota(jnp.int32, (1, docs), 1)
    slot = jnp.where(in_hot, first + rank, place - rank)
    slot_ref[...] = slot

    sort = (lax.broadcasted_iota(jnp.int32, (lanes, docs), 0) == slot).astype(F32).astype(BF16)
    cluster_rows = jnp.broadcast_to(cluster.astype(F32), (META, docs)).astype(BF16)
    sorted_n = jnp.dot(sort[:rest, :], vectors[...], preferred_element_type=F32).astype(BF16)
    sorted_h = jnp.dot(sort[first:flag, :], vectors[...], preferred_element_type=F32).astype(BF16)
    ids = lax.dot_general(
        cluster_rows, sort, (((1,), (1,)), ((), ())), preferred_element_type=F32
    )
    ids = ids.astype(BF16)


    def fill_n(ref):
        ref[:rest, :] = sorted_n
        ref[rest:, :] = jnp.zeros((META, ref.shape[1]), BF16)
        ref[rest:, :first] = ids[:, :first]
        ref[rest:, first:first + 128] = jnp.broadcast_to(doubt.astype(BF16), (META, 128))

    def fill_h(ref):
        ref[:hot, :] = sorted_h
        ref[hot:, :] = jnp.zeros((rest + META - hot, ref.shape[1]), BF16)
        ref[rest:, :lanes - first] = ids[:, first:]
        ref[rest:, first:first + 128] = jnp.broadcast_to(doubt.astype(BF16), (META, 128))

    even = lax.rem(place_ref[0], 2) == 0

    @pl.when(even)
    def _():
        fill_h(same_ref)
        fill_n(other_ref)

    @pl.when(jnp.logical_not(even))
    def _():
        fill_n(same_ref)
        fill_h(other_ref)


def prep(hot, place, cluster_of, states, proj_weight):
    docs, width = states.shape[0], proj_weight.shape[1]
    rest = docs - hot
    shape = jax.ShapeDtypeStruct
    vmem = pl.BlockSpec(memory_space=pltpu.VMEM)
    return pl.pallas_call(
        lambda *refs: prep_kernel(hot, *refs),
        out_shape=(
            shape((rest + META, width), BF16),
            shape((rest + META, width), BF16),
            shape((1, docs), jnp.int32),
        ),
        in_specs=[pl.BlockSpec(memory_space=pltpu.SMEM), vmem] + [pl.BlockSpec(memory_space=pl.ANY)] * 2,
        scratch_shapes=[
            pltpu.VMEM((docs, width), BF16), pltpu.VMEM(states.shape, BF16), pltpu.VMEM(proj_weight.shape, BF16),
            pltpu.VMEM((docs, width), F32), pltpu.SemaphoreType.DMA((4,)),
        ],
        compiler_params=pltpu.CompilerParams(vmem_limit_bytes=24 * 2**20),
        name="prep",
    )(place, cluster_of.reshape(1, docs), states, proj_weight)


OWN, PAIR = "own", "pair"
CORE, PAIR_CORE = "core", "pair_core"
ROW, PAIR_ROW = "row", "pair_row"
DIAG, PAIR_DIAG = "diag", "pair_diag"
NEXT, FAR = "next", "far"
GROUPS = ((OWN, PAIR, ROW, PAIR_ROW), (CORE, PAIR_CORE, DIAG, PAIR_DIAG), (NEXT,), (FAR,))
TILE = 256
HERE, THERE, ACROSS = (OWN, CORE), (PAIR, PAIR_CORE), (ROW, DIAG)


def score_kernel(docs, hot, names, given, made, tasks, doubted, carries, *refs):
    rest, first, flag, lanes = layout(docs, hot)
    place_ref, refs = refs[0], refs[1:]
    blocks, refs = dict(zip(names, refs[:len(names)])), refs[len(names):]
    pairs, refs = {p: refs[2 * k:2 * k + 2] for k, p in enumerate(given)}, refs[2 * len(given):]
    before, refs = refs[:len(GROUPS) * carries], refs[len(GROUPS) * carries:]
    outs, refs = refs[:len(GROUPS)], refs[len(GROUPS):]
    if made:
        pairs[made], refs = refs[:2], refs[2:]
    parts = refs[-1]
    for k, out in enumerate(outs):
        out[...] = before[k][...] if carries else jnp.zeros(out.shape, F32)
    spots = {name: (out, k) for out, group in zip(outs, GROUPS) for k, name in enumerate(group)}
    z, y, c = place_ref[0], place_ref[1], place_ref[2]
    when = {"core0": c == 0, "core1": c == 1, "row0": y == 0, "row1": y == 1}
    middle = (z == 1) | (z == 2)

    def meet(count, start):
        lane = slice(start, start + count)
        wide, two = up(count, 128), 2 * count
        columns = {name: ref[rest:, 0:wide].astype(F32)[0:8, :].T[0:count, :] for name, ref in blocks.items()}
        if made:
            turned, notes = pairs[made]
            turned[:, 0:two] = jnp.concatenate([blocks[name][:count, :] for name in made], axis=0).T
            notes[:, 0:two] = jnp.concatenate([columns[name] for name in made], axis=0).T

        for left in dict.fromkeys(task[0] for task in tasks):

            def work(left=left):
                own_tasks = [task for task in tasks if task[0] == left]
                rows = count * len(left)
                block = blocks[left[0]][:count, :]
                column = columns[left[0]][:, 0:1]
                for name in left[1:]:
                    block = jnp.concatenate([block, blocks[name][:count, :]], axis=0)
                    column = jnp.concatenate([column, columns[name][:, 0:1]], axis=0)
                fresh = True
                for _, right, both, _ in own_tasks:
                    if right in blocks:
                        span, rights, diagonal = count, (right,), False
                        ids = blocks[right][rest:, 0:wide].astype(F32)[0:1, 0:count]
                    else:
                        turned, notes = pairs[right]
                        span, rights, diagonal = two if both else wide, right[:1 + both], left == right[:1]
                        ids = notes[0:1, 0:span]
                        if not both:
                            ids = jnp.where(lax.broadcasted_iota(jnp.int32, ids.shape, 1) < count, ids, -1.0)
                    totals = []
                    for low in range(0, span, TILE):
                        high = min(low + TILE, span)
                        if right in blocks:
                            inner = lax.dot_general(
                                block, blocks[right][low:high, :], (((1,), (1,)), ((), ())),
                                preferred_element_type=F32,
                            )
                        else:
                            inner = jnp.dot(block, turned[:, low:high], preferred_element_type=F32)
                        same = column == ids[:, low:high]
                        if diagonal:
                            same &= lax.broadcasted_iota(jnp.int32, inner.shape, 0) != (
                                lax.broadcasted_iota(jnp.int32, inner.shape, 1) + low
                            )
                        weights = jnp.where(same, jnp.exp2(inner), 0.0)
                        totals.append(jnp.sum(weights, axis=0, keepdims=True))
                        if not diagonal:
                            part = None
                            for t in range(0, high - low, 128):
                                piece = weights[:, t:t + 128]
                                if piece.shape[1] < 128:
                                    blank = jnp.zeros((rows, 128 - piece.shape[1]), F32)
                                    piece = jnp.concatenate([piece, blank], axis=1)
                                part = piece if part is None else part + piece
                            if fresh:
                                parts[0:rows, :] = part
                            else:
                                parts[0:rows, :] += part
                            fresh = False
                    total = jnp.concatenate(totals, axis=1) if len(totals) > 1 else totals[0]
                    for k, name in enumerate(rights):
                        out, spot = spots[name]
                        out[spot, :, lane] += total[:, k * count:(k + 1) * count]
                if not fresh:
                    part = parts[0:rows, :]
                    high = part.astype(BF16)
                    low = (part - high.astype(F32)).astype(BF16)
                    total = lax.dot_general(
                        jnp.ones((16, 256), BF16), jnp.concatenate([high, low], axis=1),
                        (((1,), (1,)), ((), ())), preferred_element_type=F32,
                    )
                    for k, name in enumerate(left):
                        out, spot = spots[name]
                        out[spot, :, lane] += total[0:1, k * count:(k + 1) * count]

            condition = [task[3] for task in tasks if task[0] == left][0]
            if left[0] in (NEXT, FAR):
                pl.when(middle)(work)
            elif condition:
                pl.when(when[condition])(work)
            else:
                work()

    pl.when(lax.rem(z, 2) == 0)(lambda: meet(hot, first))
    pl.when(lax.rem(z, 2) == 1)(lambda: meet(rest, 0))

    if doubted:
        doubt = sum(blocks[name][rest:, first:first + 128].astype(F32)[0:1, 0:1] for name in doubted)
        out, k = spots[FAR]
        out[k] += jnp.where(lax.broadcasted_iota(jnp.int32, (1, lanes), 1) == flag, doubt, 0.0)


def score(name, docs, hot, place, blocks, pairs, made, tasks, sums, doubted=(), weight=1):
    rest, _, _, lanes = layout(docs, hot)
    names = list(dict.fromkeys([
        *made, *(name for task in tasks for name in task[0]), *(task[1] for task in tasks if task[1] in blocks),
    ]))
    given = [p for p in pairs if any(p == task[1] for task in tasks)]
    width = blocks[OWN].shape[1]
    vmem = pl.BlockSpec(memory_space=pltpu.VMEM)
    arrays = [blocks[b] for b in names] + [a for p in given for a in pairs[p]] + list(sums)
    shapes = [jax.ShapeDtypeStruct((len(group), 1, lanes), F32) for group in GROUPS]
    if made:
        shapes += [jax.ShapeDtypeStruct((width, 2 * rest), BF16), jax.ShapeDtypeStruct((8, 2 * rest), F32)]
    out = pl.pallas_call(
        lambda *refs: score_kernel(docs, hot, names, given, made, tasks, doubted or made, bool(sums), *refs),
        out_shape=tuple(shapes),
        in_specs=[pl.BlockSpec(memory_space=pltpu.SMEM)] + [vmem] * len(arrays),
        out_specs=tuple(vmem for _ in shapes),
        scratch_shapes=[pltpu.VMEM((2 * rest, 128), F32)],
        compiler_params=pltpu.CompilerParams(vmem_limit_bytes=20 * 2**20),
        cost_estimate=pl.CostEstimate(flops=weight, bytes_accessed=2**10, transcendentals=0),
        name=name,
    )(place, *arrays)
    count = len(GROUPS)
    return out[:count], {**pairs, made: out[count:]} if made else pairs


def finish_kernel(slot_ref, *refs):
    sums, out_ref = refs[:-1], refs[-1]
    total = sums[0][0]
    for ref in sums[1:]:
        total += ref[0]
    lanes, docs = total.shape[1], slot_ref.shape[1]
    values = jnp.broadcast_to(jnp.log(1.0 + total * 2.0**-SHIFT), (8, lanes)).T[:, 0:1]
    here = lax.broadcasted_iota(jnp.int32, (lanes, docs), 0) == slot_ref[...]
    out_ref[...] = jnp.sum(jnp.where(here, values, 0.0), axis=0, keepdims=True)


def finish(slot, sums):
    return pl.pallas_call(
        finish_kernel,
        out_shape=jax.ShapeDtypeStruct(slot.shape, F32),
        compiler_params=pltpu.CompilerParams(vmem_limit_bytes=6 * 2**20),
        name="finish",
    )(slot, *sums)


def decide_kernel(flag, mine_ref, theirs_ref, out_ref):
    out_ref[0] = (jnp.sum(mine_ref[0][:, flag:flag + 1] + theirs_ref[0][:, flag:flag + 1]) > 0.0).astype(jnp.int32)


def decide(flag, mine, theirs):
    return pl.pallas_call(
        lambda *refs: decide_kernel(flag, *refs),
        out_shape=jax.ShapeDtypeStruct((1,), jnp.int32),
        out_specs=pl.BlockSpec(memory_space=pltpu.SMEM),
        compiler_params=pltpu.CompilerParams(vmem_limit_bytes=2 * 2**20),
        name="decide",
    )(mine, theirs)


def meeting_plan(states, proj_weight, cluster_of):
    owners = lax.axis_size("owner")
    columns = owners // ROWS
    docs = states.shape[0]
    hot = 3 * docs // owners
    flag = layout(docs, hot)[2]

    owner, core = lax.axis_index("owner"), lax.axis_index("split")
    place = jnp.stack([owner // ROWS, owner % ROWS, core]).astype(jnp.int32)
    same, other, slot = prep(hot, place, cluster_of, states, proj_weight)

    def move(a, to, row=0, core=0):
        pairs = [
            (
                (z * ROWS + y) * 2 + c,
                (to[z] * ROWS + (y ^ row)) * 2 + (c ^ (core if row or to[z] != z else 1)),
            )
            for z in range(columns) for y in range(ROWS) for c in range(2)
        ]
        return lax.ppermute(a, ("owner", "split"), pairs)

    STAY, OUTER, MIDDLE, TWO = (0, 1, 2, 3), (1, 0, 3, 2), (0, 2, 1, 3), (2, 3, 0, 1)
    TO_MIDDLE = (2, 0, 3, 1)

    def meet(name, made, tasks, **options):
        return score(name, docs, hot, place, blocks, pairs, made, tasks, sums, **options)

    blocks, pairs, sums = {OWN: same}, {}, ()
    blocks[CORE] = move(same, STAY, core=1)
    blocks[PAIR] = move(other, OUTER)
    blocks[CORE], still_same, other = lax.optimization_barrier((blocks[CORE], same, other))
    blocks[ROW] = move(still_same, STAY, row=1)
    blocks[NEXT] = move(other, MIDDLE)
    sums, pairs = meet("own", HERE, [((OWN,), HERE, False, None), ((CORE,), HERE, False, "core0")], weight=2**33)

    blocks[PAIR], _ = lax.optimization_barrier((blocks[PAIR], sums[0]))
    blocks[ROW], blocks[NEXT] = lax.optimization_barrier((blocks[ROW], blocks[NEXT]))
    blocks[FAR] = move(same, TO_MIDDLE)
    blocks[PAIR_ROW] = move(blocks[PAIR], STAY, row=1)
    blocks[PAIR_CORE] = move(blocks[PAIR], STAY, core=1)
    blocks[DIAG] = move(blocks[ROW], STAY, core=1)
    sums, pairs = meet(
        "pair", THERE,
        [((PAIR,), THERE, False, None), ((PAIR_CORE,), THERE, False, "core1"), ((NEXT,), HERE, True, None),
         ((NEXT,), THERE, True, None)],
        weight=2**33,
    )
    sums, pairs = meet(
        "row", ACROSS,
        [((PAIR,), HERE, True, None), ((PAIR,), ACROSS, True, None), ((NEXT,), ACROSS, True, None),
         ((ROW,), HERE, False, "row0"), ((DIAG,), HERE, False, "row1")],
    )
    blocks[PAIR_ROW], _ = lax.optimization_barrier((blocks[PAIR_ROW], sums[0]))
    blocks[PAIR_DIAG] = move(blocks[PAIR_ROW], STAY, core=1)
    sums, pairs = meet(
        "far", (),
        [((FAR,), p, True, None) for p in (HERE, THERE, ACROSS)]
        + [((NEXT, FAR), PAIR_ROW, False, None), ((PAIR_ROW,), THERE, False, "row1")],
        doubted=(PAIR_ROW,),
    )
    sums, pairs = meet(
        "last", (),
        [((NEXT, FAR), PAIR_DIAG, False, None), ((PAIR_DIAG,), THERE, False, "row0")],
        doubted=(PAIR_DIAG,),
    )
    kept, by_core, to_next, to_far = sums
    from_core, from_far = move(by_core, STAY, core=1), move(to_far, TWO)
    from_core, to_next = lax.optimization_barrier((from_core, to_next))
    from_next = move(to_next, MIDDLE)
    from_next, from_far = lax.optimization_barrier((from_next, from_far))
    own, pair, row, pair_row = (kept[k:k + 1] + from_core[k:k + 1] for k in (0, 1, 2, 3))
    home = [
        own, from_next, from_far,
        move(pair, OUTER), move(row, STAY, row=1), move(pair_row, OUTER, row=1),
    ]
    return lax.cond(
        decide(flag, to_far, from_far)[0] > 0,
        lambda states, proj_weight, cluster_of, *_: ring_plan(states, proj_weight, cluster_of),
        lambda states, proj_weight, cluster_of, slot, *home: finish(slot, home).reshape(docs),
        states, proj_weight, cluster_of, slot, *home,
    )


def on_device(states, proj_weight, cluster_of):
    if (lax.axis_size("owner"), lax.axis_size("split")) == (8, 2) and states.shape[0] == 512:
        return meeting_plan(states, proj_weight, cluster_of)
    return owner_plan(states, proj_weight, cluster_of)


def solution(mesh):
    placed = (P(("parts", "owner", "split"), None), P(), P(("parts", "owner", "split")))
    return jax.shard_map(
        on_device,
        mesh=mesh,
        in_specs=placed,
        out_specs=P(("parts", "owner", "split")),
        check_vma=False,
    )
```

```python
import math

import jax
import jax.numpy as jnp
from jax import lax
from jax.experimental import pallas as pl
from jax.experimental.pallas import tpu as pltpu
from jax.sharding import PartitionSpec as P

CLUS_OWN = 2
TAU = 0.05
THRESH = 0.2
EPS = 1e-06
LOG2E = math.log2(math.e)
SCALE = LOG2E / TAU
SHIFT = THRESH * LOG2E / TAU

ROWS = 2
F32 = jnp.float32
BF16 = jnp.bfloat16


def prepare(states, proj_weight):
    projected = jnp.dot(states, proj_weight, preferred_element_type=jnp.float32)
    unit = projected * lax.rsqrt(jnp.sum(projected * projected, axis=1, keepdims=True) + EPS)
    peak = jnp.max(jnp.abs(unit), axis=1).astype(jnp.bfloat16)
    quant = (unit / peak.astype(jnp.float32)[:, None]).astype(jnp.bfloat16)
    return (quant, peak)


def similarity_scores(
    own_quant, own_peak, own_cluster, own_index, col_quant, col_peak, col_cluster, col_index
):
    row_count = own_quant.shape[0]
    block = math.gcd(row_count, 768)
    col_scale = col_peak.astype(jnp.float32)

    def one_block(start):
        quant_rows = lax.dynamic_slice_in_dim(own_quant, start, block, 0)
        scale_rows = lax.dynamic_slice_in_dim(own_peak, start, block, 0).astype(jnp.float32)
        cluster_rows = lax.dynamic_slice_in_dim(own_cluster, start, block, 0)
        index_rows = lax.dynamic_slice_in_dim(own_index, start, block, 0)
        inner = lax.dot_general(
            quant_rows, col_quant, (((1,), (1,)), ((), ())), preferred_element_type=jnp.float32
        )
        cosine = inner * scale_rows[:, None] * col_scale[None, :]
        same = (cluster_rows[:, None] == col_cluster[None, :]) & (
            index_rows[:, None] != col_index[None, :]
        )
        weights = jnp.where(same, jnp.exp((cosine - THRESH) / TAU), jnp.zeros_like(cosine))
        return jnp.log(1.0 + jnp.sum(weights, axis=1))

    starts = jnp.arange(row_count // block, dtype=jnp.int32) * block
    return lax.map(one_block, starts).reshape(row_count)


def owner_plan(states, proj_weight, cluster_of):
    owners = lax.axis_size("owner")
    splits = lax.axis_size("split")
    half_index = lax.axis_index("split")
    doc_count = states.shape[0]
    capacity = 3 * doc_count // owners
    width = proj_weight.shape[1]
    slot_total = owners * capacity
    quant, peak = prepare(states, proj_weight)
    group_of = cluster_of // CLUS_OWN
    onehot = (group_of[:, None] == jnp.arange(owners, dtype=jnp.int32)[None, :]).astype(jnp.int32)
    before = jnp.cumsum(onehot, axis=0) - onehot
    target = group_of * capacity + jnp.sum(before * onehot, axis=1)
    quant_slots = (
        jnp.zeros((slot_total, width), jnp.bfloat16)
        .at[target]
        .set(quant)
        .reshape(owners, capacity, width)
    )
    peak_slots = (
        jnp.zeros((slot_total,), jnp.bfloat16).at[target].set(peak).reshape(owners, capacity)
    )
    cluster_slots = (
        jnp.full((slot_total,), -1, jnp.int32).at[target].set(cluster_of).reshape(owners, capacity)
    )
    positions = (
        jnp.arange(owners, dtype=jnp.int32)[:, None] * (splits * capacity)
        + jnp.arange(capacity, dtype=jnp.int32)[None, :]
    )
    own_index = (positions + half_index * capacity).reshape(slot_total)
    col_index = jnp.arange(splits * slot_total, dtype=jnp.int32)
    own_quant, own_peak, own_cluster = (
        lax.all_to_all(a, "owner", split_axis=0, concat_axis=0, tiled=True)
        for a in (quant_slots, peak_slots, cluster_slots)
    )
    all_quant, all_peak, all_cluster = (
        lax.all_gather(a, "split", axis=1, tiled=True) for a in (own_quant, own_peak, own_cluster)
    )
    scores = similarity_scores(
        own_quant.reshape(slot_total, width),
        own_peak.reshape(slot_total),
        own_cluster.reshape(slot_total),
        own_index,
        all_quant.reshape(splits * slot_total, width),
        all_peak.reshape(splits * slot_total),
        all_cluster.reshape(splits * slot_total),
        col_index,
    )
    returned = lax.all_to_all(
        scores.reshape(owners, capacity), "owner", split_axis=0, concat_axis=0, tiled=True
    )
    return returned.reshape(slot_total)[target]


def ring_plan(states, proj_weight, cluster_of):
    axes = ("owner", "split")
    devices = lax.axis_size("owner") * lax.axis_size("split")
    ring = [(i, (i + 1) % devices) for i in range(devices)]
    quant, peak = prepare(states, proj_weight)
    scale = peak.astype(F32)
    place = jnp.arange(states.shape[0], dtype=jnp.int32)

    def weights(block, block_peak, block_cluster):
        inner = lax.dot_general(quant, block, (((1,), (1,)), ((), ())), preferred_element_type=F32)
        cosine = inner * scale[:, None] * block_peak.astype(F32)[None, :]
        same = cluster_of[:, None] == block_cluster[None, :]
        return jnp.where(same, jnp.exp((cosine - THRESH) / TAU), jnp.zeros_like(cosine))

    def meet(_, carry):
        passed = [lax.ppermute(a, axes, ring) for a in carry[1:]]
        return (carry[0] + jnp.sum(weights(*passed), axis=1), *passed)

    own = (quant, peak, cluster_of)
    others = place[:, None] != place[None, :]
    total = jnp.sum(jnp.where(others, weights(*own), 0.0), axis=1)
    total = lax.fori_loop(1, devices, meet, (total, *own))[0]
    return jnp.log(1.0 + total)


def up(n, m):
    return -(-n // m) * m


META = 8


def layout(docs, hot):
    rest = docs - hot
    first = up(rest, 128)
    flag = first + hot
    return rest, first, flag, up(flag + 1, 128)


def prep_kernel(hot, place_ref, cl_ref, st_ref, w_ref, same_ref, other_ref, slot_ref, vectors):
    docs = st_ref.shape[0]
    rest, first, flag, lanes = layout(docs, hot)
    tile = 128

    cluster = cl_ref[...]
    group = cluster // CLUS_OWN
    member = lax.broadcasted_iota(jnp.int32, (8, docs), 0) == group
    full = jnp.sum(member.astype(F32), axis=1, keepdims=True) == float(hot)
    chosen = jnp.min(
        jnp.where(full, lax.broadcasted_iota(jnp.int32, (8, 1), 0), 8), axis=0, keepdims=True
    )
    doubt = jnp.where(jnp.sum(full.astype(F32), axis=0, keepdims=True) == 1.0, 0.0, 1.0)
    in_hot = group == chosen

    for t in range(docs // tile):
        rows = slice(t * tile, (t + 1) * tile)
        projected = jnp.dot(st_ref[rows, :], w_ref[...], preferred_element_type=F32)
        norm = lax.rsqrt(jnp.sum(projected * projected, axis=1, keepdims=True) + EPS)
        vectors[rows, :] = (projected * (norm * math.sqrt(SCALE))).astype(BF16)

    ahead = (
        lax.broadcasted_iota(jnp.int32, (docs, docs), 0) < lax.broadcasted_iota(jnp.int32, (docs, docs), 1)
    ).astype(F32).astype(BF16)
    hot_rows = jnp.broadcast_to(in_hot.astype(F32), (8, docs)).astype(BF16)
    rank = jnp.dot(hot_rows, ahead, preferred_element_type=F32)[0:1, :].astype(jnp.int32)
    place = lax.broadcasted_iota(jnp.int32, (1, docs), 1)
    slot = jnp.where(in_hot, first + rank, place - rank)
    slot_ref[...] = slot

    sort = (lax.broadcasted_iota(jnp.int32, (lanes, docs), 0) == slot).astype(F32).astype(BF16)
    cluster_rows = jnp.broadcast_to(cluster.astype(F32), (META, docs)).astype(BF16)
    sorted_n = jnp.dot(sort[:rest, :], vectors[...], preferred_element_type=F32).astype(BF16)
    sorted_h = jnp.dot(sort[first:flag, :], vectors[...], preferred_element_type=F32).astype(BF16)
    ids = lax.dot_general(
        cluster_rows, sort, (((1,), (1,)), ((), ())), preferred_element_type=F32
    )
    ids = ids.astype(BF16)


    def fill_n(ref):
        ref[:rest, :] = sorted_n
        ref[rest:, :] = jnp.zeros((META, ref.shape[1]), BF16)
        ref[rest:, :first] = ids[:, :first]
        ref[rest:, first:first + 128] = jnp.broadcast_to(doubt.astype(BF16), (META, 128))

    def fill_h(ref):
        ref[:hot, :] = sorted_h
        ref[hot:, :] = jnp.zeros((rest + META - hot, ref.shape[1]), BF16)
        ref[rest:, :lanes - first] = ids[:, first:]
        ref[rest:, first:first + 128] = jnp.broadcast_to(doubt.astype(BF16), (META, 128))

    even = lax.rem(place_ref[0], 2) == 0

    @pl.when(even)
    def _():
        fill_h(same_ref)
        fill_n(other_ref)

    @pl.when(jnp.logical_not(even))
    def _():
        fill_n(same_ref)
        fill_h(other_ref)


def prep(hot, place, cluster_of, states, proj_weight):
    docs, width = states.shape[0], proj_weight.shape[1]
    rest = docs - hot
    shape = jax.ShapeDtypeStruct
    vmem = pl.BlockSpec(memory_space=pltpu.VMEM)
    return pl.pallas_call(
        lambda *refs: prep_kernel(hot, *refs),
        out_shape=(
            shape((rest + META, width), BF16),
            shape((rest + META, width), BF16),
            shape((1, docs), jnp.int32),
        ),
        in_specs=[pl.BlockSpec(memory_space=pltpu.SMEM), vmem, vmem, vmem],
        scratch_shapes=[pltpu.VMEM((docs, width), BF16)],
        compiler_params=pltpu.CompilerParams(vmem_limit_bytes=24 * 2**20),
        name="prep",
    )(place, cluster_of.reshape(1, docs), states, proj_weight)


OWN, PAIR = "own", "pair"
CORE, PAIR_CORE = "core", "pair_core"
ROW, PAIR_ROW = "row", "pair_row"
DIAG, PAIR_DIAG = "diag", "pair_diag"
NEXT, FAR = "next", "far"
GROUPS = ((OWN, PAIR, ROW, PAIR_ROW), (CORE, PAIR_CORE, DIAG, PAIR_DIAG), (NEXT,), (FAR,))
TILE = 256
HERE, THERE, ACROSS = (OWN, CORE), (PAIR, PAIR_CORE), (ROW, DIAG)


def score_kernel(docs, hot, names, given, made, tasks, doubted, carries, *refs):
    rest, first, flag, lanes = layout(docs, hot)
    place_ref, refs = refs[0], refs[1:]
    blocks, refs = dict(zip(names, refs[:len(names)])), refs[len(names):]
    pairs, refs = {p: refs[2 * k:2 * k + 2] for k, p in enumerate(given)}, refs[2 * len(given):]
    before, refs = refs[:len(GROUPS) * carries], refs[len(GROUPS) * carries:]
    outs, refs = refs[:len(GROUPS)], refs[len(GROUPS):]
    if made:
        pairs[made], refs = refs[:2], refs[2:]
    parts = refs[-1]
    for k, out in enumerate(outs):
        out[...] = before[k][...] if carries else jnp.zeros(out.shape, F32)
    spots = {name: (out, k) for out, group in zip(outs, GROUPS) for k, name in enumerate(group)}
    z, y, c = place_ref[0], place_ref[1], place_ref[2]
    when = {"core0": c == 0, "core1": c == 1, "row0": y == 0, "row1": y == 1}
    middle = (z == 1) | (z == 2)

    def meet(count, start):
        lane = slice(start, start + count)
        wide, two = up(count, 128), 2 * count
        columns = {name: ref[rest:, 0:wide].astype(F32)[0:8, :].T[0:count, :] for name, ref in blocks.items()}
        if made:
            turned, notes = pairs[made]
            turned[:, 0:two] = jnp.concatenate([blocks[name][:count, :] for name in made], axis=0).T
            notes[:, 0:two] = jnp.concatenate([columns[name] for name in made], axis=0).T

        for left in dict.fromkeys(task[0] for task in tasks):

            def work(left=left):
                own_tasks = [task for task in tasks if task[0] == left]
                rows = count * len(left)
                block = blocks[left[0]][:count, :]
                column = columns[left[0]][:, 0:1]
                for name in left[1:]:
                    block = jnp.concatenate([block, blocks[name][:count, :]], axis=0)
                    column = jnp.concatenate([column, columns[name][:, 0:1]], axis=0)
                fresh = True
                for _, right, both, _ in own_tasks:
                    if right in blocks:
                        span, rights, diagonal = count, (right,), False
                        ids = blocks[right][rest:, 0:wide].astype(F32)[0:1, 0:count]
                    else:
                        turned, notes = pairs[right]
                        span, rights, diagonal = two if both else wide, right[:1 + both], left == right[:1]
                        ids = notes[0:1, 0:span]
                        if not both:
                            ids = jnp.where(lax.broadcasted_iota(jnp.int32, ids.shape, 1) < count, ids, -1.0)
                    totals = []
                    for low in range(0, span, TILE):
                        high = min(low + TILE, span)
                        if right in blocks:
                            inner = lax.dot_general(
                                block, blocks[right][low:high, :], (((1,), (1,)), ((), ())),
                                preferred_element_type=F32,
                            )
                        else:
                            inner = jnp.dot(block, turned[:, low:high], preferred_element_type=F32)
                        same = column == ids[:, low:high]
                        if diagonal:
                            same &= lax.broadcasted_iota(jnp.int32, inner.shape, 0) != (
                                lax.broadcasted_iota(jnp.int32, inner.shape, 1) + low
                            )
                        weights = jnp.where(same, jnp.exp2(inner), 0.0)
                        totals.append(jnp.sum(weights, axis=0, keepdims=True))
                        if not diagonal:
                            part = None
                            for t in range(0, high - low, 128):
                                piece = weights[:, t:t + 128]
                                if piece.shape[1] < 128:
                                    blank = jnp.zeros((rows, 128 - piece.shape[1]), F32)
                                    piece = jnp.concatenate([piece, blank], axis=1)
                                part = piece if part is None else part + piece
                            if fresh:
                                parts[0:rows, :] = part
                            else:
                                parts[0:rows, :] += part
                            fresh = False
                    total = jnp.concatenate(totals, axis=1) if len(totals) > 1 else totals[0]
                    for k, name in enumerate(rights):
                        out, spot = spots[name]
                        out[spot, :, lane] += total[:, k * count:(k + 1) * count]
                if not fresh:
                    part = parts[0:rows, :]
                    high = part.astype(BF16)
                    low = (part - high.astype(F32)).astype(BF16)
                    total = lax.dot_general(
                        jnp.ones((16, 256), BF16), jnp.concatenate([high, low], axis=1),
                        (((1,), (1,)), ((), ())), preferred_element_type=F32,
                    )
                    for k, name in enumerate(left):
                        out, spot = spots[name]
                        out[spot, :, lane] += total[0:1, k * count:(k + 1) * count]

            condition = [task[3] for task in tasks if task[0] == left][0]
            if left[0] in (NEXT, FAR):
                pl.when(middle)(work)
            elif condition:
                pl.when(when[condition])(work)
            else:
                work()

    pl.when(lax.rem(z, 2) == 0)(lambda: meet(hot, first))
    pl.when(lax.rem(z, 2) == 1)(lambda: meet(rest, 0))

    if doubted:
        doubt = sum(blocks[name][rest:, first:first + 128].astype(F32)[0:1, 0:1] for name in doubted)
        out, k = spots[FAR]
        out[k] += jnp.where(lax.broadcasted_iota(jnp.int32, (1, lanes), 1) == flag, doubt, 0.0)


def score(name, docs, hot, place, blocks, pairs, made, tasks, sums, doubted=(), weight=1):
    rest, _, _, lanes = layout(docs, hot)
    names = list(dict.fromkeys([
        *made, *(name for task in tasks for name in task[0]), *(task[1] for task in tasks if task[1] in blocks),
    ]))
    given = [p for p in pairs if any(p == task[1] for task in tasks)]
    width = blocks[OWN].shape[1]
    vmem = pl.BlockSpec(memory_space=pltpu.VMEM)
    arrays = [blocks[b] for b in names] + [a for p in given for a in pairs[p]] + list(sums)
    shapes = [jax.ShapeDtypeStruct((len(group), 1, lanes), F32) for group in GROUPS]
    if made:
        shapes += [jax.ShapeDtypeStruct((width, 2 * rest), BF16), jax.ShapeDtypeStruct((8, 2 * rest), F32)]
    out = pl.pallas_call(
        lambda *refs: score_kernel(docs, hot, names, given, made, tasks, doubted or made, bool(sums), *refs),
        out_shape=tuple(shapes),
        in_specs=[pl.BlockSpec(memory_space=pltpu.SMEM)] + [vmem] * len(arrays),
        out_specs=tuple(vmem for _ in shapes),
        scratch_shapes=[pltpu.VMEM((2 * rest, 128), F32)],
        compiler_params=pltpu.CompilerParams(vmem_limit_bytes=20 * 2**20),
        cost_estimate=pl.CostEstimate(flops=weight, bytes_accessed=2**10, transcendentals=0),
        name=name,
    )(place, *arrays)
    count = len(GROUPS)
    return out[:count], {**pairs, made: out[count:]} if made else pairs


def finish_kernel(slot_ref, *refs):
    sums, out_ref = refs[:-1], refs[-1]
    total = sums[0][0]
    for ref in sums[1:]:
        total += ref[0]
    lanes, docs = total.shape[1], slot_ref.shape[1]
    values = jnp.broadcast_to(jnp.log(1.0 + total * 2.0**-SHIFT), (8, lanes)).T[:, 0:1]
    here = lax.broadcasted_iota(jnp.int32, (lanes, docs), 0) == slot_ref[...]
    out_ref[...] = jnp.sum(jnp.where(here, values, 0.0), axis=0, keepdims=True)


def finish(slot, sums):
    return pl.pallas_call(
        finish_kernel,
        out_shape=jax.ShapeDtypeStruct(slot.shape, F32),
        compiler_params=pltpu.CompilerParams(vmem_limit_bytes=6 * 2**20),
        name="finish",
    )(slot, *sums)


def decide_kernel(flag, mine_ref, theirs_ref, out_ref):
    out_ref[0] = (jnp.sum(mine_ref[0][:, flag:flag + 1] + theirs_ref[0][:, flag:flag + 1]) > 0.0).astype(jnp.int32)


def decide(flag, mine, theirs):
    return pl.pallas_call(
        lambda *refs: decide_kernel(flag, *refs),
        out_shape=jax.ShapeDtypeStruct((1,), jnp.int32),
        out_specs=pl.BlockSpec(memory_space=pltpu.SMEM),
        compiler_params=pltpu.CompilerParams(vmem_limit_bytes=2 * 2**20),
        name="decide",
    )(mine, theirs)


def meeting_plan(states, proj_weight, cluster_of):
    owners = lax.axis_size("owner")
    columns = owners // ROWS
    docs = states.shape[0]
    hot = 3 * docs // owners
    flag = layout(docs, hot)[2]

    owner, core = lax.axis_index("owner"), lax.axis_index("split")
    place = jnp.stack([owner // ROWS, owner % ROWS, core]).astype(jnp.int32)
    same, other, slot = prep(hot, place, cluster_of, states, proj_weight)

    def move(a, to, row=0, core=0):
        pairs = [
            (
                (z * ROWS + y) * 2 + c,
                (to[z] * ROWS + (y ^ row)) * 2 + (c ^ (core if row or to[z] != z else 1)),
            )
            for z in range(columns) for y in range(ROWS) for c in range(2)
        ]
        return lax.ppermute(a, ("owner", "split"), pairs)

    STAY, OUTER, MIDDLE, TWO = (0, 1, 2, 3), (1, 0, 3, 2), (0, 2, 1, 3), (2, 3, 0, 1)
    TO_MIDDLE = (2, 0, 3, 1)

    def meet(name, made, tasks, **options):
        return score(name, docs, hot, place, blocks, pairs, made, tasks, sums, **options)

    blocks, pairs, sums = {OWN: same}, {}, ()
    blocks[CORE] = move(same, STAY, core=1)
    blocks[PAIR] = move(other, OUTER)
    blocks[CORE], still_same, other = lax.optimization_barrier((blocks[CORE], same, other))
    blocks[ROW] = move(still_same, STAY, row=1)
    blocks[NEXT] = move(other, MIDDLE)
    sums, pairs = meet("own", HERE, [((OWN,), HERE, False, None), ((CORE,), HERE, False, "core0")], weight=2**33)

    blocks[PAIR], _ = lax.optimization_barrier((blocks[PAIR], sums[0]))
    blocks[ROW], blocks[NEXT] = lax.optimization_barrier((blocks[ROW], blocks[NEXT]))
    blocks[FAR] = move(same, TO_MIDDLE)
    blocks[PAIR_ROW] = move(blocks[PAIR], STAY, row=1)
    blocks[PAIR_CORE] = move(blocks[PAIR], STAY, core=1)
    blocks[DIAG] = move(blocks[ROW], STAY, core=1)
    sums, pairs = meet(
        "pair", THERE,
        [((PAIR,), THERE, False, None), ((PAIR_CORE,), THERE, False, "core1"), ((NEXT,), HERE, True, None),
         ((NEXT,), THERE, True, None)],
        weight=2**33,
    )
    sums, pairs = meet(
        "row", ACROSS,
        [((PAIR,), HERE, True, None), ((PAIR,), ACROSS, True, None), ((NEXT,), ACROSS, True, None),
         ((ROW,), HERE, False, "row0"), ((DIAG,), HERE, False, "row1")],
    )
    blocks[PAIR_ROW], _ = lax.optimization_barrier((blocks[PAIR_ROW], sums[0]))
    blocks[PAIR_DIAG] = move(blocks[PAIR_ROW], STAY, core=1)
    sums, pairs = meet("far", (), [((FAR,), p, True, None) for p in (HERE, THERE, ACROSS)])
    sums, pairs = meet(
        "diag", (),
        [((NEXT, FAR), PAIR_DIAG, False, None), ((PAIR_DIAG,), THERE, False, "row0")],
        doubted=(PAIR_DIAG,),
    )
    by_core = sums[1]
    sums, pairs = meet(
        "last", (),
        [((NEXT, FAR), PAIR_ROW, False, None), ((PAIR_ROW,), THERE, False, "row1")],
        doubted=(PAIR_ROW,),
    )
    kept, _, to_next, to_far = sums
    from_core, from_far = move(by_core, STAY, core=1), move(to_far, TWO)
    from_core, to_next = lax.optimization_barrier((from_core, to_next))
    from_next = move(to_next, MIDDLE)
    own, pair, row, pair_row = (kept[k:k + 1] + from_core[k:k + 1] for k in (0, 1, 2, 3))
    home = [
        own, from_next, from_far,
        move(pair, OUTER), move(row, STAY, row=1), move(pair_row, OUTER, row=1),
    ]
    return lax.cond(
        decide(flag, to_far, from_far)[0] > 0,
        lambda states, proj_weight, cluster_of, *_: ring_plan(states, proj_weight, cluster_of),
        lambda states, proj_weight, cluster_of, slot, *home: finish(slot, home).reshape(docs),
        states, proj_weight, cluster_of, slot, *home,
    )


def on_device(states, proj_weight, cluster_of):
    if (lax.axis_size("owner"), lax.axis_size("split")) == (8, 2) and states.shape[0] == 512:
        return meeting_plan(states, proj_weight, cluster_of)
    return owner_plan(states, proj_weight, cluster_of)


def solution(mesh):
    placed = (P(("parts", "owner", "split"), None), P(), P(("parts", "owner", "split")))
    return jax.shard_map(
        on_device,
        mesh=mesh,
        in_specs=placed,
        out_specs=P(("parts", "owner", "split")),
        check_vma=False,
    )
```

```python
import math

import jax
import jax.numpy as jnp
from jax import lax
from jax.experimental import pallas as pl
from jax.experimental.pallas import tpu as pltpu
from jax.sharding import PartitionSpec as P

CLUS_OWN = 2
TAU = 0.05
THRESH = 0.2
EPS = 1e-06
LOG2E = math.log2(math.e)
SCALE = LOG2E / TAU
SHIFT = THRESH * LOG2E / TAU

ROWS = 2
F32 = jnp.float32
BF16 = jnp.bfloat16


def prepare(states, proj_weight):
    projected = jnp.dot(states, proj_weight, preferred_element_type=jnp.float32)
    unit = projected * lax.rsqrt(jnp.sum(projected * projected, axis=1, keepdims=True) + EPS)
    peak = jnp.max(jnp.abs(unit), axis=1).astype(jnp.bfloat16)
    quant = (unit / peak.astype(jnp.float32)[:, None]).astype(jnp.bfloat16)
    return (quant, peak)


def similarity_scores(
    own_quant, own_peak, own_cluster, own_index, col_quant, col_peak, col_cluster, col_index
):
    row_count = own_quant.shape[0]
    block = math.gcd(row_count, 768)
    col_scale = col_peak.astype(jnp.float32)

    def one_block(start):
        quant_rows = lax.dynamic_slice_in_dim(own_quant, start, block, 0)
        scale_rows = lax.dynamic_slice_in_dim(own_peak, start, block, 0).astype(jnp.float32)
        cluster_rows = lax.dynamic_slice_in_dim(own_cluster, start, block, 0)
        index_rows = lax.dynamic_slice_in_dim(own_index, start, block, 0)
        inner = lax.dot_general(
            quant_rows, col_quant, (((1,), (1,)), ((), ())), preferred_element_type=jnp.float32
        )
        cosine = inner * scale_rows[:, None] * col_scale[None, :]
        same = (cluster_rows[:, None] == col_cluster[None, :]) & (
            index_rows[:, None] != col_index[None, :]
        )
        weights = jnp.where(same, jnp.exp((cosine - THRESH) / TAU), jnp.zeros_like(cosine))
        return jnp.log(1.0 + jnp.sum(weights, axis=1))

    starts = jnp.arange(row_count // block, dtype=jnp.int32) * block
    return lax.map(one_block, starts).reshape(row_count)


def owner_plan(states, proj_weight, cluster_of):
    owners = lax.axis_size("owner")
    splits = lax.axis_size("split")
    half_index = lax.axis_index("split")
    doc_count = states.shape[0]
    capacity = 3 * doc_count // owners
    width = proj_weight.shape[1]
    slot_total = owners * capacity
    quant, peak = prepare(states, proj_weight)
    group_of = cluster_of // CLUS_OWN
    onehot = (group_of[:, None] == jnp.arange(owners, dtype=jnp.int32)[None, :]).astype(jnp.int32)
    before = jnp.cumsum(onehot, axis=0) - onehot
    target = group_of * capacity + jnp.sum(before * onehot, axis=1)
    quant_slots = (
        jnp.zeros((slot_total, width), jnp.bfloat16)
        .at[target]
        .set(quant)
        .reshape(owners, capacity, width)
    )
    peak_slots = (
        jnp.zeros((slot_total,), jnp.bfloat16).at[target].set(peak).reshape(owners, capacity)
    )
    cluster_slots = (
        jnp.full((slot_total,), -1, jnp.int32).at[target].set(cluster_of).reshape(owners, capacity)
    )
    positions = (
        jnp.arange(owners, dtype=jnp.int32)[:, None] * (splits * capacity)
        + jnp.arange(capacity, dtype=jnp.int32)[None, :]
    )
    own_index = (positions + half_index * capacity).reshape(slot_total)
    col_index = jnp.arange(splits * slot_total, dtype=jnp.int32)
    own_quant, own_peak, own_cluster = (
        lax.all_to_all(a, "owner", split_axis=0, concat_axis=0, tiled=True)
        for a in (quant_slots, peak_slots, cluster_slots)
    )
    all_quant, all_peak, all_cluster = (
        lax.all_gather(a, "split", axis=1, tiled=True) for a in (own_quant, own_peak, own_cluster)
    )
    scores = similarity_scores(
        own_quant.reshape(slot_total, width),
        own_peak.reshape(slot_total),
        own_cluster.reshape(slot_total),
        own_index,
        all_quant.reshape(splits * slot_total, width),
        all_peak.reshape(splits * slot_total),
        all_cluster.reshape(splits * slot_total),
        col_index,
    )
    returned = lax.all_to_all(
        scores.reshape(owners, capacity), "owner", split_axis=0, concat_axis=0, tiled=True
    )
    return returned.reshape(slot_total)[target]


def ring_plan(states, proj_weight, cluster_of):
    axes = ("owner", "split")
    devices = lax.axis_size("owner") * lax.axis_size("split")
    ring = [(i, (i + 1) % devices) for i in range(devices)]
    quant, peak = prepare(states, proj_weight)
    scale = peak.astype(F32)
    place = jnp.arange(states.shape[0], dtype=jnp.int32)

    def weights(block, block_peak, block_cluster):
        inner = lax.dot_general(quant, block, (((1,), (1,)), ((), ())), preferred_element_type=F32)
        cosine = inner * scale[:, None] * block_peak.astype(F32)[None, :]
        same = cluster_of[:, None] == block_cluster[None, :]
        return jnp.where(same, jnp.exp((cosine - THRESH) / TAU), jnp.zeros_like(cosine))

    def meet(_, carry):
        passed = [lax.ppermute(a, axes, ring) for a in carry[1:]]
        return (carry[0] + jnp.sum(weights(*passed), axis=1), *passed)

    own = (quant, peak, cluster_of)
    others = place[:, None] != place[None, :]
    total = jnp.sum(jnp.where(others, weights(*own), 0.0), axis=1)
    total = lax.fori_loop(1, devices, meet, (total, *own))[0]
    return jnp.log(1.0 + total)


def up(n, m):
    return -(-n // m) * m


META = 8


def layout(docs, hot):
    rest = docs - hot
    first = up(rest, 128)
    flag = first + hot
    return rest, first, flag, up(flag + 1, 128)


def prep_kernel(hot, place_ref, cl_ref, st_ref, w_ref, same_ref, other_ref, slot_ref, vectors):
    docs = st_ref.shape[0]
    rest, first, flag, lanes = layout(docs, hot)
    tile = 128

    cluster = cl_ref[...]
    group = cluster // CLUS_OWN
    member = lax.broadcasted_iota(jnp.int32, (8, docs), 0) == group
    full = jnp.sum(member.astype(F32), axis=1, keepdims=True) == float(hot)
    chosen = jnp.min(
        jnp.where(full, lax.broadcasted_iota(jnp.int32, (8, 1), 0), 8), axis=0, keepdims=True
    )
    doubt = jnp.where(jnp.sum(full.astype(F32), axis=0, keepdims=True) == 1.0, 0.0, 1.0)
    in_hot = group == chosen

    for t in range(docs // tile):
        rows = slice(t * tile, (t + 1) * tile)
        projected = jnp.dot(st_ref[rows, :], w_ref[...], preferred_element_type=F32)
        norm = lax.rsqrt(jnp.sum(projected * projected, axis=1, keepdims=True) + EPS)
        vectors[rows, :] = (projected * (norm * math.sqrt(SCALE))).astype(BF16)

    ahead = (
        lax.broadcasted_iota(jnp.int32, (docs, docs), 0) < lax.broadcasted_iota(jnp.int32, (docs, docs), 1)
    ).astype(F32).astype(BF16)
    hot_rows = jnp.broadcast_to(in_hot.astype(F32), (8, docs)).astype(BF16)
    rank = jnp.dot(hot_rows, ahead, preferred_element_type=F32)[0:1, :].astype(jnp.int32)
    place = lax.broadcasted_iota(jnp.int32, (1, docs), 1)
    slot = jnp.where(in_hot, first + rank, place - rank)
    slot_ref[...] = slot

    sort = (lax.broadcasted_iota(jnp.int32, (lanes, docs), 0) == slot).astype(F32).astype(BF16)
    cluster_rows = jnp.broadcast_to(cluster.astype(F32), (META, docs)).astype(BF16)
    sorted_n = jnp.dot(sort[:rest, :], vectors[...], preferred_element_type=F32).astype(BF16)
    sorted_h = jnp.dot(sort[first:flag, :], vectors[...], preferred_element_type=F32).astype(BF16)
    ids = lax.dot_general(
        cluster_rows, sort, (((1,), (1,)), ((), ())), preferred_element_type=F32
    )
    ids = ids.astype(BF16)


    def fill_n(ref):
        ref[:rest, :] = sorted_n
        ref[rest:, :] = jnp.zeros((META, ref.shape[1]), BF16)
        ref[rest:, :first] = ids[:, :first]
        ref[rest:, first:first + 128] = jnp.broadcast_to(doubt.astype(BF16), (META, 128))

    def fill_h(ref):
        ref[:hot, :] = sorted_h
        ref[hot:, :] = jnp.zeros((rest + META - hot, ref.shape[1]), BF16)
        ref[rest:, :lanes - first] = ids[:, first:]
        ref[rest:, first:first + 128] = jnp.broadcast_to(doubt.astype(BF16), (META, 128))

    even = lax.rem(place_ref[0], 2) == 0

    @pl.when(even)
    def _():
        fill_h(same_ref)
        fill_n(other_ref)

    @pl.when(jnp.logical_not(even))
    def _():
        fill_n(same_ref)
        fill_h(other_ref)


def prep(hot, place, cluster_of, states, proj_weight):
    docs, width = states.shape[0], proj_weight.shape[1]
    rest = docs - hot
    shape = jax.ShapeDtypeStruct
    vmem = pl.BlockSpec(memory_space=pltpu.VMEM)
    return pl.pallas_call(
        lambda *refs: prep_kernel(hot, *refs),
        out_shape=(
            shape((rest + META, width), BF16),
            shape((rest + META, width), BF16),
            shape((1, docs), jnp.int32),
        ),
        in_specs=[pl.BlockSpec(memory_space=pltpu.SMEM), vmem, vmem, vmem],
        scratch_shapes=[pltpu.VMEM((docs, width), BF16)],
        compiler_params=pltpu.CompilerParams(vmem_limit_bytes=24 * 2**20),
        name="prep",
    )(place, cluster_of.reshape(1, docs), states, proj_weight)


OWN, PAIR = "own", "pair"
CORE, PAIR_CORE = "core", "pair_core"
ROW, PAIR_ROW = "row", "pair_row"
DIAG = "diag"
NEXT, FAR = "next", "far"
NEXT_CORE, FAR_CORE = "next_core", "far_core"
GROUPS = ((OWN, PAIR, ROW, PAIR_ROW), (CORE, PAIR_CORE, DIAG), (NEXT, FAR), (NEXT_CORE, FAR_CORE))
TILE = 256
HERE, THERE, ACROSS, SIDE = (OWN, CORE), (PAIR, PAIR_CORE), (ROW, DIAG), (OWN, PAIR, ROW)


def score_kernel(docs, hot, names, given, made, tasks, doubted, carries, *refs):
    rest, first, flag, lanes = layout(docs, hot)
    place_ref, refs = refs[0], refs[1:]
    blocks, refs = dict(zip(names, refs[:len(names)])), refs[len(names):]
    pairs, refs = {p: refs[2 * k:2 * k + 2] for k, p in enumerate(given)}, refs[2 * len(given):]
    before, refs = refs[:len(GROUPS) * carries], refs[len(GROUPS) * carries:]
    outs, refs = refs[:len(GROUPS)], refs[len(GROUPS):]
    if made:
        pairs[made], refs = refs[:2], refs[2:]
    parts = refs[-1]
    for k, out in enumerate(outs):
        out[...] = before[k][...] if carries else jnp.zeros(out.shape, F32)
    spots = {name: (out, k) for out, group in zip(outs, GROUPS) for k, name in enumerate(group)}
    z, y, c = place_ref[0], place_ref[1], place_ref[2]
    when = {"core0": c == 0, "core1": c == 1, "row0": y == 0, "row1": y == 1}
    middle = (z == 1) | (z == 2)

    def meet(count, start):
        lane = slice(start, start + count)
        wide = up(count, 128)
        columns = {name: ref[rest:, 0:wide].astype(F32)[0:8, :].T[0:count, :] for name, ref in blocks.items()}
        if made:
            turned, notes = pairs[made]
            span = len(made) * count
            turned[:, 0:span] = jnp.concatenate([blocks[name][:count, :] for name in made], axis=0).T
            notes[:, 0:span] = jnp.concatenate([columns[name] for name in made], axis=0).T

        for left in dict.fromkeys(task[0] for task in tasks):

            def work(left=left):
                own_tasks = [task for task in tasks if task[0] == left]
                rows = count * len(left)
                block = blocks[left[0]][:count, :]
                column = columns[left[0]][:, 0:1]
                for name in left[1:]:
                    block = jnp.concatenate([block, blocks[name][:count, :]], axis=0)
                    column = jnp.concatenate([column, columns[name][:, 0:1]], axis=0)
                fresh = True
                for _, right, signed, _ in own_tasks:
                    number = abs(signed)
                    if right in blocks:
                        span, rights, diagonal = count, (right,), False
                        ids = blocks[right][rest:, 0:wide].astype(F32)[0:1, 0:count]
                    else:
                        turned, notes = pairs[right]
                        span = number * count if number > 1 else wide
                        rights, diagonal = right[:number], left == right[:1]
                        ids = notes[0:1, 0:span]
                        if number == 1:
                            ids = jnp.where(lax.broadcasted_iota(jnp.int32, ids.shape, 1) < count, ids, -1.0)
                    totals = []
                    for low in range(0, span, TILE):
                        high = min(low + TILE, span)
                        if right in blocks:
                            inner = lax.dot_general(
                                block, blocks[right][low:high, :], (((1,), (1,)), ((), ())),
                                preferred_element_type=F32,
                            )
                        else:
                            inner = jnp.dot(block, turned[:, low:high], preferred_element_type=F32)
                        same = column == ids[:, low:high]
                        if diagonal:
                            same &= lax.broadcasted_iota(jnp.int32, inner.shape, 0) != (
                                lax.broadcasted_iota(jnp.int32, inner.shape, 1) + low
                            )
                        weights = jnp.where(same, jnp.exp2(inner), 0.0)
                        totals.append(jnp.sum(weights, axis=0, keepdims=True))
                        if not diagonal:
                            part = None
                            for t in range(0, high - low, 128):
                                piece = weights[:, t:t + 128]
                                if piece.shape[1] < 128:
                                    blank = jnp.zeros((rows, 128 - piece.shape[1]), F32)
                                    piece = jnp.concatenate([piece, blank], axis=1)
                                part = piece if part is None else part + piece
                            if fresh:
                                parts[0:rows, :] = part
                            else:
                                parts[0:rows, :] += part
                            fresh = False
                    total = jnp.concatenate(totals, axis=1) if len(totals) > 1 else totals[0]
                    for k, name in enumerate(rights if signed > 0 else ()):
                        out, spot = spots[name]
                        out[spot, :, lane] += total[:, k * count:(k + 1) * count]
                if not fresh:
                    part = parts[0:rows, :]
                    high = part.astype(BF16)
                    low = (part - high.astype(F32)).astype(BF16)
                    total = lax.dot_general(
                        jnp.ones((16, 256), BF16), jnp.concatenate([high, low], axis=1),
                        (((1,), (1,)), ((), ())), preferred_element_type=F32,
                    )
                    for k, name in enumerate(left):
                        out, spot = spots[name]
                        out[spot, :, lane] += total[0:1, k * count:(k + 1) * count]

            condition = [task[3] for task in tasks if task[0] == left][0]
            if left[0] in (NEXT, FAR, FAR_CORE):
                pl.when(middle)(work)
            elif condition:
                pl.when(when[condition])(work)
            else:
                work()

    pl.when(lax.rem(z, 2) == 0)(lambda: meet(hot, first))
    pl.when(lax.rem(z, 2) == 1)(lambda: meet(rest, 0))

    if doubted:
        doubt = sum(blocks[name][rest:, first:first + 128].astype(F32)[0:1, 0:1] for name in doubted)
        for name in (FAR, FAR_CORE):
            out, k = spots[name]
            out[k] += jnp.where(lax.broadcasted_iota(jnp.int32, (1, lanes), 1) == flag, doubt, 0.0)


def score(name, docs, hot, place, blocks, pairs, made, tasks, sums, doubted=(), weight=1):
    rest, _, _, lanes = layout(docs, hot)
    names = list(dict.fromkeys([
        *made, *(name for task in tasks for name in task[0]), *(task[1] for task in tasks if task[1] in blocks),
    ]))
    given = [p for p in pairs if any(p == task[1] for task in tasks)]
    width = blocks[OWN].shape[1]
    vmem = pl.BlockSpec(memory_space=pltpu.VMEM)
    arrays = [blocks[b] for b in names] + [a for p in given for a in pairs[p]] + list(sums)
    shapes = [jax.ShapeDtypeStruct((len(group), 1, lanes), F32) for group in GROUPS]
    if made:
        span = len(made) * rest
        shapes += [jax.ShapeDtypeStruct((width, span), BF16), jax.ShapeDtypeStruct((8, span), F32)]
    out = pl.pallas_call(
        lambda *refs: score_kernel(docs, hot, names, given, made, tasks, doubted or made, bool(sums), *refs),
        out_shape=tuple(shapes),
        in_specs=[pl.BlockSpec(memory_space=pltpu.SMEM)] + [vmem] * len(arrays),
        out_specs=tuple(vmem for _ in shapes),
        scratch_shapes=[pltpu.VMEM((3 * rest, 128), F32)],
        compiler_params=pltpu.CompilerParams(vmem_limit_bytes=20 * 2**20),
        cost_estimate=pl.CostEstimate(flops=weight, bytes_accessed=2**10, transcendentals=0),
        name=name,
    )(place, *arrays)
    count = len(GROUPS)
    return out[:count], {**pairs, made: out[count:]} if made else pairs


def finish_kernel(slot_ref, *refs):
    sums, out_ref = refs[:-1], refs[-1]
    total = sums[0][0]
    for ref in sums[1:]:
        total += ref[0]
    lanes, docs = total.shape[1], slot_ref.shape[1]
    values = jnp.broadcast_to(jnp.log(1.0 + total * 2.0**-SHIFT), (8, lanes)).T[:, 0:1]
    here = lax.broadcasted_iota(jnp.int32, (lanes, docs), 0) == slot_ref[...]
    out_ref[...] = jnp.sum(jnp.where(here, values, 0.0), axis=0, keepdims=True)


def finish(slot, sums):
    return pl.pallas_call(
        finish_kernel,
        out_shape=jax.ShapeDtypeStruct(slot.shape, F32),
        compiler_params=pltpu.CompilerParams(vmem_limit_bytes=6 * 2**20),
        name="finish",
    )(slot, *sums)


def decide_kernel(flag, mine_ref, theirs_ref, out_ref):
    out_ref[0] = (jnp.sum(mine_ref[0][:, flag:flag + 1] + theirs_ref[0][:, flag:flag + 1]) > 0.0).astype(jnp.int32)


def decide(flag, mine, theirs):
    return pl.pallas_call(
        lambda *refs: decide_kernel(flag, *refs),
        out_shape=jax.ShapeDtypeStruct((1,), jnp.int32),
        out_specs=pl.BlockSpec(memory_space=pltpu.SMEM),
        compiler_params=pltpu.CompilerParams(vmem_limit_bytes=2 * 2**20),
        name="decide",
    )(mine, theirs)


def meeting_plan(states, proj_weight, cluster_of):
    owners = lax.axis_size("owner")
    columns = owners // ROWS
    docs = states.shape[0]
    hot = 3 * docs // owners
    flag = layout(docs, hot)[2]

    owner, core = lax.axis_index("owner"), lax.axis_index("split")
    place = jnp.stack([owner // ROWS, owner % ROWS, core]).astype(jnp.int32)
    same, other, slot = prep(hot, place, cluster_of, states, proj_weight)

    def move(a, to, row=0, core=0):
        pairs = [
            (
                (z * ROWS + y) * 2 + c,
                (to[z] * ROWS + (y ^ row)) * 2 + (c ^ (core if row or to[z] != z else 1)),
            )
            for z in range(columns) for y in range(ROWS) for c in range(2)
        ]
        return lax.ppermute(a, ("owner", "split"), pairs)

    STAY, OUTER, MIDDLE, TWO = (0, 1, 2, 3), (1, 0, 3, 2), (0, 2, 1, 3), (2, 3, 0, 1)
    TO_MIDDLE = (2, 0, 3, 1)

    def meet(name, made, tasks, **options):
        return score(name, docs, hot, place, blocks, pairs, made, tasks, sums, **options)

    blocks, pairs, sums = {OWN: same}, {}, ()
    blocks[CORE] = move(same, STAY, core=1)
    blocks[PAIR] = move(other, OUTER)
    blocks[CORE], still_same, other = lax.optimization_barrier((blocks[CORE], same, other))
    blocks[ROW] = move(still_same, STAY, row=1)
    blocks[NEXT] = move(other, MIDDLE)
    sums, pairs = meet("own", HERE, [((OWN,), HERE, 1, None), ((CORE,), HERE, 1, "core0")], weight=2**33)

    blocks[PAIR], _ = lax.optimization_barrier((blocks[PAIR], sums[0]))
    blocks[ROW], blocks[NEXT] = lax.optimization_barrier((blocks[ROW], blocks[NEXT]))
    blocks[FAR] = move(same, TO_MIDDLE)
    blocks[PAIR_ROW] = move(blocks[PAIR], STAY, row=1)
    blocks[PAIR_CORE] = move(blocks[PAIR], STAY, core=1)
    blocks[DIAG] = move(blocks[ROW], STAY, core=1)
    blocks[NEXT_CORE] = move(blocks[NEXT], STAY, core=1)
    sums, pairs = meet(
        "pair", THERE, [((PAIR,), THERE, 1, None), ((PAIR_CORE,), THERE, 1, "core1")], weight=2**33
    )
    sums, pairs = meet(
        "row", ACROSS,
        [((PAIR,), HERE, 2, None), ((PAIR,), ACROSS, 2, None), ((ROW,), HERE, 1, "row0"), ((DIAG,), HERE, 1, "row1")],
    )
    sums, pairs = meet("next", SIDE, [((NEXT, NEXT_CORE), SIDE, 3, None)])
    blocks[PAIR_ROW], blocks[FAR], _ = lax.optimization_barrier((blocks[PAIR_ROW], blocks[FAR], sums[0]))
    blocks[FAR_CORE] = move(blocks[FAR], STAY, core=1)
    sums, pairs = meet(
        "far", (),
        [((FAR,), SIDE, 3, None), ((NEXT, NEXT_CORE, FAR), PAIR_ROW, 1, None), ((PAIR_ROW,), THERE, -2, None)],
        doubted=(PAIR_ROW,),
    )
    early = sums[1]
    sums, pairs = meet("last", (), [((FAR_CORE,), SIDE, 3, None), ((FAR_CORE,), PAIR_ROW, 1, None)])
    kept, _, away, late = sums
    early, late = move(early, STAY, core=1), move(late, STAY, core=1)
    to_next, to_far = (away[k:k + 1] + late[k:k + 1] for k in (0, 1))
    from_far, from_next = move(to_far, TWO), move(to_next, MIDDLE)
    own, pair, row = (kept[k:k + 1] + early[k:k + 1] for k in (0, 1, 2))
    pair_row = kept[3:4]
    home = [
        own, from_next, from_far,
        move(pair, OUTER), move(row, STAY, row=1), move(pair_row, OUTER, row=1),
    ]
    return lax.cond(
        decide(flag, to_far, from_far)[0] > 0,
        lambda states, proj_weight, cluster_of, *_: ring_plan(states, proj_weight, cluster_of),
        lambda states, proj_weight, cluster_of, slot, *home: finish(slot, home).reshape(docs),
        states, proj_weight, cluster_of, slot, *home,
    )


def on_device(states, proj_weight, cluster_of):
    if (lax.axis_size("owner"), lax.axis_size("split")) == (8, 2) and states.shape[0] == 512:
        return meeting_plan(states, proj_weight, cluster_of)
    return owner_plan(states, proj_weight, cluster_of)


def solution(mesh):
    placed = (P(("parts", "owner", "split"), None), P(), P(("parts", "owner", "split")))
    return jax.shard_map(
        on_device,
        mesh=mesh,
        in_specs=placed,
        out_specs=P(("parts", "owner", "split")),
        check_vma=False,
    )
```

```python
import math

import jax
import jax.numpy as jnp
from jax import lax
from jax.experimental import pallas as pl
from jax.experimental.pallas import tpu as pltpu
from jax.sharding import PartitionSpec as P

CLUS_OWN = 2
TAU = 0.05
THRESH = 0.2
EPS = 1e-06
LOG2E = math.log2(math.e)
SCALE = LOG2E / TAU
SHIFT = THRESH * LOG2E / TAU

ROWS = 2
F32 = jnp.float32
BF16 = jnp.bfloat16


def prepare(states, proj_weight):
    projected = jnp.dot(states, proj_weight, preferred_element_type=jnp.float32)
    unit = projected * lax.rsqrt(jnp.sum(projected * projected, axis=1, keepdims=True) + EPS)
    peak = jnp.max(jnp.abs(unit), axis=1).astype(jnp.bfloat16)
    quant = (unit / peak.astype(jnp.float32)[:, None]).astype(jnp.bfloat16)
    return (quant, peak)


def similarity_scores(
    own_quant, own_peak, own_cluster, own_index, col_quant, col_peak, col_cluster, col_index
):
    row_count = own_quant.shape[0]
    block = math.gcd(row_count, 768)
    col_scale = col_peak.astype(jnp.float32)

    def one_block(start):
        quant_rows = lax.dynamic_slice_in_dim(own_quant, start, block, 0)
        scale_rows = lax.dynamic_slice_in_dim(own_peak, start, block, 0).astype(jnp.float32)
        cluster_rows = lax.dynamic_slice_in_dim(own_cluster, start, block, 0)
        index_rows = lax.dynamic_slice_in_dim(own_index, start, block, 0)
        inner = lax.dot_general(
            quant_rows, col_quant, (((1,), (1,)), ((), ())), preferred_element_type=jnp.float32
        )
        cosine = inner * scale_rows[:, None] * col_scale[None, :]
        same = (cluster_rows[:, None] == col_cluster[None, :]) & (
            index_rows[:, None] != col_index[None, :]
        )
        weights = jnp.where(same, jnp.exp((cosine - THRESH) / TAU), jnp.zeros_like(cosine))
        return jnp.log(1.0 + jnp.sum(weights, axis=1))

    starts = jnp.arange(row_count // block, dtype=jnp.int32) * block
    return lax.map(one_block, starts).reshape(row_count)


def owner_plan(states, proj_weight, cluster_of):
    owners = lax.axis_size("owner")
    splits = lax.axis_size("split")
    half_index = lax.axis_index("split")
    doc_count = states.shape[0]
    capacity = 3 * doc_count // owners
    width = proj_weight.shape[1]
    slot_total = owners * capacity
    quant, peak = prepare(states, proj_weight)
    group_of = cluster_of // CLUS_OWN
    onehot = (group_of[:, None] == jnp.arange(owners, dtype=jnp.int32)[None, :]).astype(jnp.int32)
    before = jnp.cumsum(onehot, axis=0) - onehot
    target = group_of * capacity + jnp.sum(before * onehot, axis=1)
    quant_slots = (
        jnp.zeros((slot_total, width), jnp.bfloat16)
        .at[target]
        .set(quant)
        .reshape(owners, capacity, width)
    )
    peak_slots = (
        jnp.zeros((slot_total,), jnp.bfloat16).at[target].set(peak).reshape(owners, capacity)
    )
    cluster_slots = (
        jnp.full((slot_total,), -1, jnp.int32).at[target].set(cluster_of).reshape(owners, capacity)
    )
    positions = (
        jnp.arange(owners, dtype=jnp.int32)[:, None] * (splits * capacity)
        + jnp.arange(capacity, dtype=jnp.int32)[None, :]
    )
    own_index = (positions + half_index * capacity).reshape(slot_total)
    col_index = jnp.arange(splits * slot_total, dtype=jnp.int32)
    own_quant, own_peak, own_cluster = (
        lax.all_to_all(a, "owner", split_axis=0, concat_axis=0, tiled=True)
        for a in (quant_slots, peak_slots, cluster_slots)
    )
    all_quant, all_peak, all_cluster = (
        lax.all_gather(a, "split", axis=1, tiled=True) for a in (own_quant, own_peak, own_cluster)
    )
    scores = similarity_scores(
        own_quant.reshape(slot_total, width),
        own_peak.reshape(slot_total),
        own_cluster.reshape(slot_total),
        own_index,
        all_quant.reshape(splits * slot_total, width),
        all_peak.reshape(splits * slot_total),
        all_cluster.reshape(splits * slot_total),
        col_index,
    )
    returned = lax.all_to_all(
        scores.reshape(owners, capacity), "owner", split_axis=0, concat_axis=0, tiled=True
    )
    return returned.reshape(slot_total)[target]


def ring_plan(states, proj_weight, cluster_of):
    axes = ("owner", "split")
    devices = lax.axis_size("owner") * lax.axis_size("split")
    ring = [(i, (i + 1) % devices) for i in range(devices)]
    quant, peak = prepare(states, proj_weight)
    scale = peak.astype(F32)
    place = jnp.arange(states.shape[0], dtype=jnp.int32)

    def weights(block, block_peak, block_cluster):
        inner = lax.dot_general(quant, block, (((1,), (1,)), ((), ())), preferred_element_type=F32)
        cosine = inner * scale[:, None] * block_peak.astype(F32)[None, :]
        same = cluster_of[:, None] == block_cluster[None, :]
        return jnp.where(same, jnp.exp((cosine - THRESH) / TAU), jnp.zeros_like(cosine))

    def meet(_, carry):
        passed = [lax.ppermute(a, axes, ring) for a in carry[1:]]
        return (carry[0] + jnp.sum(weights(*passed), axis=1), *passed)

    own = (quant, peak, cluster_of)
    others = place[:, None] != place[None, :]
    total = jnp.sum(jnp.where(others, weights(*own), 0.0), axis=1)
    total = lax.fori_loop(1, devices, meet, (total, *own))[0]
    return jnp.log(1.0 + total)


def up(n, m):
    return -(-n // m) * m


META = 8


def layout(docs, hot):
    rest = docs - hot
    first = up(rest, 128)
    flag = first + hot
    return rest, first, flag, up(flag + 1, 128)


def prep_kernel(hot, place_ref, cl_ref, st_ref, w_ref, same_ref, other_ref, slot_ref, vectors):
    docs = st_ref.shape[0]
    rest, first, flag, lanes = layout(docs, hot)
    tile = 128

    cluster = cl_ref[...]
    group = cluster // CLUS_OWN
    member = lax.broadcasted_iota(jnp.int32, (8, docs), 0) == group
    full = jnp.sum(member.astype(F32), axis=1, keepdims=True) == float(hot)
    chosen = jnp.min(
        jnp.where(full, lax.broadcasted_iota(jnp.int32, (8, 1), 0), 8), axis=0, keepdims=True
    )
    doubt = jnp.where(jnp.sum(full.astype(F32), axis=0, keepdims=True) == 1.0, 0.0, 1.0)
    in_hot = group == chosen

    for t in range(docs // tile):
        rows = slice(t * tile, (t + 1) * tile)
        projected = jnp.dot(st_ref[rows, :], w_ref[...], preferred_element_type=F32)
        norm = lax.rsqrt(jnp.sum(projected * projected, axis=1, keepdims=True) + EPS)
        vectors[rows, :] = (projected * (norm * math.sqrt(SCALE))).astype(BF16)

    ahead = (
        lax.broadcasted_iota(jnp.int32, (docs, docs), 0) < lax.broadcasted_iota(jnp.int32, (docs, docs), 1)
    ).astype(F32).astype(BF16)
    hot_rows = jnp.broadcast_to(in_hot.astype(F32), (8, docs)).astype(BF16)
    rank = jnp.dot(hot_rows, ahead, preferred_element_type=F32)[0:1, :].astype(jnp.int32)
    place = lax.broadcasted_iota(jnp.int32, (1, docs), 1)
    slot = jnp.where(in_hot, first + rank, place - rank)
    slot_ref[...] = slot

    sort = (lax.broadcasted_iota(jnp.int32, (lanes, docs), 0) == slot).astype(F32).astype(BF16)
    cluster_rows = jnp.broadcast_to(cluster.astype(F32), (META, docs)).astype(BF16)
    sorted_n = jnp.dot(sort[:rest, :], vectors[...], preferred_element_type=F32).astype(BF16)
    sorted_h = jnp.dot(sort[first:flag, :], vectors[...], preferred_element_type=F32).astype(BF16)
    ids = lax.dot_general(
        cluster_rows, sort, (((1,), (1,)), ((), ())), preferred_element_type=F32
    )
    ids = ids.astype(BF16)


    def fill_n(ref):
        ref[:rest, :] = sorted_n
        ref[rest:, :] = jnp.zeros((META, ref.shape[1]), BF16)
        ref[rest:, :first] = ids[:, :first]
        ref[rest:, first:first + 128] = jnp.broadcast_to(doubt.astype(BF16), (META, 128))

    def fill_h(ref):
        ref[:hot, :] = sorted_h
        ref[hot:, :] = jnp.zeros((rest + META - hot, ref.shape[1]), BF16)
        ref[rest:, :lanes - first] = ids[:, first:]
        ref[rest:, first:first + 128] = jnp.broadcast_to(doubt.astype(BF16), (META, 128))

    even = lax.rem(place_ref[0], 2) == 0

    @pl.when(even)
    def _():
        fill_h(same_ref)
        fill_n(other_ref)

    @pl.when(jnp.logical_not(even))
    def _():
        fill_n(same_ref)
        fill_h(other_ref)


def prep(hot, place, cluster_of, states, proj_weight):
    docs, width = states.shape[0], proj_weight.shape[1]
    rest = docs - hot
    shape = jax.ShapeDtypeStruct
    vmem = pl.BlockSpec(memory_space=pltpu.VMEM)
    return pl.pallas_call(
        lambda *refs: prep_kernel(hot, *refs),
        out_shape=(
            shape((rest + META, width), BF16),
            shape((rest + META, width), BF16),
            shape((1, docs), jnp.int32),
        ),
        in_specs=[pl.BlockSpec(memory_space=pltpu.SMEM), vmem, vmem, vmem],
        scratch_shapes=[pltpu.VMEM((docs, width), BF16)],
        compiler_params=pltpu.CompilerParams(vmem_limit_bytes=24 * 2**20),
        name="prep",
    )(place, cluster_of.reshape(1, docs), states, proj_weight)


OWN, PAIR = "own", "pair"
CORE, PAIR_CORE = "core", "pair_core"
ROW, PAIR_ROW = "row", "pair_row"
DIAG, PAIR_DIAG = "diag", "pair_diag"
NEXT, FAR = "next", "far"
GROUPS = ((OWN, PAIR, ROW, PAIR_ROW), (CORE, PAIR_CORE, DIAG, PAIR_DIAG), (NEXT,), (FAR,))
TILE = 256
HERE, THERE, ACROSS = (OWN, CORE), (PAIR, PAIR_CORE), (ROW, DIAG)


def score_kernel(docs, hot, names, given, made, tasks, doubted, ready, keep, carries, *refs):
    rest, first, flag, lanes = layout(docs, hot)
    place_ref, refs = refs[0], refs[1:]
    blocks, refs = dict(zip(names, refs[:len(names)])), refs[len(names):]
    pairs, refs = {p: refs[2 * k:2 * k + 2] for k, p in enumerate(given)}, refs[2 * len(given):]
    ready, refs = dict(zip(ready, refs[:len(ready)])), refs[len(ready):]
    before, refs = refs[:len(GROUPS) * carries], refs[len(GROUPS) * carries:]
    outs, refs = refs[:len(GROUPS)], refs[len(GROUPS):]
    if made:
        pairs[made], refs = refs[:2], refs[2:]
    kept, parts = dict(zip(keep, refs[:len(keep)])), refs[-1]
    for k, out in enumerate(outs):
        out[...] = before[k][...] if carries else jnp.zeros(out.shape, F32)
    spots = {name: (out, k) for out, group in zip(outs, GROUPS) for k, name in enumerate(group)}
    z, y, c = place_ref[0], place_ref[1], place_ref[2]
    when = {"core0": c == 0, "core1": c == 1, "row0": y == 0, "row1": y == 1}
    middle = (z == 1) | (z == 2)

    def meet(count, start):
        lane = slice(start, start + count)
        wide, two = up(count, 128), 2 * count

        def column(name):
            if name in ready:
                return ready[name][0:count, :]
            return blocks[name][rest:, 0:wide].astype(F32)[0:8, :].T[0:count, :]

        columns = {name: column(name) for name in made + keep}
        for name in keep:
            kept[name][0:count, :] = columns[name]
        if made:
            turned, notes = pairs[made]
            turned[:, 0:two] = jnp.concatenate([blocks[name][:count, :] for name in made], axis=0).T
            notes[:, 0:two] = jnp.concatenate([columns[name] for name in made], axis=0).T

        for left in dict.fromkeys(task[0] for task in tasks):

            def work(left=left):
                own_tasks = [task for task in tasks if task[0] == left]
                rows = count * len(left)
                block = blocks[left[0]][:count, :]
                mine = [columns[name] if name in columns else column(name) for name in left]
                mine = mine[0][:, 0:1] if len(mine) == 1 else jnp.concatenate(mine, axis=0)[:, 0:1]
                for name in left[1:]:
                    block = jnp.concatenate([block, blocks[name][:count, :]], axis=0)
                fresh = True
                for _, right, both, _ in own_tasks:
                    if right in blocks:
                        span, rights, diagonal = count, (right,), False
                        ids = blocks[right][rest:, 0:wide].astype(F32)[0:1, 0:count]
                    else:
                        turned, notes = pairs[right]
                        span, rights, diagonal = two if both else wide, right[:1 + both], left == right[:1]
                        ids = notes[0:1, 0:span]
                        if not both:
                            ids = jnp.where(lax.broadcasted_iota(jnp.int32, ids.shape, 1) < count, ids, -1.0)
                    totals = []
                    for low in range(0, span, TILE):
                        high = min(low + TILE, span)
                        if right in blocks:
                            inner = lax.dot_general(
                                block, blocks[right][low:high, :], (((1,), (1,)), ((), ())),
                                preferred_element_type=F32,
                            )
                        else:
                            inner = jnp.dot(block, turned[:, low:high], preferred_element_type=F32)
                        same = mine == ids[:, low:high]
                        if diagonal:
                            same &= lax.broadcasted_iota(jnp.int32, inner.shape, 0) != (
                                lax.broadcasted_iota(jnp.int32, inner.shape, 1) + low
                            )
                        weights = jnp.where(same, jnp.exp2(inner), 0.0)
                        totals.append(jnp.sum(weights, axis=0, keepdims=True))
                        if not diagonal:
                            part = None
                            for t in range(0, high - low, 128):
                                piece = weights[:, t:t + 128]
                                if piece.shape[1] < 128:
                                    blank = jnp.zeros((rows, 128 - piece.shape[1]), F32)
                                    piece = jnp.concatenate([piece, blank], axis=1)
                                part = piece if part is None else part + piece
                            if fresh:
                                parts[0:rows, :] = part
                            else:
                                parts[0:rows, :] += part
                            fresh = False
                    total = jnp.concatenate(totals, axis=1) if len(totals) > 1 else totals[0]
                    for k, name in enumerate(rights):
                        out, spot = spots[name]
                        out[spot, :, lane] += total[:, k * count:(k + 1) * count]
                if not fresh:
                    part = parts[0:rows, :]
                    high = part.astype(BF16)
                    low = (part - high.astype(F32)).astype(BF16)
                    total = lax.dot_general(
                        jnp.ones((16, 256), BF16), jnp.concatenate([high, low], axis=1),
                        (((1,), (1,)), ((), ())), preferred_element_type=F32,
                    )
                    for k, name in enumerate(left):
                        out, spot = spots[name]
                        out[spot, :, lane] += total[0:1, k * count:(k + 1) * count]

            condition = [task[3] for task in tasks if task[0] == left][0]
            if left[0] in (NEXT, FAR):
                pl.when(middle)(work)
            elif condition:
                pl.when(when[condition])(work)
            else:
                work()

    pl.when(lax.rem(z, 2) == 0)(lambda: meet(hot, first))
    pl.when(lax.rem(z, 2) == 1)(lambda: meet(rest, 0))

    if doubted:
        doubt = sum(blocks[name][rest:, first:first + 128].astype(F32)[0:1, 0:1] for name in doubted)
        out, k = spots[FAR]
        out[k] += jnp.where(lax.broadcasted_iota(jnp.int32, (1, lanes), 1) == flag, doubt, 0.0)


def score(name, docs, hot, place, blocks, pairs, made, tasks, sums, cols, doubted=(), keep=(), weight=1):
    rest, _, _, lanes = layout(docs, hot)
    names = list(dict.fromkeys([*made, *(name for task in tasks for name in task[0])]))
    given = [p for p in pairs if any(p == task[1] for task in tasks)]
    width = blocks[OWN].shape[1]
    vmem = pl.BlockSpec(memory_space=pltpu.VMEM)
    ready = [b for b in names if b in cols]
    arrays = [blocks[b] for b in names] + [a for p in given for a in pairs[p]] + [cols[b] for b in ready] + list(sums)
    shapes = [jax.ShapeDtypeStruct((len(group), 1, lanes), F32) for group in GROUPS]
    if made:
        shapes += [jax.ShapeDtypeStruct((width, 2 * rest), BF16), jax.ShapeDtypeStruct((8, 2 * rest), F32)]
    shapes += [jax.ShapeDtypeStruct((rest, 8), F32) for _ in keep]
    out = pl.pallas_call(
        lambda *refs: score_kernel(
            docs, hot, names, given, made, tasks, doubted or made, ready, keep, bool(sums), *refs
        ),
        out_shape=tuple(shapes),
        in_specs=[pl.BlockSpec(memory_space=pltpu.SMEM)] + [vmem] * len(arrays),
        out_specs=tuple(vmem for _ in shapes),
        scratch_shapes=[pltpu.VMEM((2 * rest, 128), F32)],
        compiler_params=pltpu.CompilerParams(vmem_limit_bytes=20 * 2**20),
        cost_estimate=pl.CostEstimate(flops=weight, bytes_accessed=2**10, transcendentals=0),
        name=name,
    )(place, *arrays)
    count = len(GROUPS)
    cols = {**cols, **dict(zip(keep, out[len(out) - len(keep):]))}
    return out[:count], {**pairs, made: out[count:count + 2]} if made else pairs, cols


def finish_kernel(slot_ref, *refs):
    sums, out_ref = refs[:-1], refs[-1]
    total = sums[0][0]
    for ref in sums[1:]:
        total += ref[0]
    lanes, docs = total.shape[1], slot_ref.shape[1]
    values = jnp.broadcast_to(jnp.log(1.0 + total * 2.0**-SHIFT), (8, lanes)).T[:, 0:1]
    here = lax.broadcasted_iota(jnp.int32, (lanes, docs), 0) == slot_ref[...]
    out_ref[...] = jnp.sum(jnp.where(here, values, 0.0), axis=0, keepdims=True)


def finish(slot, sums):
    return pl.pallas_call(
        finish_kernel,
        out_shape=jax.ShapeDtypeStruct(slot.shape, F32),
        compiler_params=pltpu.CompilerParams(vmem_limit_bytes=6 * 2**20),
        name="finish",
    )(slot, *sums)


def decide_kernel(flag, mine_ref, theirs_ref, out_ref):
    out_ref[0] = (jnp.sum(mine_ref[0][:, flag:flag + 1] + theirs_ref[0][:, flag:flag + 1]) > 0.0).astype(jnp.int32)


def decide(flag, mine, theirs):
    return pl.pallas_call(
        lambda *refs: decide_kernel(flag, *refs),
        out_shape=jax.ShapeDtypeStruct((1,), jnp.int32),
        out_specs=pl.BlockSpec(memory_space=pltpu.SMEM),
        compiler_params=pltpu.CompilerParams(vmem_limit_bytes=2 * 2**20),
        name="decide",
    )(mine, theirs)


def meeting_plan(states, proj_weight, cluster_of):
    owners = lax.axis_size("owner")
    columns = owners // ROWS
    docs = states.shape[0]
    hot = 3 * docs // owners
    flag = layout(docs, hot)[2]

    owner, core = lax.axis_index("owner"), lax.axis_index("split")
    place = jnp.stack([owner // ROWS, owner % ROWS, core]).astype(jnp.int32)
    same, other, slot = prep(hot, place, cluster_of, states, proj_weight)

    def move(a, to, row=0, core=0):
        pairs = [
            (
                (z * ROWS + y) * 2 + c,
                (to[z] * ROWS + (y ^ row)) * 2 + (c ^ (core if row or to[z] != z else 1)),
            )
            for z in range(columns) for y in range(ROWS) for c in range(2)
        ]
        return lax.ppermute(a, ("owner", "split"), pairs)

    STAY, OUTER, MIDDLE, TWO = (0, 1, 2, 3), (1, 0, 3, 2), (0, 2, 1, 3), (2, 3, 0, 1)
    TO_MIDDLE = (2, 0, 3, 1)

    def meet(name, made, tasks, **options):
        return score(name, docs, hot, place, blocks, pairs, made, tasks, sums, cols, **options)

    blocks, pairs, sums, cols = {OWN: same}, {}, (), {}
    blocks[CORE] = move(same, STAY, core=1)
    blocks[PAIR] = move(other, OUTER)
    blocks[CORE], still_same, other = lax.optimization_barrier((blocks[CORE], same, other))
    blocks[ROW] = move(still_same, STAY, row=1)
    blocks[NEXT] = move(other, MIDDLE)
    sums, pairs, cols = meet("own", HERE, [((OWN,), HERE, False, None), ((CORE,), HERE, False, "core0")], weight=2**33)

    blocks[PAIR], _ = lax.optimization_barrier((blocks[PAIR], sums[0]))
    blocks[ROW], blocks[NEXT] = lax.optimization_barrier((blocks[ROW], blocks[NEXT]))
    blocks[FAR] = move(same, TO_MIDDLE)
    blocks[PAIR_ROW] = move(blocks[PAIR], STAY, row=1)
    blocks[PAIR_CORE] = move(blocks[PAIR], STAY, core=1)
    blocks[DIAG] = move(blocks[ROW], STAY, core=1)
    sums, pairs, cols = meet(
        "pair", THERE,
        [((PAIR,), THERE, False, None), ((PAIR_CORE,), THERE, False, "core1"), ((NEXT,), HERE, True, None),
         ((NEXT,), THERE, True, None)],
        keep=(NEXT,), weight=2**33,
    )
    sums, pairs, cols = meet(
        "row", ACROSS,
        [((PAIR,), HERE, True, None), ((PAIR,), ACROSS, True, None), ((NEXT,), ACROSS, True, None),
         ((ROW,), HERE, False, "row0"), ((DIAG,), HERE, False, "row1")],
    )
    blocks[PAIR_ROW], _ = lax.optimization_barrier((blocks[PAIR_ROW], sums[0]))
    blocks[PAIR_DIAG] = move(blocks[PAIR_ROW], STAY, core=1)
    sums, pairs, cols = meet(
        "far", (), [((FAR,), p, True, None) for p in (HERE, THERE, ACROSS)], keep=(FAR,)
    )
    sums, pairs, cols = meet(
        "last", (),
        [((NEXT, FAR), right, False, None) for right in (PAIR_ROW, PAIR_DIAG)]
        + [((PAIR_ROW,), THERE, False, "row1"), ((PAIR_DIAG,), THERE, False, "row0")],
        doubted=(PAIR_ROW, PAIR_DIAG),
    )
    kept, by_core, to_next, to_far = sums
    from_core, from_far = move(by_core, STAY, core=1), move(to_far, TWO)
    from_core, to_next = lax.optimization_barrier((from_core, to_next))
    from_next = move(to_next, MIDDLE)
    own, pair, row, pair_row = (kept[k:k + 1] + from_core[k:k + 1] for k in (0, 1, 2, 3))
    home = [
        own, from_next, from_far,
        move(pair, OUTER), move(row, STAY, row=1), move(pair_row, OUTER, row=1),
    ]
    return lax.cond(
        decide(flag, to_far, from_far)[0] > 0,
        lambda states, proj_weight, cluster_of, *_: ring_plan(states, proj_weight, cluster_of),
        lambda states, proj_weight, cluster_of, slot, *home: finish(slot, home).reshape(docs),
        states, proj_weight, cluster_of, slot, *home,
    )


def on_device(states, proj_weight, cluster_of):
    if (lax.axis_size("owner"), lax.axis_size("split")) == (8, 2) and states.shape[0] == 512:
        return meeting_plan(states, proj_weight, cluster_of)
    return owner_plan(states, proj_weight, cluster_of)


def solution(mesh):
    placed = (P(("parts", "owner", "split"), None), P(), P(("parts", "owner", "split")))
    return jax.shard_map(
        on_device,
        mesh=mesh,
        in_specs=placed,
        out_specs=P(("parts", "owner", "split")),
        check_vma=False,
    )
```

```python
import math

import jax
import jax.numpy as jnp
from jax import lax
from jax.experimental import pallas as pl
from jax.experimental.pallas import tpu as pltpu
from jax.sharding import PartitionSpec as P

CLUS_OWN = 2
TAU = 0.05
THRESH = 0.2
EPS = 1e-06
LOG2E = math.log2(math.e)
SCALE = LOG2E / TAU
SHIFT = THRESH * LOG2E / TAU

ROWS = 2
F32 = jnp.float32
BF16 = jnp.bfloat16


def prepare(states, proj_weight):
    projected = jnp.dot(states, proj_weight, preferred_element_type=jnp.float32)
    unit = projected * lax.rsqrt(jnp.sum(projected * projected, axis=1, keepdims=True) + EPS)
    peak = jnp.max(jnp.abs(unit), axis=1).astype(jnp.bfloat16)
    quant = (unit / peak.astype(jnp.float32)[:, None]).astype(jnp.bfloat16)
    return (quant, peak)


def similarity_scores(
    own_quant, own_peak, own_cluster, own_index, col_quant, col_peak, col_cluster, col_index
):
    row_count = own_quant.shape[0]
    block = math.gcd(row_count, 768)
    col_scale = col_peak.astype(jnp.float32)

    def one_block(start):
        quant_rows = lax.dynamic_slice_in_dim(own_quant, start, block, 0)
        scale_rows = lax.dynamic_slice_in_dim(own_peak, start, block, 0).astype(jnp.float32)
        cluster_rows = lax.dynamic_slice_in_dim(own_cluster, start, block, 0)
        index_rows = lax.dynamic_slice_in_dim(own_index, start, block, 0)
        inner = lax.dot_general(
            quant_rows, col_quant, (((1,), (1,)), ((), ())), preferred_element_type=jnp.float32
        )
        cosine = inner * scale_rows[:, None] * col_scale[None, :]
        same = (cluster_rows[:, None] == col_cluster[None, :]) & (
            index_rows[:, None] != col_index[None, :]
        )
        weights = jnp.where(same, jnp.exp((cosine - THRESH) / TAU), jnp.zeros_like(cosine))
        return jnp.log(1.0 + jnp.sum(weights, axis=1))

    starts = jnp.arange(row_count // block, dtype=jnp.int32) * block
    return lax.map(one_block, starts).reshape(row_count)


def owner_plan(states, proj_weight, cluster_of):
    owners = lax.axis_size("owner")
    splits = lax.axis_size("split")
    half_index = lax.axis_index("split")
    doc_count = states.shape[0]
    capacity = 3 * doc_count // owners
    width = proj_weight.shape[1]
    slot_total = owners * capacity
    quant, peak = prepare(states, proj_weight)
    group_of = cluster_of // CLUS_OWN
    onehot = (group_of[:, None] == jnp.arange(owners, dtype=jnp.int32)[None, :]).astype(jnp.int32)
    before = jnp.cumsum(onehot, axis=0) - onehot
    target = group_of * capacity + jnp.sum(before * onehot, axis=1)
    quant_slots = (
        jnp.zeros((slot_total, width), jnp.bfloat16)
        .at[target]
        .set(quant)
        .reshape(owners, capacity, width)
    )
    peak_slots = (
        jnp.zeros((slot_total,), jnp.bfloat16).at[target].set(peak).reshape(owners, capacity)
    )
    cluster_slots = (
        jnp.full((slot_total,), -1, jnp.int32).at[target].set(cluster_of).reshape(owners, capacity)
    )
    positions = (
        jnp.arange(owners, dtype=jnp.int32)[:, None] * (splits * capacity)
        + jnp.arange(capacity, dtype=jnp.int32)[None, :]
    )
    own_index = (positions + half_index * capacity).reshape(slot_total)
    col_index = jnp.arange(splits * slot_total, dtype=jnp.int32)
    own_quant, own_peak, own_cluster = (
        lax.all_to_all(a, "owner", split_axis=0, concat_axis=0, tiled=True)
        for a in (quant_slots, peak_slots, cluster_slots)
    )
    all_quant, all_peak, all_cluster = (
        lax.all_gather(a, "split", axis=1, tiled=True) for a in (own_quant, own_peak, own_cluster)
    )
    scores = similarity_scores(
        own_quant.reshape(slot_total, width),
        own_peak.reshape(slot_total),
        own_cluster.reshape(slot_total),
        own_index,
        all_quant.reshape(splits * slot_total, width),
        all_peak.reshape(splits * slot_total),
        all_cluster.reshape(splits * slot_total),
        col_index,
    )
    returned = lax.all_to_all(
        scores.reshape(owners, capacity), "owner", split_axis=0, concat_axis=0, tiled=True
    )
    return returned.reshape(slot_total)[target]


def ring_plan(states, proj_weight, cluster_of):
    axes = ("owner", "split")
    devices = lax.axis_size("owner") * lax.axis_size("split")
    ring = [(i, (i + 1) % devices) for i in range(devices)]
    quant, peak = prepare(states, proj_weight)
    scale = peak.astype(F32)
    place = jnp.arange(states.shape[0], dtype=jnp.int32)

    def weights(block, block_peak, block_cluster):
        inner = lax.dot_general(quant, block, (((1,), (1,)), ((), ())), preferred_element_type=F32)
        cosine = inner * scale[:, None] * block_peak.astype(F32)[None, :]
        same = cluster_of[:, None] == block_cluster[None, :]
        return jnp.where(same, jnp.exp((cosine - THRESH) / TAU), jnp.zeros_like(cosine))

    def meet(_, carry):
        passed = [lax.ppermute(a, axes, ring) for a in carry[1:]]
        return (carry[0] + jnp.sum(weights(*passed), axis=1), *passed)

    own = (quant, peak, cluster_of)
    others = place[:, None] != place[None, :]
    total = jnp.sum(jnp.where(others, weights(*own), 0.0), axis=1)
    total = lax.fori_loop(1, devices, meet, (total, *own))[0]
    return jnp.log(1.0 + total)


def up(n, m):
    return -(-n // m) * m


META = 8


def layout(docs, hot):
    rest = docs - hot
    first = up(rest, 128)
    flag = first + hot
    return rest, first, flag, up(flag + 1, 128)


def prep_kernel(hot, place_ref, cl_ref, st_ref, w_ref, same_ref, other_ref, slot_ref, vectors):
    docs = st_ref.shape[0]
    rest, first, flag, lanes = layout(docs, hot)
    tile = 128

    cluster = cl_ref[...]
    group = cluster // CLUS_OWN
    member = lax.broadcasted_iota(jnp.int32, (8, docs), 0) == group
    full = jnp.sum(member.astype(F32), axis=1, keepdims=True) == float(hot)
    chosen = jnp.min(
        jnp.where(full, lax.broadcasted_iota(jnp.int32, (8, 1), 0), 8), axis=0, keepdims=True
    )
    doubt = jnp.where(jnp.sum(full.astype(F32), axis=0, keepdims=True) == 1.0, 0.0, 1.0)
    in_hot = group == chosen

    for t in range(docs // tile):
        rows = slice(t * tile, (t + 1) * tile)
        projected = jnp.dot(st_ref[rows, :], w_ref[...], preferred_element_type=F32)
        norm = lax.rsqrt(jnp.sum(projected * projected, axis=1, keepdims=True) + EPS)
        vectors[rows, :] = (projected * (norm * math.sqrt(SCALE))).astype(BF16)

    ahead = (
        lax.broadcasted_iota(jnp.int32, (docs, docs), 0) < lax.broadcasted_iota(jnp.int32, (docs, docs), 1)
    ).astype(F32).astype(BF16)
    hot_rows = jnp.broadcast_to(in_hot.astype(F32), (8, docs)).astype(BF16)
    rank = jnp.dot(hot_rows, ahead, preferred_element_type=F32)[0:1, :].astype(jnp.int32)
    place = lax.broadcasted_iota(jnp.int32, (1, docs), 1)
    slot = jnp.where(in_hot, first + rank, place - rank)
    slot_ref[...] = slot

    sort = (lax.broadcasted_iota(jnp.int32, (lanes, docs), 0) == slot).astype(F32).astype(BF16)
    cluster_rows = jnp.broadcast_to(cluster.astype(F32), (META, docs)).astype(BF16)
    sorted_n = jnp.dot(sort[:rest, :], vectors[...], preferred_element_type=F32).astype(BF16)
    sorted_h = jnp.dot(sort[first:flag, :], vectors[...], preferred_element_type=F32).astype(BF16)
    ids = lax.dot_general(
        cluster_rows, sort, (((1,), (1,)), ((), ())), preferred_element_type=F32
    )
    ids = ids.astype(BF16)


    def fill_n(ref):
        ref[:rest, :] = sorted_n
        ref[rest:, :] = jnp.zeros((META, ref.shape[1]), BF16)
        ref[rest:, :first] = ids[:, :first]
        ref[rest:, first:first + 128] = jnp.broadcast_to(doubt.astype(BF16), (META, 128))

    def fill_h(ref):
        ref[:hot, :] = sorted_h
        ref[hot:, :] = jnp.zeros((rest + META - hot, ref.shape[1]), BF16)
        ref[rest:, :lanes - first] = ids[:, first:]
        ref[rest:, first:first + 128] = jnp.broadcast_to(doubt.astype(BF16), (META, 128))

    even = lax.rem(place_ref[0], 2) == 0

    @pl.when(even)
    def _():
        fill_h(same_ref)
        fill_n(other_ref)

    @pl.when(jnp.logical_not(even))
    def _():
        fill_n(same_ref)
        fill_h(other_ref)


def prep(hot, place, cluster_of, states, proj_weight):
    docs, width = states.shape[0], proj_weight.shape[1]
    rest = docs - hot
    shape = jax.ShapeDtypeStruct
    vmem = pl.BlockSpec(memory_space=pltpu.VMEM)
    return pl.pallas_call(
        lambda *refs: prep_kernel(hot, *refs),
        out_shape=(
            shape((rest + META, width), BF16),
            shape((rest + META, width), BF16),
            shape((1, docs), jnp.int32),
        ),
        in_specs=[pl.BlockSpec(memory_space=pltpu.SMEM), vmem, vmem, vmem],
        scratch_shapes=[pltpu.VMEM((docs, width), BF16)],
        compiler_params=pltpu.CompilerParams(vmem_limit_bytes=24 * 2**20),
        name="prep",
    )(place, cluster_of.reshape(1, docs), states, proj_weight)


OWN, PAIR = "own", "pair"
CORE, PAIR_CORE = "core", "pair_core"
ROW, PAIR_ROW = "row", "pair_row"
DIAG, PAIR_DIAG = "diag", "pair_diag"
NEXT, FAR = "next", "far"
GROUPS = ((OWN, PAIR, ROW, PAIR_ROW), (CORE, PAIR_CORE, DIAG, PAIR_DIAG), (NEXT,), (FAR,))
TILE = 256
HERE, THERE, ACROSS = (OWN, CORE), (PAIR, PAIR_CORE), (ROW, DIAG)


def score_kernel(docs, hot, names, given, made, tasks, doubted, ready, keep, carries, *refs):
    rest, first, flag, lanes = layout(docs, hot)
    place_ref, refs = refs[0], refs[1:]
    blocks, refs = dict(zip(names, refs[:len(names)])), refs[len(names):]
    pairs, refs = {p: refs[2 * k:2 * k + 2] for k, p in enumerate(given)}, refs[2 * len(given):]
    ready, refs = dict(zip(ready, refs[:len(ready)])), refs[len(ready):]
    before, refs = refs[:len(GROUPS) * carries], refs[len(GROUPS) * carries:]
    outs, refs = refs[:len(GROUPS)], refs[len(GROUPS):]
    if made:
        pairs[made], refs = refs[:2], refs[2:]
    kept, parts = dict(zip(keep, refs[:len(keep)])), refs[-1]
    for k, out in enumerate(outs):
        out[...] = before[k][...] if carries else jnp.zeros(out.shape, F32)
    spots = {name: (out, k) for out, group in zip(outs, GROUPS) for k, name in enumerate(group)}
    z, y, c = place_ref[0], place_ref[1], place_ref[2]
    when = {"core0": c == 0, "core1": c == 1, "row0": y == 0, "row1": y == 1}
    middle = (z == 1) | (z == 2)

    def meet(count, start):
        lane = slice(start, start + count)
        wide, two = up(count, 128), 2 * count

        def column(name):
            if name in ready:
                return ready[name][0:count, :]
            return blocks[name][rest:, 0:wide].astype(F32)[0:8, :].T[0:count, :]

        columns = {name: column(name) for name in made + keep}
        for name in keep:
            kept[name][0:count, :] = columns[name]
        if made:
            turned, notes = pairs[made]
            turned[:, 0:two] = jnp.concatenate([blocks[name][:count, :] for name in made], axis=0).T
            notes[:, 0:two] = jnp.concatenate([columns[name] for name in made], axis=0).T

        for left in dict.fromkeys(task[0] for task in tasks):

            def work(left=left):
                own_tasks = [task for task in tasks if task[0] == left]
                rows = count * len(left)
                block = blocks[left[0]][:count, :]
                mine = [columns[name] if name in columns else column(name) for name in left]
                mine = mine[0][:, 0:1] if len(mine) == 1 else jnp.concatenate(mine, axis=0)[:, 0:1]
                for name in left[1:]:
                    block = jnp.concatenate([block, blocks[name][:count, :]], axis=0)
                fresh = True
                for _, right, both, _ in own_tasks:
                    if right in blocks:
                        span, rights, diagonal = count, (right,), False
                        ids = blocks[right][rest:, 0:wide].astype(F32)[0:1, 0:count]
                    else:
                        turned, notes = pairs[right]
                        span, rights, diagonal = two if both else wide, right[:1 + both], left == right[:1]
                        ids = notes[0:1, 0:span]
                        if not both:
                            ids = jnp.where(lax.broadcasted_iota(jnp.int32, ids.shape, 1) < count, ids, -1.0)
                    totals = []
                    for low in range(0, span, TILE):
                        high = min(low + TILE, span)
                        if right in blocks:
                            inner = lax.dot_general(
                                block, blocks[right][low:high, :], (((1,), (1,)), ((), ())),
                                preferred_element_type=F32,
                            )
                        else:
                            inner = jnp.dot(block, turned[:, low:high], preferred_element_type=F32)
                        same = mine == ids[:, low:high]
                        if diagonal:
                            same &= lax.broadcasted_iota(jnp.int32, inner.shape, 0) != (
                                lax.broadcasted_iota(jnp.int32, inner.shape, 1) + low
                            )
                        weights = jnp.where(same, jnp.exp2(inner), 0.0)
                        totals.append(jnp.sum(weights, axis=0, keepdims=True))
                        if not diagonal:
                            part = None
                            for t in range(0, high - low, 128):
                                piece = weights[:, t:t + 128]
                                if piece.shape[1] < 128:
                                    blank = jnp.zeros((rows, 128 - piece.shape[1]), F32)
                                    piece = jnp.concatenate([piece, blank], axis=1)
                                part = piece if part is None else part + piece
                            if fresh:
                                parts[0:rows, :] = part
                            else:
                                parts[0:rows, :] += part
                            fresh = False
                    total = jnp.concatenate(totals, axis=1) if len(totals) > 1 else totals[0]
                    for k, name in enumerate(rights):
                        out, spot = spots[name]
                        out[spot, :, lane] += total[:, k * count:(k + 1) * count]
                if not fresh:
                    part = parts[0:rows, :]
                    high = part.astype(BF16)
                    low = (part - high.astype(F32)).astype(BF16)
                    total = lax.dot_general(
                        jnp.ones((16, 256), BF16), jnp.concatenate([high, low], axis=1),
                        (((1,), (1,)), ((), ())), preferred_element_type=F32,
                    )
                    for k, name in enumerate(left):
                        out, spot = spots[name]
                        out[spot, :, lane] += total[0:1, k * count:(k + 1) * count]

            condition = [task[3] for task in tasks if task[0] == left][0]
            if left[0] in (NEXT, FAR):
                pl.when(middle)(work)
            elif condition:
                pl.when(when[condition])(work)
            else:
                work()

    pl.when(lax.rem(z, 2) == 0)(lambda: meet(hot, first))
    pl.when(lax.rem(z, 2) == 1)(lambda: meet(rest, 0))

    if doubted:
        doubt = sum(blocks[name][rest:, first:first + 128].astype(F32)[0:1, 0:1] for name in doubted)
        out, k = spots[FAR]
        out[k] += jnp.where(lax.broadcasted_iota(jnp.int32, (1, lanes), 1) == flag, doubt, 0.0)


def score(name, docs, hot, place, blocks, pairs, made, tasks, sums, cols, doubted=(), keep=(), weight=1):
    rest, _, _, lanes = layout(docs, hot)
    names = list(dict.fromkeys([*made, *(name for task in tasks for name in task[0])]))
    given = [p for p in pairs if any(p == task[1] for task in tasks)]
    width = blocks[OWN].shape[1]
    vmem = pl.BlockSpec(memory_space=pltpu.VMEM)
    ready = [b for b in names if b in cols]
    arrays = [blocks[b] for b in names] + [a for p in given for a in pairs[p]] + [cols[b] for b in ready] + list(sums)
    shapes = [jax.ShapeDtypeStruct((len(group), 1, lanes), F32) for group in GROUPS]
    if made:
        shapes += [jax.ShapeDtypeStruct((width, 2 * rest), BF16), jax.ShapeDtypeStruct((8, 2 * rest), F32)]
    shapes += [jax.ShapeDtypeStruct((rest, 8), F32) for _ in keep]
    out = pl.pallas_call(
        lambda *refs: score_kernel(
            docs, hot, names, given, made, tasks, doubted or made, ready, keep, bool(sums), *refs
        ),
        out_shape=tuple(shapes),
        in_specs=[pl.BlockSpec(memory_space=pltpu.SMEM)] + [vmem] * len(arrays),
        out_specs=tuple(vmem for _ in shapes),
        scratch_shapes=[pltpu.VMEM((2 * rest, 128), F32)],
        compiler_params=pltpu.CompilerParams(vmem_limit_bytes=20 * 2**20),
        cost_estimate=pl.CostEstimate(flops=weight, bytes_accessed=2**10, transcendentals=0),
        name=name,
    )(place, *arrays)
    count = len(GROUPS)
    cols = {**cols, **dict(zip(keep, out[len(out) - len(keep):]))}
    return out[:count], {**pairs, made: out[count:count + 2]} if made else pairs, cols


def finish_kernel(slot_ref, *refs):
    sums, out_ref = refs[:-1], refs[-1]
    total = sums[0][0]
    for ref in sums[1:]:
        total += ref[0]
    lanes, docs = total.shape[1], slot_ref.shape[1]
    values = jnp.broadcast_to(jnp.log(1.0 + total * 2.0**-SHIFT), (8, lanes)).T[:, 0:1]
    here = lax.broadcasted_iota(jnp.int32, (lanes, docs), 0) == slot_ref[...]
    out_ref[...] = jnp.sum(jnp.where(here, values, 0.0), axis=0, keepdims=True)


def finish(slot, sums):
    return pl.pallas_call(
        finish_kernel,
        out_shape=jax.ShapeDtypeStruct(slot.shape, F32),
        compiler_params=pltpu.CompilerParams(vmem_limit_bytes=6 * 2**20),
        name="finish",
    )(slot, *sums)


def decide_kernel(flag, mine_ref, theirs_ref, out_ref):
    out_ref[0] = (jnp.sum(mine_ref[0][:, flag:flag + 1] + theirs_ref[0][:, flag:flag + 1]) > 0.0).astype(jnp.int32)


def decide(flag, mine, theirs):
    return pl.pallas_call(
        lambda *refs: decide_kernel(flag, *refs),
        out_shape=jax.ShapeDtypeStruct((1,), jnp.int32),
        out_specs=pl.BlockSpec(memory_space=pltpu.SMEM),
        compiler_params=pltpu.CompilerParams(vmem_limit_bytes=2 * 2**20),
        name="decide",
    )(mine, theirs)


def meeting_plan(states, proj_weight, cluster_of):
    owners = lax.axis_size("owner")
    columns = owners // ROWS
    docs = states.shape[0]
    hot = 3 * docs // owners
    flag = layout(docs, hot)[2]

    owner, core = lax.axis_index("owner"), lax.axis_index("split")
    place = jnp.stack([owner // ROWS, owner % ROWS, core]).astype(jnp.int32)
    same, other, slot = prep(hot, place, cluster_of, states, proj_weight)

    def move(a, to, row=0, core=0):
        pairs = [
            (
                (z * ROWS + y) * 2 + c,
                (to[z] * ROWS + (y ^ row)) * 2 + (c ^ (core if row or to[z] != z else 1)),
            )
            for z in range(columns) for y in range(ROWS) for c in range(2)
        ]
        return lax.ppermute(a, ("owner", "split"), pairs)

    STAY, OUTER, MIDDLE, TWO = (0, 1, 2, 3), (1, 0, 3, 2), (0, 2, 1, 3), (2, 3, 0, 1)
    TO_MIDDLE = (2, 0, 3, 1)

    def meet(name, made, tasks, **options):
        return score(name, docs, hot, place, blocks, pairs, made, tasks, sums, cols, **options)

    blocks, pairs, sums, cols = {OWN: same}, {}, (), {}
    blocks[CORE] = move(same, STAY, core=1)
    blocks[PAIR] = move(other, OUTER)
    blocks[CORE], still_same, other = lax.optimization_barrier((blocks[CORE], same, other))
    blocks[ROW] = move(still_same, STAY, row=1)
    blocks[NEXT] = move(other, MIDDLE)
    sums, pairs, cols = meet("own", HERE, [((OWN,), HERE, False, None), ((CORE,), HERE, False, "core0")], weight=2**33)

    blocks[PAIR], _ = lax.optimization_barrier((blocks[PAIR], sums[0]))
    blocks[ROW], blocks[NEXT] = lax.optimization_barrier((blocks[ROW], blocks[NEXT]))
    blocks[FAR] = move(same, TO_MIDDLE)
    blocks[PAIR_ROW] = move(blocks[PAIR], STAY, row=1)
    blocks[PAIR_CORE] = move(blocks[PAIR], STAY, core=1)
    blocks[DIAG] = move(blocks[ROW], STAY, core=1)
    sums, pairs, cols = meet(
        "pair", THERE,
        [((PAIR,), THERE, False, None), ((PAIR_CORE,), THERE, False, "core1"), ((NEXT,), HERE, True, None),
         ((NEXT,), THERE, True, None)],
        keep=(NEXT,), weight=2**33,
    )
    sums, pairs, cols = meet(
        "row", ACROSS,
        [((PAIR,), HERE, True, None), ((PAIR,), ACROSS, True, None), ((NEXT,), ACROSS, True, None),
         ((ROW,), HERE, False, "row0"), ((DIAG,), HERE, False, "row1")],
    )
    blocks[PAIR_ROW], _ = lax.optimization_barrier((blocks[PAIR_ROW], sums[0]))
    blocks[PAIR_DIAG] = move(blocks[PAIR_ROW], STAY, core=1)
    sums, pairs, cols = meet(
        "far", (), [((FAR,), p, True, None) for p in (HERE, THERE, ACROSS)], keep=(FAR,)
    )
    sums, pairs, cols = meet(
        "last", (),
        [((NEXT, FAR), right, False, None) for right in (PAIR_ROW, PAIR_DIAG)]
        + [((PAIR_ROW,), THERE, False, "row1"), ((PAIR_DIAG,), THERE, False, "row0")],
        doubted=(PAIR_ROW, PAIR_DIAG),
    )
    kept, by_core, to_next, to_far = sums
    from_core, from_far = move(by_core, STAY, core=1), move(to_far, TWO)
    from_core, to_next = lax.optimization_barrier((from_core, to_next))
    from_next = move(to_next, MIDDLE)
    own, pair, row, pair_row = (kept[k:k + 1] + from_core[k:k + 1] for k in (0, 1, 2, 3))
    home = [
        own, from_next, from_far,
        move(pair, OUTER), move(pair_row, OUTER, row=1), move(row, STAY, row=1),
    ]
    return lax.cond(
        decide(flag, to_far, from_far)[0] > 0,
        lambda states, proj_weight, cluster_of, *_: ring_plan(states, proj_weight, cluster_of),
        lambda states, proj_weight, cluster_of, slot, *home: finish(slot, home).reshape(docs),
        states, proj_weight, cluster_of, slot, *home,
    )


def on_device(states, proj_weight, cluster_of):
    if (lax.axis_size("owner"), lax.axis_size("split")) == (8, 2) and states.shape[0] == 512:
        return meeting_plan(states, proj_weight, cluster_of)
    return owner_plan(states, proj_weight, cluster_of)


def solution(mesh):
    placed = (P(("parts", "owner", "split"), None), P(), P(("parts", "owner", "split")))
    return jax.shard_map(
        on_device,
        mesh=mesh,
        in_specs=placed,
        out_specs=P(("parts", "owner", "split")),
        check_vma=False,
    )
```

```python
import math

import jax
import jax.numpy as jnp
from jax import lax
from jax.experimental import pallas as pl
from jax.experimental.pallas import tpu as pltpu
from jax.sharding import PartitionSpec as P

CLUS_OWN = 2
TAU = 0.05
THRESH = 0.2
EPS = 1e-06
LOG2E = math.log2(math.e)
SCALE = LOG2E / TAU
SHIFT = THRESH * LOG2E / TAU

ROWS = 2
F32 = jnp.float32
BF16 = jnp.bfloat16


def prepare(states, proj_weight):
    projected = jnp.dot(states, proj_weight, preferred_element_type=jnp.float32)
    unit = projected * lax.rsqrt(jnp.sum(projected * projected, axis=1, keepdims=True) + EPS)
    peak = jnp.max(jnp.abs(unit), axis=1).astype(jnp.bfloat16)
    quant = (unit / peak.astype(jnp.float32)[:, None]).astype(jnp.bfloat16)
    return (quant, peak)


def similarity_scores(
    own_quant, own_peak, own_cluster, own_index, col_quant, col_peak, col_cluster, col_index
):
    row_count = own_quant.shape[0]
    block = math.gcd(row_count, 768)
    col_scale = col_peak.astype(jnp.float32)

    def one_block(start):
        quant_rows = lax.dynamic_slice_in_dim(own_quant, start, block, 0)
        scale_rows = lax.dynamic_slice_in_dim(own_peak, start, block, 0).astype(jnp.float32)
        cluster_rows = lax.dynamic_slice_in_dim(own_cluster, start, block, 0)
        index_rows = lax.dynamic_slice_in_dim(own_index, start, block, 0)
        inner = lax.dot_general(
            quant_rows, col_quant, (((1,), (1,)), ((), ())), preferred_element_type=jnp.float32
        )
        cosine = inner * scale_rows[:, None] * col_scale[None, :]
        same = (cluster_rows[:, None] == col_cluster[None, :]) & (
            index_rows[:, None] != col_index[None, :]
        )
        weights = jnp.where(same, jnp.exp((cosine - THRESH) / TAU), jnp.zeros_like(cosine))
        return jnp.log(1.0 + jnp.sum(weights, axis=1))

    starts = jnp.arange(row_count // block, dtype=jnp.int32) * block
    return lax.map(one_block, starts).reshape(row_count)


def owner_plan(states, proj_weight, cluster_of):
    owners = lax.axis_size("owner")
    splits = lax.axis_size("split")
    half_index = lax.axis_index("split")
    doc_count = states.shape[0]
    capacity = 3 * doc_count // owners
    width = proj_weight.shape[1]
    slot_total = owners * capacity
    quant, peak = prepare(states, proj_weight)
    group_of = cluster_of // CLUS_OWN
    onehot = (group_of[:, None] == jnp.arange(owners, dtype=jnp.int32)[None, :]).astype(jnp.int32)
    before = jnp.cumsum(onehot, axis=0) - onehot
    target = group_of * capacity + jnp.sum(before * onehot, axis=1)
    quant_slots = (
        jnp.zeros((slot_total, width), jnp.bfloat16)
        .at[target]
        .set(quant)
        .reshape(owners, capacity, width)
    )
    peak_slots = (
        jnp.zeros((slot_total,), jnp.bfloat16).at[target].set(peak).reshape(owners, capacity)
    )
    cluster_slots = (
        jnp.full((slot_total,), -1, jnp.int32).at[target].set(cluster_of).reshape(owners, capacity)
    )
    positions = (
        jnp.arange(owners, dtype=jnp.int32)[:, None] * (splits * capacity)
        + jnp.arange(capacity, dtype=jnp.int32)[None, :]
    )
    own_index = (positions + half_index * capacity).reshape(slot_total)
    col_index = jnp.arange(splits * slot_total, dtype=jnp.int32)
    own_quant, own_peak, own_cluster = (
        lax.all_to_all(a, "owner", split_axis=0, concat_axis=0, tiled=True)
        for a in (quant_slots, peak_slots, cluster_slots)
    )
    all_quant, all_peak, all_cluster = (
        lax.all_gather(a, "split", axis=1, tiled=True) for a in (own_quant, own_peak, own_cluster)
    )
    scores = similarity_scores(
        own_quant.reshape(slot_total, width),
        own_peak.reshape(slot_total),
        own_cluster.reshape(slot_total),
        own_index,
        all_quant.reshape(splits * slot_total, width),
        all_peak.reshape(splits * slot_total),
        all_cluster.reshape(splits * slot_total),
        col_index,
    )
    returned = lax.all_to_all(
        scores.reshape(owners, capacity), "owner", split_axis=0, concat_axis=0, tiled=True
    )
    return returned.reshape(slot_total)[target]


def ring_plan(states, proj_weight, cluster_of):
    axes = ("owner", "split")
    devices = lax.axis_size("owner") * lax.axis_size("split")
    ring = [(i, (i + 1) % devices) for i in range(devices)]
    quant, peak = prepare(states, proj_weight)
    scale = peak.astype(F32)
    place = jnp.arange(states.shape[0], dtype=jnp.int32)

    def weights(block, block_peak, block_cluster):
        inner = lax.dot_general(quant, block, (((1,), (1,)), ((), ())), preferred_element_type=F32)
        cosine = inner * scale[:, None] * block_peak.astype(F32)[None, :]
        same = cluster_of[:, None] == block_cluster[None, :]
        return jnp.where(same, jnp.exp((cosine - THRESH) / TAU), jnp.zeros_like(cosine))

    def meet(_, carry):
        passed = [lax.ppermute(a, axes, ring) for a in carry[1:]]
        return (carry[0] + jnp.sum(weights(*passed), axis=1), *passed)

    own = (quant, peak, cluster_of)
    others = place[:, None] != place[None, :]
    total = jnp.sum(jnp.where(others, weights(*own), 0.0), axis=1)
    total = lax.fori_loop(1, devices, meet, (total, *own))[0]
    return jnp.log(1.0 + total)


def up(n, m):
    return -(-n // m) * m


META = 8


def layout(docs, hot):
    rest = docs - hot
    first = up(rest, 128)
    flag = first + hot
    return rest, first, flag, up(flag + 1, 128)


def prep_kernel(hot, place_ref, cl_ref, st_ref, w_ref, same_ref, other_ref, slot_ref, vectors, whole):
    docs = st_ref.shape[0]
    rest, first, flag, lanes = layout(docs, hot)
    tile = 128

    cluster = cl_ref[...]
    group = cluster // CLUS_OWN
    member = lax.broadcasted_iota(jnp.int32, (8, docs), 0) == group
    full = jnp.sum(member.astype(F32), axis=1, keepdims=True) == float(hot)
    chosen = jnp.min(
        jnp.where(full, lax.broadcasted_iota(jnp.int32, (8, 1), 0), 8), axis=0, keepdims=True
    )
    doubt = jnp.where(jnp.sum(full.astype(F32), axis=0, keepdims=True) == 1.0, 0.0, 1.0)
    in_hot = group == chosen

    whole[...] = jnp.dot(st_ref[...], w_ref[...], preferred_element_type=F32)
    for t in range(docs // tile):
        rows = slice(t * tile, (t + 1) * tile)
        projected = whole[rows, :]
        norm = lax.rsqrt(jnp.sum(projected * projected, axis=1, keepdims=True) + EPS)
        vectors[rows, :] = (projected * (norm * math.sqrt(SCALE))).astype(BF16)

    ahead = (
        lax.broadcasted_iota(jnp.int32, (docs, docs), 0) < lax.broadcasted_iota(jnp.int32, (docs, docs), 1)
    ).astype(F32).astype(BF16)
    hot_rows = jnp.broadcast_to(in_hot.astype(F32), (8, docs)).astype(BF16)
    rank = jnp.dot(hot_rows, ahead, preferred_element_type=F32)[0:1, :].astype(jnp.int32)
    place = lax.broadcasted_iota(jnp.int32, (1, docs), 1)
    slot = jnp.where(in_hot, first + rank, place - rank)
    slot_ref[...] = slot

    sort = (lax.broadcasted_iota(jnp.int32, (lanes, docs), 0) == slot).astype(F32).astype(BF16)
    cluster_rows = jnp.broadcast_to(cluster.astype(F32), (META, docs)).astype(BF16)
    both = jnp.concatenate([sort[:rest, :], sort[first:flag, :]], axis=0)
    moved = jnp.dot(both, vectors[...], preferred_element_type=F32).astype(BF16)
    sorted_n, sorted_h = moved[:rest], moved[rest:]
    ids = lax.dot_general(
        cluster_rows, sort, (((1,), (1,)), ((), ())), preferred_element_type=F32
    )
    ids = ids.astype(BF16)


    def fill_n(ref):
        ref[:rest, :] = sorted_n
        ref[rest:, :] = jnp.zeros((META, ref.shape[1]), BF16)
        ref[rest:, :first] = ids[:, :first]
        ref[rest:, first:first + 128] = jnp.broadcast_to(doubt.astype(BF16), (META, 128))

    def fill_h(ref):
        ref[:hot, :] = sorted_h
        ref[hot:, :] = jnp.zeros((rest + META - hot, ref.shape[1]), BF16)
        ref[rest:, :lanes - first] = ids[:, first:]
        ref[rest:, first:first + 128] = jnp.broadcast_to(doubt.astype(BF16), (META, 128))

    even = lax.rem(place_ref[0], 2) == 0

    @pl.when(even)
    def _():
        fill_h(same_ref)
        fill_n(other_ref)

    @pl.when(jnp.logical_not(even))
    def _():
        fill_n(same_ref)
        fill_h(other_ref)


def prep(hot, place, cluster_of, states, proj_weight):
    docs, width = states.shape[0], proj_weight.shape[1]
    rest = docs - hot
    shape = jax.ShapeDtypeStruct
    vmem = pl.BlockSpec(memory_space=pltpu.VMEM)
    return pl.pallas_call(
        lambda *refs: prep_kernel(hot, *refs),
        out_shape=(
            shape((rest + META, width), BF16),
            shape((rest + META, width), BF16),
            shape((1, docs), jnp.int32),
        ),
        in_specs=[pl.BlockSpec(memory_space=pltpu.SMEM), vmem, vmem, vmem],
        scratch_shapes=[pltpu.VMEM((docs, width), BF16), pltpu.VMEM((docs, width), F32)],
        compiler_params=pltpu.CompilerParams(vmem_limit_bytes=24 * 2**20),
        name="prep",
    )(place, cluster_of.reshape(1, docs), states, proj_weight)


OWN, PAIR = "own", "pair"
CORE, PAIR_CORE = "core", "pair_core"
ROW, PAIR_ROW = "row", "pair_row"
DIAG, PAIR_DIAG = "diag", "pair_diag"
NEXT, FAR = "next", "far"
GROUPS = ((OWN, PAIR, ROW, PAIR_ROW), (CORE, PAIR_CORE, DIAG, PAIR_DIAG), (NEXT,), (FAR,))
TILE = 256
HERE, THERE, ACROSS = (OWN, CORE), (PAIR, PAIR_CORE), (ROW, DIAG)


def score_kernel(docs, hot, names, given, made, tasks, doubted, carries, *refs):
    rest, first, flag, lanes = layout(docs, hot)
    place_ref, refs = refs[0], refs[1:]
    blocks, refs = dict(zip(names, refs[:len(names)])), refs[len(names):]
    pairs, refs = {p: refs[2 * k:2 * k + 2] for k, p in enumerate(given)}, refs[2 * len(given):]
    before, refs = refs[:len(GROUPS) * carries], refs[len(GROUPS) * carries:]
    outs, refs = refs[:len(GROUPS)], refs[len(GROUPS):]
    if made:
        pairs[made], refs = refs[:2], refs[2:]
    parts = refs[-1]
    for k, out in enumerate(outs):
        out[...] = before[k][...] if carries else jnp.zeros(out.shape, F32)
    spots = {name: (out, k) for out, group in zip(outs, GROUPS) for k, name in enumerate(group)}
    z, y, c = place_ref[0], place_ref[1], place_ref[2]
    when = {"core0": c == 0, "core1": c == 1, "row0": y == 0, "row1": y == 1}
    middle = (z == 1) | (z == 2)

    def meet(count, start):
        lane = slice(start, start + count)
        wide, two = up(count, 128), 2 * count
        columns = {name: ref[rest:, 0:wide].astype(F32)[0:8, :].T[0:count, :] for name, ref in blocks.items()}
        if made:
            turned, notes = pairs[made]
            turned[:, 0:two] = jnp.concatenate([blocks[name][:count, :] for name in made], axis=0).T
            notes[:, 0:two] = jnp.concatenate([columns[name] for name in made], axis=0).T

        for left in dict.fromkeys(task[0] for task in tasks):

            def work(left=left):
                own_tasks = [task for task in tasks if task[0] == left]
                rows = count * len(left)
                block = blocks[left[0]][:count, :]
                column = columns[left[0]][:, 0:1]
                for name in left[1:]:
                    block = jnp.concatenate([block, blocks[name][:count, :]], axis=0)
                    column = jnp.concatenate([column, columns[name][:, 0:1]], axis=0)
                fresh = True
                for _, right, both, _ in own_tasks:
                    if right in blocks:
                        span, rights, diagonal = count, (right,), False
                        ids = blocks[right][rest:, 0:wide].astype(F32)[0:1, 0:count]
                    else:
                        turned, notes = pairs[right]
                        span, rights, diagonal = two if both else wide, right[:1 + both], left == right[:1]
                        ids = notes[0:1, 0:span]
                        if not both:
                            ids = jnp.where(lax.broadcasted_iota(jnp.int32, ids.shape, 1) < count, ids, -1.0)
                    totals = []
                    for low in range(0, span, TILE):
                        high = min(low + TILE, span)
                        if right in blocks:
                            inner = lax.dot_general(
                                block, blocks[right][low:high, :], (((1,), (1,)), ((), ())),
                                preferred_element_type=F32,
                            )
                        else:
                            inner = jnp.dot(block, turned[:, low:high], preferred_element_type=F32)
                        same = column == ids[:, low:high]
                        if diagonal:
                            same &= lax.broadcasted_iota(jnp.int32, inner.shape, 0) != (
                                lax.broadcasted_iota(jnp.int32, inner.shape, 1) + low
                            )
                        weights = jnp.where(same, jnp.exp2(inner), 0.0)
                        totals.append(jnp.sum(weights, axis=0, keepdims=True))
                        if not diagonal:
                            part = None
                            for t in range(0, high - low, 128):
                                piece = weights[:, t:t + 128]
                                if piece.shape[1] < 128:
                                    blank = jnp.zeros((rows, 128 - piece.shape[1]), F32)
                                    piece = jnp.concatenate([piece, blank], axis=1)
                                part = piece if part is None else part + piece
                            if fresh:
                                parts[0:rows, :] = part
                            else:
                                parts[0:rows, :] += part
                            fresh = False
                    total = jnp.concatenate(totals, axis=1) if len(totals) > 1 else totals[0]
                    for k, name in enumerate(rights):
                        out, spot = spots[name]
                        out[spot, :, lane] += total[:, k * count:(k + 1) * count]
                if not fresh:
                    part = parts[0:rows, :]
                    high = part.astype(BF16)
                    low = (part - high.astype(F32)).astype(BF16)
                    total = lax.dot_general(
                        jnp.ones((16, 256), BF16), jnp.concatenate([high, low], axis=1),
                        (((1,), (1,)), ((), ())), preferred_element_type=F32,
                    )
                    for k, name in enumerate(left):
                        out, spot = spots[name]
                        out[spot, :, lane] += total[0:1, k * count:(k + 1) * count]

            condition = [task[3] for task in tasks if task[0] == left][0]
            if left[0] in (NEXT, FAR):
                pl.when(middle)(work)
            elif condition:
                pl.when(when[condition])(work)
            else:
                work()

    pl.when(lax.rem(z, 2) == 0)(lambda: meet(hot, first))
    pl.when(lax.rem(z, 2) == 1)(lambda: meet(rest, 0))

    if doubted:
        doubt = sum(blocks[name][rest:, first:first + 128].astype(F32)[0:1, 0:1] for name in doubted)
        out, k = spots[FAR]
        out[k] += jnp.where(lax.broadcasted_iota(jnp.int32, (1, lanes), 1) == flag, doubt, 0.0)


def score(name, docs, hot, place, blocks, pairs, made, tasks, sums, doubted=(), weight=1):
    rest, _, _, lanes = layout(docs, hot)
    names = list(dict.fromkeys([*made, *(name for task in tasks for name in task[0])]))
    given = [p for p in pairs if any(p == task[1] for task in tasks)]
    width = blocks[OWN].shape[1]
    vmem = pl.BlockSpec(memory_space=pltpu.VMEM)
    arrays = [blocks[b] for b in names] + [a for p in given for a in pairs[p]] + list(sums)
    shapes = [jax.ShapeDtypeStruct((len(group), 1, lanes), F32) for group in GROUPS]
    if made:
        shapes += [jax.ShapeDtypeStruct((width, 2 * rest), BF16), jax.ShapeDtypeStruct((8, 2 * rest), F32)]
    out = pl.pallas_call(
        lambda *refs: score_kernel(docs, hot, names, given, made, tasks, doubted or made, bool(sums), *refs),
        out_shape=tuple(shapes),
        in_specs=[pl.BlockSpec(memory_space=pltpu.SMEM)] + [vmem] * len(arrays),
        out_specs=tuple(vmem for _ in shapes),
        scratch_shapes=[pltpu.VMEM((2 * rest, 128), F32)],
        compiler_params=pltpu.CompilerParams(vmem_limit_bytes=20 * 2**20),
        cost_estimate=pl.CostEstimate(flops=weight, bytes_accessed=2**10, transcendentals=0),
        name=name,
    )(place, *arrays)
    count = len(GROUPS)
    return out[:count], {**pairs, made: out[count:]} if made else pairs


def finish_kernel(slot_ref, *refs):
    sums, out_ref = refs[:-1], refs[-1]
    total = sums[0][0]
    for ref in sums[1:]:
        total += ref[0]
    lanes, docs = total.shape[1], slot_ref.shape[1]
    values = jnp.broadcast_to(jnp.log(1.0 + total * 2.0**-SHIFT), (8, lanes)).T[:, 0:1]
    here = lax.broadcasted_iota(jnp.int32, (lanes, docs), 0) == slot_ref[...]
    out_ref[...] = jnp.sum(jnp.where(here, values, 0.0), axis=0, keepdims=True)


def finish(slot, sums):
    return pl.pallas_call(
        finish_kernel,
        out_shape=jax.ShapeDtypeStruct(slot.shape, F32),
        compiler_params=pltpu.CompilerParams(vmem_limit_bytes=6 * 2**20),
        name="finish",
    )(slot, *sums)


def decide_kernel(flag, mine_ref, theirs_ref, out_ref):
    out_ref[0] = (jnp.sum(mine_ref[0][:, flag:flag + 1] + theirs_ref[0][:, flag:flag + 1]) > 0.0).astype(jnp.int32)


def decide(flag, mine, theirs):
    return pl.pallas_call(
        lambda *refs: decide_kernel(flag, *refs),
        out_shape=jax.ShapeDtypeStruct((1,), jnp.int32),
        out_specs=pl.BlockSpec(memory_space=pltpu.SMEM),
        compiler_params=pltpu.CompilerParams(vmem_limit_bytes=2 * 2**20),
        name="decide",
    )(mine, theirs)


def meeting_plan(states, proj_weight, cluster_of):
    owners = lax.axis_size("owner")
    columns = owners // ROWS
    docs = states.shape[0]
    hot = 3 * docs // owners
    flag = layout(docs, hot)[2]

    owner, core = lax.axis_index("owner"), lax.axis_index("split")
    place = jnp.stack([owner // ROWS, owner % ROWS, core]).astype(jnp.int32)
    same, other, slot = prep(hot, place, cluster_of, states, proj_weight)

    def move(a, to, row=0, core=0):
        pairs = [
            (
                (z * ROWS + y) * 2 + c,
                (to[z] * ROWS + (y ^ row)) * 2 + (c ^ (core if row or to[z] != z else 1)),
            )
            for z in range(columns) for y in range(ROWS) for c in range(2)
        ]
        return lax.ppermute(a, ("owner", "split"), pairs)

    STAY, OUTER, MIDDLE, TWO = (0, 1, 2, 3), (1, 0, 3, 2), (0, 2, 1, 3), (2, 3, 0, 1)
    TO_MIDDLE = (2, 0, 3, 1)

    def meet(name, made, tasks, **options):
        return score(name, docs, hot, place, blocks, pairs, made, tasks, sums, **options)

    blocks, pairs, sums = {OWN: same}, {}, ()
    blocks[CORE] = move(same, STAY, core=1)
    blocks[PAIR] = move(other, OUTER)
    blocks[CORE], still_same, other = lax.optimization_barrier((blocks[CORE], same, other))
    blocks[ROW] = move(still_same, STAY, row=1)
    blocks[NEXT] = move(other, MIDDLE)
    sums, pairs = meet("own", HERE, [((OWN,), HERE, False, None), ((CORE,), HERE, False, "core0")], weight=2**33)

    blocks[PAIR], _ = lax.optimization_barrier((blocks[PAIR], sums[0]))
    blocks[ROW], blocks[NEXT] = lax.optimization_barrier((blocks[ROW], blocks[NEXT]))
    blocks[FAR] = move(same, TO_MIDDLE)
    blocks[PAIR_ROW] = move(blocks[PAIR], STAY, row=1)
    blocks[PAIR_CORE] = move(blocks[PAIR], STAY, core=1)
    blocks[DIAG] = move(blocks[ROW], STAY, core=1)
    sums, pairs = meet(
        "pair", THERE,
        [((PAIR,), THERE, False, None), ((PAIR_CORE,), THERE, False, "core1"), ((NEXT,), HERE, True, None),
         ((NEXT,), THERE, True, None)],
        weight=2**33,
    )
    sums, pairs = meet(
        "row", ACROSS,
        [((PAIR,), HERE, True, None), ((PAIR,), ACROSS, True, None), ((NEXT,), ACROSS, True, None),
         ((ROW,), HERE, False, "row0"), ((DIAG,), HERE, False, "row1")],
    )
    blocks[PAIR_ROW], _ = lax.optimization_barrier((blocks[PAIR_ROW], sums[0]))
    blocks[PAIR_DIAG] = move(blocks[PAIR_ROW], STAY, core=1)
    sums, pairs = meet("far", (), [((FAR,), p, True, None) for p in (HERE, THERE, ACROSS)])
    sums, pairs = meet(
        "last", (),
        [((NEXT, FAR), right, False, None) for right in (PAIR_ROW, PAIR_DIAG)]
        + [((PAIR_ROW,), THERE, False, "row1"), ((PAIR_DIAG,), THERE, False, "row0")],
        doubted=(PAIR_ROW, PAIR_DIAG),
    )
    kept, by_core, to_next, to_far = sums
    from_core, from_far = move(by_core, STAY, core=1), move(to_far, TWO)
    from_core, to_next = lax.optimization_barrier((from_core, to_next))
    from_next = move(to_next, MIDDLE)
    own, pair, row, pair_row = (kept[k:k + 1] + from_core[k:k + 1] for k in (0, 1, 2, 3))
    home = [
        own, from_next, from_far,
        move(pair, OUTER), move(row, STAY, row=1), move(pair_row, OUTER, row=1),
    ]
    return lax.cond(
        decide(flag, to_far, from_far)[0] > 0,
        lambda states, proj_weight, cluster_of, *_: ring_plan(states, proj_weight, cluster_of),
        lambda states, proj_weight, cluster_of, slot, *home: finish(slot, home).reshape(docs),
        states, proj_weight, cluster_of, slot, *home,
    )


def on_device(states, proj_weight, cluster_of):
    if (lax.axis_size("owner"), lax.axis_size("split")) == (8, 2) and states.shape[0] == 512:
        return meeting_plan(states, proj_weight, cluster_of)
    return owner_plan(states, proj_weight, cluster_of)


def solution(mesh):
    placed = (P(("parts", "owner", "split"), None), P(), P(("parts", "owner", "split")))
    return jax.shard_map(
        on_device,
        mesh=mesh,
        in_specs=placed,
        out_specs=P(("parts", "owner", "split")),
        check_vma=False,
    )
```

```python
import math

import jax
import jax.numpy as jnp
from jax import lax
from jax.experimental import pallas as pl
from jax.experimental.pallas import tpu as pltpu
from jax.sharding import PartitionSpec as P

CLUS_OWN = 2
TAU = 0.05
THRESH = 0.2
EPS = 1e-06
LOG2E = math.log2(math.e)
SCALE = LOG2E / TAU
SHIFT = THRESH * LOG2E / TAU

ROWS = 2
F32 = jnp.float32
BF16 = jnp.bfloat16


def prepare(states, proj_weight):
    projected = jnp.dot(states, proj_weight, preferred_element_type=jnp.float32)
    unit = projected * lax.rsqrt(jnp.sum(projected * projected, axis=1, keepdims=True) + EPS)
    peak = jnp.max(jnp.abs(unit), axis=1).astype(jnp.bfloat16)
    quant = (unit / peak.astype(jnp.float32)[:, None]).astype(jnp.bfloat16)
    return (quant, peak)


def similarity_scores(
    own_quant, own_peak, own_cluster, own_index, col_quant, col_peak, col_cluster, col_index
):
    row_count = own_quant.shape[0]
    block = math.gcd(row_count, 768)
    col_scale = col_peak.astype(jnp.float32)

    def one_block(start):
        quant_rows = lax.dynamic_slice_in_dim(own_quant, start, block, 0)
        scale_rows = lax.dynamic_slice_in_dim(own_peak, start, block, 0).astype(jnp.float32)
        cluster_rows = lax.dynamic_slice_in_dim(own_cluster, start, block, 0)
        index_rows = lax.dynamic_slice_in_dim(own_index, start, block, 0)
        inner = lax.dot_general(
            quant_rows, col_quant, (((1,), (1,)), ((), ())), preferred_element_type=jnp.float32
        )
        cosine = inner * scale_rows[:, None] * col_scale[None, :]
        same = (cluster_rows[:, None] == col_cluster[None, :]) & (
            index_rows[:, None] != col_index[None, :]
        )
        weights = jnp.where(same, jnp.exp((cosine - THRESH) / TAU), jnp.zeros_like(cosine))
        return jnp.log(1.0 + jnp.sum(weights, axis=1))

    starts = jnp.arange(row_count // block, dtype=jnp.int32) * block
    return lax.map(one_block, starts).reshape(row_count)


def owner_plan(states, proj_weight, cluster_of):
    owners = lax.axis_size("owner")
    splits = lax.axis_size("split")
    half_index = lax.axis_index("split")
    doc_count = states.shape[0]
    capacity = 3 * doc_count // owners
    width = proj_weight.shape[1]
    slot_total = owners * capacity
    quant, peak = prepare(states, proj_weight)
    group_of = cluster_of // CLUS_OWN
    onehot = (group_of[:, None] == jnp.arange(owners, dtype=jnp.int32)[None, :]).astype(jnp.int32)
    before = jnp.cumsum(onehot, axis=0) - onehot
    target = group_of * capacity + jnp.sum(before * onehot, axis=1)
    quant_slots = (
        jnp.zeros((slot_total, width), jnp.bfloat16)
        .at[target]
        .set(quant)
        .reshape(owners, capacity, width)
    )
    peak_slots = (
        jnp.zeros((slot_total,), jnp.bfloat16).at[target].set(peak).reshape(owners, capacity)
    )
    cluster_slots = (
        jnp.full((slot_total,), -1, jnp.int32).at[target].set(cluster_of).reshape(owners, capacity)
    )
    positions = (
        jnp.arange(owners, dtype=jnp.int32)[:, None] * (splits * capacity)
        + jnp.arange(capacity, dtype=jnp.int32)[None, :]
    )
    own_index = (positions + half_index * capacity).reshape(slot_total)
    col_index = jnp.arange(splits * slot_total, dtype=jnp.int32)
    own_quant, own_peak, own_cluster = (
        lax.all_to_all(a, "owner", split_axis=0, concat_axis=0, tiled=True)
        for a in (quant_slots, peak_slots, cluster_slots)
    )
    all_quant, all_peak, all_cluster = (
        lax.all_gather(a, "split", axis=1, tiled=True) for a in (own_quant, own_peak, own_cluster)
    )
    scores = similarity_scores(
        own_quant.reshape(slot_total, width),
        own_peak.reshape(slot_total),
        own_cluster.reshape(slot_total),
        own_index,
        all_quant.reshape(splits * slot_total, width),
        all_peak.reshape(splits * slot_total),
        all_cluster.reshape(splits * slot_total),
        col_index,
    )
    returned = lax.all_to_all(
        scores.reshape(owners, capacity), "owner", split_axis=0, concat_axis=0, tiled=True
    )
    return returned.reshape(slot_total)[target]


def ring_plan(states, proj_weight, cluster_of):
    axes = ("owner", "split")
    devices = lax.axis_size("owner") * lax.axis_size("split")
    ring = [(i, (i + 1) % devices) for i in range(devices)]
    quant, peak = prepare(states, proj_weight)
    scale = peak.astype(F32)
    place = jnp.arange(states.shape[0], dtype=jnp.int32)

    def weights(block, block_peak, block_cluster):
        inner = lax.dot_general(quant, block, (((1,), (1,)), ((), ())), preferred_element_type=F32)
        cosine = inner * scale[:, None] * block_peak.astype(F32)[None, :]
        same = cluster_of[:, None] == block_cluster[None, :]
        return jnp.where(same, jnp.exp((cosine - THRESH) / TAU), jnp.zeros_like(cosine))

    def meet(_, carry):
        passed = [lax.ppermute(a, axes, ring) for a in carry[1:]]
        return (carry[0] + jnp.sum(weights(*passed), axis=1), *passed)

    own = (quant, peak, cluster_of)
    others = place[:, None] != place[None, :]
    total = jnp.sum(jnp.where(others, weights(*own), 0.0), axis=1)
    total = lax.fori_loop(1, devices, meet, (total, *own))[0]
    return jnp.log(1.0 + total)


def up(n, m):
    return -(-n // m) * m


META = 8


def layout(docs, hot):
    rest = docs - hot
    first = up(rest, 128)
    flag = first + hot
    return rest, first, flag, up(flag + 1, 128)


def prep_kernel(hot, place_ref, cl_ref, st_ref, w_ref, same_ref, other_ref, slot_ref, vectors):
    docs = st_ref.shape[0]
    rest, first, flag, lanes = layout(docs, hot)
    tile = 128

    cluster = cl_ref[...]
    group = cluster // CLUS_OWN
    member = lax.broadcasted_iota(jnp.int32, (8, docs), 0) == group
    full = jnp.sum(member.astype(F32), axis=1, keepdims=True) == float(hot)
    chosen = jnp.min(
        jnp.where(full, lax.broadcasted_iota(jnp.int32, (8, 1), 0), 8), axis=0, keepdims=True
    )
    doubt = jnp.where(jnp.sum(full.astype(F32), axis=0, keepdims=True) == 1.0, 0.0, 1.0)
    in_hot = group == chosen

    for t in range(docs // tile):
        rows = slice(t * tile, (t + 1) * tile)
        projected = jnp.dot(st_ref[rows, :], w_ref[...], preferred_element_type=F32)
        norm = lax.rsqrt(jnp.sum(projected * projected, axis=1, keepdims=True) + EPS)
        vectors[rows, :] = (projected * (norm * math.sqrt(SCALE))).astype(BF16)

    ahead = (
        lax.broadcasted_iota(jnp.int32, (docs, docs), 0) < lax.broadcasted_iota(jnp.int32, (docs, docs), 1)
    ).astype(F32).astype(BF16)
    hot_rows = jnp.broadcast_to(in_hot.astype(F32), (8, docs)).astype(BF16)
    rank = jnp.dot(hot_rows, ahead, preferred_element_type=F32)[0:1, :].astype(jnp.int32)
    place = lax.broadcasted_iota(jnp.int32, (1, docs), 1)
    slot = jnp.where(in_hot, first + rank, place - rank)
    slot_ref[...] = slot

    sort = (lax.broadcasted_iota(jnp.int32, (lanes, docs), 0) == slot).astype(F32).astype(BF16)
    cluster_rows = jnp.broadcast_to(cluster.astype(F32), (META, docs)).astype(BF16)
    sorted_n = jnp.dot(sort[:rest, :], vectors[...], preferred_element_type=F32).astype(BF16)
    sorted_h = jnp.dot(sort[first:flag, :], vectors[...], preferred_element_type=F32).astype(BF16)
    ids = lax.dot_general(
        cluster_rows, sort, (((1,), (1,)), ((), ())), preferred_element_type=F32
    )
    ids = ids.astype(BF16)


    def fill_n(ref):
        ref[:rest, :] = sorted_n
        ref[rest:, :] = jnp.zeros((META, ref.shape[1]), BF16)
        ref[rest:, :first] = ids[:, :first]
        ref[rest:, first:first + 128] = jnp.broadcast_to(doubt.astype(BF16), (META, 128))

    def fill_h(ref):
        ref[:hot, :] = sorted_h
        ref[hot:, :] = jnp.zeros((rest + META - hot, ref.shape[1]), BF16)
        ref[rest:, :lanes - first] = ids[:, first:]
        ref[rest:, first:first + 128] = jnp.broadcast_to(doubt.astype(BF16), (META, 128))

    even = lax.rem(place_ref[0], 2) == 0

    @pl.when(even)
    def _():
        fill_h(same_ref)
        fill_n(other_ref)

    @pl.when(jnp.logical_not(even))
    def _():
        fill_n(same_ref)
        fill_h(other_ref)


def prep(hot, place, cluster_of, states, proj_weight):
    docs, width = states.shape[0], proj_weight.shape[1]
    rest = docs - hot
    shape = jax.ShapeDtypeStruct
    vmem = pl.BlockSpec(memory_space=pltpu.VMEM)
    return pl.pallas_call(
        lambda *refs: prep_kernel(hot, *refs),
        out_shape=(
            shape((rest + META, width), BF16),
            shape((rest + META, width), BF16),
            shape((1, docs), jnp.int32),
        ),
        in_specs=[pl.BlockSpec(memory_space=pltpu.SMEM), vmem, vmem, vmem],
        scratch_shapes=[pltpu.VMEM((docs, width), BF16)],
        compiler_params=pltpu.CompilerParams(vmem_limit_bytes=24 * 2**20),
        name="prep",
    )(place, cluster_of.reshape(1, docs), states, proj_weight)


OWN, PAIR = "own", "pair"
CORE, PAIR_CORE = "core", "pair_core"
ROW, PAIR_ROW = "row", "pair_row"
DIAG, PAIR_DIAG = "diag", "pair_diag"
NEXT, FAR = "next", "far"
GROUPS = ((OWN, PAIR, ROW, PAIR_ROW), (CORE, PAIR_CORE, DIAG, PAIR_DIAG), (NEXT,), (FAR,))
HERE, THERE, ACROSS = (OWN, CORE), (PAIR, PAIR_CORE), (ROW, DIAG)


def score_kernel(docs, hot, names, given, made, tasks, doubted, carries, *refs):
    rest, first, flag, lanes = layout(docs, hot)
    place_ref, refs = refs[0], refs[1:]
    blocks, refs = dict(zip(names, refs[:len(names)])), refs[len(names):]
    pairs, refs = {p: refs[2 * k:2 * k + 2] for k, p in enumerate(given)}, refs[2 * len(given):]
    before, refs = refs[:len(GROUPS) * carries], refs[len(GROUPS) * carries:]
    outs, refs = refs[:len(GROUPS)], refs[len(GROUPS):]
    if made:
        pairs[made], refs = refs[:2], refs[2:]
    parts = refs[-1]
    for k, out in enumerate(outs):
        out[...] = before[k][...] if carries else jnp.zeros(out.shape, F32)
    spots = {name: (out, k) for out, group in zip(outs, GROUPS) for k, name in enumerate(group)}
    z, y, c = place_ref[0], place_ref[1], place_ref[2]
    when = {"core0": c == 0, "core1": c == 1, "row0": y == 0, "row1": y == 1}
    middle = (z == 1) | (z == 2)

    def meet(count, start):
        lane = slice(start, start + count)
        wide, two = up(count, 128), 2 * count
        columns = {name: ref[rest:, 0:wide].astype(F32)[0:8, :].T[0:count, :] for name, ref in blocks.items()}
        if made:
            turned, notes = pairs[made]
            turned[:, 0:two] = jnp.concatenate([blocks[name][:count, :] for name in made], axis=0).T
            notes[:, 0:two] = jnp.concatenate([columns[name] for name in made], axis=0).T

        for left in dict.fromkeys(task[0] for task in tasks):

            def work(left=left):
                own_tasks = [task for task in tasks if task[0] == left]
                rows = count * len(left)
                block = blocks[left[0]][:count, :]
                column = columns[left[0]][:, 0:1]
                for name in left[1:]:
                    block = jnp.concatenate([block, blocks[name][:count, :]], axis=0)
                    column = jnp.concatenate([column, columns[name][:, 0:1]], axis=0)
                step = count // 2
                totals = [None] * len(own_tasks)
                fresh = True
                for top in range(0, rows, step):
                    part = None
                    for index, (_, right, both, _) in enumerate(own_tasks):
                        if right in blocks:
                            span, diagonal = count, False
                            ids = blocks[right][rest:, 0:wide].astype(F32)[0:1, 0:count]
                            inner = lax.dot_general(
                                block[top:top + step], blocks[right][:count, :], (((1,), (1,)), ((), ())),
                                preferred_element_type=F32,
                            )
                        else:
                            turned, notes = pairs[right]
                            span, diagonal = two if both else wide, left == right[:1]
                            ids = notes[0:1, 0:span]
                            if not both:
                                ids = jnp.where(lax.broadcasted_iota(jnp.int32, ids.shape, 1) < count, ids, -1.0)
                            inner = jnp.dot(
                                block[top:top + step], turned[:, 0:span], preferred_element_type=F32
                            )
                        same = column[top:top + step] == ids
                        if diagonal:
                            same &= lax.broadcasted_iota(jnp.int32, inner.shape, 0) + top != (
                                lax.broadcasted_iota(jnp.int32, inner.shape, 1)
                            )
                        weights = jnp.where(same, jnp.exp2(inner), 0.0)
                        total = jnp.sum(weights, axis=0, keepdims=True)
                        totals[index] = total if totals[index] is None else totals[index] + total
                        if not diagonal:
                            fresh = False
                            for t in range(0, span, 128):
                                piece = weights[:, t:t + 128]
                                if piece.shape[1] < 128:
                                    blank = jnp.zeros((step, 128 - piece.shape[1]), F32)
                                    piece = jnp.concatenate([piece, blank], axis=1)
                                part = piece if part is None else part + piece
                    if part is not None:
                        parts[top:top + step, :] = part
                for (_, right, both, _), total in zip(own_tasks, totals):
                    for k, name in enumerate((right,) if right in blocks else right[:1 + both]):
                        out, spot = spots[name]
                        out[spot, :, lane] += total[:, k * count:(k + 1) * count]
                if not fresh:
                    part = parts[0:rows, :]
                    high = part.astype(BF16)
                    low = (part - high.astype(F32)).astype(BF16)
                    total = lax.dot_general(
                        jnp.ones((16, 256), BF16), jnp.concatenate([high, low], axis=1),
                        (((1,), (1,)), ((), ())), preferred_element_type=F32,
                    )
                    for k, name in enumerate(left):
                        out, spot = spots[name]
                        out[spot, :, lane] += total[0:1, k * count:(k + 1) * count]

            condition = [task[3] for task in tasks if task[0] == left][0]
            if left[0] in (NEXT, FAR):
                pl.when(middle)(work)
            elif condition:
                pl.when(when[condition])(work)
            else:
                work()

    pl.when(lax.rem(z, 2) == 0)(lambda: meet(hot, first))
    pl.when(lax.rem(z, 2) == 1)(lambda: meet(rest, 0))

    if doubted:
        doubt = sum(blocks[name][rest:, first:first + 128].astype(F32)[0:1, 0:1] for name in doubted)
        out, k = spots[FAR]
        out[k] += jnp.where(lax.broadcasted_iota(jnp.int32, (1, lanes), 1) == flag, doubt, 0.0)


def score(name, docs, hot, place, blocks, pairs, made, tasks, sums, doubted=(), weight=1):
    rest, _, _, lanes = layout(docs, hot)
    names = list(dict.fromkeys([*made, *(name for task in tasks for name in task[0])]))
    given = [p for p in pairs if any(p == task[1] for task in tasks)]
    width = blocks[OWN].shape[1]
    vmem = pl.BlockSpec(memory_space=pltpu.VMEM)
    arrays = [blocks[b] for b in names] + [a for p in given for a in pairs[p]] + list(sums)
    shapes = [jax.ShapeDtypeStruct((len(group), 1, lanes), F32) for group in GROUPS]
    if made:
        shapes += [jax.ShapeDtypeStruct((width, 2 * rest), BF16), jax.ShapeDtypeStruct((8, 2 * rest), F32)]
    out = pl.pallas_call(
        lambda *refs: score_kernel(docs, hot, names, given, made, tasks, doubted or made, bool(sums), *refs),
        out_shape=tuple(shapes),
        in_specs=[pl.BlockSpec(memory_space=pltpu.SMEM)] + [vmem] * len(arrays),
        out_specs=tuple(vmem for _ in shapes),
        scratch_shapes=[pltpu.VMEM((2 * rest, 128), F32)],
        compiler_params=pltpu.CompilerParams(vmem_limit_bytes=20 * 2**20),
        cost_estimate=pl.CostEstimate(flops=weight, bytes_accessed=2**10, transcendentals=0),
        name=name,
    )(place, *arrays)
    count = len(GROUPS)
    return out[:count], {**pairs, made: out[count:]} if made else pairs


def finish_kernel(slot_ref, *refs):
    sums, out_ref = refs[:-1], refs[-1]
    total = sums[0][0]
    for ref in sums[1:]:
        total += ref[0]
    lanes, docs = total.shape[1], slot_ref.shape[1]
    values = jnp.broadcast_to(jnp.log(1.0 + total * 2.0**-SHIFT), (8, lanes)).T[:, 0:1]
    here = lax.broadcasted_iota(jnp.int32, (lanes, docs), 0) == slot_ref[...]
    out_ref[...] = jnp.sum(jnp.where(here, values, 0.0), axis=0, keepdims=True)


def finish(slot, sums):
    return pl.pallas_call(
        finish_kernel,
        out_shape=jax.ShapeDtypeStruct(slot.shape, F32),
        compiler_params=pltpu.CompilerParams(vmem_limit_bytes=6 * 2**20),
        name="finish",
    )(slot, *sums)


def decide_kernel(flag, mine_ref, theirs_ref, out_ref):
    out_ref[0] = (jnp.sum(mine_ref[0][:, flag:flag + 1] + theirs_ref[0][:, flag:flag + 1]) > 0.0).astype(jnp.int32)


def decide(flag, mine, theirs):
    return pl.pallas_call(
        lambda *refs: decide_kernel(flag, *refs),
        out_shape=jax.ShapeDtypeStruct((1,), jnp.int32),
        out_specs=pl.BlockSpec(memory_space=pltpu.SMEM),
        compiler_params=pltpu.CompilerParams(vmem_limit_bytes=2 * 2**20),
        name="decide",
    )(mine, theirs)


def meeting_plan(states, proj_weight, cluster_of):
    owners = lax.axis_size("owner")
    columns = owners // ROWS
    docs = states.shape[0]
    hot = 3 * docs // owners
    flag = layout(docs, hot)[2]

    owner, core = lax.axis_index("owner"), lax.axis_index("split")
    place = jnp.stack([owner // ROWS, owner % ROWS, core]).astype(jnp.int32)
    same, other, slot = prep(hot, place, cluster_of, states, proj_weight)

    def move(a, to, row=0, core=0):
        pairs = [
            (
                (z * ROWS + y) * 2 + c,
                (to[z] * ROWS + (y ^ row)) * 2 + (c ^ (core if row or to[z] != z else 1)),
            )
            for z in range(columns) for y in range(ROWS) for c in range(2)
        ]
        return lax.ppermute(a, ("owner", "split"), pairs)

    STAY, OUTER, MIDDLE, TWO = (0, 1, 2, 3), (1, 0, 3, 2), (0, 2, 1, 3), (2, 3, 0, 1)
    TO_MIDDLE = (2, 0, 3, 1)

    def meet(name, made, tasks, **options):
        return score(name, docs, hot, place, blocks, pairs, made, tasks, sums, **options)

    blocks, pairs, sums = {OWN: same}, {}, ()
    blocks[CORE] = move(same, STAY, core=1)
    blocks[PAIR] = move(other, OUTER)
    blocks[CORE], still_same, other = lax.optimization_barrier((blocks[CORE], same, other))
    blocks[ROW] = move(still_same, STAY, row=1)
    blocks[NEXT] = move(other, MIDDLE)
    sums, pairs = meet("own", HERE, [((OWN,), HERE, False, None), ((CORE,), HERE, False, "core0")], weight=2**33)

    blocks[PAIR], _ = lax.optimization_barrier((blocks[PAIR], sums[0]))
    blocks[ROW], blocks[NEXT] = lax.optimization_barrier((blocks[ROW], blocks[NEXT]))
    blocks[FAR] = move(same, TO_MIDDLE)
    blocks[PAIR_ROW] = move(blocks[PAIR], STAY, row=1)
    blocks[PAIR_CORE] = move(blocks[PAIR], STAY, core=1)
    blocks[DIAG] = move(blocks[ROW], STAY, core=1)
    sums, pairs = meet(
        "pair", THERE,
        [((PAIR,), THERE, False, None), ((PAIR_CORE,), THERE, False, "core1"), ((NEXT,), HERE, True, None),
         ((NEXT,), THERE, True, None)],
        weight=2**33,
    )
    sums, pairs = meet(
        "row", ACROSS,
        [((PAIR,), HERE, True, None), ((PAIR,), ACROSS, True, None), ((NEXT,), ACROSS, True, None),
         ((ROW,), HERE, False, "row0"), ((DIAG,), HERE, False, "row1")],
    )
    blocks[PAIR_ROW], _ = lax.optimization_barrier((blocks[PAIR_ROW], sums[0]))
    blocks[PAIR_DIAG] = move(blocks[PAIR_ROW], STAY, core=1)
    sums, pairs = meet("far", (), [((FAR,), p, True, None) for p in (HERE, THERE, ACROSS)])
    sums, pairs = meet(
        "last", (),
        [((NEXT, FAR), right, False, None) for right in (PAIR_ROW, PAIR_DIAG)]
        + [((PAIR_ROW,), THERE, False, "row1"), ((PAIR_DIAG,), THERE, False, "row0")],
        doubted=(PAIR_ROW, PAIR_DIAG),
    )
    kept, by_core, to_next, to_far = sums
    from_core, from_far = move(by_core, STAY, core=1), move(to_far, TWO)
    from_core, to_next = lax.optimization_barrier((from_core, to_next))
    from_next = move(to_next, MIDDLE)
    own, pair, row, pair_row = (kept[k:k + 1] + from_core[k:k + 1] for k in (0, 1, 2, 3))
    home = [
        own, from_next, from_far,
        move(pair, OUTER), move(row, STAY, row=1), move(pair_row, OUTER, row=1),
    ]
    return lax.cond(
        decide(flag, to_far, from_far)[0] > 0,
        lambda states, proj_weight, cluster_of, *_: ring_plan(states, proj_weight, cluster_of),
        lambda states, proj_weight, cluster_of, slot, *home: finish(slot, home).reshape(docs),
        states, proj_weight, cluster_of, slot, *home,
    )


def on_device(states, proj_weight, cluster_of):
    if (lax.axis_size("owner"), lax.axis_size("split")) == (8, 2) and states.shape[0] == 512:
        return meeting_plan(states, proj_weight, cluster_of)
    return owner_plan(states, proj_weight, cluster_of)


def solution(mesh):
    placed = (P(("parts", "owner", "split"), None), P(), P(("parts", "owner", "split")))
    return jax.shard_map(
        on_device,
        mesh=mesh,
        in_specs=placed,
        out_specs=P(("parts", "owner", "split")),
        check_vma=False,
    )
```

```python
import math

import jax
import jax.numpy as jnp
from jax import lax
from jax.experimental import pallas as pl
from jax.experimental.pallas import tpu as pltpu
from jax.sharding import PartitionSpec as P

CLUS_OWN = 2
TAU = 0.05
THRESH = 0.2
EPS = 1e-06
LOG2E = math.log2(math.e)
SCALE = LOG2E / TAU
SHIFT = THRESH * LOG2E / TAU

ROWS = 2
F32 = jnp.float32
BF16 = jnp.bfloat16


def prepare(states, proj_weight):
    projected = jnp.dot(states, proj_weight, preferred_element_type=jnp.float32)
    unit = projected * lax.rsqrt(jnp.sum(projected * projected, axis=1, keepdims=True) + EPS)
    peak = jnp.max(jnp.abs(unit), axis=1).astype(jnp.bfloat16)
    quant = (unit / peak.astype(jnp.float32)[:, None]).astype(jnp.bfloat16)
    return (quant, peak)


def similarity_scores(
    own_quant, own_peak, own_cluster, own_index, col_quant, col_peak, col_cluster, col_index
):
    row_count = own_quant.shape[0]
    block = math.gcd(row_count, 768)
    col_scale = col_peak.astype(jnp.float32)

    def one_block(start):
        quant_rows = lax.dynamic_slice_in_dim(own_quant, start, block, 0)
        scale_rows = lax.dynamic_slice_in_dim(own_peak, start, block, 0).astype(jnp.float32)
        cluster_rows = lax.dynamic_slice_in_dim(own_cluster, start, block, 0)
        index_rows = lax.dynamic_slice_in_dim(own_index, start, block, 0)
        inner = lax.dot_general(
            quant_rows, col_quant, (((1,), (1,)), ((), ())), preferred_element_type=jnp.float32
        )
        cosine = inner * scale_rows[:, None] * col_scale[None, :]
        same = (cluster_rows[:, None] == col_cluster[None, :]) & (
            index_rows[:, None] != col_index[None, :]
        )
        weights = jnp.where(same, jnp.exp((cosine - THRESH) / TAU), jnp.zeros_like(cosine))
        return jnp.log(1.0 + jnp.sum(weights, axis=1))

    starts = jnp.arange(row_count // block, dtype=jnp.int32) * block
    return lax.map(one_block, starts).reshape(row_count)


def owner_plan(states, proj_weight, cluster_of):
    owners = lax.axis_size("owner")
    splits = lax.axis_size("split")
    half_index = lax.axis_index("split")
    doc_count = states.shape[0]
    capacity = 3 * doc_count // owners
    width = proj_weight.shape[1]
    slot_total = owners * capacity
    quant, peak = prepare(states, proj_weight)
    group_of = cluster_of // CLUS_OWN
    onehot = (group_of[:, None] == jnp.arange(owners, dtype=jnp.int32)[None, :]).astype(jnp.int32)
    before = jnp.cumsum(onehot, axis=0) - onehot
    target = group_of * capacity + jnp.sum(before * onehot, axis=1)
    quant_slots = (
        jnp.zeros((slot_total, width), jnp.bfloat16)
        .at[target]
        .set(quant)
        .reshape(owners, capacity, width)
    )
    peak_slots = (
        jnp.zeros((slot_total,), jnp.bfloat16).at[target].set(peak).reshape(owners, capacity)
    )
    cluster_slots = (
        jnp.full((slot_total,), -1, jnp.int32).at[target].set(cluster_of).reshape(owners, capacity)
    )
    positions = (
        jnp.arange(owners, dtype=jnp.int32)[:, None] * (splits * capacity)
        + jnp.arange(capacity, dtype=jnp.int32)[None, :]
    )
    own_index = (positions + half_index * capacity).reshape(slot_total)
    col_index = jnp.arange(splits * slot_total, dtype=jnp.int32)
    own_quant, own_peak, own_cluster = (
        lax.all_to_all(a, "owner", split_axis=0, concat_axis=0, tiled=True)
        for a in (quant_slots, peak_slots, cluster_slots)
    )
    all_quant, all_peak, all_cluster = (
        lax.all_gather(a, "split", axis=1, tiled=True) for a in (own_quant, own_peak, own_cluster)
    )
    scores = similarity_scores(
        own_quant.reshape(slot_total, width),
        own_peak.reshape(slot_total),
        own_cluster.reshape(slot_total),
        own_index,
        all_quant.reshape(splits * slot_total, width),
        all_peak.reshape(splits * slot_total),
        all_cluster.reshape(splits * slot_total),
        col_index,
    )
    returned = lax.all_to_all(
        scores.reshape(owners, capacity), "owner", split_axis=0, concat_axis=0, tiled=True
    )
    return returned.reshape(slot_total)[target]


def ring_plan(states, proj_weight, cluster_of):
    axes = ("owner", "split")
    devices = lax.axis_size("owner") * lax.axis_size("split")
    ring = [(i, (i + 1) % devices) for i in range(devices)]
    quant, peak = prepare(states, proj_weight)
    scale = peak.astype(F32)
    place = jnp.arange(states.shape[0], dtype=jnp.int32)

    def weights(block, block_peak, block_cluster):
        inner = lax.dot_general(quant, block, (((1,), (1,)), ((), ())), preferred_element_type=F32)
        cosine = inner * scale[:, None] * block_peak.astype(F32)[None, :]
        same = cluster_of[:, None] == block_cluster[None, :]
        return jnp.where(same, jnp.exp((cosine - THRESH) / TAU), jnp.zeros_like(cosine))

    def meet(_, carry):
        passed = [lax.ppermute(a, axes, ring) for a in carry[1:]]
        return (carry[0] + jnp.sum(weights(*passed), axis=1), *passed)

    own = (quant, peak, cluster_of)
    others = place[:, None] != place[None, :]
    total = jnp.sum(jnp.where(others, weights(*own), 0.0), axis=1)
    total = lax.fori_loop(1, devices, meet, (total, *own))[0]
    return jnp.log(1.0 + total)


def up(n, m):
    return -(-n // m) * m


META = 8


def layout(docs, hot):
    rest = docs - hot
    first = up(rest, 128)
    flag = first + hot
    return rest, first, flag, up(flag + 1, 128)


def prep_kernel(hot, place_ref, cl_ref, st_ref, w_ref, same_ref, other_ref, slot_ref, vectors):
    docs = st_ref.shape[0]
    rest, first, flag, lanes = layout(docs, hot)
    tile = 128

    cluster = cl_ref[...]
    group = cluster // CLUS_OWN
    member = lax.broadcasted_iota(jnp.int32, (8, docs), 0) == group
    full = jnp.sum(member.astype(F32), axis=1, keepdims=True) == float(hot)
    chosen = jnp.min(
        jnp.where(full, lax.broadcasted_iota(jnp.int32, (8, 1), 0), 8), axis=0, keepdims=True
    )
    doubt = jnp.where(jnp.sum(full.astype(F32), axis=0, keepdims=True) == 1.0, 0.0, 1.0)
    in_hot = group == chosen

    for t in range(docs // tile):
        rows = slice(t * tile, (t + 1) * tile)
        projected = jnp.dot(st_ref[rows, :], w_ref[...], preferred_element_type=F32)
        norm = lax.rsqrt(jnp.sum(projected * projected, axis=1, keepdims=True) + EPS)
        vectors[rows, :] = (projected * (norm * math.sqrt(SCALE))).astype(BF16)

    hot_row = in_hot.astype(F32)
    runs = [hot_row[:, t:t + 128] for t in range(0, docs, 128)]
    ahead = (
        lax.broadcasted_iota(jnp.int32, (128, 128), 0) < lax.broadcasted_iota(jnp.int32, (128, 128), 1)
    ).astype(F32).astype(BF16)
    stack = jnp.concatenate(runs + [jnp.zeros((16 - len(runs), 128), F32)], axis=0)
    within = jnp.dot(stack.astype(BF16), ahead, preferred_element_type=F32)
    sizes = jnp.sum(stack, axis=1, keepdims=True)
    ranks, before = [], jnp.zeros((1, 1), F32)
    for k in range(len(runs)):
        ranks.append(within[k:k + 1, :] + before)
        before = before + sizes[k:k + 1, :]
    rank = jnp.concatenate(ranks, axis=1).astype(jnp.int32)
    place = lax.broadcasted_iota(jnp.int32, (1, docs), 1)
    slot = jnp.where(in_hot, first + rank, place - rank)
    slot_ref[...] = slot

    sort = (lax.broadcasted_iota(jnp.int32, (lanes, docs), 0) == slot).astype(F32).astype(BF16)
    cluster_rows = jnp.broadcast_to(cluster.astype(F32), (META, docs)).astype(BF16)
    sorted_n = jnp.dot(sort[:rest, :], vectors[...], preferred_element_type=F32).astype(BF16)
    sorted_h = jnp.dot(sort[first:flag, :], vectors[...], preferred_element_type=F32).astype(BF16)
    ids = lax.dot_general(
        cluster_rows, sort, (((1,), (1,)), ((), ())), preferred_element_type=F32
    )
    ids = ids.astype(BF16)


    def fill_n(ref):
        ref[:rest, :] = sorted_n
        ref[rest:, :] = jnp.zeros((META, ref.shape[1]), BF16)
        ref[rest:, :first] = ids[:, :first]
        ref[rest:, first:first + 128] = jnp.broadcast_to(doubt.astype(BF16), (META, 128))

    def fill_h(ref):
        ref[:hot, :] = sorted_h
        ref[hot:, :] = jnp.zeros((rest + META - hot, ref.shape[1]), BF16)
        ref[rest:, :lanes - first] = ids[:, first:]
        ref[rest:, first:first + 128] = jnp.broadcast_to(doubt.astype(BF16), (META, 128))

    even = lax.rem(place_ref[0], 2) == 0

    @pl.when(even)
    def _():
        fill_h(same_ref)
        fill_n(other_ref)

    @pl.when(jnp.logical_not(even))
    def _():
        fill_n(same_ref)
        fill_h(other_ref)


def prep(hot, place, cluster_of, states, proj_weight):
    docs, width = states.shape[0], proj_weight.shape[1]
    rest = docs - hot
    shape = jax.ShapeDtypeStruct
    vmem = pl.BlockSpec(memory_space=pltpu.VMEM)
    return pl.pallas_call(
        lambda *refs: prep_kernel(hot, *refs),
        out_shape=(
            shape((rest + META, width), BF16),
            shape((rest + META, width), BF16),
            shape((1, docs), jnp.int32),
        ),
        in_specs=[pl.BlockSpec(memory_space=pltpu.SMEM), vmem, vmem, vmem],
        scratch_shapes=[pltpu.VMEM((docs, width), BF16)],
        compiler_params=pltpu.CompilerParams(vmem_limit_bytes=24 * 2**20),
        name="prep",
    )(place, cluster_of.reshape(1, docs), states, proj_weight)


OWN, PAIR = "own", "pair"
CORE, PAIR_CORE = "core", "pair_core"
ROW, PAIR_ROW = "row", "pair_row"
DIAG, PAIR_DIAG = "diag", "pair_diag"
NEXT, FAR = "next", "far"
GROUPS = ((OWN, PAIR, ROW, PAIR_ROW), (CORE, PAIR_CORE, DIAG, PAIR_DIAG), (NEXT,), (FAR,))
TILE = 256
HERE, THERE, ACROSS = (OWN, CORE), (PAIR, PAIR_CORE), (ROW, DIAG)


def score_kernel(docs, hot, names, given, made, tasks, doubted, carries, *refs):
    rest, first, flag, lanes = layout(docs, hot)
    place_ref, refs = refs[0], refs[1:]
    blocks, refs = dict(zip(names, refs[:len(names)])), refs[len(names):]
    pairs, refs = {p: refs[2 * k:2 * k + 2] for k, p in enumerate(given)}, refs[2 * len(given):]
    before, refs = refs[:len(GROUPS) * carries], refs[len(GROUPS) * carries:]
    outs, refs = refs[:len(GROUPS)], refs[len(GROUPS):]
    if made:
        pairs[made], refs = refs[:2], refs[2:]
    parts = refs[-1]
    for k, out in enumerate(outs):
        out[...] = before[k][...] if carries else jnp.zeros(out.shape, F32)
    spots = {name: (out, k) for out, group in zip(outs, GROUPS) for k, name in enumerate(group)}
    z, y, c = place_ref[0], place_ref[1], place_ref[2]
    when = {"core0": c == 0, "core1": c == 1, "row0": y == 0, "row1": y == 1}
    middle = (z == 1) | (z == 2)

    def meet(count, start):
        lane = slice(start, start + count)
        wide, two = up(count, 128), 2 * count
        columns = {name: ref[rest:, 0:wide].astype(F32)[0:8, :].T[0:count, :] for name, ref in blocks.items()}
        if made:
            turned, notes = pairs[made]
            turned[:, 0:two] = jnp.concatenate([blocks[name][:count, :] for name in made], axis=0).T
            notes[:, 0:two] = jnp.concatenate([columns[name] for name in made], axis=0).T

        for left in dict.fromkeys(task[0] for task in tasks):

            def work(left=left):
                own_tasks = [task for task in tasks if task[0] == left]
                rows = count * len(left)
                block = blocks[left[0]][:count, :]
                column = columns[left[0]][:, 0:1]
                for name in left[1:]:
                    block = jnp.concatenate([block, blocks[name][:count, :]], axis=0)
                    column = jnp.concatenate([column, columns[name][:, 0:1]], axis=0)
                fresh = True
                for _, right, both, _ in own_tasks:
                    if right in blocks:
                        span, rights, diagonal = count, (right,), False
                        ids = blocks[right][rest:, 0:wide].astype(F32)[0:1, 0:count]
                    else:
                        turned, notes = pairs[right]
                        span, rights, diagonal = two if both else wide, right[:1 + both], left == right[:1]
                        ids = notes[0:1, 0:span]
                        if not both:
                            ids = jnp.where(lax.broadcasted_iota(jnp.int32, ids.shape, 1) < count, ids, -1.0)
                    totals = []
                    for low in range(0, span, TILE):
                        high = min(low + TILE, span)
                        if right in blocks:
                            inner = lax.dot_general(
                                block, blocks[right][low:high, :], (((1,), (1,)), ((), ())),
                                preferred_element_type=F32,
                            )
                        else:
                            inner = jnp.dot(block, turned[:, low:high], preferred_element_type=F32)
                        same = column == ids[:, low:high]
                        if diagonal:
                            same &= lax.broadcasted_iota(jnp.int32, inner.shape, 0) != (
                                lax.broadcasted_iota(jnp.int32, inner.shape, 1) + low
                            )
                        weights = jnp.where(same, jnp.exp2(inner), 0.0)
                        totals.append(jnp.sum(weights, axis=0, keepdims=True))
                        if not diagonal:
                            part = None
                            for t in range(0, high - low, 128):
                                piece = weights[:, t:t + 128]
                                if piece.shape[1] < 128:
                                    blank = jnp.zeros((rows, 128 - piece.shape[1]), F32)
                                    piece = jnp.concatenate([piece, blank], axis=1)
                                part = piece if part is None else part + piece
                            if fresh:
                                parts[0:rows, :] = part
                            else:
                                parts[0:rows, :] += part
                            fresh = False
                    total = jnp.concatenate(totals, axis=1) if len(totals) > 1 else totals[0]
                    for k, name in enumerate(rights):
                        out, spot = spots[name]
                        out[spot, :, lane] += total[:, k * count:(k + 1) * count]
                if not fresh:
                    part = parts[0:rows, :]
                    high = part.astype(BF16)
                    low = (part - high.astype(F32)).astype(BF16)
                    total = lax.dot_general(
                        jnp.ones((16, 256), BF16), jnp.concatenate([high, low], axis=1),
                        (((1,), (1,)), ((), ())), preferred_element_type=F32,
                    )
                    for k, name in enumerate(left):
                        out, spot = spots[name]
                        out[spot, :, lane] += total[0:1, k * count:(k + 1) * count]

            condition = [task[3] for task in tasks if task[0] == left][0]
            if left[0] in (NEXT, FAR):
                pl.when(middle)(work)
            elif condition:
                pl.when(when[condition])(work)
            else:
                work()

    pl.when(lax.rem(z, 2) == 0)(lambda: meet(hot, first))
    pl.when(lax.rem(z, 2) == 1)(lambda: meet(rest, 0))

    if doubted:
        doubt = sum(blocks[name][rest:, first:first + 128].astype(F32)[0:1, 0:1] for name in doubted)
        out, k = spots[FAR]
        out[k] += jnp.where(lax.broadcasted_iota(jnp.int32, (1, lanes), 1) == flag, doubt, 0.0)


def score(name, docs, hot, place, blocks, pairs, made, tasks, sums, doubted=(), weight=1):
    rest, _, _, lanes = layout(docs, hot)
    names = list(dict.fromkeys([*made, *(name for task in tasks for name in task[0])]))
    given = [p for p in pairs if any(p == task[1] for task in tasks)]
    width = blocks[OWN].shape[1]
    vmem = pl.BlockSpec(memory_space=pltpu.VMEM)
    arrays = [blocks[b] for b in names] + [a for p in given for a in pairs[p]] + list(sums)
    shapes = [jax.ShapeDtypeStruct((len(group), 1, lanes), F32) for group in GROUPS]
    if made:
        shapes += [jax.ShapeDtypeStruct((width, 2 * rest), BF16), jax.ShapeDtypeStruct((8, 2 * rest), F32)]
    out = pl.pallas_call(
        lambda *refs: score_kernel(docs, hot, names, given, made, tasks, doubted or made, bool(sums), *refs),
        out_shape=tuple(shapes),
        in_specs=[pl.BlockSpec(memory_space=pltpu.SMEM)] + [vmem] * len(arrays),
        out_specs=tuple(vmem for _ in shapes),
        scratch_shapes=[pltpu.VMEM((2 * rest, 128), F32)],
        compiler_params=pltpu.CompilerParams(vmem_limit_bytes=20 * 2**20),
        cost_estimate=pl.CostEstimate(flops=weight, bytes_accessed=2**10, transcendentals=0),
        name=name,
    )(place, *arrays)
    count = len(GROUPS)
    return out[:count], {**pairs, made: out[count:]} if made else pairs


def finish_kernel(slot_ref, *refs):
    sums, out_ref = refs[:-1], refs[-1]
    total = sums[0][0]
    for ref in sums[1:]:
        total += ref[0]
    lanes, docs = total.shape[1], slot_ref.shape[1]
    values = jnp.broadcast_to(jnp.log(1.0 + total * 2.0**-SHIFT), (8, lanes)).T[:, 0:1]
    here = lax.broadcasted_iota(jnp.int32, (lanes, docs), 0) == slot_ref[...]
    out_ref[...] = jnp.sum(jnp.where(here, values, 0.0), axis=0, keepdims=True)


def finish(slot, sums):
    return pl.pallas_call(
        finish_kernel,
        out_shape=jax.ShapeDtypeStruct(slot.shape, F32),
        compiler_params=pltpu.CompilerParams(vmem_limit_bytes=6 * 2**20),
        name="finish",
    )(slot, *sums)


def decide_kernel(flag, mine_ref, theirs_ref, out_ref):
    out_ref[0] = (jnp.sum(mine_ref[0][:, flag:flag + 1] + theirs_ref[0][:, flag:flag + 1]) > 0.0).astype(jnp.int32)


def decide(flag, mine, theirs):
    return pl.pallas_call(
        lambda *refs: decide_kernel(flag, *refs),
        out_shape=jax.ShapeDtypeStruct((1,), jnp.int32),
        out_specs=pl.BlockSpec(memory_space=pltpu.SMEM),
        compiler_params=pltpu.CompilerParams(vmem_limit_bytes=2 * 2**20),
        name="decide",
    )(mine, theirs)


def meeting_plan(states, proj_weight, cluster_of):
    owners = lax.axis_size("owner")
    columns = owners // ROWS
    docs = states.shape[0]
    hot = 3 * docs // owners
    flag = layout(docs, hot)[2]

    owner, core = lax.axis_index("owner"), lax.axis_index("split")
    place = jnp.stack([owner // ROWS, owner % ROWS, core]).astype(jnp.int32)
    same, other, slot = prep(hot, place, cluster_of, states, proj_weight)

    def move(a, to, row=0, core=0):
        pairs = [
            (
                (z * ROWS + y) * 2 + c,
                (to[z] * ROWS + (y ^ row)) * 2 + (c ^ (core if row or to[z] != z else 1)),
            )
            for z in range(columns) for y in range(ROWS) for c in range(2)
        ]
        return lax.ppermute(a, ("owner", "split"), pairs)

    STAY, OUTER, MIDDLE, TWO = (0, 1, 2, 3), (1, 0, 3, 2), (0, 2, 1, 3), (2, 3, 0, 1)
    TO_MIDDLE = (2, 0, 3, 1)

    def meet(name, made, tasks, **options):
        return score(name, docs, hot, place, blocks, pairs, made, tasks, sums, **options)

    blocks, pairs, sums = {OWN: same}, {}, ()
    blocks[CORE] = move(same, STAY, core=1)
    blocks[PAIR] = move(other, OUTER)
    blocks[CORE], still_same, other = lax.optimization_barrier((blocks[CORE], same, other))
    blocks[ROW] = move(still_same, STAY, row=1)
    blocks[NEXT] = move(other, MIDDLE)
    sums, pairs = meet("own", HERE, [((OWN,), HERE, False, None), ((CORE,), HERE, False, "core0")], weight=2**33)

    blocks[PAIR], _ = lax.optimization_barrier((blocks[PAIR], sums[0]))
    blocks[ROW], blocks[NEXT] = lax.optimization_barrier((blocks[ROW], blocks[NEXT]))
    blocks[FAR] = move(same, TO_MIDDLE)
    blocks[PAIR_ROW] = move(blocks[PAIR], STAY, row=1)
    blocks[PAIR_CORE] = move(blocks[PAIR], STAY, core=1)
    blocks[DIAG] = move(blocks[ROW], STAY, core=1)
    sums, pairs = meet(
        "pair", THERE,
        [((PAIR,), THERE, False, None), ((PAIR_CORE,), THERE, False, "core1"), ((NEXT,), HERE, True, None),
         ((NEXT,), THERE, True, None)],
        weight=2**33,
    )
    sums, pairs = meet(
        "row", ACROSS,
        [((PAIR,), HERE, True, None), ((PAIR,), ACROSS, True, None), ((NEXT,), ACROSS, True, None),
         ((ROW,), HERE, False, "row0"), ((DIAG,), HERE, False, "row1")],
    )
    blocks[PAIR_ROW], _ = lax.optimization_barrier((blocks[PAIR_ROW], sums[0]))
    blocks[PAIR_DIAG] = move(blocks[PAIR_ROW], STAY, core=1)
    sums, pairs = meet("far", (), [((FAR,), p, True, None) for p in (HERE, THERE, ACROSS)])
    sums, pairs = meet(
        "last", (),
        [((NEXT, FAR), right, False, None) for right in (PAIR_ROW, PAIR_DIAG)]
        + [((PAIR_ROW,), THERE, False, "row1"), ((PAIR_DIAG,), THERE, False, "row0")],
        doubted=(PAIR_ROW, PAIR_DIAG),
    )
    kept, by_core, to_next, to_far = sums
    from_core, from_far = move(by_core, STAY, core=1), move(to_far, TWO)
    from_core, to_next = lax.optimization_barrier((from_core, to_next))
    from_next = move(to_next, MIDDLE)
    own, pair, row, pair_row = (kept[k:k + 1] + from_core[k:k + 1] for k in (0, 1, 2, 3))
    home = [
        own, from_next, from_far,
        move(pair, OUTER), move(row, STAY, row=1), move(pair_row, OUTER, row=1),
    ]
    return lax.cond(
        decide(flag, to_far, from_far)[0] > 0,
        lambda states, proj_weight, cluster_of, *_: ring_plan(states, proj_weight, cluster_of),
        lambda states, proj_weight, cluster_of, slot, *home: finish(slot, home).reshape(docs),
        states, proj_weight, cluster_of, slot, *home,
    )


def on_device(states, proj_weight, cluster_of):
    if (lax.axis_size("owner"), lax.axis_size("split")) == (8, 2) and states.shape[0] == 512:
        return meeting_plan(states, proj_weight, cluster_of)
    return owner_plan(states, proj_weight, cluster_of)


def solution(mesh):
    placed = (P(("parts", "owner", "split"), None), P(), P(("parts", "owner", "split")))
    return jax.shard_map(
        on_device,
        mesh=mesh,
        in_specs=placed,
        out_specs=P(("parts", "owner", "split")),
        check_vma=False,
    )
```

```python
import math

import jax
import jax.numpy as jnp
from jax import lax
from jax.experimental import pallas as pl
from jax.experimental.pallas import tpu as pltpu
from jax.sharding import PartitionSpec as P

CLUS_OWN = 2
TAU = 0.05
THRESH = 0.2
EPS = 1e-06
LOG2E = math.log2(math.e)
SCALE = LOG2E / TAU
SHIFT = THRESH * LOG2E / TAU

ROWS = 2
F32 = jnp.float32
BF16 = jnp.bfloat16


def prepare(states, proj_weight):
    projected = jnp.dot(states, proj_weight, preferred_element_type=jnp.float32)
    unit = projected * lax.rsqrt(jnp.sum(projected * projected, axis=1, keepdims=True) + EPS)
    peak = jnp.max(jnp.abs(unit), axis=1).astype(jnp.bfloat16)
    quant = (unit / peak.astype(jnp.float32)[:, None]).astype(jnp.bfloat16)
    return (quant, peak)


def similarity_scores(
    own_quant, own_peak, own_cluster, own_index, col_quant, col_peak, col_cluster, col_index
):
    row_count = own_quant.shape[0]
    block = math.gcd(row_count, 768)
    col_scale = col_peak.astype(jnp.float32)

    def one_block(start):
        quant_rows = lax.dynamic_slice_in_dim(own_quant, start, block, 0)
        scale_rows = lax.dynamic_slice_in_dim(own_peak, start, block, 0).astype(jnp.float32)
        cluster_rows = lax.dynamic_slice_in_dim(own_cluster, start, block, 0)
        index_rows = lax.dynamic_slice_in_dim(own_index, start, block, 0)
        inner = lax.dot_general(
            quant_rows, col_quant, (((1,), (1,)), ((), ())), preferred_element_type=jnp.float32
        )
        cosine = inner * scale_rows[:, None] * col_scale[None, :]
        same = (cluster_rows[:, None] == col_cluster[None, :]) & (
            index_rows[:, None] != col_index[None, :]
        )
        weights = jnp.where(same, jnp.exp((cosine - THRESH) / TAU), jnp.zeros_like(cosine))
        return jnp.log(1.0 + jnp.sum(weights, axis=1))

    starts = jnp.arange(row_count // block, dtype=jnp.int32) * block
    return lax.map(one_block, starts).reshape(row_count)


def owner_plan(states, proj_weight, cluster_of):
    owners = lax.axis_size("owner")
    splits = lax.axis_size("split")
    half_index = lax.axis_index("split")
    doc_count = states.shape[0]
    capacity = 3 * doc_count // owners
    width = proj_weight.shape[1]
    slot_total = owners * capacity
    quant, peak = prepare(states, proj_weight)
    group_of = cluster_of // CLUS_OWN
    onehot = (group_of[:, None] == jnp.arange(owners, dtype=jnp.int32)[None, :]).astype(jnp.int32)
    before = jnp.cumsum(onehot, axis=0) - onehot
    target = group_of * capacity + jnp.sum(before * onehot, axis=1)
    quant_slots = (
        jnp.zeros((slot_total, width), jnp.bfloat16)
        .at[target]
        .set(quant)
        .reshape(owners, capacity, width)
    )
    peak_slots = (
        jnp.zeros((slot_total,), jnp.bfloat16).at[target].set(peak).reshape(owners, capacity)
    )
    cluster_slots = (
        jnp.full((slot_total,), -1, jnp.int32).at[target].set(cluster_of).reshape(owners, capacity)
    )
    positions = (
        jnp.arange(owners, dtype=jnp.int32)[:, None] * (splits * capacity)
        + jnp.arange(capacity, dtype=jnp.int32)[None, :]
    )
    own_index = (positions + half_index * capacity).reshape(slot_total)
    col_index = jnp.arange(splits * slot_total, dtype=jnp.int32)
    own_quant, own_peak, own_cluster = (
        lax.all_to_all(a, "owner", split_axis=0, concat_axis=0, tiled=True)
        for a in (quant_slots, peak_slots, cluster_slots)
    )
    all_quant, all_peak, all_cluster = (
        lax.all_gather(a, "split", axis=1, tiled=True) for a in (own_quant, own_peak, own_cluster)
    )
    scores = similarity_scores(
        own_quant.reshape(slot_total, width),
        own_peak.reshape(slot_total),
        own_cluster.reshape(slot_total),
        own_index,
        all_quant.reshape(splits * slot_total, width),
        all_peak.reshape(splits * slot_total),
        all_cluster.reshape(splits * slot_total),
        col_index,
    )
    returned = lax.all_to_all(
        scores.reshape(owners, capacity), "owner", split_axis=0, concat_axis=0, tiled=True
    )
    return returned.reshape(slot_total)[target]


def ring_plan(states, proj_weight, cluster_of):
    axes = ("owner", "split")
    devices = lax.axis_size("owner") * lax.axis_size("split")
    ring = [(i, (i + 1) % devices) for i in range(devices)]
    quant, peak = prepare(states, proj_weight)
    scale = peak.astype(F32)
    place = jnp.arange(states.shape[0], dtype=jnp.int32)

    def weights(block, block_peak, block_cluster):
        inner = lax.dot_general(quant, block, (((1,), (1,)), ((), ())), preferred_element_type=F32)
        cosine = inner * scale[:, None] * block_peak.astype(F32)[None, :]
        same = cluster_of[:, None] == block_cluster[None, :]
        return jnp.where(same, jnp.exp((cosine - THRESH) / TAU), jnp.zeros_like(cosine))

    def meet(_, carry):
        passed = [lax.ppermute(a, axes, ring) for a in carry[1:]]
        return (carry[0] + jnp.sum(weights(*passed), axis=1), *passed)

    own = (quant, peak, cluster_of)
    others = place[:, None] != place[None, :]
    total = jnp.sum(jnp.where(others, weights(*own), 0.0), axis=1)
    total = lax.fori_loop(1, devices, meet, (total, *own))[0]
    return jnp.log(1.0 + total)


def up(n, m):
    return -(-n // m) * m


META = 8


def layout(docs, hot):
    rest = docs - hot
    first = up(rest, 128)
    flag = first + hot
    return rest, first, flag, up(flag + 1, 128)


def prep_kernel(hot, place_ref, cl_ref, st_ref, w_ref, same_ref, other_ref, slot_ref, vectors):
    docs = st_ref.shape[0]
    rest, first, flag, lanes = layout(docs, hot)
    tile = 128

    cluster = cl_ref[...]
    group = cluster // CLUS_OWN
    member = lax.broadcasted_iota(jnp.int32, (8, docs), 0) == group
    full = jnp.sum(member.astype(F32), axis=1, keepdims=True) == float(hot)
    chosen = jnp.min(
        jnp.where(full, lax.broadcasted_iota(jnp.int32, (8, 1), 0), 8), axis=0, keepdims=True
    )
    doubt = jnp.where(jnp.sum(full.astype(F32), axis=0, keepdims=True) == 1.0, 0.0, 1.0)
    in_hot = group == chosen

    for t in range(docs // tile):
        rows = slice(t * tile, (t + 1) * tile)
        projected = jnp.dot(st_ref[rows, :], w_ref[...], preferred_element_type=F32)
        norm = lax.rsqrt(jnp.sum(projected * projected, axis=1, keepdims=True) + EPS)
        vectors[rows, :] = (projected * (norm * math.sqrt(SCALE))).astype(BF16)

    ahead = (
        lax.broadcasted_iota(jnp.int32, (docs, docs), 0) < lax.broadcasted_iota(jnp.int32, (docs, docs), 1)
    ).astype(F32).astype(BF16)
    hot_rows = jnp.broadcast_to(in_hot.astype(F32), (8, docs)).astype(BF16)
    rank = jnp.dot(hot_rows, ahead, preferred_element_type=F32)[0:1, :].astype(jnp.int32)
    place = lax.broadcasted_iota(jnp.int32, (1, docs), 1)
    slot = jnp.where(in_hot, first + rank, place - rank)
    slot_ref[...] = slot

    sort = (lax.broadcasted_iota(jnp.int32, (lanes, docs), 0) == slot).astype(F32).astype(BF16)
    cluster_rows = jnp.broadcast_to(cluster.astype(F32), (META, docs)).astype(BF16)
    sorted_n = jnp.dot(sort[:rest, :], vectors[...], preferred_element_type=F32).astype(BF16)
    sorted_h = jnp.dot(sort[first:flag, :], vectors[...], preferred_element_type=F32).astype(BF16)
    ids = lax.dot_general(
        cluster_rows, sort, (((1,), (1,)), ((), ())), preferred_element_type=F32
    )
    ids = ids.astype(BF16)


    def fill_n(ref):
        ref[:rest, :] = sorted_n
        ref[rest:, :] = jnp.zeros((META, ref.shape[1]), BF16)
        ref[rest:, :first] = ids[:, :first]
        ref[rest:, first:first + 128] = jnp.broadcast_to(doubt.astype(BF16), (META, 128))

    def fill_h(ref):
        ref[:hot, :] = sorted_h
        ref[hot:, :] = jnp.zeros((rest + META - hot, ref.shape[1]), BF16)
        ref[rest:, :lanes - first] = ids[:, first:]
        ref[rest:, first:first + 128] = jnp.broadcast_to(doubt.astype(BF16), (META, 128))

    even = lax.rem(place_ref[0], 2) == 0

    @pl.when(even)
    def _():
        fill_h(same_ref)
        fill_n(other_ref)

    @pl.when(jnp.logical_not(even))
    def _():
        fill_n(same_ref)
        fill_h(other_ref)


def prep(hot, place, cluster_of, states, proj_weight):
    docs, width = states.shape[0], proj_weight.shape[1]
    rest = docs - hot
    shape = jax.ShapeDtypeStruct
    vmem = pl.BlockSpec(memory_space=pltpu.VMEM)
    return pl.pallas_call(
        lambda *refs: prep_kernel(hot, *refs),
        out_shape=(
            shape((rest + META, width), BF16),
            shape((rest + META, width), BF16),
            shape((1, docs), jnp.int32),
        ),
        in_specs=[pl.BlockSpec(memory_space=pltpu.SMEM), vmem, vmem, vmem],
        scratch_shapes=[pltpu.VMEM((docs, width), BF16)],
        compiler_params=pltpu.CompilerParams(vmem_limit_bytes=24 * 2**20),
        name="prep",
    )(place, cluster_of.reshape(1, docs), states, proj_weight)


OWN, PAIR = "own", "pair"
CORE, PAIR_CORE = "core", "pair_core"
ROW, PAIR_ROW = "row", "pair_row"
DIAG, PAIR_DIAG = "diag", "pair_diag"
NEXT, FAR = "next", "far"
GROUPS = ((OWN, PAIR, ROW, PAIR_ROW), (CORE, PAIR_CORE, DIAG, PAIR_DIAG), (NEXT,), (FAR,))
TILE = 256
HERE, THERE, ACROSS = (OWN, CORE), (PAIR, PAIR_CORE), (ROW, DIAG)


def score_kernel(docs, hot, names, given, made, tasks, doubted, carries, *refs):
    rest, first, flag, lanes = layout(docs, hot)
    place_ref, refs = refs[0], refs[1:]
    blocks, refs = dict(zip(names, refs[:len(names)])), refs[len(names):]
    pairs, refs = {p: refs[2 * k:2 * k + 2] for k, p in enumerate(given)}, refs[2 * len(given):]
    before, refs = refs[:len(GROUPS) * carries], refs[len(GROUPS) * carries:]
    outs, refs = refs[:len(GROUPS)], refs[len(GROUPS):]
    if made:
        pairs[made], refs = refs[:2], refs[2:]
    parts = refs[-1]
    for k, out in enumerate(outs):
        out[...] = before[k][...] if carries else jnp.zeros(out.shape, F32)
    spots = {name: (out, k) for out, group in zip(outs, GROUPS) for k, name in enumerate(group)}
    z, y, c = place_ref[0], place_ref[1], place_ref[2]
    when = {"core0": c == 0, "core1": c == 1, "row0": y == 0, "row1": y == 1}
    middle = (z == 1) | (z == 2)

    def meet(count, start):
        lane = slice(start, start + count)
        wide, two = up(count, 128), 2 * count
        columns = {name: ref[rest:, 0:wide].astype(F32)[0:8, :].T[0:count, :] for name, ref in blocks.items()}
        if made:
            turned, notes = pairs[made]
            turned[:, 0:two] = jnp.concatenate([blocks[name][:count, :] for name in made], axis=0).T
            notes[:, 0:two] = jnp.concatenate([columns[name] for name in made], axis=0).T

        for left in dict.fromkeys(task[0] for task in tasks):

            def work(left=left):
                own_tasks = [task for task in tasks if task[0] == left]
                rows = count * len(left)
                block = blocks[left[0]][:count, :]
                column = columns[left[0]][:, 0:1]
                for name in left[1:]:
                    block = jnp.concatenate([block, blocks[name][:count, :]], axis=0)
                    column = jnp.concatenate([column, columns[name][:, 0:1]], axis=0)
                fresh = True
                for _, right, both, _ in own_tasks:
                    if right in blocks:
                        span, rights, diagonal = count, (right,), False
                        ids = blocks[right][rest:, 0:wide].astype(F32)[0:1, 0:count]
                    else:
                        turned, notes = pairs[right]
                        span, rights, diagonal = two if both else wide, right[:1 + both], left == right[:1]
                        ids = notes[0:1, 0:span]
                        if not both:
                            ids = jnp.where(lax.broadcasted_iota(jnp.int32, ids.shape, 1) < count, ids, -1.0)
                    totals = []
                    for low in range(0, span, TILE):
                        high = min(low + TILE, span)
                        if right in blocks:
                            inner = lax.dot_general(
                                block, blocks[right][low:high, :], (((1,), (1,)), ((), ())),
                                preferred_element_type=F32,
                            )
                        else:
                            inner = jnp.dot(block, turned[:, low:high], preferred_element_type=F32)
                        same = column == ids[:, low:high]
                        if diagonal:
                            same &= lax.broadcasted_iota(jnp.int32, inner.shape, 0) != (
                                lax.broadcasted_iota(jnp.int32, inner.shape, 1) + low
                            )
                        weights = jnp.where(same, jnp.exp2(inner), 0.0)
                        totals.append(jnp.sum(weights, axis=0, keepdims=True))
                        if not diagonal:
                            part = None
                            for t in range(0, high - low, 128):
                                piece = weights[:, t:t + 128]
                                if piece.shape[1] < 128:
                                    blank = jnp.zeros((rows, 128 - piece.shape[1]), F32)
                                    piece = jnp.concatenate([piece, blank], axis=1)
                                part = piece if part is None else part + piece
                            if fresh:
                                parts[0:rows, :] = part
                            else:
                                parts[0:rows, :] += part
                            fresh = False
                    total = jnp.concatenate(totals, axis=1) if len(totals) > 1 else totals[0]
                    for k, name in enumerate(rights):
                        out, spot = spots[name]
                        out[spot, :, lane] += total[:, k * count:(k + 1) * count]
                if not fresh:
                    part = parts[0:rows, :]
                    high = part.astype(BF16)
                    low = (part - high.astype(F32)).astype(BF16)
                    total = lax.dot_general(
                        jnp.ones((16, 256), BF16), jnp.concatenate([high, low], axis=1),
                        (((1,), (1,)), ((), ())), preferred_element_type=F32,
                    )
                    for k, name in enumerate(left):
                        out, spot = spots[name]
                        out[spot, :, lane] += total[0:1, k * count:(k + 1) * count]

            condition = [task[3] for task in tasks if task[0] == left][0]
            if left[0] in (NEXT, FAR):
                pl.when(middle)(work)
            elif condition:
                pl.when(when[condition])(work)
            else:
                work()

    pl.when(lax.rem(z, 2) == 0)(lambda: meet(hot, first))
    pl.when(lax.rem(z, 2) == 1)(lambda: meet(rest, 0))

    if doubted:
        doubt = sum(blocks[name][rest:, first:first + 128].astype(F32)[0:1, 0:1] for name in doubted)
        out, k = spots[FAR]
        out[k] += jnp.where(lax.broadcasted_iota(jnp.int32, (1, lanes), 1) == flag, doubt, 0.0)


def score(name, docs, hot, place, blocks, pairs, made, tasks, sums, doubted=(), weight=1):
    rest, _, _, lanes = layout(docs, hot)
    names = list(dict.fromkeys([*made, *(name for task in tasks for name in task[0])]))
    given = [p for p in pairs if any(p == task[1] for task in tasks)]
    width = blocks[OWN].shape[1]
    vmem = pl.BlockSpec(memory_space=pltpu.VMEM)
    arrays = [blocks[b] for b in names] + [a for p in given for a in pairs[p]] + list(sums)
    shapes = [jax.ShapeDtypeStruct((len(group), 1, lanes), F32) for group in GROUPS]
    if made:
        shapes += [jax.ShapeDtypeStruct((width, 2 * rest), BF16), jax.ShapeDtypeStruct((8, 2 * rest), F32)]
    out = pl.pallas_call(
        lambda *refs: score_kernel(docs, hot, names, given, made, tasks, doubted or made, bool(sums), *refs),
        out_shape=tuple(shapes),
        in_specs=[pl.BlockSpec(memory_space=pltpu.SMEM)] + [vmem] * len(arrays),
        out_specs=tuple(vmem for _ in shapes),
        scratch_shapes=[pltpu.VMEM((2 * rest, 128), F32)],
        compiler_params=pltpu.CompilerParams(vmem_limit_bytes=20 * 2**20),
        cost_estimate=pl.CostEstimate(flops=weight, bytes_accessed=2**10, transcendentals=0),
        name=name,
    )(place, *arrays)
    count = len(GROUPS)
    return out[:count], {**pairs, made: out[count:]} if made else pairs


def finish_kernel(slot_ref, *refs):
    sums, out_ref = refs[:-1], refs[-1]
    total = sums[0][0]
    for ref in sums[1:]:
        total += ref[0]
    lanes, docs = total.shape[1], slot_ref.shape[1]
    values = jnp.broadcast_to(jnp.log(1.0 + total * 2.0**-SHIFT), (8, lanes)).T[:, 0:1]
    here = lax.broadcasted_iota(jnp.int32, (lanes, docs), 0) == slot_ref[...]
    out_ref[...] = jnp.sum(jnp.where(here, values, 0.0), axis=0, keepdims=True)


def finish(slot, sums):
    return pl.pallas_call(
        finish_kernel,
        out_shape=jax.ShapeDtypeStruct(slot.shape, F32),
        compiler_params=pltpu.CompilerParams(vmem_limit_bytes=6 * 2**20),
        name="finish",
    )(slot, *sums)


def decide_kernel(flag, mine_ref, theirs_ref, out_ref):
    out_ref[0] = (jnp.sum(mine_ref[0][:, flag:flag + 1] + theirs_ref[0][:, flag:flag + 1]) > 0.0).astype(jnp.int32)


def decide(flag, mine, theirs):
    return pl.pallas_call(
        lambda *refs: decide_kernel(flag, *refs),
        out_shape=jax.ShapeDtypeStruct((1,), jnp.int32),
        out_specs=pl.BlockSpec(memory_space=pltpu.SMEM),
        compiler_params=pltpu.CompilerParams(vmem_limit_bytes=2 * 2**20),
        name="decide",
    )(mine, theirs)


def meeting_plan(states, proj_weight, cluster_of):
    owners = lax.axis_size("owner")
    columns = owners // ROWS
    docs = states.shape[0]
    hot = 3 * docs // owners
    flag = layout(docs, hot)[2]

    owner, core = lax.axis_index("owner"), lax.axis_index("split")
    place = jnp.stack([owner // ROWS, owner % ROWS, core]).astype(jnp.int32)
    same, other, slot = prep(hot, place, cluster_of, states, proj_weight)

    def move(a, to, row=0, core=0):
        pairs = [
            (
                (z * ROWS + y) * 2 + c,
                (to[z] * ROWS + (y ^ row)) * 2 + (c ^ (core if row or to[z] != z else 1)),
            )
            for z in range(columns) for y in range(ROWS) for c in range(2)
        ]
        return lax.ppermute(a, ("owner", "split"), pairs)

    STAY, OUTER, MIDDLE, TWO = (0, 1, 2, 3), (1, 0, 3, 2), (0, 2, 1, 3), (2, 3, 0, 1)
    TO_MIDDLE = (2, 0, 3, 1)

    def meet(name, made, tasks, **options):
        return score(name, docs, hot, place, blocks, pairs, made, tasks, sums, **options)

    blocks, pairs, sums = {OWN: same}, {}, ()
    blocks[CORE] = move(same, STAY, core=1)
    blocks[PAIR] = move(other, OUTER)
    blocks[CORE], still_same, other = lax.optimization_barrier((blocks[CORE], same, other))
    blocks[ROW] = move(still_same, STAY, row=1)
    blocks[NEXT] = move(other, MIDDLE)
    sums, pairs = meet("own", HERE, [((OWN,), HERE, False, None), ((CORE,), HERE, False, "core0")], weight=2**33)

    blocks[PAIR], _ = lax.optimization_barrier((blocks[PAIR], sums[0]))
    blocks[ROW], blocks[NEXT] = lax.optimization_barrier((blocks[ROW], blocks[NEXT]))
    blocks[FAR] = move(same, TO_MIDDLE)
    blocks[PAIR_ROW] = move(blocks[PAIR], STAY, row=1)
    blocks[PAIR_CORE] = move(blocks[PAIR], STAY, core=1)
    blocks[DIAG] = move(blocks[ROW], STAY, core=1)
    sums, pairs = meet(
        "pair", THERE,
        [((PAIR,), THERE, False, None), ((PAIR_CORE,), THERE, False, "core1"), ((NEXT,), HERE, True, None),
         ((NEXT,), THERE, True, None)],
        weight=2**33,
    )
    sums, pairs = meet(
        "row", ACROSS,
        [((PAIR,), HERE, True, None), ((PAIR,), ACROSS, True, None), ((NEXT,), ACROSS, True, None),
         ((ROW,), HERE, False, "row0"), ((DIAG,), HERE, False, "row1")],
    )
    blocks[PAIR_ROW], _ = lax.optimization_barrier((blocks[PAIR_ROW], sums[0]))
    blocks[PAIR_DIAG] = move(blocks[PAIR_ROW], STAY, core=1)
    sums, pairs = meet("far", (), [((FAR,), p, True, None) for p in (HERE, THERE, ACROSS)])
    sums, pairs = meet(
        "last", (),
        [((NEXT, FAR), right, False, None) for right in (PAIR_ROW, PAIR_DIAG)]
        + [((PAIR_ROW,), THERE, False, "row1"), ((PAIR_DIAG,), THERE, False, "row0")],
        doubted=(PAIR_ROW, PAIR_DIAG),
    )
    kept, by_core, to_next, to_far = sums
    from_core, from_far = move(by_core, STAY, core=1), move(to_far, TWO)
    from_core, to_next = lax.optimization_barrier((from_core, to_next))
    from_next = move(to_next, MIDDLE)
    own, pair, row, pair_row = (kept[k:k + 1] + from_core[k:k + 1] for k in (0, 1, 2, 3))
    home = [
        own, from_next, from_far,
        move(row, STAY, row=1), move(pair, OUTER), move(pair_row, OUTER, row=1),
    ]
    return lax.cond(
        decide(flag, to_far, from_far)[0] > 0,
        lambda states, proj_weight, cluster_of, *_: ring_plan(states, proj_weight, cluster_of),
        lambda states, proj_weight, cluster_of, slot, *home: finish(slot, home).reshape(docs),
        states, proj_weight, cluster_of, slot, *home,
    )


def on_device(states, proj_weight, cluster_of):
    if (lax.axis_size("owner"), lax.axis_size("split")) == (8, 2) and states.shape[0] == 512:
        return meeting_plan(states, proj_weight, cluster_of)
    return owner_plan(states, proj_weight, cluster_of)


def solution(mesh):
    placed = (P(("parts", "owner", "split"), None), P(), P(("parts", "owner", "split")))
    return jax.shard_map(
        on_device,
        mesh=mesh,
        in_specs=placed,
        out_specs=P(("parts", "owner", "split")),
        check_vma=False,
    )
```

```python
import math

import jax
import jax.numpy as jnp
from jax import lax
from jax.experimental import pallas as pl
from jax.experimental.pallas import tpu as pltpu
from jax.sharding import PartitionSpec as P

CLUS_OWN = 2
TAU = 0.05
THRESH = 0.2
EPS = 1e-06
LOG2E = math.log2(math.e)
SCALE = LOG2E / TAU
SHIFT = THRESH * LOG2E / TAU

ROWS = 2
F32 = jnp.float32
BF16 = jnp.bfloat16


def prepare(states, proj_weight):
    projected = jnp.dot(states, proj_weight, preferred_element_type=jnp.float32)
    unit = projected * lax.rsqrt(jnp.sum(projected * projected, axis=1, keepdims=True) + EPS)
    peak = jnp.max(jnp.abs(unit), axis=1).astype(jnp.bfloat16)
    quant = (unit / peak.astype(jnp.float32)[:, None]).astype(jnp.bfloat16)
    return (quant, peak)


def similarity_scores(
    own_quant, own_peak, own_cluster, own_index, col_quant, col_peak, col_cluster, col_index
):
    row_count = own_quant.shape[0]
    block = math.gcd(row_count, 768)
    col_scale = col_peak.astype(jnp.float32)

    def one_block(start):
        quant_rows = lax.dynamic_slice_in_dim(own_quant, start, block, 0)
        scale_rows = lax.dynamic_slice_in_dim(own_peak, start, block, 0).astype(jnp.float32)
        cluster_rows = lax.dynamic_slice_in_dim(own_cluster, start, block, 0)
        index_rows = lax.dynamic_slice_in_dim(own_index, start, block, 0)
        inner = lax.dot_general(
            quant_rows, col_quant, (((1,), (1,)), ((), ())), preferred_element_type=jnp.float32
        )
        cosine = inner * scale_rows[:, None] * col_scale[None, :]
        same = (cluster_rows[:, None] == col_cluster[None, :]) & (
            index_rows[:, None] != col_index[None, :]
        )
        weights = jnp.where(same, jnp.exp((cosine - THRESH) / TAU), jnp.zeros_like(cosine))
        return jnp.log(1.0 + jnp.sum(weights, axis=1))

    starts = jnp.arange(row_count // block, dtype=jnp.int32) * block
    return lax.map(one_block, starts).reshape(row_count)


def owner_plan(states, proj_weight, cluster_of):
    owners = lax.axis_size("owner")
    splits = lax.axis_size("split")
    half_index = lax.axis_index("split")
    doc_count = states.shape[0]
    capacity = 3 * doc_count // owners
    width = proj_weight.shape[1]
    slot_total = owners * capacity
    quant, peak = prepare(states, proj_weight)
    group_of = cluster_of // CLUS_OWN
    onehot = (group_of[:, None] == jnp.arange(owners, dtype=jnp.int32)[None, :]).astype(jnp.int32)
    before = jnp.cumsum(onehot, axis=0) - onehot
    target = group_of * capacity + jnp.sum(before * onehot, axis=1)
    quant_slots = (
        jnp.zeros((slot_total, width), jnp.bfloat16)
        .at[target]
        .set(quant)
        .reshape(owners, capacity, width)
    )
    peak_slots = (
        jnp.zeros((slot_total,), jnp.bfloat16).at[target].set(peak).reshape(owners, capacity)
    )
    cluster_slots = (
        jnp.full((slot_total,), -1, jnp.int32).at[target].set(cluster_of).reshape(owners, capacity)
    )
    positions = (
        jnp.arange(owners, dtype=jnp.int32)[:, None] * (splits * capacity)
        + jnp.arange(capacity, dtype=jnp.int32)[None, :]
    )
    own_index = (positions + half_index * capacity).reshape(slot_total)
    col_index = jnp.arange(splits * slot_total, dtype=jnp.int32)
    own_quant, own_peak, own_cluster = (
        lax.all_to_all(a, "owner", split_axis=0, concat_axis=0, tiled=True)
        for a in (quant_slots, peak_slots, cluster_slots)
    )
    all_quant, all_peak, all_cluster = (
        lax.all_gather(a, "split", axis=1, tiled=True) for a in (own_quant, own_peak, own_cluster)
    )
    scores = similarity_scores(
        own_quant.reshape(slot_total, width),
        own_peak.reshape(slot_total),
        own_cluster.reshape(slot_total),
        own_index,
        all_quant.reshape(splits * slot_total, width),
        all_peak.reshape(splits * slot_total),
        all_cluster.reshape(splits * slot_total),
        col_index,
    )
    returned = lax.all_to_all(
        scores.reshape(owners, capacity), "owner", split_axis=0, concat_axis=0, tiled=True
    )
    return returned.reshape(slot_total)[target]


def ring_plan(states, proj_weight, cluster_of):
    axes = ("owner", "split")
    devices = lax.axis_size("owner") * lax.axis_size("split")
    ring = [(i, (i + 1) % devices) for i in range(devices)]
    quant, peak = prepare(states, proj_weight)
    scale = peak.astype(F32)
    place = jnp.arange(states.shape[0], dtype=jnp.int32)

    def weights(block, block_peak, block_cluster):
        inner = lax.dot_general(quant, block, (((1,), (1,)), ((), ())), preferred_element_type=F32)
        cosine = inner * scale[:, None] * block_peak.astype(F32)[None, :]
        same = cluster_of[:, None] == block_cluster[None, :]
        return jnp.where(same, jnp.exp((cosine - THRESH) / TAU), jnp.zeros_like(cosine))

    def meet(_, carry):
        passed = [lax.ppermute(a, axes, ring) for a in carry[1:]]
        return (carry[0] + jnp.sum(weights(*passed), axis=1), *passed)

    own = (quant, peak, cluster_of)
    others = place[:, None] != place[None, :]
    total = jnp.sum(jnp.where(others, weights(*own), 0.0), axis=1)
    total = lax.fori_loop(1, devices, meet, (total, *own))[0]
    return jnp.log(1.0 + total)


def up(n, m):
    return -(-n // m) * m


META = 8


def layout(docs, hot):
    rest = docs - hot
    first = up(rest, 128)
    flag = first + hot
    return rest, first, flag, up(flag + 1, 128)


def prep_kernel(hot, place_ref, cl_ref, st_ref, w_ref, same_ref, other_ref, slot_ref, vectors):
    docs = st_ref.shape[0]
    rest, first, flag, lanes = layout(docs, hot)
    tile = 256

    cluster = cl_ref[...]
    group = cluster // CLUS_OWN
    member = lax.broadcasted_iota(jnp.int32, (8, docs), 0) == group
    full = jnp.sum(member.astype(F32), axis=1, keepdims=True) == float(hot)
    chosen = jnp.min(
        jnp.where(full, lax.broadcasted_iota(jnp.int32, (8, 1), 0), 8), axis=0, keepdims=True
    )
    doubt = jnp.where(jnp.sum(full.astype(F32), axis=0, keepdims=True) == 1.0, 0.0, 1.0)
    in_hot = group == chosen

    for t in range(docs // tile):
        rows = slice(t * tile, (t + 1) * tile)
        projected = jnp.dot(st_ref[rows, :], w_ref[...], preferred_element_type=F32)
        norm = lax.rsqrt(jnp.sum(projected * projected, axis=1, keepdims=True) + EPS)
        vectors[rows, :] = (projected * (norm * math.sqrt(SCALE))).astype(BF16)

    ahead = (
        lax.broadcasted_iota(jnp.int32, (docs, docs), 0) < lax.broadcasted_iota(jnp.int32, (docs, docs), 1)
    ).astype(F32).astype(BF16)
    hot_rows = jnp.broadcast_to(in_hot.astype(F32), (8, docs)).astype(BF16)
    rank = jnp.dot(hot_rows, ahead, preferred_element_type=F32)[0:1, :].astype(jnp.int32)
    place = lax.broadcasted_iota(jnp.int32, (1, docs), 1)
    slot = jnp.where(in_hot, first + rank, place - rank)
    slot_ref[...] = slot

    sort = (lax.broadcasted_iota(jnp.int32, (lanes, docs), 0) == slot).astype(F32).astype(BF16)
    cluster_rows = jnp.broadcast_to(cluster.astype(F32), (META, docs)).astype(BF16)
    sorted_n = jnp.dot(sort[:rest, :], vectors[...], preferred_element_type=F32).astype(BF16)
    sorted_h = jnp.dot(sort[first:flag, :], vectors[...], preferred_element_type=F32).astype(BF16)
    ids = lax.dot_general(
        cluster_rows, sort, (((1,), (1,)), ((), ())), preferred_element_type=F32
    )
    ids = ids.astype(BF16)


    def fill_n(ref):
        ref[:rest, :] = sorted_n
        ref[rest:, :] = jnp.zeros((META, ref.shape[1]), BF16)
        ref[rest:, :first] = ids[:, :first]
        ref[rest:, first:first + 128] = jnp.broadcast_to(doubt.astype(BF16), (META, 128))

    def fill_h(ref):
        ref[:hot, :] = sorted_h
        ref[hot:, :] = jnp.zeros((rest + META - hot, ref.shape[1]), BF16)
        ref[rest:, :lanes - first] = ids[:, first:]
        ref[rest:, first:first + 128] = jnp.broadcast_to(doubt.astype(BF16), (META, 128))

    even = lax.rem(place_ref[0], 2) == 0

    @pl.when(even)
    def _():
        fill_h(same_ref)
        fill_n(other_ref)

    @pl.when(jnp.logical_not(even))
    def _():
        fill_n(same_ref)
        fill_h(other_ref)


def prep(hot, place, cluster_of, states, proj_weight):
    docs, width = states.shape[0], proj_weight.shape[1]
    rest = docs - hot
    shape = jax.ShapeDtypeStruct
    vmem = pl.BlockSpec(memory_space=pltpu.VMEM)
    return pl.pallas_call(
        lambda *refs: prep_kernel(hot, *refs),
        out_shape=(
            shape((rest + META, width), BF16),
            shape((rest + META, width), BF16),
            shape((1, docs), jnp.int32),
        ),
        in_specs=[pl.BlockSpec(memory_space=pltpu.SMEM), vmem, vmem, vmem],
        scratch_shapes=[pltpu.VMEM((docs, width), BF16)],
        compiler_params=pltpu.CompilerParams(vmem_limit_bytes=24 * 2**20),
        name="prep",
    )(place, cluster_of.reshape(1, docs), states, proj_weight)


OWN, PAIR = "own", "pair"
CORE, PAIR_CORE = "core", "pair_core"
ROW, PAIR_ROW = "row", "pair_row"
DIAG, PAIR_DIAG = "diag", "pair_diag"
NEXT, FAR = "next", "far"
GROUPS = ((OWN, PAIR, ROW, PAIR_ROW), (CORE, PAIR_CORE, DIAG, PAIR_DIAG), (NEXT,), (FAR,))
TILE = 256
HERE, THERE, ACROSS = (OWN, CORE), (PAIR, PAIR_CORE), (ROW, DIAG)


def score_kernel(docs, hot, names, given, made, tasks, doubted, carries, *refs):
    rest, first, flag, lanes = layout(docs, hot)
    place_ref, refs = refs[0], refs[1:]
    blocks, refs = dict(zip(names, refs[:len(names)])), refs[len(names):]
    pairs, refs = {p: refs[2 * k:2 * k + 2] for k, p in enumerate(given)}, refs[2 * len(given):]
    before, refs = refs[:len(GROUPS) * carries], refs[len(GROUPS) * carries:]
    outs, refs = refs[:len(GROUPS)], refs[len(GROUPS):]
    if made:
        pairs[made], refs = refs[:2], refs[2:]
    parts = refs[-1]
    for k, out in enumerate(outs):
        out[...] = before[k][...] if carries else jnp.zeros(out.shape, F32)
    spots = {name: (out, k) for out, group in zip(outs, GROUPS) for k, name in enumerate(group)}
    z, y, c = place_ref[0], place_ref[1], place_ref[2]
    when = {"core0": c == 0, "core1": c == 1, "row0": y == 0, "row1": y == 1}
    middle = (z == 1) | (z == 2)

    def meet(count, start):
        lane = slice(start, start + count)
        wide, two = up(count, 128), 2 * count
        columns = {name: ref[rest:, 0:wide].astype(F32)[0:8, :].T[0:count, :] for name, ref in blocks.items()}
        if made:
            turned, notes = pairs[made]
            turned[:, 0:two] = jnp.concatenate([blocks[name][:count, :] for name in made], axis=0).T
            notes[:, 0:two] = jnp.concatenate([columns[name] for name in made], axis=0).T

        for left in dict.fromkeys(task[0] for task in tasks):

            def work(left=left):
                own_tasks = [task for task in tasks if task[0] == left]
                rows = count * len(left)
                block = blocks[left[0]][:count, :]
                column = columns[left[0]][:, 0:1]
                for name in left[1:]:
                    block = jnp.concatenate([block, blocks[name][:count, :]], axis=0)
                    column = jnp.concatenate([column, columns[name][:, 0:1]], axis=0)
                fresh = True
                for _, right, both, _ in own_tasks:
                    if right in blocks:
                        span, rights, diagonal = count, (right,), False
                        ids = blocks[right][rest:, 0:wide].astype(F32)[0:1, 0:count]
                    else:
                        turned, notes = pairs[right]
                        span, rights, diagonal = two if both else wide, right[:1 + both], left == right[:1]
                        ids = notes[0:1, 0:span]
                        if not both:
                            ids = jnp.where(lax.broadcasted_iota(jnp.int32, ids.shape, 1) < count, ids, -1.0)
                    totals = []
                    for low in range(0, span, TILE):
                        high = min(low + TILE, span)
                        if right in blocks:
                            inner = lax.dot_general(
                                block, blocks[right][low:high, :], (((1,), (1,)), ((), ())),
                                preferred_element_type=F32,
                            )
                        else:
                            inner = jnp.dot(block, turned[:, low:high], preferred_element_type=F32)
                        same = column == ids[:, low:high]
                        if diagonal:
                            same &= lax.broadcasted_iota(jnp.int32, inner.shape, 0) != (
                                lax.broadcasted_iota(jnp.int32, inner.shape, 1) + low
                            )
                        weights = jnp.where(same, jnp.exp2(inner), 0.0)
                        totals.append(jnp.sum(weights, axis=0, keepdims=True))
                        if not diagonal:
                            part = None
                            for t in range(0, high - low, 128):
                                piece = weights[:, t:t + 128]
                                if piece.shape[1] < 128:
                                    blank = jnp.zeros((rows, 128 - piece.shape[1]), F32)
                                    piece = jnp.concatenate([piece, blank], axis=1)
                                part = piece if part is None else part + piece
                            if fresh:
                                parts[0:rows, :] = part
                            else:
                                parts[0:rows, :] += part
                            fresh = False
                    total = jnp.concatenate(totals, axis=1) if len(totals) > 1 else totals[0]
                    for k, name in enumerate(rights):
                        out, spot = spots[name]
                        out[spot, :, lane] += total[:, k * count:(k + 1) * count]
                if not fresh:
                    part = parts[0:rows, :]
                    high = part.astype(BF16)
                    low = (part - high.astype(F32)).astype(BF16)
                    total = lax.dot_general(
                        jnp.ones((16, 256), BF16), jnp.concatenate([high, low], axis=1),
                        (((1,), (1,)), ((), ())), preferred_element_type=F32,
                    )
                    for k, name in enumerate(left):
                        out, spot = spots[name]
                        out[spot, :, lane] += total[0:1, k * count:(k + 1) * count]

            condition = [task[3] for task in tasks if task[0] == left][0]
            if left[0] in (NEXT, FAR):
                pl.when(middle)(work)
            elif condition:
                pl.when(when[condition])(work)
            else:
                work()

    pl.when(lax.rem(z, 2) == 0)(lambda: meet(hot, first))
    pl.when(lax.rem(z, 2) == 1)(lambda: meet(rest, 0))

    if doubted:
        doubt = sum(blocks[name][rest:, first:first + 128].astype(F32)[0:1, 0:1] for name in doubted)
        out, k = spots[FAR]
        out[k] += jnp.where(lax.broadcasted_iota(jnp.int32, (1, lanes), 1) == flag, doubt, 0.0)


def score(name, docs, hot, place, blocks, pairs, made, tasks, sums, doubted=(), weight=1):
    rest, _, _, lanes = layout(docs, hot)
    names = list(dict.fromkeys([*made, *(name for task in tasks for name in task[0])]))
    given = [p for p in pairs if any(p == task[1] for task in tasks)]
    width = blocks[OWN].shape[1]
    vmem = pl.BlockSpec(memory_space=pltpu.VMEM)
    arrays = [blocks[b] for b in names] + [a for p in given for a in pairs[p]] + list(sums)
    shapes = [jax.ShapeDtypeStruct((len(group), 1, lanes), F32) for group in GROUPS]
    if made:
        shapes += [jax.ShapeDtypeStruct((width, 2 * rest), BF16), jax.ShapeDtypeStruct((8, 2 * rest), F32)]
    out = pl.pallas_call(
        lambda *refs: score_kernel(docs, hot, names, given, made, tasks, doubted or made, bool(sums), *refs),
        out_shape=tuple(shapes),
        in_specs=[pl.BlockSpec(memory_space=pltpu.SMEM)] + [vmem] * len(arrays),
        out_specs=tuple(vmem for _ in shapes),
        scratch_shapes=[pltpu.VMEM((2 * rest, 128), F32)],
        compiler_params=pltpu.CompilerParams(vmem_limit_bytes=20 * 2**20),
        cost_estimate=pl.CostEstimate(flops=weight, bytes_accessed=2**10, transcendentals=0),
        name=name,
    )(place, *arrays)
    count = len(GROUPS)
    return out[:count], {**pairs, made: out[count:]} if made else pairs


def finish_kernel(slot_ref, *refs):
    sums, out_ref = refs[:-1], refs[-1]
    total = sums[0][0]
    for ref in sums[1:]:
        total += ref[0]
    lanes, docs = total.shape[1], slot_ref.shape[1]
    values = jnp.broadcast_to(jnp.log(1.0 + total * 2.0**-SHIFT), (8, lanes)).T[:, 0:1]
    here = lax.broadcasted_iota(jnp.int32, (lanes, docs), 0) == slot_ref[...]
    out_ref[...] = jnp.sum(jnp.where(here, values, 0.0), axis=0, keepdims=True)


def finish(slot, sums):
    return pl.pallas_call(
        finish_kernel,
        out_shape=jax.ShapeDtypeStruct(slot.shape, F32),
        compiler_params=pltpu.CompilerParams(vmem_limit_bytes=6 * 2**20),
        name="finish",
    )(slot, *sums)


def decide_kernel(flag, mine_ref, theirs_ref, out_ref):
    out_ref[0] = (jnp.sum(mine_ref[0][:, flag:flag + 1] + theirs_ref[0][:, flag:flag + 1]) > 0.0).astype(jnp.int32)


def decide(flag, mine, theirs):
    return pl.pallas_call(
        lambda *refs: decide_kernel(flag, *refs),
        out_shape=jax.ShapeDtypeStruct((1,), jnp.int32),
        out_specs=pl.BlockSpec(memory_space=pltpu.SMEM),
        compiler_params=pltpu.CompilerParams(vmem_limit_bytes=2 * 2**20),
        name="decide",
    )(mine, theirs)


def meeting_plan(states, proj_weight, cluster_of):
    owners = lax.axis_size("owner")
    columns = owners // ROWS
    docs = states.shape[0]
    hot = 3 * docs // owners
    flag = layout(docs, hot)[2]

    owner, core = lax.axis_index("owner"), lax.axis_index("split")
    place = jnp.stack([owner // ROWS, owner % ROWS, core]).astype(jnp.int32)
    same, other, slot = prep(hot, place, cluster_of, states, proj_weight)

    def move(a, to, row=0, core=0):
        pairs = [
            (
                (z * ROWS + y) * 2 + c,
                (to[z] * ROWS + (y ^ row)) * 2 + (c ^ (core if row or to[z] != z else 1)),
            )
            for z in range(columns) for y in range(ROWS) for c in range(2)
        ]
        return lax.ppermute(a, ("owner", "split"), pairs)

    STAY, OUTER, MIDDLE, TWO = (0, 1, 2, 3), (1, 0, 3, 2), (0, 2, 1, 3), (2, 3, 0, 1)
    TO_MIDDLE = (2, 0, 3, 1)

    def meet(name, made, tasks, **options):
        return score(name, docs, hot, place, blocks, pairs, made, tasks, sums, **options)

    blocks, pairs, sums = {OWN: same}, {}, ()
    blocks[CORE] = move(same, STAY, core=1)
    blocks[PAIR] = move(other, OUTER)
    blocks[CORE], still_same, other = lax.optimization_barrier((blocks[CORE], same, other))
    blocks[ROW] = move(still_same, STAY, row=1)
    blocks[NEXT] = move(other, MIDDLE)
    sums, pairs = meet("own", HERE, [((OWN,), HERE, False, None), ((CORE,), HERE, False, "core0")], weight=2**33)

    blocks[PAIR], _ = lax.optimization_barrier((blocks[PAIR], sums[0]))
    blocks[ROW], blocks[NEXT] = lax.optimization_barrier((blocks[ROW], blocks[NEXT]))
    blocks[FAR] = move(same, TO_MIDDLE)
    blocks[PAIR_ROW] = move(blocks[PAIR], STAY, row=1)
    blocks[PAIR_CORE] = move(blocks[PAIR], STAY, core=1)
    blocks[DIAG] = move(blocks[ROW], STAY, core=1)
    sums, pairs = meet(
        "pair", THERE,
        [((PAIR,), THERE, False, None), ((PAIR_CORE,), THERE, False, "core1"), ((NEXT,), HERE, True, None),
         ((NEXT,), THERE, True, None)],
        weight=2**33,
    )
    sums, pairs = meet(
        "row", ACROSS,
        [((PAIR,), HERE, True, None), ((PAIR,), ACROSS, True, None), ((NEXT,), ACROSS, True, None),
         ((ROW,), HERE, False, "row0"), ((DIAG,), HERE, False, "row1")],
    )
    blocks[PAIR_ROW], _ = lax.optimization_barrier((blocks[PAIR_ROW], sums[0]))
    blocks[PAIR_DIAG] = move(blocks[PAIR_ROW], STAY, core=1)
    sums, pairs = meet("far", (), [((FAR,), p, True, None) for p in (HERE, THERE, ACROSS)])
    sums, pairs = meet(
        "last", (),
        [((NEXT, FAR), right, False, None) for right in (PAIR_ROW, PAIR_DIAG)]
        + [((PAIR_ROW,), THERE, False, "row1"), ((PAIR_DIAG,), THERE, False, "row0")],
        doubted=(PAIR_ROW, PAIR_DIAG),
    )
    kept, by_core, to_next, to_far = sums
    from_core, from_far = move(by_core, STAY, core=1), move(to_far, TWO)
    from_core, to_next = lax.optimization_barrier((from_core, to_next))
    from_next = move(to_next, MIDDLE)
    own, pair, row, pair_row = (kept[k:k + 1] + from_core[k:k + 1] for k in (0, 1, 2, 3))
    home = [
        own, from_next, from_far,
        move(pair, OUTER), move(row, STAY, row=1), move(pair_row, OUTER, row=1),
    ]
    return lax.cond(
        decide(flag, to_far, from_far)[0] > 0,
        lambda states, proj_weight, cluster_of, *_: ring_plan(states, proj_weight, cluster_of),
        lambda states, proj_weight, cluster_of, slot, *home: finish(slot, home).reshape(docs),
        states, proj_weight, cluster_of, slot, *home,
    )


def on_device(states, proj_weight, cluster_of):
    if (lax.axis_size("owner"), lax.axis_size("split")) == (8, 2) and states.shape[0] == 512:
        return meeting_plan(states, proj_weight, cluster_of)
    return owner_plan(states, proj_weight, cluster_of)


def solution(mesh):
    placed = (P(("parts", "owner", "split"), None), P(), P(("parts", "owner", "split")))
    return jax.shard_map(
        on_device,
        mesh=mesh,
        in_specs=placed,
        out_specs=P(("parts", "owner", "split")),
        check_vma=False,
    )
```

```python
import math

import jax
import jax.numpy as jnp
from jax import lax
from jax.experimental import pallas as pl
from jax.experimental.pallas import tpu as pltpu
from jax.sharding import PartitionSpec as P

CLUS_OWN = 2
TAU = 0.05
THRESH = 0.2
EPS = 1e-06
LOG2E = math.log2(math.e)
SCALE = LOG2E / TAU
SHIFT = THRESH * LOG2E / TAU

ROWS = 2
F32 = jnp.float32
BF16 = jnp.bfloat16


def prepare(states, proj_weight):
    projected = jnp.dot(states, proj_weight, preferred_element_type=jnp.float32)
    unit = projected * lax.rsqrt(jnp.sum(projected * projected, axis=1, keepdims=True) + EPS)
    peak = jnp.max(jnp.abs(unit), axis=1).astype(jnp.bfloat16)
    quant = (unit / peak.astype(jnp.float32)[:, None]).astype(jnp.bfloat16)
    return (quant, peak)


def similarity_scores(
    own_quant, own_peak, own_cluster, own_index, col_quant, col_peak, col_cluster, col_index
):
    row_count = own_quant.shape[0]
    block = math.gcd(row_count, 768)
    col_scale = col_peak.astype(jnp.float32)

    def one_block(start):
        quant_rows = lax.dynamic_slice_in_dim(own_quant, start, block, 0)
        scale_rows = lax.dynamic_slice_in_dim(own_peak, start, block, 0).astype(jnp.float32)
        cluster_rows = lax.dynamic_slice_in_dim(own_cluster, start, block, 0)
        index_rows = lax.dynamic_slice_in_dim(own_index, start, block, 0)
        inner = lax.dot_general(
            quant_rows, col_quant, (((1,), (1,)), ((), ())), preferred_element_type=jnp.float32
        )
        cosine = inner * scale_rows[:, None] * col_scale[None, :]
        same = (cluster_rows[:, None] == col_cluster[None, :]) & (
            index_rows[:, None] != col_index[None, :]
        )
        weights = jnp.where(same, jnp.exp((cosine - THRESH) / TAU), jnp.zeros_like(cosine))
        return jnp.log(1.0 + jnp.sum(weights, axis=1))

    starts = jnp.arange(row_count // block, dtype=jnp.int32) * block
    return lax.map(one_block, starts).reshape(row_count)


def owner_plan(states, proj_weight, cluster_of):
    owners = lax.axis_size("owner")
    splits = lax.axis_size("split")
    half_index = lax.axis_index("split")
    doc_count = states.shape[0]
    capacity = 3 * doc_count // owners
    width = proj_weight.shape[1]
    slot_total = owners * capacity
    quant, peak = prepare(states, proj_weight)
    group_of = cluster_of // CLUS_OWN
    onehot = (group_of[:, None] == jnp.arange(owners, dtype=jnp.int32)[None, :]).astype(jnp.int32)
    before = jnp.cumsum(onehot, axis=0) - onehot
    target = group_of * capacity + jnp.sum(before * onehot, axis=1)
    quant_slots = (
        jnp.zeros((slot_total, width), jnp.bfloat16)
        .at[target]
        .set(quant)
        .reshape(owners, capacity, width)
    )
    peak_slots = (
        jnp.zeros((slot_total,), jnp.bfloat16).at[target].set(peak).reshape(owners, capacity)
    )
    cluster_slots = (
        jnp.full((slot_total,), -1, jnp.int32).at[target].set(cluster_of).reshape(owners, capacity)
    )
    positions = (
        jnp.arange(owners, dtype=jnp.int32)[:, None] * (splits * capacity)
        + jnp.arange(capacity, dtype=jnp.int32)[None, :]
    )
    own_index = (positions + half_index * capacity).reshape(slot_total)
    col_index = jnp.arange(splits * slot_total, dtype=jnp.int32)
    own_quant, own_peak, own_cluster = (
        lax.all_to_all(a, "owner", split_axis=0, concat_axis=0, tiled=True)
        for a in (quant_slots, peak_slots, cluster_slots)
    )
    all_quant, all_peak, all_cluster = (
        lax.all_gather(a, "split", axis=1, tiled=True) for a in (own_quant, own_peak, own_cluster)
    )
    scores = similarity_scores(
        own_quant.reshape(slot_total, width),
        own_peak.reshape(slot_total),
        own_cluster.reshape(slot_total),
        own_index,
        all_quant.reshape(splits * slot_total, width),
        all_peak.reshape(splits * slot_total),
        all_cluster.reshape(splits * slot_total),
        col_index,
    )
    returned = lax.all_to_all(
        scores.reshape(owners, capacity), "owner", split_axis=0, concat_axis=0, tiled=True
    )
    return returned.reshape(slot_total)[target]


def ring_plan(states, proj_weight, cluster_of):
    axes = ("owner", "split")
    devices = lax.axis_size("owner") * lax.axis_size("split")
    ring = [(i, (i + 1) % devices) for i in range(devices)]
    quant, peak = prepare(states, proj_weight)
    scale = peak.astype(F32)
    place = jnp.arange(states.shape[0], dtype=jnp.int32)

    def weights(block, block_peak, block_cluster):
        inner = lax.dot_general(quant, block, (((1,), (1,)), ((), ())), preferred_element_type=F32)
        cosine = inner * scale[:, None] * block_peak.astype(F32)[None, :]
        same = cluster_of[:, None] == block_cluster[None, :]
        return jnp.where(same, jnp.exp((cosine - THRESH) / TAU), jnp.zeros_like(cosine))

    def meet(_, carry):
        passed = [lax.ppermute(a, axes, ring) for a in carry[1:]]
        return (carry[0] + jnp.sum(weights(*passed), axis=1), *passed)

    own = (quant, peak, cluster_of)
    others = place[:, None] != place[None, :]
    total = jnp.sum(jnp.where(others, weights(*own), 0.0), axis=1)
    total = lax.fori_loop(1, devices, meet, (total, *own))[0]
    return jnp.log(1.0 + total)


def up(n, m):
    return -(-n // m) * m


META = 8


def layout(docs, hot):
    rest = docs - hot
    first = up(rest, 128)
    flag = first + hot
    return rest, first, flag, up(flag + 1, 128)


def prep_kernel(hot, place_ref, cl_ref, st_ref, w_ref, same_ref, other_ref, slot_ref, vectors):
    docs = st_ref.shape[0]
    rest, first, flag, lanes = layout(docs, hot)
    tile = 128

    cluster = cl_ref[...]
    group = cluster // CLUS_OWN
    member = lax.broadcasted_iota(jnp.int32, (8, docs), 0) == group
    full = jnp.sum(member.astype(F32), axis=1, keepdims=True) == float(hot)
    chosen = jnp.min(
        jnp.where(full, lax.broadcasted_iota(jnp.int32, (8, 1), 0), 8), axis=0, keepdims=True
    )
    doubt = jnp.where(jnp.sum(full.astype(F32), axis=0, keepdims=True) == 1.0, 0.0, 1.0)
    in_hot = group == chosen

    for t in range(docs // tile):
        rows = slice(t * tile, (t + 1) * tile)
        projected = jnp.dot(st_ref[rows, :], w_ref[...], preferred_element_type=F32)
        norm = lax.rsqrt(jnp.sum(projected * projected, axis=1, keepdims=True) + EPS)
        vectors[rows, :] = (projected * (norm * math.sqrt(SCALE))).astype(BF16)

    ahead = (
        lax.broadcasted_iota(jnp.int32, (docs, docs), 0) < lax.broadcasted_iota(jnp.int32, (docs, docs), 1)
    ).astype(F32).astype(BF16)
    hot_rows = jnp.broadcast_to(in_hot.astype(F32), (8, docs)).astype(BF16)
    rank = jnp.dot(hot_rows, ahead, preferred_element_type=F32)[0:1, :].astype(jnp.int32)
    place = lax.broadcasted_iota(jnp.int32, (1, docs), 1)
    slot = jnp.where(in_hot, first + rank, place - rank)
    slot_ref[...] = slot

    sort = (lax.broadcasted_iota(jnp.int32, (lanes, docs), 0) == slot).astype(F32).astype(BF16)
    cluster_rows = jnp.broadcast_to(cluster.astype(F32), (META, docs)).astype(BF16)
    sorted_n = jnp.dot(sort[:rest, :], vectors[...], preferred_element_type=F32).astype(BF16)
    sorted_h = jnp.dot(sort[first:flag, :], vectors[...], preferred_element_type=F32).astype(BF16)
    ids = lax.dot_general(
        cluster_rows, sort, (((1,), (1,)), ((), ())), preferred_element_type=F32
    )
    ids = ids.astype(BF16)


    def fill_n(ref):
        ref[:rest, :] = sorted_n
        ref[rest:, :] = jnp.zeros((META, ref.shape[1]), BF16)
        ref[rest:, :first] = ids[:, :first]
        ref[rest:, first:first + 128] = jnp.broadcast_to(doubt.astype(BF16), (META, 128))

    def fill_h(ref):
        ref[:hot, :] = sorted_h
        ref[hot:, :] = jnp.zeros((rest + META - hot, ref.shape[1]), BF16)
        ref[rest:, :lanes - first] = ids[:, first:]
        ref[rest:, first:first + 128] = jnp.broadcast_to(doubt.astype(BF16), (META, 128))

    even = lax.rem(place_ref[0], 2) == 0

    @pl.when(even)
    def _():
        fill_h(same_ref)
        fill_n(other_ref)

    @pl.when(jnp.logical_not(even))
    def _():
        fill_n(same_ref)
        fill_h(other_ref)


def prep(hot, place, cluster_of, states, proj_weight):
    docs, width = states.shape[0], proj_weight.shape[1]
    rest = docs - hot
    shape = jax.ShapeDtypeStruct
    vmem = pl.BlockSpec(memory_space=pltpu.VMEM)
    return pl.pallas_call(
        lambda *refs: prep_kernel(hot, *refs),
        out_shape=(
            shape((rest + META, width), BF16),
            shape((rest + META, width), BF16),
            shape((1, docs), jnp.int32),
        ),
        in_specs=[pl.BlockSpec(memory_space=pltpu.SMEM), vmem, vmem, vmem],
        scratch_shapes=[pltpu.VMEM((docs, width), BF16)],
        compiler_params=pltpu.CompilerParams(vmem_limit_bytes=24 * 2**20),
        name="prep",
    )(place, cluster_of.reshape(1, docs), states, proj_weight)


OWN, PAIR = "own", "pair"
CORE, PAIR_CORE = "core", "pair_core"
ROW, PAIR_ROW = "row", "pair_row"
DIAG, PAIR_DIAG = "diag", "pair_diag"
NEXT, FAR = "next", "far"
GROUPS = ((OWN, PAIR, ROW, PAIR_ROW), (CORE, PAIR_CORE, DIAG, PAIR_DIAG), (NEXT,), (FAR,))
TILE = 256
HERE, THERE, ACROSS = (OWN, CORE), (PAIR, PAIR_CORE), (ROW, DIAG)


def score_kernel(docs, hot, names, given, made, tasks, doubted, ready, keep, carries, *refs):
    rest, first, flag, lanes = layout(docs, hot)
    place_ref, refs = refs[0], refs[1:]
    blocks, refs = dict(zip(names, refs[:len(names)])), refs[len(names):]
    pairs, refs = {p: refs[2 * k:2 * k + 2] for k, p in enumerate(given)}, refs[2 * len(given):]
    ready, refs = dict(zip(ready, refs[:len(ready)])), refs[len(ready):]
    before, refs = refs[:len(GROUPS) * carries], refs[len(GROUPS) * carries:]
    outs, refs = refs[:len(GROUPS)], refs[len(GROUPS):]
    if made:
        pairs[made], refs = refs[:2], refs[2:]
    kept, parts = dict(zip(keep, refs[:len(keep)])), refs[-1]
    for k, out in enumerate(outs):
        out[...] = before[k][...] if carries else jnp.zeros(out.shape, F32)
    spots = {name: (out, k) for out, group in zip(outs, GROUPS) for k, name in enumerate(group)}
    z, y, c = place_ref[0], place_ref[1], place_ref[2]
    when = {"core0": c == 0, "core1": c == 1, "row0": y == 0, "row1": y == 1}
    middle = (z == 1) | (z == 2)

    def meet(count, start):
        lane = slice(start, start + count)
        wide, two = up(count, 128), 2 * count

        def column(name):
            if name in ready:
                return ready[name][0:count, :]
            return blocks[name][rest:, 0:wide].astype(F32)[0:8, :].T[0:count, :]

        columns = {name: column(name) for name in made + keep}
        for name in keep:
            kept[name][0:count, :] = columns[name]
        if made:
            turned, notes = pairs[made]
            turned[:, 0:two] = jnp.concatenate([blocks[name][:count, :] for name in made], axis=0).T
            notes[:, 0:two] = jnp.concatenate([columns[name] for name in made], axis=0).T

        for left in dict.fromkeys(task[0] for task in tasks):

            def work(left=left):
                own_tasks = [task for task in tasks if task[0] == left]
                rows = count * len(left)
                block = blocks[left[0]][:count, :]
                mine = [columns[name] if name in columns else column(name) for name in left]
                mine = mine[0][:, 0:1] if len(mine) == 1 else jnp.concatenate(mine, axis=0)[:, 0:1]
                for name in left[1:]:
                    block = jnp.concatenate([block, blocks[name][:count, :]], axis=0)
                fresh = True
                for _, right, both, _ in own_tasks:
                    if right in blocks:
                        span, rights, diagonal = count, (right,), False
                        ids = blocks[right][rest:, 0:wide].astype(F32)[0:1, 0:count]
                    else:
                        turned, notes = pairs[right]
                        span, rights, diagonal = two if both else wide, right[:1 + both], left == right[:1]
                        ids = notes[0:1, 0:span]
                        if not both:
                            ids = jnp.where(lax.broadcasted_iota(jnp.int32, ids.shape, 1) < count, ids, -1.0)
                    totals = []
                    for low in range(0, span, TILE):
                        high = min(low + TILE, span)
                        if right in blocks:
                            inner = lax.dot_general(
                                block, blocks[right][low:high, :], (((1,), (1,)), ((), ())),
                                preferred_element_type=F32,
                            )
                        else:
                            inner = jnp.dot(block, turned[:, low:high], preferred_element_type=F32)
                        same = mine == ids[:, low:high]
                        if diagonal:
                            same &= lax.broadcasted_iota(jnp.int32, inner.shape, 0) != (
                                lax.broadcasted_iota(jnp.int32, inner.shape, 1) + low
                            )
                        weights = jnp.where(same, jnp.exp2(inner), 0.0)
                        totals.append(jnp.sum(weights, axis=0, keepdims=True))
                        if not diagonal:
                            part = None
                            for t in range(0, high - low, 128):
                                piece = weights[:, t:t + 128]
                                if piece.shape[1] < 128:
                                    blank = jnp.zeros((rows, 128 - piece.shape[1]), F32)
                                    piece = jnp.concatenate([piece, blank], axis=1)
                                part = piece if part is None else part + piece
                            if fresh:
                                parts[0:rows, :] = part
                            else:
                                parts[0:rows, :] += part
                            fresh = False
                    total = jnp.concatenate(totals, axis=1) if len(totals) > 1 else totals[0]
                    for k, name in enumerate(rights):
                        out, spot = spots[name]
                        out[spot, :, lane] += total[:, k * count:(k + 1) * count]
                if not fresh:
                    part = parts[0:rows, :]
                    high = part.astype(BF16)
                    low = (part - high.astype(F32)).astype(BF16)
                    total = lax.dot_general(
                        jnp.ones((16, 256), BF16), jnp.concatenate([high, low], axis=1),
                        (((1,), (1,)), ((), ())), preferred_element_type=F32,
                    )
                    for k, name in enumerate(left):
                        out, spot = spots[name]
                        out[spot, :, lane] += total[0:1, k * count:(k + 1) * count]

            condition = [task[3] for task in tasks if task[0] == left][0]
            if left[0] in (NEXT, FAR):
                pl.when(middle)(work)
            elif condition:
                pl.when(when[condition])(work)
            else:
                work()

    pl.when(lax.rem(z, 2) == 0)(lambda: meet(hot, first))
    pl.when(lax.rem(z, 2) == 1)(lambda: meet(rest, 0))

    if doubted:
        doubt = sum(blocks[name][rest:, first:first + 128].astype(F32)[0:1, 0:1] for name in doubted)
        out, k = spots[FAR]
        out[k] += jnp.where(lax.broadcasted_iota(jnp.int32, (1, lanes), 1) == flag, doubt, 0.0)


def score(name, docs, hot, place, blocks, pairs, made, tasks, sums, cols, doubted=(), keep=(), weight=1):
    rest, _, _, lanes = layout(docs, hot)
    names = list(dict.fromkeys([*made, *(name for task in tasks for name in task[0])]))
    given = [p for p in pairs if any(p == task[1] for task in tasks)]
    width = blocks[OWN].shape[1]
    vmem = pl.BlockSpec(memory_space=pltpu.VMEM)
    ready = [b for b in names if b in cols]
    arrays = [blocks[b] for b in names] + [a for p in given for a in pairs[p]] + [cols[b] for b in ready] + list(sums)
    shapes = [jax.ShapeDtypeStruct((len(group), 1, lanes), F32) for group in GROUPS]
    if made:
        shapes += [jax.ShapeDtypeStruct((width, 2 * rest), BF16), jax.ShapeDtypeStruct((8, 2 * rest), F32)]
    shapes += [jax.ShapeDtypeStruct((rest, 8), F32) for _ in keep]
    out = pl.pallas_call(
        lambda *refs: score_kernel(
            docs, hot, names, given, made, tasks, doubted or made, ready, keep, bool(sums), *refs
        ),
        out_shape=tuple(shapes),
        in_specs=[pl.BlockSpec(memory_space=pltpu.SMEM)] + [vmem] * len(arrays),
        out_specs=tuple(vmem for _ in shapes),
        scratch_shapes=[pltpu.VMEM((2 * rest, 128), F32)],
        compiler_params=pltpu.CompilerParams(vmem_limit_bytes=20 * 2**20),
        cost_estimate=pl.CostEstimate(flops=weight, bytes_accessed=2**10, transcendentals=0),
        name=name,
    )(place, *arrays)
    count = len(GROUPS)
    cols = {**cols, **dict(zip(keep, out[len(out) - len(keep):]))}
    return out[:count], {**pairs, made: out[count:count + 2]} if made else pairs, cols


def finish_kernel(slot_ref, *refs):
    sums, out_ref = refs[:-1], refs[-1]
    total = sums[0][0]
    for ref in sums[1:]:
        total += ref[0]
    lanes, docs = total.shape[1], slot_ref.shape[1]
    values = jnp.broadcast_to(jnp.log(1.0 + total * 2.0**-SHIFT), (8, lanes)).T[:, 0:1]
    here = lax.broadcasted_iota(jnp.int32, (lanes, docs), 0) == slot_ref[...]
    out_ref[...] = jnp.sum(jnp.where(here, values, 0.0), axis=0, keepdims=True)


def finish(slot, sums):
    return pl.pallas_call(
        finish_kernel,
        out_shape=jax.ShapeDtypeStruct(slot.shape, F32),
        compiler_params=pltpu.CompilerParams(vmem_limit_bytes=6 * 2**20),
        name="finish",
    )(slot, *sums)


def decide_kernel(flag, mine_ref, theirs_ref, out_ref):
    out_ref[0] = (jnp.sum(mine_ref[0][:, flag:flag + 1] + theirs_ref[0][:, flag:flag + 1]) > 0.0).astype(jnp.int32)


def decide(flag, mine, theirs):
    return pl.pallas_call(
        lambda *refs: decide_kernel(flag, *refs),
        out_shape=jax.ShapeDtypeStruct((1,), jnp.int32),
        out_specs=pl.BlockSpec(memory_space=pltpu.SMEM),
        compiler_params=pltpu.CompilerParams(vmem_limit_bytes=2 * 2**20),
        name="decide",
    )(mine, theirs)


def meeting_plan(states, proj_weight, cluster_of):
    owners = lax.axis_size("owner")
    columns = owners // ROWS
    docs = states.shape[0]
    hot = 3 * docs // owners
    flag = layout(docs, hot)[2]

    owner, core = lax.axis_index("owner"), lax.axis_index("split")
    place = jnp.stack([owner // ROWS, owner % ROWS, core]).astype(jnp.int32)
    same, other, slot = prep(hot, place, cluster_of, states, proj_weight)

    def move(a, to, row=0, core=0):
        pairs = [
            (
                (z * ROWS + y) * 2 + c,
                (to[z] * ROWS + (y ^ row)) * 2 + (c ^ (core if row or to[z] != z else 1)),
            )
            for z in range(columns) for y in range(ROWS) for c in range(2)
        ]
        return lax.ppermute(a, ("owner", "split"), pairs)

    STAY, OUTER, MIDDLE, TWO = (0, 1, 2, 3), (1, 0, 3, 2), (0, 2, 1, 3), (2, 3, 0, 1)
    TO_MIDDLE = (2, 0, 3, 1)

    def meet(name, made, tasks, **options):
        return score(name, docs, hot, place, blocks, pairs, made, tasks, sums, cols, **options)

    blocks, pairs, sums, cols = {OWN: same}, {}, (), {}
    blocks[CORE] = move(same, STAY, core=1)
    blocks[PAIR] = move(other, OUTER)
    blocks[CORE], still_same, other = lax.optimization_barrier((blocks[CORE], same, other))
    blocks[ROW] = move(still_same, STAY, row=1)
    blocks[NEXT] = move(other, MIDDLE)
    sums, pairs, cols = meet("own", HERE, [((OWN,), HERE, False, None), ((CORE,), HERE, False, "core0")], weight=2**33)

    blocks[PAIR], _ = lax.optimization_barrier((blocks[PAIR], sums[0]))
    blocks[ROW], blocks[NEXT] = lax.optimization_barrier((blocks[ROW], blocks[NEXT]))
    blocks[FAR] = move(same, TO_MIDDLE)
    blocks[PAIR_ROW] = move(blocks[PAIR], STAY, row=1)
    blocks[PAIR_CORE] = move(blocks[PAIR], STAY, core=1)
    blocks[DIAG] = move(blocks[ROW], STAY, core=1)
    sums, pairs, cols = meet(
        "pair", THERE,
        [((PAIR,), THERE, False, None), ((PAIR_CORE,), THERE, False, "core1"), ((NEXT,), HERE, True, None),
         ((NEXT,), THERE, True, None)],
        keep=(NEXT,), weight=2**33,
    )
    sums, pairs, cols = meet(
        "row", ACROSS,
        [((PAIR,), HERE, True, None), ((PAIR,), ACROSS, True, None), ((NEXT,), ACROSS, True, None),
         ((ROW,), HERE, False, "row0"), ((DIAG,), HERE, False, "row1")],
    )
    blocks[PAIR_ROW], _ = lax.optimization_barrier((blocks[PAIR_ROW], sums[0]))
    blocks[PAIR_DIAG] = move(blocks[PAIR_ROW], STAY, core=1)
    sums, pairs, cols = meet(
        "far", (), [((FAR,), p, True, None) for p in (HERE, THERE, ACROSS)], keep=(FAR,)
    )
    sums, pairs, cols = meet(
        "last", (),
        [((NEXT, FAR), right, False, None) for right in (PAIR_ROW, PAIR_DIAG)]
        + [((PAIR_ROW,), THERE, False, "row1"), ((PAIR_DIAG,), THERE, False, "row0")],
        doubted=(PAIR_ROW, PAIR_DIAG),
    )
    kept, by_core, to_next, to_far = sums
    from_core, from_far = move(by_core, STAY, core=1), move(to_far, TWO)
    from_core, to_next = lax.optimization_barrier((from_core, to_next))
    from_next = move(to_next, MIDDLE)
    own, pair, row, pair_row = (kept[k:k + 1] + from_core[k:k + 1] for k in (0, 1, 2, 3))
    home = [
        own, from_next, from_far,
        move(pair_row, OUTER, row=1), move(row, STAY, row=1), move(pair, OUTER),
    ]
    return lax.cond(
        decide(flag, to_far, from_far)[0] > 0,
        lambda states, proj_weight, cluster_of, *_: ring_plan(states, proj_weight, cluster_of),
        lambda states, proj_weight, cluster_of, slot, *home: finish(slot, home).reshape(docs),
        states, proj_weight, cluster_of, slot, *home,
    )


def on_device(states, proj_weight, cluster_of):
    if (lax.axis_size("owner"), lax.axis_size("split")) == (8, 2) and states.shape[0] == 512:
        return meeting_plan(states, proj_weight, cluster_of)
    return owner_plan(states, proj_weight, cluster_of)


def solution(mesh):
    placed = (P(("parts", "owner", "split"), None), P(), P(("parts", "owner", "split")))
    return jax.shard_map(
        on_device,
        mesh=mesh,
        in_specs=placed,
        out_specs=P(("parts", "owner", "split")),
        check_vma=False,
    )
```

```python
import math

import jax
import jax.numpy as jnp
from jax import lax
from jax.experimental import pallas as pl
from jax.experimental.pallas import tpu as pltpu
from jax.sharding import PartitionSpec as P

CLUS_OWN = 2
TAU = 0.05
THRESH = 0.2
EPS = 1e-06
LOG2E = math.log2(math.e)
SCALE = LOG2E / TAU
SHIFT = THRESH * LOG2E / TAU

ROWS = 2
F32 = jnp.float32
BF16 = jnp.bfloat16


def prepare(states, proj_weight):
    projected = jnp.dot(states, proj_weight, preferred_element_type=jnp.float32)
    unit = projected * lax.rsqrt(jnp.sum(projected * projected, axis=1, keepdims=True) + EPS)
    peak = jnp.max(jnp.abs(unit), axis=1).astype(jnp.bfloat16)
    quant = (unit / peak.astype(jnp.float32)[:, None]).astype(jnp.bfloat16)
    return (quant, peak)


def similarity_scores(
    own_quant, own_peak, own_cluster, own_index, col_quant, col_peak, col_cluster, col_index
):
    row_count = own_quant.shape[0]
    block = math.gcd(row_count, 768)
    col_scale = col_peak.astype(jnp.float32)

    def one_block(start):
        quant_rows = lax.dynamic_slice_in_dim(own_quant, start, block, 0)
        scale_rows = lax.dynamic_slice_in_dim(own_peak, start, block, 0).astype(jnp.float32)
        cluster_rows = lax.dynamic_slice_in_dim(own_cluster, start, block, 0)
        index_rows = lax.dynamic_slice_in_dim(own_index, start, block, 0)
        inner = lax.dot_general(
            quant_rows, col_quant, (((1,), (1,)), ((), ())), preferred_element_type=jnp.float32
        )
        cosine = inner * scale_rows[:, None] * col_scale[None, :]
        same = (cluster_rows[:, None] == col_cluster[None, :]) & (
            index_rows[:, None] != col_index[None, :]
        )
        weights = jnp.where(same, jnp.exp((cosine - THRESH) / TAU), jnp.zeros_like(cosine))
        return jnp.log(1.0 + jnp.sum(weights, axis=1))

    starts = jnp.arange(row_count // block, dtype=jnp.int32) * block
    return lax.map(one_block, starts).reshape(row_count)


def owner_plan(states, proj_weight, cluster_of):
    owners = lax.axis_size("owner")
    splits = lax.axis_size("split")
    half_index = lax.axis_index("split")
    doc_count = states.shape[0]
    capacity = 3 * doc_count // owners
    width = proj_weight.shape[1]
    slot_total = owners * capacity
    quant, peak = prepare(states, proj_weight)
    group_of = cluster_of // CLUS_OWN
    onehot = (group_of[:, None] == jnp.arange(owners, dtype=jnp.int32)[None, :]).astype(jnp.int32)
    before = jnp.cumsum(onehot, axis=0) - onehot
    target = group_of * capacity + jnp.sum(before * onehot, axis=1)
    quant_slots = (
        jnp.zeros((slot_total, width), jnp.bfloat16)
        .at[target]
        .set(quant)
        .reshape(owners, capacity, width)
    )
    peak_slots = (
        jnp.zeros((slot_total,), jnp.bfloat16).at[target].set(peak).reshape(owners, capacity)
    )
    cluster_slots = (
        jnp.full((slot_total,), -1, jnp.int32).at[target].set(cluster_of).reshape(owners, capacity)
    )
    positions = (
        jnp.arange(owners, dtype=jnp.int32)[:, None] * (splits * capacity)
        + jnp.arange(capacity, dtype=jnp.int32)[None, :]
    )
    own_index = (positions + half_index * capacity).reshape(slot_total)
    col_index = jnp.arange(splits * slot_total, dtype=jnp.int32)
    own_quant, own_peak, own_cluster = (
        lax.all_to_all(a, "owner", split_axis=0, concat_axis=0, tiled=True)
        for a in (quant_slots, peak_slots, cluster_slots)
    )
    all_quant, all_peak, all_cluster = (
        lax.all_gather(a, "split", axis=1, tiled=True) for a in (own_quant, own_peak, own_cluster)
    )
    scores = similarity_scores(
        own_quant.reshape(slot_total, width),
        own_peak.reshape(slot_total),
        own_cluster.reshape(slot_total),
        own_index,
        all_quant.reshape(splits * slot_total, width),
        all_peak.reshape(splits * slot_total),
        all_cluster.reshape(splits * slot_total),
        col_index,
    )
    returned = lax.all_to_all(
        scores.reshape(owners, capacity), "owner", split_axis=0, concat_axis=0, tiled=True
    )
    return returned.reshape(slot_total)[target]


def ring_plan(states, proj_weight, cluster_of):
    axes = ("owner", "split")
    devices = lax.axis_size("owner") * lax.axis_size("split")
    ring = [(i, (i + 1) % devices) for i in range(devices)]
    quant, peak = prepare(states, proj_weight)
    scale = peak.astype(F32)
    place = jnp.arange(states.shape[0], dtype=jnp.int32)

    def weights(block, block_peak, block_cluster):
        inner = lax.dot_general(quant, block, (((1,), (1,)), ((), ())), preferred_element_type=F32)
        cosine = inner * scale[:, None] * block_peak.astype(F32)[None, :]
        same = cluster_of[:, None] == block_cluster[None, :]
        return jnp.where(same, jnp.exp((cosine - THRESH) / TAU), jnp.zeros_like(cosine))

    def meet(_, carry):
        passed = [lax.ppermute(a, axes, ring) for a in carry[1:]]
        return (carry[0] + jnp.sum(weights(*passed), axis=1), *passed)

    own = (quant, peak, cluster_of)
    others = place[:, None] != place[None, :]
    total = jnp.sum(jnp.where(others, weights(*own), 0.0), axis=1)
    total = lax.fori_loop(1, devices, meet, (total, *own))[0]
    return jnp.log(1.0 + total)


def up(n, m):
    return -(-n // m) * m


META = 8


def layout(docs, hot):
    rest = docs - hot
    first = up(rest, 128)
    flag = first + hot
    return rest, first, flag, up(flag + 1, 128)


def prep_kernel(hot, place_ref, cl_ref, st_ref, w_ref, same_ref, other_ref, slot_ref, vectors):
    docs = st_ref.shape[0]
    rest, first, flag, lanes = layout(docs, hot)
    tile = 256

    cluster = cl_ref[...]
    group = cluster // CLUS_OWN
    member = lax.broadcasted_iota(jnp.int32, (8, docs), 0) == group
    full = jnp.sum(member.astype(F32), axis=1, keepdims=True) == float(hot)
    chosen = jnp.min(
        jnp.where(full, lax.broadcasted_iota(jnp.int32, (8, 1), 0), 8), axis=0, keepdims=True
    )
    doubt = jnp.where(jnp.sum(full.astype(F32), axis=0, keepdims=True) == 1.0, 0.0, 1.0)
    in_hot = group == chosen

    for t in range(docs // tile):
        rows = slice(t * tile, (t + 1) * tile)
        projected = jnp.dot(st_ref[rows, :], w_ref[...], preferred_element_type=F32)
        norm = lax.rsqrt(jnp.sum(projected * projected, axis=1, keepdims=True) + EPS)
        vectors[rows, :] = (projected * (norm * math.sqrt(SCALE))).astype(BF16)

    hot_row = in_hot.astype(F32)
    runs = [hot_row[:, t:t + 128] for t in range(0, docs, 128)]
    ahead = (
        lax.broadcasted_iota(jnp.int32, (128, 128), 0) < lax.broadcasted_iota(jnp.int32, (128, 128), 1)
    ).astype(F32).astype(BF16)
    stack = jnp.concatenate(runs + [jnp.zeros((16 - len(runs), 128), F32)], axis=0)
    within = jnp.dot(stack.astype(BF16), ahead, preferred_element_type=F32)
    sizes = jnp.sum(stack, axis=1, keepdims=True)
    ranks, before = [], jnp.zeros((1, 1), F32)
    for k in range(len(runs)):
        ranks.append(within[k:k + 1, :] + before)
        before = before + sizes[k:k + 1, :]
    rank = jnp.concatenate(ranks, axis=1).astype(jnp.int32)
    place = lax.broadcasted_iota(jnp.int32, (1, docs), 1)
    slot = jnp.where(in_hot, first + rank, place - rank)
    slot_ref[...] = slot

    sort = (lax.broadcasted_iota(jnp.int32, (lanes, docs), 0) == slot).astype(F32).astype(BF16)
    cluster_rows = jnp.broadcast_to(cluster.astype(F32), (META, docs)).astype(BF16)
    sorted_n = jnp.dot(sort[:rest, :], vectors[...], preferred_element_type=F32).astype(BF16)
    sorted_h = jnp.dot(sort[first:flag, :], vectors[...], preferred_element_type=F32).astype(BF16)
    ids = lax.dot_general(
        cluster_rows, sort, (((1,), (1,)), ((), ())), preferred_element_type=F32
    )
    ids = ids.astype(BF16)


    def fill_n(ref):
        ref[:rest, :] = sorted_n
        ref[rest:, :] = jnp.zeros((META, ref.shape[1]), BF16)
        ref[rest:, :first] = ids[:, :first]
        ref[rest:, first:first + 128] = jnp.broadcast_to(doubt.astype(BF16), (META, 128))

    def fill_h(ref):
        ref[:hot, :] = sorted_h
        ref[hot:, :] = jnp.zeros((rest + META - hot, ref.shape[1]), BF16)
        ref[rest:, :lanes - first] = ids[:, first:]
        ref[rest:, first:first + 128] = jnp.broadcast_to(doubt.astype(BF16), (META, 128))

    even = lax.rem(place_ref[0], 2) == 0

    @pl.when(even)
    def _():
        fill_h(same_ref)
        fill_n(other_ref)

    @pl.when(jnp.logical_not(even))
    def _():
        fill_n(same_ref)
        fill_h(other_ref)


def prep(hot, place, cluster_of, states, proj_weight):
    docs, width = states.shape[0], proj_weight.shape[1]
    rest = docs - hot
    shape = jax.ShapeDtypeStruct
    vmem = pl.BlockSpec(memory_space=pltpu.VMEM)
    return pl.pallas_call(
        lambda *refs: prep_kernel(hot, *refs),
        out_shape=(
            shape((rest + META, width), BF16),
            shape((rest + META, width), BF16),
            shape((1, docs), jnp.int32),
        ),
        in_specs=[pl.BlockSpec(memory_space=pltpu.SMEM), vmem, vmem, vmem],
        scratch_shapes=[pltpu.VMEM((docs, width), BF16)],
        compiler_params=pltpu.CompilerParams(vmem_limit_bytes=24 * 2**20),
        name="prep",
    )(place, cluster_of.reshape(1, docs), states, proj_weight)


OWN, PAIR = "own", "pair"
CORE, PAIR_CORE = "core", "pair_core"
ROW, PAIR_ROW = "row", "pair_row"
DIAG, PAIR_DIAG = "diag", "pair_diag"
NEXT, FAR = "next", "far"
GROUPS = ((OWN, PAIR, ROW, PAIR_ROW), (CORE, PAIR_CORE, DIAG, PAIR_DIAG), (NEXT,), (FAR,))
TILE = 256
HERE, THERE, ACROSS = (OWN, CORE), (PAIR, PAIR_CORE), (ROW, DIAG)


def score_kernel(docs, hot, names, given, made, tasks, doubted, ready, keep, carries, *refs):
    rest, first, flag, lanes = layout(docs, hot)
    place_ref, refs = refs[0], refs[1:]
    blocks, refs = dict(zip(names, refs[:len(names)])), refs[len(names):]
    pairs, refs = {p: refs[2 * k:2 * k + 2] for k, p in enumerate(given)}, refs[2 * len(given):]
    ready, refs = dict(zip(ready, refs[:len(ready)])), refs[len(ready):]
    before, refs = refs[:len(GROUPS) * carries], refs[len(GROUPS) * carries:]
    outs, refs = refs[:len(GROUPS)], refs[len(GROUPS):]
    if made:
        pairs[made], refs = refs[:2], refs[2:]
    kept, parts = dict(zip(keep, refs[:len(keep)])), refs[-1]
    for k, out in enumerate(outs):
        out[...] = before[k][...] if carries else jnp.zeros(out.shape, F32)
    spots = {name: (out, k) for out, group in zip(outs, GROUPS) for k, name in enumerate(group)}
    z, y, c = place_ref[0], place_ref[1], place_ref[2]
    when = {"core0": c == 0, "core1": c == 1, "row0": y == 0, "row1": y == 1}
    middle = (z == 1) | (z == 2)

    def meet(count, start):
        lane = slice(start, start + count)
        wide, two = up(count, 128), 2 * count

        def column(name):
            if name in ready:
                return ready[name][0:count, :]
            return blocks[name][rest:, 0:wide].astype(F32)[0:8, :].T[0:count, :]

        columns = {name: column(name) for name in made + keep}
        for name in keep:
            kept[name][0:count, :] = columns[name]
        if made:
            turned, notes = pairs[made]
            turned[:, 0:two] = jnp.concatenate([blocks[name][:count, :] for name in made], axis=0).T
            notes[:, 0:two] = jnp.concatenate([columns[name] for name in made], axis=0).T

        for left in dict.fromkeys(task[0] for task in tasks):

            def work(left=left):
                own_tasks = [task for task in tasks if task[0] == left]
                rows = count * len(left)
                block = blocks[left[0]][:count, :]
                mine = [columns[name] if name in columns else column(name) for name in left]
                mine = mine[0][:, 0:1] if len(mine) == 1 else jnp.concatenate(mine, axis=0)[:, 0:1]
                for name in left[1:]:
                    block = jnp.concatenate([block, blocks[name][:count, :]], axis=0)
                fresh = True
                for _, right, both, _ in own_tasks:
                    if right in blocks:
                        span, rights, diagonal = count, (right,), False
                        ids = blocks[right][rest:, 0:wide].astype(F32)[0:1, 0:count]
                    else:
                        turned, notes = pairs[right]
                        span, rights, diagonal = two if both else wide, right[:1 + both], left == right[:1]
                        ids = notes[0:1, 0:span]
                        if not both:
                            ids = jnp.where(lax.broadcasted_iota(jnp.int32, ids.shape, 1) < count, ids, -1.0)
                    totals = []
                    for low in range(0, span, TILE):
                        high = min(low + TILE, span)
                        if right in blocks:
                            inner = lax.dot_general(
                                block, blocks[right][low:high, :], (((1,), (1,)), ((), ())),
                                preferred_element_type=F32,
                            )
                        else:
                            inner = jnp.dot(block, turned[:, low:high], preferred_element_type=F32)
                        same = mine == ids[:, low:high]
                        if diagonal:
                            same &= lax.broadcasted_iota(jnp.int32, inner.shape, 0) != (
                                lax.broadcasted_iota(jnp.int32, inner.shape, 1) + low
                            )
                        weights = jnp.where(same, jnp.exp2(inner), 0.0)
                        totals.append(jnp.sum(weights, axis=0, keepdims=True))
                        if not diagonal:
                            part = None
                            for t in range(0, high - low, 128):
                                piece = weights[:, t:t + 128]
                                if piece.shape[1] < 128:
                                    blank = jnp.zeros((rows, 128 - piece.shape[1]), F32)
                                    piece = jnp.concatenate([piece, blank], axis=1)
                                part = piece if part is None else part + piece
                            if fresh:
                                parts[0:rows, :] = part
                            else:
                                parts[0:rows, :] += part
                            fresh = False
                    total = jnp.concatenate(totals, axis=1) if len(totals) > 1 else totals[0]
                    for k, name in enumerate(rights):
                        out, spot = spots[name]
                        out[spot, :, lane] += total[:, k * count:(k + 1) * count]
                if not fresh:
                    part = parts[0:rows, :]
                    high = part.astype(BF16)
                    low = (part - high.astype(F32)).astype(BF16)
                    total = lax.dot_general(
                        jnp.ones((16, 256), BF16), jnp.concatenate([high, low], axis=1),
                        (((1,), (1,)), ((), ())), preferred_element_type=F32,
                    )
                    for k, name in enumerate(left):
                        out, spot = spots[name]
                        out[spot, :, lane] += total[0:1, k * count:(k + 1) * count]

            condition = [task[3] for task in tasks if task[0] == left][0]
            if left[0] in (NEXT, FAR):
                pl.when(middle)(work)
            elif condition:
                pl.when(when[condition])(work)
            else:
                work()

    pl.when(lax.rem(z, 2) == 0)(lambda: meet(hot, first))
    pl.when(lax.rem(z, 2) == 1)(lambda: meet(rest, 0))

    if doubted:
        doubt = sum(blocks[name][rest:, first:first + 128].astype(F32)[0:1, 0:1] for name in doubted)
        out, k = spots[FAR]
        out[k] += jnp.where(lax.broadcasted_iota(jnp.int32, (1, lanes), 1) == flag, doubt, 0.0)


def score(name, docs, hot, place, blocks, pairs, made, tasks, sums, cols, doubted=(), keep=(), weight=1):
    rest, _, _, lanes = layout(docs, hot)
    names = list(dict.fromkeys([*made, *(name for task in tasks for name in task[0])]))
    given = [p for p in pairs if any(p == task[1] for task in tasks)]
    width = blocks[OWN].shape[1]
    vmem = pl.BlockSpec(memory_space=pltpu.VMEM)
    ready = [b for b in names if b in cols]
    arrays = [blocks[b] for b in names] + [a for p in given for a in pairs[p]] + [cols[b] for b in ready] + list(sums)
    shapes = [jax.ShapeDtypeStruct((len(group), 1, lanes), F32) for group in GROUPS]
    if made:
        shapes += [jax.ShapeDtypeStruct((width, 2 * rest), BF16), jax.ShapeDtypeStruct((8, 2 * rest), F32)]
    shapes += [jax.ShapeDtypeStruct((rest, 8), F32) for _ in keep]
    out = pl.pallas_call(
        lambda *refs: score_kernel(
            docs, hot, names, given, made, tasks, doubted or made, ready, keep, bool(sums), *refs
        ),
        out_shape=tuple(shapes),
        in_specs=[pl.BlockSpec(memory_space=pltpu.SMEM)] + [vmem] * len(arrays),
        out_specs=tuple(vmem for _ in shapes),
        scratch_shapes=[pltpu.VMEM((2 * rest, 128), F32)],
        compiler_params=pltpu.CompilerParams(vmem_limit_bytes=20 * 2**20),
        cost_estimate=pl.CostEstimate(flops=weight, bytes_accessed=2**10, transcendentals=0),
        name=name,
    )(place, *arrays)
    count = len(GROUPS)
    cols = {**cols, **dict(zip(keep, out[len(out) - len(keep):]))}
    return out[:count], {**pairs, made: out[count:count + 2]} if made else pairs, cols


def finish_kernel(slot_ref, *refs):
    sums, out_ref = refs[:-1], refs[-1]
    total = sums[0][0]
    for ref in sums[1:]:
        total += ref[0]
    lanes, docs = total.shape[1], slot_ref.shape[1]
    values = jnp.broadcast_to(jnp.log(1.0 + total * 2.0**-SHIFT), (8, lanes)).T[:, 0:1]
    here = lax.broadcasted_iota(jnp.int32, (lanes, docs), 0) == slot_ref[...]
    out_ref[...] = jnp.sum(jnp.where(here, values, 0.0), axis=0, keepdims=True)


def finish(slot, sums):
    return pl.pallas_call(
        finish_kernel,
        out_shape=jax.ShapeDtypeStruct(slot.shape, F32),
        compiler_params=pltpu.CompilerParams(vmem_limit_bytes=6 * 2**20),
        name="finish",
    )(slot, *sums)


def decide_kernel(flag, mine_ref, theirs_ref, out_ref):
    out_ref[0] = (jnp.sum(mine_ref[0][:, flag:flag + 1] + theirs_ref[0][:, flag:flag + 1]) > 0.0).astype(jnp.int32)


def decide(flag, mine, theirs):
    return pl.pallas_call(
        lambda *refs: decide_kernel(flag, *refs),
        out_shape=jax.ShapeDtypeStruct((1,), jnp.int32),
        out_specs=pl.BlockSpec(memory_space=pltpu.SMEM),
        compiler_params=pltpu.CompilerParams(vmem_limit_bytes=2 * 2**20),
        name="decide",
    )(mine, theirs)


def meeting_plan(states, proj_weight, cluster_of):
    owners = lax.axis_size("owner")
    columns = owners // ROWS
    docs = states.shape[0]
    hot = 3 * docs // owners
    flag = layout(docs, hot)[2]

    owner, core = lax.axis_index("owner"), lax.axis_index("split")
    place = jnp.stack([owner // ROWS, owner % ROWS, core]).astype(jnp.int32)
    same, other, slot = prep(hot, place, cluster_of, states, proj_weight)

    def move(a, to, row=0, core=0):
        pairs = [
            (
                (z * ROWS + y) * 2 + c,
                (to[z] * ROWS + (y ^ row)) * 2 + (c ^ (core if row or to[z] != z else 1)),
            )
            for z in range(columns) for y in range(ROWS) for c in range(2)
        ]
        return lax.ppermute(a, ("owner", "split"), pairs)

    STAY, OUTER, MIDDLE, TWO = (0, 1, 2, 3), (1, 0, 3, 2), (0, 2, 1, 3), (2, 3, 0, 1)
    TO_MIDDLE = (2, 0, 3, 1)

    def meet(name, made, tasks, **options):
        return score(name, docs, hot, place, blocks, pairs, made, tasks, sums, cols, **options)

    blocks, pairs, sums, cols = {OWN: same}, {}, (), {}
    blocks[CORE] = move(same, STAY, core=1)
    blocks[PAIR] = move(other, OUTER)
    blocks[CORE], still_same, other = lax.optimization_barrier((blocks[CORE], same, other))
    blocks[ROW] = move(still_same, STAY, row=1)
    blocks[NEXT] = move(other, MIDDLE)
    sums, pairs, cols = meet("own", HERE, [((OWN,), HERE, False, None), ((CORE,), HERE, False, "core0")], weight=2**33)

    blocks[PAIR], _ = lax.optimization_barrier((blocks[PAIR], sums[0]))
    blocks[ROW], blocks[NEXT] = lax.optimization_barrier((blocks[ROW], blocks[NEXT]))
    blocks[FAR] = move(same, TO_MIDDLE)
    blocks[PAIR_ROW] = move(blocks[PAIR], STAY, row=1)
    blocks[PAIR_CORE] = move(blocks[PAIR], STAY, core=1)
    blocks[DIAG] = move(blocks[ROW], STAY, core=1)
    sums, pairs, cols = meet(
        "pair", THERE,
        [((PAIR,), THERE, False, None), ((PAIR_CORE,), THERE, False, "core1"), ((NEXT,), HERE, True, None),
         ((NEXT,), THERE, True, None)],
        keep=(NEXT,), weight=2**33,
    )
    sums, pairs, cols = meet(
        "row", ACROSS,
        [((PAIR,), HERE, True, None), ((PAIR,), ACROSS, True, None), ((NEXT,), ACROSS, True, None),
         ((ROW,), HERE, False, "row0"), ((DIAG,), HERE, False, "row1")],
    )
    blocks[PAIR_ROW], _ = lax.optimization_barrier((blocks[PAIR_ROW], sums[0]))
    blocks[PAIR_DIAG] = move(blocks[PAIR_ROW], STAY, core=1)
    sums, pairs, cols = meet(
        "far", (), [((FAR,), p, True, None) for p in (HERE, THERE, ACROSS)], keep=(FAR,)
    )
    sums, pairs, cols = meet(
        "last", (),
        [((NEXT, FAR), right, False, None) for right in (PAIR_ROW, PAIR_DIAG)]
        + [((PAIR_ROW,), THERE, False, "row1"), ((PAIR_DIAG,), THERE, False, "row0")],
        doubted=(PAIR_ROW, PAIR_DIAG),
    )
    kept, by_core, to_next, to_far = sums
    from_core, from_far = move(by_core, STAY, core=1), move(to_far, TWO)
    from_core, to_next = lax.optimization_barrier((from_core, to_next))
    from_next = move(to_next, MIDDLE)
    own, pair, row, pair_row = (kept[k:k + 1] + from_core[k:k + 1] for k in (0, 1, 2, 3))
    home = [
        own, from_next, from_far,
        move(pair_row, OUTER, row=1), move(row, STAY, row=1), move(pair, OUTER),
    ]
    return lax.cond(
        decide(flag, to_far, from_far)[0] > 0,
        lambda states, proj_weight, cluster_of, *_: ring_plan(states, proj_weight, cluster_of),
        lambda states, proj_weight, cluster_of, slot, *home: finish(slot, home).reshape(docs),
        states, proj_weight, cluster_of, slot, *home,
    )


def on_device(states, proj_weight, cluster_of):
    if (lax.axis_size("owner"), lax.axis_size("split")) == (8, 2) and states.shape[0] == 512:
        return meeting_plan(states, proj_weight, cluster_of)
    return owner_plan(states, proj_weight, cluster_of)


def solution(mesh):
    placed = (P(("parts", "owner", "split"), None), P(), P(("parts", "owner", "split")))
    return jax.shard_map(
        on_device,
        mesh=mesh,
        in_specs=placed,
        out_specs=P(("parts", "owner", "split")),
        check_vma=False,
    )
```
